32 devices in a mesh: dp: 8 (over z, y), head: 4 (over x, core).
Axes of the slice: x: 2, y: 2, z: 4, core: 2. Of those that a mesh axis runs over, the one named last changes fastest.
Arguments:
- tokens: bfloat16 [8192, 960], P(('dp', 'head')), may hold values from -6 to 6
- cotangent: bfloat16 [8192, 960], P(('dp', 'head')), may hold values from -6 to 6
- lengths: int32 [8], P('dp'), may hold values from 769 to 1024, as said below
- attn_gain: bfloat16 [960], replicated, may hold values from 0.25 to 1.75
- w_query: bfloat16 [960, 960], replicated, may hold values from -0.1875 to 0.1875
- w_key: bfloat16 [960, 320], replicated, may hold values from -0.1875 to 0.1875
- w_value: bfloat16 [960, 320], replicated, may hold values from -0.1875 to 0.1875
- w_output: bfloat16 [960, 960], replicated, may hold values from -2 to 2
- ffn_gain: bfloat16 [960], replicated, may hold values from 0.25 to 1.75
- w_gate: bfloat16 [960, 2560], P(None, 'head'), may hold values from -0.1875 to 0.1875
- w_up: bfloat16 [960, 2560], P(None, 'head'), may hold values from -0.1875 to 0.1875
- w_down: bfloat16 [2560, 960], P('head'), may hold values from -0.125 to 0.125
Outputs:
- block_out: bfloat16 [8192, 960], P(('dp', 'head'))
- input_grad: float32 [8192, 960], P(('dp', 'head'))
- attn_gain_grad: float32 [960], P('dp')
- w_query_grad: float32 [960, 960], P('dp')
- w_key_grad: float32 [960, 320], P('dp')
- w_value_grad: float32 [960, 320], P('dp')
- w_output_grad: float32 [960, 960], P(None, 'dp')
- ffn_gain_grad: float32 [960], P('dp')
- w_gate_grad: float32 [960, 2560], P('dp', 'head')
- w_up_grad: float32 [960, 2560], P('dp', 'head')
- w_down_grad: float32 [2560, 960], P('head', 'dp')
The draws below stay inside these ranges and needn't reach their ends.
Inputs may be any that keep to these rules, and one draw needn't show every extreme that they name: `lengths`: each sequence's valid tokens cover more than three quarters of its 1024 rows; some sequence is full and some has the fewest allowed.
All inputs are finite; a program needn't handle non-finite values.
Results may differ from the reference program's by a relative error of at most 0.03.
Values may be sent and summed in bfloat16 or wider, within the bound.
A program may use at most 192 MiB of HBM per device.

```python
import jax
import jax.numpy as jnp
from jax import lax

D = 960
HQ = 15
KVH = 5
HD = 64
FF = 2560
SEQ = 1024
SEQS = 8
TOKENS = 8192


def draw_lengths(key, part):
    first_key, second_key = jax.random.split(jax.random.fold_in(key, 11), 2)
    lowest = 3 * SEQ // 4 + 1
    values = jax.random.randint(first_key, (SEQS,), lowest, SEQ + 1)
    order = jax.random.permutation(second_key, SEQS)
    values = jnp.where(order == 0, SEQ, values)
    values = jnp.where(order == 1, lowest, values)
    return values.astype(jnp.int32)


def spiked(values, own_key, source, target, parts, factor):
    owner, partner = [(jnp.arange(values.shape[position]) // (values.shape[position] // parts)).reshape([-1 if axis == position else 1 for axis in range(values.ndim)]) for position in (source, target)]
    chosen = jax.random.permutation(own_key, parts)[partner]
    strong = (owner == chosen) | (owner == (partner + parts // 2) % parts)
    return jnp.where(strong, factor * values, values)


def level_of(stream_key, dims, cuts, least, top_value):
    level, own = 1.0, jax.random.fold_in(stream_key, 6)
    for position, shards_of in cuts:
        heights = jnp.exp(jax.random.uniform(jax.random.fold_in(own, position), (shards_of,), jnp.float32, least / len(cuts), top_value / len(cuts)))
        level = level * jnp.repeat(heights, dims[position] // shards_of).reshape([-1 if axis == position else 1 for axis in range(len(dims))])
    return level


def centred(key, shape, width, limit, shards=(), kind=jnp.bfloat16):
    values = width * jax.random.normal(key, shape, jnp.float32)
    if shards:
        values = values * level_of(key, shape, shards, -0.22, 0.18)
    return jnp.clip(values, -limit, limit).astype(kind)


def noise_with(own_key, dims, scale, limit, cuts, heavy, held_as=jnp.bfloat16):
    result = scale * jax.random.normal(own_key, dims, jnp.float32)
    if cuts:
        result = result * level_of(own_key, dims, cuts, -0.22, 0.18)
    return jnp.clip(spiked(result, jax.random.fold_in(own_key, 3), *heavy), -limit, limit).astype(held_as)


def setup_inputs(seed: int = 0) -> dict:
    arg_keys = jax.random.split(jax.random.key(seed), 13)
    tokens = centred(arg_keys[0], (TOKENS, D), 1.0, 6.0, ((0, 32),))
    cotangent = noise_with(arg_keys[1], (TOKENS, D), 1.0, 6.0, ((0, 32),), (0, 1, 32, 2.75))
    lengths = draw_lengths(jax.random.fold_in(arg_keys[12], 71), 0)
    attn_gain = jnp.clip(1.0 + 0.15 * jax.random.normal(arg_keys[3], (D,), jnp.float32), 0.25, 1.75).astype(jnp.bfloat16)
    w_query = centred(arg_keys[4], (D, HQ * HD), D ** -0.5, 0.1875)
    w_key = centred(arg_keys[5], (D, KVH * HD), D ** -0.5, 0.1875)
    w_value = centred(arg_keys[6], (D, KVH * HD), D ** -0.5, 0.1875)
    w_output = centred(arg_keys[7], (HQ * HD, D), (max(HQ * HD * 8 // SEQ, 1)) ** -0.5, 2.0)
    ffn_gain = jnp.clip(1.0 + 0.15 * jax.random.normal(arg_keys[8], (D,), jnp.float32), 0.25, 1.75).astype(jnp.bfloat16)
    w_gate = centred(arg_keys[9], (D, FF), D ** -0.5, 0.1875, ((1, 4),))
    w_up = centred(arg_keys[10], (D, FF), D ** -0.5, 0.1875, ((1, 4),))
    w_down = centred(arg_keys[11], (FF, D), FF ** -0.5, 0.125, ((0, 4),))
    return dict(tokens=tokens, cotangent=cotangent, lengths=lengths, attn_gain=attn_gain, w_query=w_query, w_key=w_key, w_value=w_value, w_output=w_output, ffn_gain=ffn_gain, w_gate=w_gate, w_up=w_up, w_down=w_down)


EPSILON = 1e-05

@jax.custom_vjp
def low(v):
    return lax.optimization_barrier(v.astype(jnp.bfloat16)).astype(jnp.float32)

@jax.custom_vjp
def low_back(v):
    return v

def low_keep(v):
    return (low(v), None)

def low_pass(kept, grad):
    return (grad,)

def back_keep(v):
    return (v, None)

def back_low(kept, grad):
    return (low(grad),)
low.defvjp(low_keep, low_pass)
low_back.defvjp(back_keep, back_low)

def matmul(left, right):
    return jnp.dot(left, right, preferred_element_type=jnp.float32, precision=lax.Precision.HIGHEST)

def norm_rows(hidden, gain):
    return hidden * lax.rsqrt(lax.optimization_barrier(jnp.mean(hidden * hidden, axis=-1, keepdims=True)) + EPSILON) * gain

def rope_tables():
    half_width = HD // 2
    frequency = 10000.0 ** (-(jnp.arange(half_width, dtype=jnp.float32) * 2.0 / HD))
    angles = jnp.arange(SEQ, dtype=jnp.float32)[:, None] * frequency[None, :]
    return (jnp.cos(angles)[:, None, :], jnp.sin(angles)[:, None, :])

def rotate(heads, cosine, sine_part):
    half_width = HD // 2
    lower_half = heads[..., :half_width]
    upper_half = heads[..., half_width:]
    return jnp.concatenate([lower_half * cosine - upper_half * sine_part, upper_half * cosine + lower_half * sine_part], axis=-1)

def attention(queries, key_heads, value_heads, length):
    block_rows = min(512, SEQ)
    block_count = SEQ // block_rows
    per_group = HQ // KVH
    key_wide = jnp.repeat(key_heads, per_group, axis=1)
    value_wide = jnp.repeat(value_heads, per_group, axis=1)
    key_pos = jnp.arange(SEQ, dtype=jnp.int32)
    query_blocks = queries.reshape(block_count, block_rows, HQ, HD)
    starts = jnp.arange(block_count, dtype=jnp.int32) * block_rows

    def one_block(inputs):
        query_block, row_start = inputs
        scores = low_back(jnp.einsum('bhd,khd->hbk', query_block, key_wide, precision=lax.Precision.HIGHEST) * HD ** (-0.5))
        query_pos = row_start + jnp.arange(block_rows, dtype=jnp.int32)
        allowed = (key_pos[None, :] <= query_pos[:, None]) & (key_pos[None, :] < length)
        scores = jnp.where(allowed[None], scores, -1e+30)
        probability = low(jax.nn.softmax(scores, axis=-1))
        return jnp.einsum('hbk,khd->bhd', probability, value_wide, precision=lax.Precision.HIGHEST)
    attended = lax.map(jax.checkpoint(one_block), (query_blocks, starts))
    return attended.reshape(SEQ, HQ * HD)

def layer_apply(hidden, params, length, cosine, sine_part):
    attn_gain, w_query, w_key, w_value, w_output, ffn_gain, w_gate, w_up, w_down = params
    normed = low(norm_rows(hidden, attn_gain))
    queries = low(rotate(low_back(matmul(normed, w_query)).reshape(SEQ, HQ, HD), cosine, sine_part))
    key_heads = low(rotate(low_back(matmul(normed, w_key)).reshape(SEQ, KVH, HD), cosine, sine_part))
    value_heads = low(low_back(matmul(normed, w_value))).reshape(SEQ, KVH, HD)
    attended = low(low_back(attention(queries, key_heads, value_heads, length)))
    middle = hidden + low_back(matmul(attended, w_output))
    normed_two = low(norm_rows(middle, ffn_gain))
    gate_act = low_back(matmul(normed_two, w_gate))
    up_act = low_back(matmul(normed_two, w_up))
    activated = low(jax.nn.silu(gate_act) * up_act)
    return middle + low_back(matmul(activated, w_down))

def reference(tokens, cotangent, lengths, attn_gain, w_query, w_key, w_value, w_output, ffn_gain, w_gate, w_up, w_down):
    params = tuple((weight.astype(jnp.float32) for weight in (attn_gain, w_query, w_key, w_value, w_output, ffn_gain, w_gate, w_up, w_down)))
    cosine, sine_part = rope_tables()
    token_seqs = tokens.astype(jnp.float32).reshape(SEQS, SEQ, D)
    cot_seqs = cotangent.astype(jnp.float32).reshape(SEQS, SEQ, D)

    def per_sequence(totals, inputs):
        rows_in, rows_cot, length = inputs
        row_mask = (jnp.arange(SEQ, dtype=jnp.int32) < length).astype(jnp.float32)

        def pair_apply(hidden, weights):
            first_out = layer_apply(hidden, weights, length, cosine, sine_part)
            return layer_apply(first_out, weights, length, cosine, sine_part)
        outputs, pullback = jax.vjp(pair_apply, rows_in, params)
        grad_in, grad_weights = pullback(rows_cot * row_mask[:, None])
        totals = jax.tree.map(lambda left, right: left + right, totals, grad_weights)
        return (totals, (outputs, grad_in))
    zero_totals = tuple((jnp.zeros_like(weight) for weight in params))
    totals, (outputs, grad_in) = lax.scan(per_sequence, zero_totals, (token_seqs, cot_seqs, lengths))
    return (outputs.reshape(TOKENS, D).astype(jnp.bfloat16), grad_in.reshape(TOKENS, D), totals[0], totals[1], totals[2], totals[3], totals[4], totals[5], totals[6], totals[7], totals[8])
```

```python
import functools

import jax
import jax.numpy as jnp
from jax import lax
from jax.experimental import pallas as pl
from jax.experimental.pallas import tpu as pltpu
from jax.sharding import PartitionSpec as P

HQ = 15
KVH = 5
HD = 64
HALF = HD // 2
PER_GROUP = HQ // KVH
KV_WIDTH = KVH * HD
EPSILON = 1e-05
SCALE = HD ** (-0.5)
BLOCKED = -1e30
LOW = jnp.bfloat16
HIGH = jnp.float32
VMEM = pl.BlockSpec(memory_space=pltpu.VMEM)
SMEM = pl.BlockSpec(memory_space=pltpu.SMEM)
ANY = pl.BlockSpec(memory_space=pl.ANY)
LIMIT = 58 * 2**20


def nn(left, right):
    return lax.dot_general(left, right, (((1,), (0,)), ((), ())), preferred_element_type=HIGH)


def nt(left, right):
    return lax.dot_general(left, right, (((1,), (1,)), ((), ())), preferred_element_type=HIGH)


def sigmoid(value):
    return 0.5 * (1.0 + jnp.tanh(0.5 * value))


def inverse_rms(rows):
    return lax.rsqrt(jnp.mean(rows * rows, axis=1, keepdims=True) + EPSILON)


def norm_back(values_in, gain, grad_normed, grad_skip):
    inverse = inverse_rms(values_in)
    normal = values_in * inverse
    gain_part = jnp.sum(grad_normed * normal, axis=0, keepdims=True)
    scaled = grad_normed * gain
    back = grad_skip + inverse * (scaled - normal * jnp.mean(scaled * normal, axis=1, keepdims=True))
    return gain_part, back


def turned(columns, cosine, sine, sign, factor):
    parts = []
    for start in range(0, columns.shape[0], HD):
        first = columns[start : start + HALF] * factor
        second = columns[start + HALF : start + HD] * factor
        parts.append(first * cosine - sign * second * sine)
        parts.append(second * cosine + sign * first * sine)
    return jnp.concatenate(parts, axis=0)


def project(hidden, gain, w_query, w_key, w_value, cosine, sine, a_ref, q_ref, kv_ref):
    normed = hidden * inverse_rms(hidden) * gain
    a_ref[...] = normed.T.astype(LOW)
    normed = normed.astype(LOW)
    queries = nn(normed, w_query[...]).T
    q_ref[...] = turned(queries, cosine, sine, 1.0, SCALE).astype(LOW)
    keys = turned(nn(normed, w_key[...]).T, cosine, sine, 1.0, 1.0)
    kv_ref[:, :KV_WIDTH] = keys.T.astype(LOW)
    kv_ref[:, KV_WIDTH:] = nn(normed, w_value[...]).astype(LOW)


def fill_bias(where_ref, bias, rows, blocks):
    me = where_ref[0]
    length = where_ref[1]
    key = lax.broadcasted_iota(jnp.int32, (rows, rows), 0)
    query = lax.broadcasted_iota(jnp.int32, (rows, rows), 1)
    for step in range(blocks):
        other = jnp.bitwise_xor(me, step)
        allowed = other * rows + key < length
        if step == 0:
            allowed &= key <= query
        else:
            allowed &= other < me
        bias[step * rows : (step + 1) * rows] = jnp.where(allowed, 0.0, BLOCKED)


def weights_in(sources, holders, sems):
    copies = []
    for which, (source, holder) in enumerate(zip(sources, holders)):
        for step in range(len(source)):
            copies.append(pltpu.make_async_copy(source[step], holder.at[step], sems.at[which, step]))
    return copies


def qkv_kernel(h_ref, gain_ref, wq_ref, wk_ref, wv_ref, cos_ref, sin_ref, a_ref, q_ref, kv_ref):
    hidden = h_ref[...].astype(HIGH)
    gain = gain_ref[...].astype(HIGH)
    project(hidden, gain, wq_ref, wk_ref, wv_ref, cos_ref[...], sin_ref[...], a_ref, q_ref, kv_ref)


def forward_kernel(last, blocks, *refs):
    where_ref, h_ref, q_ref = refs[:3]
    kv_refs = refs[3 : 3 + blocks]
    refs = refs[3 + blocks :]
    wo_ref, gain_two_ref = refs[:2]
    wg_any, wu_any, wd_any = (refs[2 + i * blocks : 2 + (i + 1) * blocks] for i in range(3))
    refs = refs[2 + 3 * blocks :]
    if not last:
        gain_one_ref, wq_ref, wk_ref, wv_ref, cos_ref, sin_ref = refs[:6]
        refs = refs[6:]
    o_ref, lse_ref, m_ref, b_ref, g_ref, u_ref, out_ref = refs[:7]
    refs = refs[7:]
    if not last:
        next_a, next_q, next_kv = refs[:3]
        refs = refs[3:]
    bias, k_sc, vt_sc, wg, wu, wd, sems = refs
    rows = h_ref.shape[0]
    copies = weights_in((wg_any, wu_any, wd_any), (wg, wu, wd), sems)
    for step in range(blocks):
        for which in range(3):
            copies[which * blocks + step].start()
    fill_bias(where_ref, bias, rows, blocks)
    for step in range(blocks):
        held = kv_refs[step][...]
        for group in range(KVH):
            k_sc[group, step * rows : (step + 1) * rows] = held[:, group * HD : (group + 1) * HD]
        vt_sc[:, step * rows : (step + 1) * rows] = held[:, KV_WIDTH:].T

    def group_body(group, carry):
        keys = k_sc[group]
        values = vt_sc[pl.ds(pl.multiple_of(group * HD, HD), HD), :]
        for member in range(PER_GROUP):
            head = group * PER_GROUP + member
            at = pl.ds(pl.multiple_of(head * HD, HD), HD)
            scores = nn(keys, q_ref[at, :]) + bias[...]
            top = jnp.max(scores, axis=0, keepdims=True)
            exponent = jnp.exp(scores - top)
            total = jnp.sum(exponent, axis=0, keepdims=True)
            attended = nn(values, exponent.astype(LOW)) * (1.0 / total)
            o_ref[at, :] = attended.astype(LOW)
            lse_ref[pl.ds(head, 1), :] = top + jnp.log(total)
        return carry

    lax.fori_loop(0, KVH, group_body, 0)
    attended = o_ref[...].T
    middle = h_ref[...].astype(HIGH) + nn(attended, wo_ref[...])
    m_ref[...] = middle
    normed = middle * inverse_rms(middle) * gain_two_ref[...].astype(HIGH)
    b_ref[...] = normed.T.astype(LOW)
    normed = normed.astype(LOW)
    total = middle
    for step in range(blocks):
        copies[step].wait()
        gate = nn(normed, wg[step])
        copies[blocks + step].wait()
        up = nn(normed, wu[step])
        g_ref[step] = gate.astype(LOW)
        u_ref[step] = up.astype(LOW)
        active = (gate * sigmoid(gate) * up).astype(LOW)
        copies[2 * blocks + step].wait()
        total = total + nn(active, wd[step])
    if last:
        out_ref[...] = total.astype(LOW)
    else:
        out_ref[...] = total
        gain_one = gain_one_ref[...].astype(HIGH)
        project(total, gain_one, wq_ref, wk_ref, wv_ref, cos_ref[...], sin_ref[...], next_a, next_q, next_kv)


def backward_kernel(first, blocks, *refs):
    where_ref, e_ref, g_ref, u_ref, m_ref, gain_ref, wo_ref, q_ref = refs[:8]
    kv_refs = refs[8 : 8 + blocks]
    refs = refs[8 + blocks :]
    o_ref, lse_ref, cos_ref, sin_ref = refs[:4]
    wg_any, wu_any, wd_any = (refs[4 + i * blocks : 4 + (i + 1) * blocks] for i in range(3))
    refs = refs[4 + 3 * blocks :]
    f_ref, mine_ref, theirs_ref, c_ref, dm_ref, dq_ref, dkv_ref, gain_part_ref = refs[:8]
    bias, k_sc, v_sc, kt_sc, do_sc, delta, wg, wu, wd, sems = refs[8:]
    rows = m_ref.shape[0]
    copies = weights_in((wg_any, wu_any, wd_any), (wg, wu, wd), sems)
    for step in range(blocks):
        for which in (2, 0, 1):
            copies[which * blocks + step].start()
    fill_bias(where_ref, bias, rows, blocks)
    for step in range(blocks):
        held = kv_refs[step][...]
        for group in range(KVH):
            at = slice(step * rows, (step + 1) * rows)
            k_sc[group, at] = held[:, group * HD : (group + 1) * HD]
            v_sc[group, at] = held[:, KV_WIDTH + group * HD : KV_WIDTH + (group + 1) * HD]
        kt_sc[:, step * rows : (step + 1) * rows] = held[:, :KV_WIDTH].T
    grad = e_ref[...].astype(HIGH)
    if first:
        row = where_ref[0] * rows + lax.broadcasted_iota(jnp.int32, (rows, 1), 0)
        grad = jnp.where(row < where_ref[1], grad, 0.0)
    f_ref[...] = grad.T.astype(LOW)
    low_grad = grad.astype(LOW)
    grad_normed = jnp.zeros(m_ref.shape, HIGH)
    for step in range(blocks):
        copies[2 * blocks + step].wait()
        grad_active = nt(low_grad, wd[step])
        gate = g_ref[step].astype(HIGH)
        up = u_ref[step].astype(HIGH)
        sig = sigmoid(gate)
        silu = gate * sig
        grad_gate = (grad_active * up * sig * (1.0 + gate * (1.0 - sig))).astype(LOW)
        grad_up = (grad_active * silu).astype(LOW)
        kept = mine_ref if step % 2 == 0 else theirs_ref
        kept[step // 2] = grad_gate
        kept[2 + step // 2] = grad_up
        kept[4 + step // 2] = (silu * up).astype(LOW)
        copies[step].wait()
        copies[blocks + step].wait()
        grad_normed = grad_normed + nt(grad_gate, wg[step]) + nt(grad_up, wu[step])
    gain_part, grad_middle = norm_back(m_ref[...], gain_ref[...].astype(HIGH), grad_normed, grad)
    gain_part_ref[...] = gain_part
    dm_ref[...] = grad_middle
    c_ref[...] = grad_middle.T.astype(LOW)
    do_sc[...] = nt(wo_ref[...], grad_middle.astype(LOW)).astype(LOW)
    for head in range(HQ):
        at = slice(head * HD, (head + 1) * HD)
        product = do_sc[at].astype(HIGH) * o_ref[at].astype(HIGH)
        delta[head : head + 1] = jnp.sum(product, axis=0, keepdims=True)
    cosine = cos_ref[...]
    sine = sin_ref[...]

    def group_body(group, carry):
        keys = k_sc[group]
        values = v_sc[group]
        keys_t = kt_sc[pl.ds(pl.multiple_of(group * HD, HD), HD), :]
        grad_keys = jnp.zeros((HD, blocks * rows), HIGH)
        grad_values = jnp.zeros((HD, blocks * rows), HIGH)
        for member in range(PER_GROUP):
            head = group * PER_GROUP + member
            at = pl.ds(pl.multiple_of(head * HD, HD), HD)
            query = q_ref[at, :]
            grad_out = do_sc[at, :]
            scores = nn(keys, query) + bias[...]
            prob = jnp.exp(scores - lse_ref[pl.ds(head, 1), :])
            grad_prob = nn(values, grad_out)
            grad_score = (prob * (grad_prob - delta[pl.ds(head, 1), :])).astype(LOW)
            dq_ref[at, :] = turned(nn(keys_t, grad_score), cosine, sine, -1.0, SCALE).astype(LOW)
            grad_keys = grad_keys + nt(query, grad_score)
            grad_values = grad_values + nt(grad_out, prob.astype(LOW))
        at = pl.ds(pl.multiple_of(group * HD, HD), HD)
        after = pl.ds(pl.multiple_of(KV_WIDTH + group * HD, HD), HD)
        for step in range(blocks):
            cut = slice(step * rows, (step + 1) * rows)
            dkv_ref[step, at, :] = grad_keys[:, cut].astype(LOW)
            dkv_ref[step, after, :] = grad_values[:, cut].astype(LOW)
        return carry

    lax.fori_loop(0, KVH, group_body, 0)


def close_kernel(parts, *refs):
    h_ref, gain_ref, dm_ref, dq_ref, wq_ref, wk_ref, wv_ref, cos_ref, sin_ref = refs[:9]
    part_refs = refs[9 : 9 + parts]
    dh_ref, dkv_ref, gain_part_ref = refs[9 + parts :]
    total = part_refs[0][...].astype(HIGH)
    for part in part_refs[1:]:
        total = total + part[...].astype(HIGH)
    dkv_ref[:KV_WIDTH] = turned(total[:KV_WIDTH], cos_ref[...], sin_ref[...], -1.0, 1.0).astype(LOW)
    dkv_ref[KV_WIDTH:] = total[KV_WIDTH:].astype(LOW)
    grad_normed = nn(wq_ref[...], dq_ref[...])
    grad_normed = grad_normed + nn(wk_ref[...], dkv_ref[:KV_WIDTH])
    grad_normed = grad_normed + nn(wv_ref[...], dkv_ref[KV_WIDTH:])
    gain_part, grad_in = norm_back(
        h_ref[...].astype(HIGH), gain_ref[...].astype(HIGH), grad_normed.T, dm_ref[...]
    )
    gain_part_ref[...] = gain_part
    dh_ref[...] = grad_in


def call(body, outs, specs, scratch, name):
    return pl.pallas_call(
        body,
        out_shape=[jax.ShapeDtypeStruct(shape, kind) for shape, kind in outs],
        in_specs=specs,
        out_specs=[VMEM] * len(outs),
        scratch_shapes=scratch,
        compiler_params=pltpu.CompilerParams(vmem_limit_bytes=LIMIT),
        name=name,
    )


def swap(value, distance):
    count = lax.axis_size("head")
    return lax.ppermute(value, "head", [(i, i ^ distance) for i in range(count)])


def scatter_rows(value, axis):
    count = lax.axis_size(axis)
    index = lax.axis_index(axis)
    value = value.reshape((count, value.shape[0] // count) + value.shape[1:])
    bit = 1
    while bit < count:
        mine = (index // bit) % 2
        value = value.reshape((value.shape[0] // 2, 2) + value.shape[1:])
        sent = lax.dynamic_index_in_dim(value, 1 - mine, 1, False)
        kept = lax.dynamic_index_in_dim(value, mine, 1, False)
        got = lax.ppermute(sent, axis, [(i, i ^ bit) for i in range(count)])
        value = kept.astype(HIGH) + got.astype(HIGH)
        bit *= 2
        if bit < count:
            value = value.astype(LOW)
    return value[0]


def shards(
    tokens,
    cotangent,
    lengths,
    attn_gain,
    w_query,
    w_key,
    w_value,
    w_output,
    ffn_gain,
    w_gate,
    w_up,
    w_down,
):
    blocks = lax.axis_size("head")
    me = lax.axis_index("head").astype(jnp.int32)
    low_bit = me % 2
    rows, width = tokens.shape
    hidden = w_gate.shape[1]
    keys = blocks * rows
    where = jnp.stack([me, lengths[0]])
    frequency = 10000.0 ** (-(jnp.arange(HALF, dtype=HIGH) * 2.0 / HD))
    position = (me * rows + jnp.arange(rows, dtype=jnp.int32)).astype(HIGH)
    angles = frequency[:, None] * position[None, :]
    cosine, sine = jnp.cos(angles), jnp.sin(angles)
    gain_one = attn_gain[None, :]
    gain_two = ffn_gain[None, :]

    def everywhere(value):
        across = swap(value, 2)
        return [value, swap(value, 1), across, swap(across, 1)]

    feature_rows = (width, rows)
    project_outs = [(feature_rows, LOW), (feature_rows, LOW), ((rows, 2 * KV_WIDTH), LOW)]
    a_one, q_one, kv_one = call(qkv_kernel, project_outs, [VMEM] * 7, [], "open")(
        tokens, gain_one, w_query, w_key, w_value, cosine, sine
    )
    kv_one = everywhere(kv_one)
    gates, ups, downs = everywhere(w_gate), everywhere(w_up), everywhere(w_down)
    weight_scratch = [
        pltpu.VMEM((blocks, width, hidden), LOW),
        pltpu.VMEM((blocks, width, hidden), LOW),
        pltpu.VMEM((blocks, hidden, width), LOW),
        pltpu.SemaphoreType.DMA((3, blocks)),
    ]

    def forward(h, queries, kv, last):
        outs = [
            (feature_rows, LOW),
            ((16, rows), HIGH),
            ((rows, width), HIGH),
            (feature_rows, LOW),
            ((blocks, rows, hidden), LOW),
            ((blocks, rows, hidden), LOW),
            ((rows, width), LOW if last else HIGH),
        ]
        specs = [SMEM] + [VMEM] * (4 + blocks) + [ANY] * (3 * blocks)
        given = [where, h, queries, *kv, w_output, gain_two, *gates, *ups, *downs]
        if not last:
            outs += project_outs
            specs += [VMEM] * 6
            given += [gain_one, w_query, w_key, w_value, cosine, sine]
        scratch = [
            pltpu.VMEM((keys, rows), HIGH),
            pltpu.VMEM((KVH, keys, HD), LOW),
            pltpu.VMEM((KV_WIDTH, keys), LOW),
        ] + weight_scratch
        body = functools.partial(forward_kernel, last, blocks)
        return call(body, outs, specs, scratch, "forward_last" if last else "forward_first")(*given)

    def backward(e, kept, first):
        queries, kv, attended, log_totals, middle, gate, up = kept
        outs = [
            (feature_rows, LOW),
            ((6, rows, hidden), LOW),
            ((6, rows, hidden), LOW),
            (feature_rows, LOW),
            ((rows, width), HIGH),
            (feature_rows, LOW),
            ((blocks, 2 * KV_WIDTH, rows), LOW),
            ((1, width), HIGH),
        ]
        specs = [SMEM] + [VMEM] * (11 + blocks) + [ANY] * (3 * blocks)
        given = [where, e, gate, up, middle, gain_two, w_output, queries, *kv, attended, log_totals]
        given += [cosine, sine, *gates, *ups, *downs]
        scratch = [
            pltpu.VMEM((keys, rows), HIGH),
            pltpu.VMEM((KVH, keys, HD), LOW),
            pltpu.VMEM((KVH, keys, HD), LOW),
            pltpu.VMEM((KV_WIDTH, keys), LOW),
            pltpu.VMEM(feature_rows, LOW),
            pltpu.VMEM((16, rows), HIGH),
        ] + weight_scratch
        body = functools.partial(backward_kernel, first, blocks)
        return call(body, outs, specs, scratch, "backward_last" if first else "backward_first")(*given)

    def close(h, grad_middle, grad_query, partial):
        sent = swap(jnp.stack([partial[1], partial[3]]), 1)
        near = sent[0]
        far = swap((partial[2].astype(HIGH) + sent[1].astype(HIGH)).astype(LOW), 2)
        outs = [((rows, width), HIGH), ((2 * KV_WIDTH, rows), LOW), ((1, width), HIGH)]
        given = [h, gain_one, grad_middle, grad_query, w_query, w_key, w_value, cosine, sine]
        given += [partial[0], near, far]
        return call(functools.partial(close_kernel, 3), outs, [VMEM] * 12, [], "close")(*given)

    o_one, lse_one, m_one, b_one, g_one, u_one, h_one, a_two, q_two, kv_two = forward(
        tokens, q_one, kv_one, False
    )
    kv_two = everywhere(kv_two)
    o_two, lse_two, m_two, b_two, g_two, u_two, block_out = forward(h_one, q_two, kv_two, True)
    f_two, mine_two, theirs_two, c_two, dm_two, dq_two, part_two, gain_two_b = backward(
        cotangent, (q_two, kv_two, o_two, lse_two, m_two, g_two, u_two), True
    )
    e_one, dkv_two, gain_one_b = close(h_one, dm_two, dq_two, part_two)
    f_one, mine_one, theirs_one, c_one, dm_one, dq_one, part_one, gain_two_a = backward(
        e_one, (q_one, kv_one, o_one, lse_one, m_one, g_one, u_one), False
    )
    input_grad, dkv_one, gain_one_a = close(tokens, dm_one, dq_one, part_one)

    def beside(parts):
        return jnp.concatenate(parts, axis=-1)

    from_two, from_one = swap(theirs_two, 1), swap(theirs_one, 1)
    b_all = beside([b_two, swap(b_two, 1), b_one, swap(b_one, 1)])
    f_all = beside([f_two, swap(f_two, 1), f_one, swap(f_one, 1)])

    def hidden_rows(which):
        return jnp.concatenate([mine_two[which], from_two[which], mine_one[which], from_one[which]], 0)

    kept, sent = [], []
    for which in range(6):
        product = nn(b_all if which < 4 else f_all, hidden_rows(which)).astype(LOW)
        (sent if which % 2 else kept).append(product)
    got = swap(beside(sent), 2)
    ffn = scatter_rows((beside(kept).astype(HIGH) + got.astype(HIGH)).astype(LOW), "dp")

    def choose(zero, one):
        return jnp.where(low_bit == 0, zero, one)

    lefts, longs, shorts, sides = [], [], [], []
    for a, c, o, dq, dkv in (
        (a_two, c_two, o_two, dq_two, dkv_two),
        (a_one, c_one, o_one, dq_one, dkv_one),
    ):
        dk, dv = dkv[:KV_WIDTH], dkv[KV_WIDTH:]
        lefts += [choose(a, c), swap(choose(c, a), 1)]
        longs += [choose(dq, o), swap(choose(o, dq), 1)]
        shorts += [choose(dk, dv), swap(choose(dv, dk), 1)]
        sides += [a, swap(a, 1)]
    long_part = nt(beside(lefts), beside(longs)).astype(LOW)
    short_part = nt(beside(sides), beside(shorts)).astype(LOW)
    attn = scatter_rows(beside([long_part, short_part]), "dp").astype(LOW)
    attn = (attn.astype(HIGH) + swap(attn, 2).astype(HIGH)).astype(LOW)
    other = swap(attn, 1)
    zero, one = choose(attn, other).astype(HIGH), choose(other, attn).astype(HIGH)
    gains = jnp.concatenate([gain_one_a + gain_one_b, gain_two_a + gain_two_b], axis=0)
    gains = lax.psum_scatter(lax.psum(gains, "head"), "dp", scatter_dimension=1, tiled=True)
    return (
        block_out,
        input_grad,
        gains[0],
        zero[:, : HQ * HD],
        zero[:, HQ * HD :],
        one[:, HQ * HD :],
        one[:, : HQ * HD].T,
        gains[1],
        ffn[:, :hidden],
        ffn[:, hidden : 2 * hidden],
        ffn[:, 2 * hidden :].T,
    )


def solution(mesh):
    return jax.shard_map(
        shards,
        mesh=mesh,
        in_specs=(
            P(("dp", "head"), None),
            P(("dp", "head"), None),
            P("dp"),
            P(),
            P(),
            P(),
            P(),
            P(),
            P(),
            P(None, "head"),
            P(None, "head"),
            P("head", None),
        ),
        out_specs=(
            P(("dp", "head"), None),
            P(("dp", "head"), None),
            P("dp"),
            P("dp", None),
            P("dp", None),
            P("dp", None),
            P(None, "dp"),
            P("dp"),
            P("dp", "head"),
            P("dp", "head"),
            P("head", "dp"),
        ),
        check_vma=False,
    )
```

```python
import functools

import jax
import jax.numpy as jnp
from jax import lax
from jax.experimental import pallas as pl
from jax.experimental.pallas import tpu as pltpu
from jax.sharding import PartitionSpec as P

HQ = 15
KVH = 5
HD = 64
HALF = HD // 2
PER_GROUP = HQ // KVH
KV_WIDTH = KVH * HD
EPSILON = 1e-05
SCALE = HD ** (-0.5)
BLOCKED = -1e30
LOW = jnp.bfloat16
HIGH = jnp.float32
VMEM = pl.BlockSpec(memory_space=pltpu.VMEM)
SMEM = pl.BlockSpec(memory_space=pltpu.SMEM)
ANY = pl.BlockSpec(memory_space=pl.ANY)
LIMIT = 58 * 2**20
MESH = pl.DeviceIdType.MESH


def nn(left, right):
    return lax.dot_general(left, right, (((1,), (0,)), ((), ())), preferred_element_type=HIGH)


def nt(left, right):
    return lax.dot_general(left, right, (((1,), (1,)), ((), ())), preferred_element_type=HIGH)


def sigmoid(value):
    return 0.5 * (1.0 + jnp.tanh(0.5 * value))


def inverse_rms(rows):
    return lax.rsqrt(jnp.mean(rows * rows, axis=1, keepdims=True) + EPSILON)


def norm_back(values_in, gain, grad_normed, grad_skip):
    inverse = inverse_rms(values_in)
    normal = values_in * inverse
    gain_part = jnp.sum(grad_normed * normal, axis=0, keepdims=True)
    scaled = grad_normed * gain
    back = grad_skip + inverse * (scaled - normal * jnp.mean(scaled * normal, axis=1, keepdims=True))
    return gain_part, back


def turned(columns, cosine, sine, sign, factor):
    parts = []
    for start in range(0, columns.shape[0], HD):
        first = columns[start : start + HALF] * factor
        second = columns[start + HALF : start + HD] * factor
        parts.append(first * cosine - sign * second * sine)
        parts.append(second * cosine + sign * first * sine)
    return jnp.concatenate(parts, axis=0)


def project(hidden, gain, w_query, w_key, w_value, cosine, sine, a_ref, q_ref, kv_ref, ready):
    normed = hidden * inverse_rms(hidden) * gain
    low = normed.astype(LOW)
    keys = turned(nn(low, w_key[...]).T, cosine, sine, 1.0, 1.0)
    kv_ref[:, :KV_WIDTH] = keys.T.astype(LOW)
    kv_ref[:, KV_WIDTH:] = nn(low, w_value[...]).astype(LOW)
    ready()
    queries = nn(low, w_query[...]).T
    q_ref[...] = turned(queries, cosine, sine, 1.0, SCALE).astype(LOW)
    a_ref[...] = normed.T.astype(LOW)


def fill_bias(where_ref, bias, rows, blocks):
    me = where_ref[0]
    length = where_ref[1]
    key = lax.broadcasted_iota(jnp.int32, (rows, rows), 0)
    query = lax.broadcasted_iota(jnp.int32, (rows, rows), 1)
    for step in range(blocks):
        other = jnp.bitwise_xor(me, step)
        allowed = other * rows + key < length
        if step == 0:
            allowed &= key <= query
        else:
            allowed &= other < me
        bias[step * rows : (step + 1) * rows] = jnp.where(allowed, 0.0, BLOCKED)


def weights_in(sources, holders, sems, order):
    copies = {}
    for step in range(2):
        for which in order:
            holder = holders[which]
            target = holder.at[0] if step == 0 else holder.at[pl.ds(1, holder.shape[0] - 1)]
            copies[step, which] = pltpu.make_async_copy(sources[2 * which + step], target, sems.at[which, step])
            copies[step, which].start()
    return copies


def attend(bias, k_sc, vt_sc, q_ref, o_ref, lse_ref, event):
    def group_body(group, carry):
        keys = k_sc[group]
        values = vt_sc[pl.ds(pl.multiple_of(group * HD, HD), HD), :]
        event(group)
        for member in range(PER_GROUP):
            head = group * PER_GROUP + member
            at = pl.ds(pl.multiple_of(head * HD, HD), HD)
            scores = nn(keys, q_ref[at, :]) + bias[...]
            top = jnp.max(scores, axis=0, keepdims=True)
            exponent = jnp.exp(scores - top)
            total = jnp.sum(exponent, axis=0, keepdims=True)
            attended = nn(values, exponent.astype(LOW)) * (1.0 / total)
            o_ref[at, :] = attended.astype(LOW)
            lse_ref[pl.ds(head, 1), :] = top + jnp.log(total)
        return carry

    lax.fori_loop(0, KVH, group_body, 0)


def lay_keys(kv_ref, k_sc, vt_sc, blocks, rows):
    for step in range(blocks):
        at = slice(step * rows, (step + 1) * rows)
        for group in range(KVH):
            k_sc[group, at] = kv_ref[step, :, group * HD : (group + 1) * HD]
        vt_sc[:, at] = kv_ref[step, :, KV_WIDTH:].T


def after_attention(h_ref, o_ref, wo_ref, gain_ref, m_ref, b_ref):
    middle = h_ref[...].astype(HIGH) + nn(o_ref[...].T, wo_ref[...])
    m_ref[...] = middle
    normed = middle * inverse_rms(middle) * gain_ref[...].astype(HIGH)
    b_ref[...] = normed.T.astype(LOW)
    return middle, normed.astype(LOW)


def hidden_part(normed, wg, wu, wd, g_ref, u_ref, step):
    gate = nn(normed, wg[step])
    up = nn(normed, wu[step])
    g_ref[step] = gate.astype(LOW)
    u_ref[step] = up.astype(LOW)
    active = (gate * sigmoid(gate) * up).astype(LOW)
    return nn(active, wd[step])


def partner(axis, distance):
    return {axis: jnp.bitwise_xor(lax.axis_index(axis), distance)}


def greet(partners):
    barrier = pltpu.get_barrier_semaphore()
    for axis, distance in partners:
        pl.semaphore_signal(barrier, inc=1, device_id=partner(axis, distance), device_id_type=MESH)
    pl.semaphore_wait(barrier, len(partners))


class Links:
    def __init__(self, send, receive):
        self.send, self.receive, self.used = send, receive, 0
        self.flying = []

    def push(self, source, target, to):
        copy = pltpu.make_async_remote_copy(
            src_ref=source,
            dst_ref=target,
            send_sem=self.send.at[self.used],
            recv_sem=self.receive.at[self.used],
            device_id=partner(*to),
            device_id_type=MESH,
        )
        self.used += 1
        self.flying.append(copy)
        return copy

    def drain(self):
        for copy in self.flying:
            copy.wait_send()


SIBLING, ACROSS, SIDE, BEYOND = ("head", 1), ("head", 2), ("dp", 1), ("dp", 2)


class Share:
    def __init__(self, links, kv_ref):
        self.near = links.push(kv_ref.at[0], kv_ref.at[1], SIBLING)
        self.far = links.push(kv_ref.at[0], kv_ref.at[2], ACROSS)
        self.forth = links.push(kv_ref.at[2], kv_ref.at[3], SIBLING)

    def start(self):
        self.far.start()
        self.near.start()

    def pass_on(self):
        self.far.wait_recv()
        self.forth.start()

    def finish(self):
        self.near.wait_recv()
        self.forth.wait_recv()


class Spread:
    def __init__(self, links, own, all_ref):
        rows = own.shape[0]
        quarter = rows // 4
        cut = quarter // 32 * 16
        place = lax.axis_index("dp") % 4

        def part(ref, which, start=0, size=quarter):
            first = jnp.bitwise_xor(place, which) * quarter + start
            return ref.at[pl.ds(pl.multiple_of(first, 16), size)]

        far, diag = all_ref.at[2], all_ref.at[3]

        def move(which, to, *piece):
            return links.push(part(far, which, *piece), part(far, which, *piece), to)

        def aside(which):
            return links.push(part(far, which), part(diag, which), SIBLING)

        self.near = links.push(own, all_ref.at[1], SIBLING)
        self.cross = links.push(part(own, 0), part(far, 0), ACROSS)
        self.side, self.beyond = move(0, SIDE), move(0, BEYOND)
        self.side_half = move(2, SIDE, cut, quarter - cut)
        self.beyond_half = move(1, BEYOND, 0, cut)
        self.asides = [aside(which) for which in range(4)]

    def start(self):
        self.cross.start()
        self.near.start()

    def first(self):
        self.cross.wait_recv()
        self.side.start()
        self.beyond.start()
        self.asides[0].start()

    def second(self):
        self.side.wait_recv()
        self.beyond_half.start()
        self.asides[1].start()
        self.beyond.wait_recv()
        self.side_half.start()
        self.asides[2].start()

    def third(self):
        self.side_half.wait_recv()
        self.beyond_half.wait_recv()
        self.asides[3].start()

    def last(self):
        for copy in self.asides:
            copy.wait_recv()


COPIES_SHARE = 3
COPIES_SPREAD = 10


def forward_first_kernel(blocks, *refs):
    where_ref, h_ref, gain_one_ref, wq_ref, wk_ref, wv_ref, cos_ref, sin_ref, wo_ref, gain_two_ref = refs[:10]
    owns = refs[10:13]
    a_ref, q_ref, kv_ref, o_ref, lse_ref, m_ref, b_ref, g_ref, u_ref, out_ref = refs[13:23]
    next_a, next_q, next_kv = refs[23:26]
    kept = refs[26:29]
    bias, k_sc, vt_sc, wg, wu, wd, load, save, send, receive = refs[29:]
    rows = h_ref.shape[0]
    links = Links(send, receive)
    held = (wg, wu, wd)
    loads = [pltpu.make_async_copy(own, all_ref.at[0], load.at[i]) for i, (own, all_ref) in enumerate(zip(owns, held))]
    spreads = [Spread(links, own, all_ref) for own, all_ref in zip(owns, held)]
    shares = [Share(links, ref) for ref in (kv_ref, next_kv)]
    greet((SIBLING, ACROSS, SIDE, BEYOND))
    for spread, copy in zip(spreads, loads):
        spread.start()
        copy.start()
    cosine, sine = cos_ref[...], sin_ref[...]
    gain_one = gain_one_ref[...].astype(HIGH)
    project(h_ref[...].astype(HIGH), gain_one, wq_ref, wk_ref, wv_ref, cosine, sine, a_ref, q_ref, kv_ref.at[0], shares[0].start)
    spreads[0].first()
    fill_bias(where_ref, bias, rows, blocks)
    shares[0].pass_on()
    spreads[1].first()
    shares[0].finish()
    lay_keys(kv_ref, k_sc, vt_sc, blocks, rows)
    events = {0: spreads[2].first, 2: spreads[0].second, 3: spreads[1].second, 4: spreads[2].second}

    def event(group):
        for when, action in events.items():
            pl.when(group == when)(action)

    attend(bias, k_sc, vt_sc, q_ref, o_ref, lse_ref, event)
    middle, normed = after_attention(h_ref, o_ref, wo_ref, gain_two_ref, m_ref, b_ref)
    saves = []

    def keep(step):
        for which in range(3):
            copy = pltpu.make_async_copy(held[which].at[step], kept[which].at[step - 1], save.at[which, step - 1])
            copy.start()
            saves.append(copy)

    for copy in loads:
        copy.wait()
    total = middle + hidden_part(normed, wg, wu, wd, g_ref, u_ref, 0)
    for spread in spreads:
        spread.third()
        spread.near.wait_recv()
    keep(1)
    total = total + hidden_part(normed, wg, wu, wd, g_ref, u_ref, 1)
    keep(2)
    total = total + hidden_part(normed, wg, wu, wd, g_ref, u_ref, 2)
    for spread in spreads:
        spread.last()
    keep(3)
    total = total + hidden_part(normed, wg, wu, wd, g_ref, u_ref, 3)
    out_ref[...] = total
    project(total, gain_one, wq_ref, wk_ref, wv_ref, cosine, sine, next_a, next_q, next_kv.at[0], shares[1].start)
    shares[1].pass_on()
    shares[1].finish()
    for copy in saves:
        copy.wait()
    links.drain()


def forward_last_kernel(blocks, *refs):
    where_ref, h_ref, q_ref, kv_ref, wo_ref, gain_two_ref = refs[:6]
    sources = refs[6:12]
    o_ref, lse_ref, m_ref, b_ref, g_ref, u_ref, out_ref = refs[12:19]
    bias, k_sc, vt_sc, wg, wu, wd, sems = refs[19:]
    rows = h_ref.shape[0]
    copies = weights_in(sources, (wg, wu, wd), sems, (0, 1, 2))
    fill_bias(where_ref, bias, rows, blocks)
    lay_keys(kv_ref, k_sc, vt_sc, blocks, rows)
    attend(bias, k_sc, vt_sc, q_ref, o_ref, lse_ref, lambda group: None)
    total, normed = after_attention(h_ref, o_ref, wo_ref, gain_two_ref, m_ref, b_ref)
    for step in range(blocks):
        if step < 2:
            for which in range(3):
                copies[step, which].wait()
        total = total + hidden_part(normed, wg, wu, wd, g_ref, u_ref, step)
    out_ref[...] = total.astype(LOW)


def backward_kernel(first, blocks, *refs):
    where_ref, e_ref, g_ref, u_ref, m_ref, gain_ref, wo_ref, q_ref, kv_ref = refs[:9]
    o_ref, lse_ref, cos_ref, sin_ref = refs[9:13]
    sources = refs[13:19]
    f_ref, mine_ref, theirs_ref, c_ref, dm_ref, dq_ref, dkv_ref, gain_part_ref = refs[19:27]
    bias, k_sc, v_sc, kt_sc, do_sc, delta, wg, wu, wd, sems = refs[27:]
    rows = m_ref.shape[0]
    copies = weights_in(sources, (wg, wu, wd), sems, (2, 0, 1))
    fill_bias(where_ref, bias, rows, blocks)
    for step in range(blocks):
        held = kv_ref[step]
        for group in range(KVH):
            at = slice(step * rows, (step + 1) * rows)
            k_sc[group, at] = held[:, group * HD : (group + 1) * HD]
            v_sc[group, at] = held[:, KV_WIDTH + group * HD : KV_WIDTH + (group + 1) * HD]
        kt_sc[:, step * rows : (step + 1) * rows] = held[:, :KV_WIDTH].T
    grad = e_ref[...].astype(HIGH)
    if first:
        row = where_ref[0] * rows + lax.broadcasted_iota(jnp.int32, (rows, 1), 0)
        grad = jnp.where(row < where_ref[1], grad, 0.0)
    f_ref[...] = grad.T.astype(LOW)
    low_grad = grad.astype(LOW)
    grad_normed = jnp.zeros(m_ref.shape, HIGH)
    for step in range(blocks):
        if step < 2:
            copies[step, 2].wait()
        grad_active = nt(low_grad, wd[step])
        gate = g_ref[step].astype(HIGH)
        up = u_ref[step].astype(HIGH)
        sig = sigmoid(gate)
        silu = gate * sig
        grad_gate = (grad_active * up * sig * (1.0 + gate * (1.0 - sig))).astype(LOW)
        grad_up = (grad_active * silu).astype(LOW)
        kept = mine_ref if step % 2 == 0 else theirs_ref
        kept[step // 2] = grad_gate
        kept[2 + step // 2] = grad_up
        kept[4 + step // 2] = (silu * up).astype(LOW)
        if step < 2:
            copies[step, 0].wait()
            copies[step, 1].wait()
        grad_normed = grad_normed + nt(grad_gate, wg[step]) + nt(grad_up, wu[step])
    gain_part, grad_middle = norm_back(m_ref[...], gain_ref[...].astype(HIGH), grad_normed, grad)
    gain_part_ref[...] = gain_part
    dm_ref[...] = grad_middle
    c_ref[...] = grad_middle.T.astype(LOW)
    do_sc[...] = nt(wo_ref[...], grad_middle.astype(LOW)).astype(LOW)
    for head in range(HQ):
        at = slice(head * HD, (head + 1) * HD)
        product = do_sc[at].astype(HIGH) * o_ref[at].astype(HIGH)
        delta[head : head + 1] = jnp.sum(product, axis=0, keepdims=True)
    cosine = cos_ref[...]
    sine = sin_ref[...]

    def group_body(group, carry):
        keys = k_sc[group]
        values = v_sc[group]
        keys_t = kt_sc[pl.ds(pl.multiple_of(group * HD, HD), HD), :]
        grad_keys = jnp.zeros((HD, blocks * rows), HIGH)
        grad_values = jnp.zeros((HD, blocks * rows), HIGH)
        for member in range(PER_GROUP):
            head = group * PER_GROUP + member
            at = pl.ds(pl.multiple_of(head * HD, HD), HD)
            query = q_ref[at, :]
            grad_out = do_sc[at, :]
            scores = nn(keys, query) + bias[...]
            prob = jnp.exp(scores - lse_ref[pl.ds(head, 1), :])
            grad_prob = nn(values, grad_out)
            grad_score = (prob * (grad_prob - delta[pl.ds(head, 1), :])).astype(LOW)
            dq_ref[at, :] = turned(nn(keys_t, grad_score), cosine, sine, -1.0, SCALE).astype(LOW)
            grad_keys = grad_keys + nt(query, grad_score)
            grad_values = grad_values + nt(grad_out, prob.astype(LOW))
        at = pl.ds(pl.multiple_of(group * HD, HD), HD)
        after = pl.ds(pl.multiple_of(KV_WIDTH + group * HD, HD), HD)
        for step in range(blocks):
            cut = slice(step * rows, (step + 1) * rows)
            dkv_ref[step, at, :] = grad_keys[:, cut].astype(LOW)
            dkv_ref[step, after, :] = grad_values[:, cut].astype(LOW)
        return carry

    lax.fori_loop(0, KVH, group_body, 0)


def close_kernel(parts, *refs):
    h_ref, gain_ref, dm_ref, dq_ref, wq_ref, wk_ref, wv_ref, cos_ref, sin_ref = refs[:9]
    part_refs = refs[9 : 9 + parts]
    dh_ref, dkv_ref, gain_part_ref = refs[9 + parts :]
    total = part_refs[0][...].astype(HIGH)
    for part in part_refs[1:]:
        total = total + part[...].astype(HIGH)
    dkv_ref[:KV_WIDTH] = turned(total[:KV_WIDTH], cos_ref[...], sin_ref[...], -1.0, 1.0).astype(LOW)
    dkv_ref[KV_WIDTH:] = total[KV_WIDTH:].astype(LOW)
    grad_normed = nn(wq_ref[...], dq_ref[...])
    grad_normed = grad_normed + nn(wk_ref[...], dkv_ref[:KV_WIDTH])
    grad_normed = grad_normed + nn(wv_ref[...], dkv_ref[KV_WIDTH:])
    gain_part, grad_in = norm_back(
        h_ref[...].astype(HIGH), gain_ref[...].astype(HIGH), grad_normed.T, dm_ref[...]
    )
    gain_part_ref[...] = gain_part
    dh_ref[...] = grad_in


def call(body, outs, specs, scratch, name, spots=0, collective=None):
    params = {"vmem_limit_bytes": LIMIT}
    if collective is not None:
        params.update(collective_id=collective, has_side_effects=True)
    return pl.pallas_call(
        body,
        out_shape=[jax.ShapeDtypeStruct(shape, kind) for shape, kind in outs],
        in_specs=specs,
        out_specs=[VMEM] * (len(outs) - spots) + [ANY] * spots,
        scratch_shapes=scratch,
        compiler_params=pltpu.CompilerParams(**params),
        name=name,
    )


def swap(value, distance):
    count = lax.axis_size("head")
    return lax.ppermute(value, "head", [(i, i ^ distance) for i in range(count)])


def scatter_rows(value, axis):
    count = lax.axis_size(axis)
    index = lax.axis_index(axis)
    value = value.reshape((count, value.shape[0] // count) + value.shape[1:])
    bit = 1
    while bit < count:
        mine = (index // bit) % 2
        value = value.reshape((value.shape[0] // 2, 2) + value.shape[1:])
        sent = lax.dynamic_index_in_dim(value, 1 - mine, 1, False)
        kept = lax.dynamic_index_in_dim(value, mine, 1, False)
        got = lax.ppermute(sent, axis, [(i, i ^ bit) for i in range(count)])
        value = kept.astype(HIGH) + got.astype(HIGH)
        bit *= 2
        if bit < count:
            value = value.astype(LOW)
    return value[0]


def shards(
    tokens,
    cotangent,
    lengths,
    attn_gain,
    w_query,
    w_key,
    w_value,
    w_output,
    ffn_gain,
    w_gate,
    w_up,
    w_down,
):
    blocks = lax.axis_size("head")
    me = lax.axis_index("head").astype(jnp.int32)
    low_bit = me % 2
    rows, width = tokens.shape
    hidden = w_gate.shape[1]
    keys = blocks * rows
    where = jnp.stack([me, lengths[0]])
    frequency = 10000.0 ** (-(jnp.arange(HALF, dtype=HIGH) * 2.0 / HD))
    position = (me * rows + jnp.arange(rows, dtype=jnp.int32)).astype(HIGH)
    angles = frequency[:, None] * position[None, :]
    cosine, sine = jnp.cos(angles), jnp.sin(angles)
    gain_one = attn_gain[None, :]
    gain_two = ffn_gain[None, :]

    feature_rows = (width, rows)
    project_outs = [(feature_rows, LOW), (feature_rows, LOW), ((blocks, rows, 2 * KV_WIDTH), LOW)]
    weight_shapes = [(width, hidden), (width, hidden), (hidden, width)]
    weight_room = [pltpu.VMEM((blocks,) + shape, LOW) for shape in weight_shapes]
    attend_room = [
        pltpu.VMEM((keys, rows), HIGH),
        pltpu.VMEM((KVH, keys, HD), LOW),
        pltpu.VMEM((KV_WIDTH, keys), LOW),
    ]
    layer_outs = [
        (feature_rows, LOW),
        ((16, rows), HIGH),
        ((rows, width), HIGH),
        (feature_rows, LOW),
        ((blocks, rows, hidden), LOW),
        ((blocks, rows, hidden), LOW),
    ]

    def forward_first():
        outs = project_outs + layer_outs + [((rows, width), HIGH)] + project_outs
        outs += [((blocks - 1,) + shape, LOW) for shape in weight_shapes]
        copies = 3 * COPIES_SPREAD + 2 * COPIES_SHARE
        scratch = attend_room + weight_room
        scratch += [pltpu.SemaphoreType.DMA((3,)), pltpu.SemaphoreType.DMA((3, blocks - 1))]
        scratch += [pltpu.SemaphoreType.DMA((copies,)), pltpu.SemaphoreType.DMA((copies,))]
        body = functools.partial(forward_first_kernel, blocks)
        specs = [SMEM] + [VMEM] * 9 + [ANY] * 3
        return call(body, outs, specs, scratch, "forward_first", 3, 1)(
            where, tokens, gain_one, w_query, w_key, w_value, cosine, sine, w_output, gain_two, w_gate, w_up, w_down
        )

    outs = forward_first()
    a_one, q_one, kv_one, o_one, lse_one, m_one, b_one, g_one, u_one, h_one, a_two, q_two, kv_two = outs[:13]
    weights = [w_gate, outs[13], w_up, outs[14], w_down, outs[15]]
    weight_scratch = weight_room + [pltpu.SemaphoreType.DMA((3, 2))]

    def forward_last():
        specs = [SMEM] + [VMEM] * 5 + [ANY] * 6
        body = functools.partial(forward_last_kernel, blocks)
        outs = layer_outs + [((rows, width), LOW)]
        return call(body, outs, specs, attend_room + weight_scratch, "forward_last")(
            where, h_one, q_two, kv_two, w_output, gain_two, *weights
        )

    def backward(e, kept, first):
        queries, kv, attended, log_totals, middle, gate, up = kept
        outs = [
            (feature_rows, LOW),
            ((6, rows, hidden), LOW),
            ((6, rows, hidden), LOW),
            (feature_rows, LOW),
            ((rows, width), HIGH),
            (feature_rows, LOW),
            ((blocks, 2 * KV_WIDTH, rows), LOW),
            ((1, width), HIGH),
        ]
        specs = [SMEM] + [VMEM] * 12 + [ANY] * 6
        given = [where, e, gate, up, middle, gain_two, w_output, queries, kv, attended, log_totals]
        given += [cosine, sine, *weights]
        scratch = [
            pltpu.VMEM((keys, rows), HIGH),
            pltpu.VMEM((KVH, keys, HD), LOW),
            pltpu.VMEM((KVH, keys, HD), LOW),
            pltpu.VMEM((KV_WIDTH, keys), LOW),
            pltpu.VMEM(feature_rows, LOW),
            pltpu.VMEM((16, rows), HIGH),
        ] + weight_scratch
        body = functools.partial(backward_kernel, first, blocks)
        return call(body, outs, specs, scratch, "backward_last" if first else "backward_first")(*given)

    def close(h, grad_middle, grad_query, partial):
        sent = swap(jnp.stack([partial[1], partial[3]]), 1)
        near = sent[0]
        far = swap((partial[2].astype(HIGH) + sent[1].astype(HIGH)).astype(LOW), 2)
        outs = [((rows, width), HIGH), ((2 * KV_WIDTH, rows), LOW), ((1, width), HIGH)]
        given = [h, gain_one, grad_middle, grad_query, w_query, w_key, w_value, cosine, sine]
        given += [partial[0], near, far]
        return call(functools.partial(close_kernel, 3), outs, [VMEM] * 12, [], "close")(*given)

    o_two, lse_two, m_two, b_two, g_two, u_two, block_out = forward_last()
    f_two, mine_two, theirs_two, c_two, dm_two, dq_two, part_two, gain_two_b = backward(
        cotangent, (q_two, kv_two, o_two, lse_two, m_two, g_two, u_two), True
    )
    e_one, dkv_two, gain_one_b = close(h_one, dm_two, dq_two, part_two)
    f_one, mine_one, theirs_one, c_one, dm_one, dq_one, part_one, gain_two_a = backward(
        e_one, (q_one, kv_one, o_one, lse_one, m_one, g_one, u_one), False
    )
    input_grad, dkv_one, gain_one_a = close(tokens, dm_one, dq_one, part_one)

    def beside(parts):
        return jnp.concatenate(parts, axis=-1)

    from_two, from_one = swap(theirs_two, 1), swap(theirs_one, 1)
    b_all = beside([b_two, swap(b_two, 1), b_one, swap(b_one, 1)])
    f_all = beside([f_two, swap(f_two, 1), f_one, swap(f_one, 1)])

    def hidden_rows(which):
        return jnp.concatenate([mine_two[which], from_two[which], mine_one[which], from_one[which]], 0)

    kept, sent = [], []
    for which in range(6):
        product = nn(b_all if which < 4 else f_all, hidden_rows(which)).astype(LOW)
        (sent if which % 2 else kept).append(product)
    got = swap(beside(sent), 2)
    ffn = scatter_rows((beside(kept).astype(HIGH) + got.astype(HIGH)).astype(LOW), "dp")

    def choose(zero, one):
        return jnp.where(low_bit == 0, zero, one)

    lefts, longs, shorts, sides = [], [], [], []
    for a, c, o, dq, dkv in (
        (a_two, c_two, o_two, dq_two, dkv_two),
        (a_one, c_one, o_one, dq_one, dkv_one),
    ):
        dk, dv = dkv[:KV_WIDTH], dkv[KV_WIDTH:]
        lefts += [choose(a, c), swap(choose(c, a), 1)]
        longs += [choose(dq, o), swap(choose(o, dq), 1)]
        shorts += [choose(dk, dv), swap(choose(dv, dk), 1)]
        sides += [a, swap(a, 1)]
    long_part = nt(beside(lefts), beside(longs)).astype(LOW)
    short_part = nt(beside(sides), beside(shorts)).astype(LOW)
    attn = scatter_rows(beside([long_part, short_part]), "dp").astype(LOW)
    attn = (attn.astype(HIGH) + swap(attn, 2).astype(HIGH)).astype(LOW)
    other = swap(attn, 1)
    zero, one = choose(attn, other).astype(HIGH), choose(other, attn).astype(HIGH)
    gains = jnp.concatenate([gain_one_a + gain_one_b, gain_two_a + gain_two_b], axis=0)
    gains = lax.psum_scatter(lax.psum(gains, "head"), "dp", scatter_dimension=1, tiled=True)
    return (
        block_out,
        input_grad,
        gains[0],
        zero[:, : HQ * HD],
        zero[:, HQ * HD :],
        one[:, HQ * HD :],
        one[:, : HQ * HD].T,
        gains[1],
        ffn[:, :hidden],
        ffn[:, hidden : 2 * hidden],
        ffn[:, 2 * hidden :].T,
    )


def solution(mesh):
    return jax.shard_map(
        shards,
        mesh=mesh,
        in_specs=(
            P(("dp", "head"), None),
            P(("dp", "head"), None),
            P("dp"),
            P(),
            P(),
            P(),
            P(),
            P(),
            P(),
            P(None, "head"),
            P(None, "head"),
            P("head", None),
        ),
        out_specs=(
            P(("dp", "head"), None),
            P(("dp", "head"), None),
            P("dp"),
            P("dp", None),
            P("dp", None),
            P("dp", None),
            P(None, "dp"),
            P("dp"),
            P("dp", "head"),
            P("dp", "head"),
            P("head", "dp"),
        ),
        check_vma=False,
    )
```

```python
import functools

import jax
import jax.numpy as jnp
from jax import lax
from jax.experimental import pallas as pl
from jax.experimental.pallas import tpu as pltpu
from jax.sharding import PartitionSpec as P

HQ = 15
KVH = 5
HD = 64
HALF = HD // 2
PER_GROUP = HQ // KVH
KV_WIDTH = KVH * HD
EPSILON = 1e-05
SCALE = HD ** (-0.5)
BLOCKED = -1e30
LOW = jnp.bfloat16
HIGH = jnp.float32
VMEM = pl.BlockSpec(memory_space=pltpu.VMEM)
SMEM = pl.BlockSpec(memory_space=pltpu.SMEM)
ANY = pl.BlockSpec(memory_space=pl.ANY)
LIMIT = 60 * 2**20
MESH = pl.DeviceIdType.MESH


def nn(left, right):
    return lax.dot_general(left, right, (((1,), (0,)), ((), ())), preferred_element_type=HIGH)


def nt(left, right):
    return lax.dot_general(left, right, (((1,), (1,)), ((), ())), preferred_element_type=HIGH)


def sigmoid(value):
    return 0.5 * (1.0 + jnp.tanh(0.5 * value))


def inverse_rms(rows):
    return lax.rsqrt(jnp.mean(rows * rows, axis=1, keepdims=True) + EPSILON)


def norm_back(values_in, gain, grad_normed, grad_skip):
    inverse = inverse_rms(values_in)
    normal = values_in * inverse
    gain_part = jnp.sum(grad_normed * normal, axis=0, keepdims=True)
    scaled = grad_normed * gain
    back = grad_skip + inverse * (scaled - normal * jnp.mean(scaled * normal, axis=1, keepdims=True))
    return gain_part, back


def turned(columns, cosine, sine, sign, factor):
    parts = []
    for start in range(0, columns.shape[0], HD):
        first = columns[start : start + HALF] * factor
        second = columns[start + HALF : start + HD] * factor
        parts.append(first * cosine - sign * second * sine)
        parts.append(second * cosine + sign * first * sine)
    return jnp.concatenate(parts, axis=0)


def project(hidden, gain, w_query, w_key, w_value, cosine, sine, a_ref, q_ref, kv_ref, ready):
    normed = hidden * inverse_rms(hidden) * gain
    low = normed.astype(LOW)
    keys = turned(nt(w_key[...], low), cosine, sine, 1.0, 1.0)
    kv_ref[:, :KV_WIDTH] = keys.T.astype(LOW)
    kv_ref[:, KV_WIDTH:] = nt(low, w_value[...]).astype(LOW)
    ready()
    queries = nn(low, w_query[...]).T
    q_ref[...] = turned(queries, cosine, sine, 1.0, SCALE).astype(LOW)
    a_ref[...] = normed.T.astype(LOW)


def fill_bias(where_ref, bias, rows, blocks):
    me = where_ref[0]
    length = where_ref[1]
    key = lax.broadcasted_iota(jnp.int32, (rows, rows), 0)
    query = lax.broadcasted_iota(jnp.int32, (rows, rows), 1)
    for step in range(blocks):
        other = jnp.bitwise_xor(me, step)
        allowed = other * rows + key < length
        if step == 0:
            allowed &= key <= query
        else:
            allowed &= other < me
        bias[step * rows : (step + 1) * rows] = jnp.where(allowed, 0.0, BLOCKED)


def weights_in(sources, holders, sems, order):
    copies = {}
    for step in range(2):
        for which in order:
            holder = holders[which]
            target = holder.at[0] if step == 0 else holder.at[pl.ds(1, holder.shape[0] - 1)]
            copies[step, which] = pltpu.make_async_copy(sources[2 * which + step], target, sems.at[which, step])
            copies[step, which].start()
    return copies


def attend(bias, k_sc, vt_sc, q_ref, o_ref, lse_ref, event):
    def group_body(group, carry):
        keys = k_sc[group]
        values = vt_sc[pl.ds(pl.multiple_of(group * HD, HD), HD), :]
        event(group)
        for member in range(PER_GROUP):
            head = group * PER_GROUP + member
            at = pl.ds(pl.multiple_of(head * HD, HD), HD)
            scores = nn(keys, q_ref[at, :]) + bias[...]
            top = jnp.max(scores, axis=0, keepdims=True)
            exponent = jnp.exp(scores - top)
            total = jnp.sum(exponent, axis=0, keepdims=True)
            attended = nn(values, exponent.astype(LOW)) * (1.0 / total)
            o_ref[at, :] = attended.astype(LOW)
            lse_ref[pl.ds(head, 1), :] = top + jnp.log(total)
        return carry

    lax.fori_loop(0, KVH, group_body, 0)


def lay_keys(kv_ref, k_sc, vt_sc, blocks, rows):
    for step in range(blocks):
        at = slice(step * rows, (step + 1) * rows)
        for group in range(KVH):
            k_sc[group, at] = kv_ref[step, :, group * HD : (group + 1) * HD]
        vt_sc[:, at] = kv_ref[step, :, KV_WIDTH:].T


def after_attention(hidden, o_ref, wo_ref, gain_ref, m_ref, b_ref):
    middle = hidden + nn(o_ref[...].T, wo_ref[...])
    m_ref[...] = middle
    normed = middle * inverse_rms(middle) * gain_ref[...].astype(HIGH)
    b_ref[...] = normed.T.astype(LOW)
    return middle, normed.astype(LOW)


def hidden_part(normed, wg, wu, wd, g_ref, u_ref, step):
    gate = nn(normed, wg[step])
    up = nn(normed, wu[step])
    g_ref[step] = gate.astype(LOW)
    u_ref[step] = up.astype(LOW)
    active = (gate * sigmoid(gate) * up).astype(LOW)
    return nt(active, wd[step])


def partner(axis, distance):
    return {axis: jnp.bitwise_xor(lax.axis_index(axis), distance)}


def greet(partners):
    barrier = pltpu.get_barrier_semaphore()
    for axis, distance in partners:
        pl.semaphore_signal(barrier, inc=1, device_id=partner(axis, distance), device_id_type=MESH)
    pl.semaphore_wait(barrier, len(partners))


class Links:
    def __init__(self, send, receive):
        self.send, self.receive, self.used = send, receive, 0
        self.flying = []

    def push(self, source, target, to):
        copy = pltpu.make_async_remote_copy(
            src_ref=source,
            dst_ref=target,
            send_sem=self.send.at[self.used],
            recv_sem=self.receive.at[self.used],
            device_id=partner(*to),
            device_id_type=MESH,
        )
        self.used += 1
        self.flying.append(copy)
        return copy

    def drain(self):
        for copy in self.flying:
            copy.wait_send()


SIBLING, ACROSS, SIDE, BEYOND = ("head", 1), ("head", 2), ("dp", 1), ("dp", 2)


class Share:
    def __init__(self, links, kv_ref):
        self.near = links.push(kv_ref.at[0], kv_ref.at[1], SIBLING)
        self.far = links.push(kv_ref.at[0], kv_ref.at[2], ACROSS)
        self.forth = links.push(kv_ref.at[2], kv_ref.at[3], SIBLING)

    def start(self):
        self.far.start()
        self.near.start()

    def pass_on(self):
        self.far.wait_recv()
        self.forth.start()

    def finish(self):
        self.near.wait_recv()
        self.forth.wait_recv()


class Spread:
    def __init__(self, links, own, all_ref):
        rows = own.shape[0]
        quarter = rows // 4
        cut = quarter // 32 * 16
        place = lax.axis_index("dp") % 4

        def part(ref, which, start=0, size=quarter):
            first = jnp.bitwise_xor(place, which) * quarter + start
            return ref.at[pl.ds(pl.multiple_of(first, 16), size)]

        far, diag = all_ref.at[2], all_ref.at[3]

        def move(which, to, *piece):
            return links.push(part(far, which, *piece), part(far, which, *piece), to)

        def aside(which):
            return links.push(part(far, which), part(diag, which), SIBLING)

        self.near = links.push(own, all_ref.at[1], SIBLING)
        self.cross = links.push(part(own, 0), part(far, 0), ACROSS)
        self.side, self.beyond = move(0, SIDE), move(0, BEYOND)
        self.side_half = move(2, SIDE, cut, quarter - cut)
        self.beyond_half = move(1, BEYOND, 0, cut)
        self.asides = [aside(which) for which in range(4)]

    def start(self):
        self.cross.start()
        self.near.start()

    def first(self):
        self.cross.wait_recv()
        self.side.start()
        self.beyond.start()
        self.asides[0].start()

    def second(self):
        self.side.wait_recv()
        self.beyond_half.start()
        self.asides[1].start()
        self.beyond.wait_recv()
        self.side_half.start()
        self.asides[2].start()

    def third(self):
        self.side_half.wait_recv()
        self.beyond_half.wait_recv()
        self.asides[3].start()

    def last(self):
        for copy in self.asides:
            copy.wait_recv()


COPIES_SHARE = 3
COPIES_SPREAD = 10


def forward_first_kernel(blocks, *refs):
    where_ref, h_ref, gain_one_ref, wq_ref, wk_ref, wv_ref, cos_ref, sin_ref, wo_ref, gain_two_ref = refs[:10]
    owns = refs[10:13]
    a_ref, q_ref, kv_ref, o_ref, lse_ref, m_ref, b_ref, g_ref, u_ref, out_ref = refs[13:23]
    next_a, next_q, next_kv = refs[23:26]
    kept = refs[26:29]
    bias, k_sc, vt_sc, wg, wu, wd, load, save, send, receive = refs[29:]
    rows = h_ref.shape[1]
    hidden = h_ref[...].astype(HIGH).T
    links = Links(send, receive)
    held = (wg, wu, wd)
    loads = [pltpu.make_async_copy(own, all_ref.at[0], load.at[i]) for i, (own, all_ref) in enumerate(zip(owns, held))]
    spreads = [Spread(links, own, all_ref) for own, all_ref in zip(owns, held)]
    shares = [Share(links, ref) for ref in (kv_ref, next_kv)]
    greet((SIBLING, ACROSS, SIDE, BEYOND))
    for spread, copy in zip(spreads, loads):
        spread.start()
        copy.start()
    cosine, sine = cos_ref[...], sin_ref[...]
    gain_one = gain_one_ref[...].astype(HIGH)
    project(hidden, gain_one, wq_ref, wk_ref, wv_ref, cosine, sine, a_ref, q_ref, kv_ref.at[0], shares[0].start)
    spreads[0].first()
    fill_bias(where_ref, bias, rows, blocks)
    shares[0].pass_on()
    spreads[1].first()
    shares[0].finish()
    lay_keys(kv_ref, k_sc, vt_sc, blocks, rows)
    events = {0: spreads[2].first, 2: spreads[0].second, 3: spreads[1].second, 4: spreads[2].second}

    def event(group):
        for when, action in events.items():
            pl.when(group == when)(action)

    attend(bias, k_sc, vt_sc, q_ref, o_ref, lse_ref, event)
    middle, normed = after_attention(hidden, o_ref, wo_ref, gain_two_ref, m_ref, b_ref)
    saves = []

    def keep(step):
        for which in range(3):
            copy = pltpu.make_async_copy(held[which].at[step], kept[which].at[step - 1], save.at[which, step - 1])
            copy.start()
            saves.append(copy)

    for copy in loads:
        copy.wait()
    total = middle + hidden_part(normed, wg, wu, wd, g_ref, u_ref, 0)
    for spread in spreads:
        spread.third()
        spread.near.wait_recv()
    keep(1)
    total = total + hidden_part(normed, wg, wu, wd, g_ref, u_ref, 1)
    keep(2)
    total = total + hidden_part(normed, wg, wu, wd, g_ref, u_ref, 2)
    for spread in spreads:
        spread.last()
    keep(3)
    total = total + hidden_part(normed, wg, wu, wd, g_ref, u_ref, 3)
    out_ref[...] = total
    project(total, gain_one, wq_ref, wk_ref, wv_ref, cosine, sine, next_a, next_q, next_kv.at[0], shares[1].start)
    shares[1].pass_on()
    shares[1].finish()
    for copy in saves:
        copy.wait()
    links.drain()


def forward_last_kernel(blocks, *refs):
    where_ref, h_ref, q_ref, kv_ref, wo_ref, gain_two_ref = refs[:6]
    sources = refs[6:12]
    o_ref, lse_ref, m_ref, b_ref, g_ref, u_ref, out_ref = refs[12:19]
    bias, k_sc, vt_sc, wg, wu, wd, sems = refs[19:]
    rows = h_ref.shape[0]
    copies = weights_in(sources, (wg, wu, wd), sems, (0, 1, 2))
    fill_bias(where_ref, bias, rows, blocks)
    lay_keys(kv_ref, k_sc, vt_sc, blocks, rows)
    attend(bias, k_sc, vt_sc, q_ref, o_ref, lse_ref, lambda group: None)
    total, normed = after_attention(h_ref[...], o_ref, wo_ref, gain_two_ref, m_ref, b_ref)
    for step in range(blocks):
        if step < 2:
            for which in range(3):
                copies[step, which].wait()
        total = total + hidden_part(normed, wg, wu, wd, g_ref, u_ref, step)
    out_ref[...] = total.T.astype(LOW)


def ffn_back(grad, copies, g_ref, u_ref, m_ref, gain_ref, wg, wu, wd, outs):
    f_ref, mine_ref, theirs_ref, c_ref, dm_ref, gain_part_ref = outs
    f_ref[...] = grad.T.astype(LOW)
    low_grad = grad.astype(LOW)
    grad_normed = jnp.zeros(m_ref.shape, HIGH)
    for step in range(wg.shape[0]):
        if step < 2:
            copies[step, 2].wait()
        grad_active = nn(low_grad, wd[step])
        gate = g_ref[step].astype(HIGH)
        up = u_ref[step].astype(HIGH)
        sig = sigmoid(gate)
        silu = gate * sig
        grad_gate = (grad_active * up * sig * (1.0 + gate * (1.0 - sig))).astype(LOW)
        grad_up = (grad_active * silu).astype(LOW)
        kept = mine_ref if step % 2 == 0 else theirs_ref
        kept[step // 2] = grad_gate
        kept[2 + step // 2] = grad_up
        kept[4 + step // 2] = (silu * up).astype(LOW)
        if step < 2:
            copies[step, 0].wait()
            copies[step, 1].wait()
        grad_normed = grad_normed + nt(grad_gate, wg[step]) + nt(grad_up, wu[step])
    gain_part, grad_middle = norm_back(m_ref[...], gain_ref[...].astype(HIGH), grad_normed, grad)
    gain_part_ref[...] = gain_part
    dm_ref[...] = grad_middle
    c_ref[...] = grad_middle.T.astype(LOW)
    return grad_middle


def attend_back(where_ref, kv_ref, wo_ref, q_ref, o_ref, lse_ref, cosine, sine, grad_middle, dq_ref, dkv_ref, room):
    bias, k_sc, v_sc, kt_sc, do_sc, delta = room
    blocks, rows = kv_ref.shape[:2]
    fill_bias(where_ref, bias, rows, blocks)
    for step in range(blocks):
        at = slice(step * rows, (step + 1) * rows)
        held = kv_ref[step]
        for group in range(KVH):
            k_sc[group, at] = held[:, group * HD : (group + 1) * HD]
            v_sc[group, at] = held[:, KV_WIDTH + group * HD : KV_WIDTH + (group + 1) * HD]
        kt_sc[:, at] = held[:, :KV_WIDTH].T
    do_sc[...] = nt(wo_ref[...], grad_middle.astype(LOW)).astype(LOW)
    for head in range(HQ):
        at = slice(head * HD, (head + 1) * HD)
        product = do_sc[at].astype(HIGH) * o_ref[at].astype(HIGH)
        delta[head : head + 1] = jnp.sum(product, axis=0, keepdims=True)

    def group_body(group, carry):
        keys = k_sc[group]
        values = v_sc[group]
        keys_t = kt_sc[pl.ds(pl.multiple_of(group * HD, HD), HD), :]
        grad_keys = jnp.zeros((HD, blocks * rows), HIGH)
        grad_values = jnp.zeros((HD, blocks * rows), HIGH)
        for member in range(PER_GROUP):
            head = group * PER_GROUP + member
            at = pl.ds(pl.multiple_of(head * HD, HD), HD)
            query = q_ref[at, :]
            grad_out = do_sc[at, :]
            scores = nn(keys, query) + bias[...]
            prob = jnp.exp(scores - lse_ref[pl.ds(head, 1), :])
            grad_prob = nn(values, grad_out)
            grad_score = (prob * (grad_prob - delta[pl.ds(head, 1), :])).astype(LOW)
            dq_ref[at, :] = turned(nn(keys_t, grad_score), cosine, sine, -1.0, SCALE).astype(LOW)
            grad_keys = grad_keys + nt(query, grad_score)
            grad_values = grad_values + nt(grad_out, prob.astype(LOW))
        at = pl.ds(pl.multiple_of(group * HD, HD), HD)
        after = pl.ds(pl.multiple_of(KV_WIDTH + group * HD, HD), HD)
        for step in range(blocks):
            cut = slice(step * rows, (step + 1) * rows)
            dkv_ref[step, at, :] = grad_keys[:, cut].astype(LOW)
            dkv_ref[step, after, :] = grad_values[:, cut].astype(LOW)
        return carry

    lax.fori_loop(0, KVH, group_body, 0)


def attention_room(blocks, rows, width):
    keys = blocks * rows
    return [
        pltpu.VMEM((keys, rows), HIGH),
        pltpu.VMEM((KVH, keys, HD), LOW),
        pltpu.VMEM((KVH, keys, HD), LOW),
        pltpu.VMEM((KV_WIDTH, keys), LOW),
        pltpu.VMEM((width, rows), LOW),
        pltpu.VMEM((16, rows), HIGH),
    ]


def backward_last_kernel(*refs):
    where_ref, e_ref, g_ref, u_ref, m_ref, gain_ref, wo_ref, q_ref, kv_ref = refs[:9]
    o_ref, lse_ref, cos_ref, sin_ref = refs[9:13]
    sources = refs[13:19]
    f_ref, mine_ref, theirs_ref, c_ref, dm_ref, dq_ref, dkv_ref, gain_part_ref = refs[19:27]
    room, (wg, wu, wd, sems) = refs[27:33], refs[33:]
    rows = m_ref.shape[0]
    copies = weights_in(sources, (wg, wu, wd), sems, (2, 0, 1))
    row = where_ref[0] * rows + lax.broadcasted_iota(jnp.int32, (rows, 1), 0)
    grad = jnp.where(row < where_ref[1], e_ref[...].astype(HIGH).T, 0.0)
    outs = (f_ref, mine_ref, theirs_ref, c_ref, dm_ref, gain_part_ref)
    grad_middle = ffn_back(grad, copies, g_ref, u_ref, m_ref, gain_ref, wg, wu, wd, outs)
    attend_back(
        where_ref, kv_ref, wo_ref, q_ref, o_ref, lse_ref, cos_ref[...], sin_ref[...], grad_middle, dq_ref, dkv_ref, room
    )


def ffn_back_kernel(*refs):
    e_ref, g_ref, u_ref, m_ref, gain_ref = refs[:5]
    sources, outs, (wg, wu, wd, sems) = refs[5:11], refs[11:17], refs[17:]
    copies = weights_in(sources, (wg, wu, wd), sems, (2, 0, 1))
    ffn_back(e_ref[...], copies, g_ref, u_ref, m_ref, gain_ref, wg, wu, wd, outs)


def attend_back_kernel(*refs):
    where_ref, dm_ref, wo_ref, q_ref, kv_ref, o_ref, lse_ref, cos_ref, sin_ref, dq_ref, dkv_ref = refs[:11]
    attend_back(
        where_ref, kv_ref, wo_ref, q_ref, o_ref, lse_ref, cos_ref[...], sin_ref[...], dm_ref[...], dq_ref, dkv_ref, refs[11:]
    )


def close_keys(total, cosine, sine, dkv_ref):
    turned_keys = turned(total[:KV_WIDTH], cosine, sine, -1.0, 1.0)
    dkv_ref[:KV_WIDTH] = turned_keys.astype(LOW)
    dkv_ref[KV_WIDTH:] = total[KV_WIDTH:].astype(LOW)
    return turned_keys.T.astype(LOW), total[KV_WIDTH:].T.astype(LOW)


def close_rows(hidden, gain, dm_ref, dq_ref, grad_keys, grad_values, wq_ref, wk_ref, wv_ref):
    grad_normed = nn(wq_ref[...], dq_ref[...]).T
    grad_normed = grad_normed + nn(grad_keys, wk_ref[...]) + nn(grad_values, wv_ref[...])
    return norm_back(hidden, gain, grad_normed, dm_ref[...])


def close_kernel(last, *refs):
    h_ref, gain_ref, dm_ref, dq_ref, wq_ref, wk_ref, wv_ref, cos_ref, sin_ref = refs[:9]
    own, near, far, dh_ref, dkv_ref, gain_part_ref = refs[9:]
    total = own[...].astype(HIGH) + near[...].astype(HIGH) + far[...].astype(HIGH)
    grad_keys, grad_values = close_keys(total, cos_ref[...], sin_ref[...], dkv_ref)
    hidden = h_ref[...].astype(HIGH)
    hidden = hidden if last else hidden.T
    gain = gain_ref[...].astype(HIGH)
    gain_part, grad_in = close_rows(hidden, gain, dm_ref, dq_ref, grad_keys, grad_values, wq_ref, wk_ref, wv_ref)
    gain_part_ref[...] = gain_part
    dh_ref[...] = grad_in if last else grad_in.T


class Halving:
    def __init__(self, links, steps):
        self.steps = [(links.push(sent, got, to), kept, got) for sent, kept, got, to in steps]

    def start(self, which):
        self.steps[which][0].start()

    def fold(self, which):
        copy, kept, got = self.steps[which]
        copy.wait_recv()
        if which == len(self.steps) - 1:
            return kept[...].astype(HIGH) + got[...].astype(HIGH)
        total = kept[...].astype(HIGH) + got[...].astype(HIGH)
        kept[...] = total.astype(kept.dtype)
        self.steps[which + 1][0].start()
        return None


FAR_SIDE = ("dp", 4)


def halved(links, whole, rooms, order):
    where = {"X": 0, "Z1": 1, "Z0": 2, "Y": 3}
    to = {"X": ACROSS, "Z1": FAR_SIDE, "Z0": BEYOND, "Y": SIDE}
    chosen = [slice(None)] * 4
    steps = []
    for axis, room in zip(order, rooms):
        sent, kept = list(chosen), list(chosen)
        sent[where[axis]], kept[where[axis]] = 1, 0
        steps.append((whole.at[tuple(sent)], whole.at[tuple(kept)], room, to[axis]))
        chosen = kept
    return Halving(links, steps)


def halving_rooms(block, columns, order):
    left = [2, 2, 2, 2]
    where = {"X": 0, "Z1": 1, "Z0": 2, "Y": 3}
    rooms = []
    for axis in order:
        left[where[axis]] = 0
        rooms.append(pltpu.VMEM(tuple(n for n in left if n) + (block, columns), LOW))
    return rooms


ORDERS = (("X", "Y", "Z0", "Z1"), ("Y", "Z0", "X", "Z1"), ("Z0", "X", "Y", "Z1"))
ATTN_ORDERS = (("X", "Y", "Z0", "Z1"), ("Y", "X", "Z0", "Z1"))
ATTN_CUTS = (256, 384)
COPIES_FINISH = 3 * 4 + 2 * 4 + 4 + 5 + 3 + 4


def finish_kernel(layers, *refs):
    where_ref, h_ref, gain_ref, dm_ref, wo_ref, q_ref, kv_ref, o_ref, lse_ref = refs[:9]
    wq_ref, wk_ref, wv_ref, cos_ref, sin_ref, a_ref, c_ref = refs[9:16]
    left_two, long_two, short_two, side_two = refs[16:20]
    gains_ref = refs[20]
    count = 4
    b_any, f_any, rhs_any = refs[21:25], refs[25:29], refs[29:33]
    dh_ref, gate_out, up_out, down_out = refs[33:37]
    query_out, key_out, value_out, output_out, gain_out = refs[37:42]
    room = refs[42:48]
    dq_ref, dkv_ref, dkv_near, dkv_sum, dkv_far, dkv_low = refs[48:54]
    b_all, f_all, rhs, left_all, long_all, short_all, side_all = refs[54:61]
    wholes, rooms = refs[61:64], (refs[64:68], refs[68:72], refs[72:76])
    attn_wholes, attn_rooms = refs[76:78], (refs[78:82], refs[82:86])
    attn_alls = refs[86:88]
    gain_whole, gain_got, gain_side = refs[88:91]
    load, send, receive = refs[91:]
    rows = h_ref.shape[1]
    block = gate_out.shape[0]
    place = lax.axis_index("dp")
    head_at = lax.axis_index("head")
    core, across = head_at % 2, head_at // 2
    links = Links(send, receive)
    reduces = [halved(links, whole, got, order) for whole, got, order in zip(wholes, rooms, ORDERS)]
    attn = [halved(links, whole, got, order) for whole, got, order in zip(attn_wholes, attn_rooms, ATTN_ORDERS)]

    loads = []

    def load_in(source, target):
        copy = pltpu.make_async_copy(source, target, load.at[len(loads)])
        loads.append(copy)
        copy.start()
        return copy

    columns = [pl.ds(i * rows, rows) for i in range(count)]
    wanted = (1, 2, 3, 4, 5, 0)

    def fetch(turn):
        return [load_in(rhs_any[i].at[wanted[turn]], rhs.at[turn % 2, columns[i]]) for i in range(count)]

    b_loads = [load_in(b_any[i], b_all.at[:, columns[i]]) for i in range(count)]
    coming = fetch(0)
    f_loads = [load_in(f_any[i], f_all.at[:, columns[i]]) for i in range(count)]
    two = ((left_two, left_all), (long_two, long_all), (short_two, short_all), (side_two, side_all))
    two_loads = [load_in(source, target.at[:, pl.ds(0, 2 * rows)]) for source, target in two]
    greet((SIBLING, ACROSS, SIDE, BEYOND, FAR_SIDE))
    for copy in b_loads:
        copy.wait()

    def lay(product, whole, first):
        for index in range(8):
            relative = jnp.bitwise_xor(index, place)
            whole[first, relative // 4, relative // 2 % 2, relative % 2] = product[
                index * block : (index + 1) * block
            ].astype(LOW)

    for turn, which in enumerate(wanted):
        for copy in coming:
            copy.wait()
        if turn < 5:
            coming = fetch(turn + 1)
        if which == 4:
            for copy in f_loads:
                copy.wait()
        lay(nn((b_all if which < 4 else f_all)[...], rhs[turn % 2]), wholes[which // 2], which % 2)
        if which == 1:
            reduces[0].start(0)
        if which == 3:
            reduces[1].start(0)
        if which == 5:
            reduces[2].start(0)

    cosine, sine = cos_ref[...], sin_ref[...]
    attend_back(where_ref, kv_ref, wo_ref, q_ref, o_ref, lse_ref, cosine, sine, dm_ref[...], dq_ref, dkv_ref, room)
    near = [links.push(dkv_ref.at[3], dkv_near.at[1], SIBLING), links.push(dkv_ref.at[1], dkv_near.at[0], SIBLING)]
    far = links.push(dkv_sum, dkv_far, ACROSS)
    for copy in near:
        copy.start()
    near[0].wait_recv()
    dkv_sum[...] = (dkv_ref[2].astype(HIGH) + dkv_near[1].astype(HIGH)).astype(LOW)
    far.start()
    for reduce in reduces:
        reduce.fold(0)
    near[1].wait_recv()
    far.wait_recv()
    total = dkv_ref[0].astype(HIGH) + dkv_near[0].astype(HIGH) + dkv_far[...].astype(HIGH)
    grad_keys, grad_values = close_keys(total, cosine, sine, dkv_low)

    low_rows, own_at, got_at = pl.ds(0, KV_WIDTH), pl.ds(2 * rows, rows), pl.ds(3 * rows, rows)
    high_rows = pl.ds(KV_WIDTH, KV_WIDTH)
    pairs = (
        (a_ref, c_ref, left_all),
        (dq_ref, o_ref, long_all),
        (dkv_low.at[low_rows], dkv_low.at[high_rows], short_all),
        (a_ref, a_ref, side_all),
    )
    swaps, first_used = [], links.used
    for index, (zero, one, target) in enumerate(pairs):
        keep_zero = load_in(zero, target.at[:, own_at]) if zero is one else None
        if keep_zero is None:
            keep_zero = pltpu.make_async_copy(zero, target.at[:, own_at], load.at[len(loads)])
            keep_one = pltpu.make_async_copy(one, target.at[:, own_at], load.at[len(loads)])
            loads.append(keep_zero)
            pl.when(core == 0)(keep_zero.start)
            pl.when(core == 1)(keep_one.start)
        send_one = links.push(one, target.at[:, got_at], SIBLING)
        if zero is one:
            send_one.start()
        else:
            links.used -= 1
            links.flying.pop()
            send_zero = links.push(zero, target.at[:, got_at], SIBLING)
            pl.when(core == 0)(send_one.start)
            pl.when(core == 1)(send_zero.start)
        swaps.append((keep_zero, send_one))
    hidden = h_ref[...].astype(HIGH).T
    gain = gain_ref[...].astype(HIGH)
    gain_part, grad_in = close_rows(hidden, gain, dm_ref, dq_ref, grad_keys, grad_values, wq_ref, wk_ref, wv_ref)
    dh_ref[...] = grad_in.T
    for copy in two_loads:
        copy.wait()
    for keep, swap_copy in swaps:
        keep.wait()
        swap_copy.wait_recv()
    long_part = nt(left_all[...], long_all[...])
    short_part = nt(side_all[...], short_all[...])
    product = jnp.concatenate([long_part, short_part], axis=1)
    start = 0
    for whole, cut in zip(attn_wholes, ATTN_CUTS):
        for half in range(2):
            lay(product[:, start : start + cut], whole, jnp.bitwise_xor(half, across))
            start += cut
    for reduce in attn:
        reduce.start(0)

    summed = gains_ref[...] + jnp.concatenate([gain_part, jnp.zeros((7, gain_part.shape[1]), HIGH)], axis=0)
    for index in range(8):
        relative = jnp.bitwise_xor(index, place)
        gain_whole[relative // 4, relative // 2 % 2, relative % 2, :, :block] = summed[
            :, index * block : (index + 1) * block
        ]
        gain_whole[relative // 4, relative // 2 % 2, relative % 2, :, block:] = jnp.zeros((8, 128 - block), HIGH)
    gain_y = links.push(gain_whole.at[:, :, 1], gain_side, SIDE)
    gain_y.start()
    for reduce in reduces:
        reduce.fold(1)
    gain_y.wait_recv()
    gain_whole[:, :, 0] = gain_whole[:, :, 0] + gain_side[...]
    gain_z = links.push(gain_whole.at[:, 1, 0], gain_got.at[pl.ds(0, 2)], BEYOND)
    gain_z.start()
    attn[0].fold(0)
    gain_z.wait_recv()
    gain_whole[:, 0, 0] = gain_whole[:, 0, 0] + gain_got[0:2]
    gain_f = links.push(gain_whole.at[1, 0, 0], gain_got.at[2], FAR_SIDE)
    gain_f.start()
    attn[1].fold(0)
    for reduce in reduces:
        reduce.fold(2)
    gain_f.wait_recv()
    gain_whole[0, 0, 0] = gain_whole[0, 0, 0] + gain_got[2]
    gain_x = links.push(gain_whole.at[0, 0, 0], gain_got.at[3], ACROSS)
    gain_x.start()
    attn[0].fold(1)
    attn[1].fold(1)
    gain_x.wait_recv()
    gain_got[4] = gain_whole[0, 0, 0] + gain_got[3]
    gain_c = links.push(gain_got.at[4], gain_got.at[5], SIBLING)
    gain_c.start()
    attn[0].fold(2)
    attn[1].fold(2)
    gain_c.wait_recv()
    gain_out[...] = gain_got[4] + gain_got[5]
    for reduce, out in zip(reduces, (gate_out, up_out, down_out)):
        out[...] = reduce.fold(3)
    shared = []
    for reduce, held in zip(attn, attn_alls):
        held[0, 0] = reduce.fold(3).astype(LOW)
        copy = links.push(held.at[0, 0], held.at[0, 1], ACROSS)
        copy.start()
        shared.append((copy, held))
    last = []
    for copy, held in shared:
        copy.wait_recv()
        copy = links.push(held.at[0], held.at[1], SIBLING)
        copy.start()
        last.append(copy)
    for copy in last:
        copy.wait_recv()
    for kind, (long_out, short_out) in enumerate(((query_out, key_out), (output_out, value_out))):
        from_core = jnp.bitwise_xor(kind, core)
        parts = [held[from_core, jnp.bitwise_xor(half, across)] for held in attn_alls for half in range(2)]
        both = jnp.concatenate([part.astype(HIGH) for part in parts], axis=1)
        long_out[...] = both[:, : long_out.shape[1]]
        short_out[...] = both[:, long_out.shape[1] :]
    links.drain()


def call(body, outs, specs, scratch, name, spots=0, collective=None):
    params = {"vmem_limit_bytes": LIMIT}
    if collective is not None:
        params.update(collective_id=collective, has_side_effects=True)
    return pl.pallas_call(
        body,
        out_shape=[jax.ShapeDtypeStruct(shape, kind) for shape, kind in outs],
        in_specs=specs,
        out_specs=[VMEM] * (len(outs) - spots) + [ANY] * spots,
        scratch_shapes=scratch,
        compiler_params=pltpu.CompilerParams(**params),
        name=name,
    )


def swap(value, distance):
    count = lax.axis_size("head")
    return lax.ppermute(value, "head", [(i, i ^ distance) for i in range(count)])


def scatter_rows(value, axis):
    count = lax.axis_size(axis)
    index = lax.axis_index(axis)
    value = value.reshape((count, value.shape[0] // count) + value.shape[1:])
    bit = 1
    while bit < count:
        mine = (index // bit) % 2
        value = value.reshape((value.shape[0] // 2, 2) + value.shape[1:])
        sent = lax.dynamic_index_in_dim(value, 1 - mine, 1, False)
        kept = lax.dynamic_index_in_dim(value, mine, 1, False)
        got = lax.ppermute(sent, axis, [(i, i ^ bit) for i in range(count)])
        value = kept.astype(HIGH) + got.astype(HIGH)
        bit *= 2
        if bit < count:
            value = value.astype(LOW)
    return value[0]


def shards(
    tokens,
    cotangent,
    lengths,
    attn_gain,
    w_query,
    w_key,
    w_value,
    w_output,
    ffn_gain,
    w_gate,
    w_up,
    w_down,
):
    blocks = lax.axis_size("head")
    me = lax.axis_index("head").astype(jnp.int32)
    low_bit = me % 2
    rows, width = tokens.shape
    hidden = w_gate.shape[1]
    keys = blocks * rows
    where = jnp.stack([me, lengths[0]])
    frequency = 10000.0 ** (-(jnp.arange(HALF, dtype=HIGH) * 2.0 / HD))
    position = (me * rows + jnp.arange(rows, dtype=jnp.int32)).astype(HIGH)
    angles = frequency[:, None] * position[None, :]
    cosine, sine = jnp.cos(angles), jnp.sin(angles)
    gain_one = attn_gain[None, :]
    gain_two = ffn_gain[None, :]

    feature_rows = (width, rows)
    project_outs = [(feature_rows, LOW), (feature_rows, LOW), ((blocks, rows, 2 * KV_WIDTH), LOW)]
    tokens, cotangent, w_key, w_value, w_down = (v.T for v in (tokens, cotangent, w_key, w_value, w_down))
    weight_room = [pltpu.VMEM((blocks, width, hidden), LOW)] * 3
    attend_room = [
        pltpu.VMEM((keys, rows), HIGH),
        pltpu.VMEM((KVH, keys, HD), LOW),
        pltpu.VMEM((KV_WIDTH, keys), LOW),
    ]
    layer_outs = [
        (feature_rows, LOW),
        ((16, rows), HIGH),
        ((rows, width), HIGH),
        (feature_rows, LOW),
        ((blocks, rows, hidden), LOW),
        ((blocks, rows, hidden), LOW),
    ]

    def forward_first():
        outs = project_outs + layer_outs + [((rows, width), HIGH)] + project_outs
        outs += [((blocks - 1, width, hidden), LOW)] * 3
        copies = 3 * COPIES_SPREAD + 2 * COPIES_SHARE
        scratch = attend_room + weight_room
        scratch += [pltpu.SemaphoreType.DMA((3,)), pltpu.SemaphoreType.DMA((3, blocks - 1))]
        scratch += [pltpu.SemaphoreType.DMA((copies,)), pltpu.SemaphoreType.DMA((copies,))]
        body = functools.partial(forward_first_kernel, blocks)
        specs = [SMEM] + [VMEM] * 9 + [ANY] * 3
        return call(body, outs, specs, scratch, "forward_first", 3, 1)(
            where, tokens, gain_one, w_query, w_key, w_value, cosine, sine, w_output, gain_two, w_gate, w_up, w_down
        )

    outs = forward_first()
    a_one, q_one, kv_one, o_one, lse_one, m_one, b_one, g_one, u_one, h_one, a_two, q_two, kv_two = outs[:13]
    weights = [w_gate, outs[13], w_up, outs[14], w_down, outs[15]]
    weight_scratch = weight_room + [pltpu.SemaphoreType.DMA((3, 2))]

    def forward_last():
        specs = [SMEM] + [VMEM] * 5 + [ANY] * 6
        body = functools.partial(forward_last_kernel, blocks)
        outs = layer_outs + [(feature_rows, LOW)]
        return call(body, outs, specs, attend_room + weight_scratch, "forward_last")(
            where, h_one, q_two, kv_two, w_output, gain_two, *weights
        )

    o_two, lse_two, m_two, b_two, g_two, u_two, block_out = forward_last()
    ffn_outs = [
        (feature_rows, LOW),
        ((6, rows, hidden), LOW),
        ((6, rows, hidden), LOW),
        (feature_rows, LOW),
        ((rows, width), HIGH),
    ]
    attend_outs = [(feature_rows, LOW), ((blocks, 2 * KV_WIDTH, rows), LOW)]
    gain_outs = [((1, width), HIGH)]
    room = attention_room(blocks, rows, width)

    def backward_last():
        given = [where, cotangent, g_two, u_two, m_two, gain_two, w_output, q_two, kv_two, o_two, lse_two]
        specs = [SMEM] + [VMEM] * 12 + [ANY] * 6
        return call(
            backward_last_kernel, ffn_outs + attend_outs + gain_outs, specs, room + weight_scratch, "backward_last"
        )(*given, cosine, sine, *weights)

    def close(h, grad_middle, grad_query, partial, last):
        sent = swap(jnp.stack([partial[1], partial[3]]), 1)
        far = swap((partial[2].astype(HIGH) + sent[1].astype(HIGH)).astype(LOW), 2)
        outs = [((rows, width) if last else feature_rows, HIGH), ((2 * KV_WIDTH, rows), LOW), ((1, width), HIGH)]
        given = [h, gain_one, grad_middle, grad_query, w_query, w_key, w_value, cosine, sine]
        given += [partial[0], sent[0], far]
        return call(functools.partial(close_kernel, last), outs, [VMEM] * 12, [], "close")(*given)

    f_two, mine_two, theirs_two, c_two, dm_two, dq_two, part_two, gain_two_b = backward_last()
    e_one, dkv_two, gain_one_b = close(h_one, dm_two, dq_two, part_two, True)
    f_one, mine_one, theirs_one, c_one, dm_one, gain_two_a = call(
        ffn_back_kernel, ffn_outs + gain_outs, [VMEM] * 5 + [ANY] * 6, weight_scratch, "ffn_back"
    )(e_one, g_one, u_one, m_one, gain_two, *weights)

    def beside(parts):
        return jnp.concatenate(parts, axis=-1)

    def choose(zero, one):
        return jnp.where(low_bit == 0, zero, one)

    def halves(a, c, o, dq, dkv):
        dk, dv = dkv[:KV_WIDTH], dkv[KV_WIDTH:]
        left = [choose(a, c), swap(choose(c, a), 1)]
        long = [choose(dq, o), swap(choose(o, dq), 1)]
        short = [choose(dk, dv), swap(choose(dv, dk), 1)]
        return beside(left), beside(long), beside(short), beside([a, swap(a, 1)])

    halves_two = halves(a_two, c_two, o_two, dq_two, dkv_two)
    b_all = [b_two, swap(b_two, 1), b_one, swap(b_one, 1)]
    f_all = [f_two, swap(f_two, 1), f_one, swap(f_one, 1)]
    sides = [mine_two, swap(theirs_two, 1), mine_one, swap(theirs_one, 1)]
    places = lax.axis_size("dp")
    block = width // places

    def finish():
        gains = jnp.concatenate([gain_one_b, gain_two_a + gain_two_b, jnp.zeros((6, width), HIGH)], axis=0)
        outs = [(feature_rows, HIGH)] + [((block, hidden), HIGH)] * 3
        outs += [((block, n), HIGH) for n in (HQ * HD, KV_WIDTH, KV_WIDTH, HQ * HD)] + [((8, 128), HIGH)]
        low_room = [feature_rows, (blocks, 2 * KV_WIDTH, rows), (2, 2 * KV_WIDTH, rows)]
        low_room += [(2 * KV_WIDTH, rows)] * 3
        low_room += [(width, 4 * rows), (width, 4 * rows), (2, 4 * rows, hidden)]
        low_room += [(width, 4 * rows), (width, 4 * rows), (KV_WIDTH, 4 * rows), (width, 4 * rows)]
        low_room += [(2, 2, 2, 2, block, hidden)] * 3
        scratch = room + [pltpu.VMEM(shape, LOW) for shape in low_room]
        for order in ORDERS:
            scratch += halving_rooms(block, hidden, order)
        scratch += [pltpu.VMEM((2, 2, 2, 2, block, cut), LOW) for cut in ATTN_CUTS]
        for order, cut in zip(ATTN_ORDERS, ATTN_CUTS):
            scratch += halving_rooms(block, cut, order)
        scratch += [pltpu.VMEM((2, 2, block, cut), LOW) for cut in ATTN_CUTS]
        scratch += [pltpu.VMEM(shape, HIGH) for shape in ((2, 2, 2, 8, 128), (8, 8, 128), (2, 2, 8, 128))]
        scratch += [pltpu.SemaphoreType.DMA((40,)), pltpu.SemaphoreType.DMA((COPIES_FINISH,))]
        scratch += [pltpu.SemaphoreType.DMA((COPIES_FINISH,))]
        given = [where, tokens, gain_one, dm_one, w_output, q_one, kv_one, o_one, lse_one]
        given += [w_query, w_key, w_value, cosine, sine, a_one, c_one, *halves_two, gains]
        specs = [SMEM] + [VMEM] * 15 + [ANY] * 4 + [VMEM] + [ANY] * 12
        return call(functools.partial(finish_kernel, 2), outs, specs, scratch, "finish", 0, 2)(
            *given, *b_all, *f_all, *sides
        )

    if places == 8 and blocks == 4:
        outs = finish()
        input_grad, gate_grad, up_grad, down_grad, query_grad, key_grad, value_grad, output_grad, gains = outs
        gains = gains[:2, :block]
    else:
        given = [where, dm_one, w_output, q_one, kv_one, o_one, lse_one, cosine, sine]
        dq_one, part_one = call(attend_back_kernel, attend_outs, [SMEM] + [VMEM] * 8, room, "attend_back")(*given)
        input_grad, dkv_one, gain_one_a = close(tokens, dm_one, dq_one, part_one, False)
        kept, sent = [], []
        for which in range(6):
            side = jnp.concatenate([each[which] for each in sides], 0)
            product = nn(beside(b_all if which < 4 else f_all), side).astype(LOW)
            (sent if which % 2 else kept).append(product)
        got = swap(beside(sent), 2)
        ffn = scatter_rows((beside(kept).astype(HIGH) + got.astype(HIGH)).astype(LOW), "dp")
        halves_one = halves(a_one, c_one, o_one, dq_one, dkv_one)
        left, long, short, side = (beside(pair) for pair in zip(halves_two, halves_one))
        attn = scatter_rows(beside([nt(left, long), nt(side, short)]).astype(LOW), "dp").astype(LOW)
        attn = (attn.astype(HIGH) + swap(attn, 2).astype(HIGH)).astype(LOW)
        other = swap(attn, 1)
        zero, one = choose(attn, other).astype(HIGH), choose(other, attn).astype(HIGH)
        gains = jnp.concatenate([gain_one_a + gain_one_b, gain_two_a + gain_two_b], axis=0)
        gains = lax.psum_scatter(lax.psum(gains, "head"), "dp", scatter_dimension=1, tiled=True)
        query_grad, key_grad = zero[:, : HQ * HD], zero[:, HQ * HD :]
        output_grad, value_grad = one[:, : HQ * HD], one[:, HQ * HD :]
        gate_grad, up_grad, down_grad = (ffn[:, i * hidden : (i + 1) * hidden] for i in range(3))
    return (
        block_out.T,
        input_grad.T,
        gains[0],
        query_grad,
        key_grad,
        value_grad,
        output_grad.T,
        gains[1],
        gate_grad,
        up_grad,
        down_grad.T,
    )


def solution(mesh):
    return jax.shard_map(
        shards,
        mesh=mesh,
        in_specs=(
            P(("dp", "head"), None),
            P(("dp", "head"), None),
            P("dp"),
            P(),
            P(),
            P(),
            P(),
            P(),
            P(),
            P(None, "head"),
            P(None, "head"),
            P("head", None),
        ),
        out_specs=(
            P(("dp", "head"), None),
            P(("dp", "head"), None),
            P("dp"),
            P("dp", None),
            P("dp", None),
            P("dp", None),
            P(None, "dp"),
            P("dp"),
            P("dp", "head"),
            P("dp", "head"),
            P("head", "dp"),
        ),
        check_vma=False,
    )
```

```python
import functools

import jax
import jax.numpy as jnp
from jax import lax
from jax.experimental import pallas as pl
from jax.experimental.pallas import tpu as pltpu
from jax.sharding import PartitionSpec as P

HQ = 15
KVH = 5
HD = 64
HALF = HD // 2
PER_GROUP = HQ // KVH
KV_WIDTH = KVH * HD
EPSILON = 1e-05
SCALE = HD ** (-0.5)
BLOCKED = -1e30
LOW = jnp.bfloat16
HIGH = jnp.float32
VMEM = pl.BlockSpec(memory_space=pltpu.VMEM)
SMEM = pl.BlockSpec(memory_space=pltpu.SMEM)
ANY = pl.BlockSpec(memory_space=pl.ANY)
LIMIT = 60 * 2**20
MESH = pl.DeviceIdType.MESH


def nn(left, right):
    return lax.dot_general(left, right, (((1,), (0,)), ((), ())), preferred_element_type=HIGH)


def nt(left, right):
    return lax.dot_general(left, right, (((1,), (1,)), ((), ())), preferred_element_type=HIGH)


def sigmoid(value):
    return 0.5 * (1.0 + jnp.tanh(0.5 * value))


def inverse_rms(rows):
    return lax.rsqrt(jnp.mean(rows * rows, axis=1, keepdims=True) + EPSILON)


def norm_back(values_in, gain, grad_normed, grad_skip):
    inverse = inverse_rms(values_in)
    normal = values_in * inverse
    gain_part = jnp.sum(grad_normed * normal, axis=0, keepdims=True)
    scaled = grad_normed * gain
    back = grad_skip + inverse * (scaled - normal * jnp.mean(scaled * normal, axis=1, keepdims=True))
    return gain_part, back


def turned(columns, cosine, sine, sign, factor):
    parts = []
    for start in range(0, columns.shape[0], HD):
        first = columns[start : start + HALF] * factor
        second = columns[start + HALF : start + HD] * factor
        parts.append(first * cosine - sign * second * sine)
        parts.append(second * cosine + sign * first * sine)
    return jnp.concatenate(parts, axis=0)


def project(hidden, gain, w_query, w_key, w_value, cosine, sine, a_ref, q_ref, kv_ref, ready):
    normed = hidden * inverse_rms(hidden) * gain
    low = normed.astype(LOW)
    keys = turned(nt(w_key[...], low), cosine, sine, 1.0, 1.0)
    kv_ref[:, :KV_WIDTH] = keys.T.astype(LOW)
    kv_ref[:, KV_WIDTH:] = nt(low, w_value[...]).astype(LOW)
    ready()
    queries = nn(low, w_query[...]).T
    q_ref[...] = turned(queries, cosine, sine, 1.0, SCALE).astype(LOW)
    a_ref[...] = normed.T.astype(LOW)


def fill_bias(where_ref, bias, rows, blocks):
    me = where_ref[0]
    length = where_ref[1]
    key = lax.broadcasted_iota(jnp.int32, (rows, rows), 0)
    query = lax.broadcasted_iota(jnp.int32, (rows, rows), 1)
    for step in range(blocks):
        other = jnp.bitwise_xor(me, step)
        allowed = other * rows + key < length
        if step == 0:
            allowed &= key <= query
        else:
            allowed &= other < me
        bias[step * rows : (step + 1) * rows] = jnp.where(allowed, 0.0, BLOCKED)


def weights_in(sources, holders, sems, order):
    copies = {}
    for step in range(2):
        for which in order:
            holder = holders[which]
            target = holder.at[0] if step == 0 else holder.at[pl.ds(1, holder.shape[0] - 1)]
            copies[step, which] = pltpu.make_async_copy(sources[2 * which + step], target, sems.at[which, step])
            copies[step, which].start()
    return copies


def attend(bias, k_sc, vt_sc, q_ref, o_ref, lse_ref, event):
    def group_body(group, carry):
        keys = k_sc[group]
        values = vt_sc[pl.ds(pl.multiple_of(group * HD, HD), HD), :]
        event(group)
        for member in range(PER_GROUP):
            head = group * PER_GROUP + member
            at = pl.ds(pl.multiple_of(head * HD, HD), HD)
            scores = nn(keys, q_ref[at, :]) + bias[...]
            top = jnp.max(scores, axis=0, keepdims=True)
            exponent = jnp.exp(scores - top)
            total = jnp.sum(exponent, axis=0, keepdims=True)
            attended = nn(values, exponent.astype(LOW)) * (1.0 / total)
            o_ref[at, :] = attended.astype(LOW)
            lse_ref[pl.ds(head, 1), :] = top + jnp.log(total)
        return carry

    lax.fori_loop(0, KVH, group_body, 0)


def lay_keys(kv_ref, k_sc, vt_sc, blocks, rows):
    for step in range(blocks):
        at = slice(step * rows, (step + 1) * rows)
        for group in range(KVH):
            k_sc[group, at] = kv_ref[step, :, group * HD : (group + 1) * HD]
        vt_sc[:, at] = kv_ref[step, :, KV_WIDTH:].T


def after_attention(hidden, o_ref, wo_ref, gain_ref, m_ref, b_ref):
    middle = hidden + nn(o_ref[...].T, wo_ref[...])
    m_ref[...] = middle
    normed = middle * inverse_rms(middle) * gain_ref[...].astype(HIGH)
    b_ref[...] = normed.T.astype(LOW)
    return middle, normed.astype(LOW)


def hidden_part(normed, wg, wu, wd, g_ref, u_ref, step):
    gate = nn(normed, wg[step])
    up = nn(normed, wu[step])
    g_ref[step] = gate.astype(LOW)
    u_ref[step] = up.astype(LOW)
    active = (gate * sigmoid(gate) * up).astype(LOW)
    return nt(active, wd[step])


def partner(axis, distance):
    return {axis: jnp.bitwise_xor(lax.axis_index(axis), distance)}


def greet(partners):
    barrier = pltpu.get_barrier_semaphore()
    for axis, distance in partners:
        pl.semaphore_signal(barrier, inc=1, device_id=partner(axis, distance), device_id_type=MESH)
    pl.semaphore_wait(barrier, len(partners))


class Links:
    def __init__(self, send, receive):
        self.send, self.receive, self.used = send, receive, 0
        self.flying = []

    def push(self, source, target, to):
        copy = pltpu.make_async_remote_copy(
            src_ref=source,
            dst_ref=target,
            send_sem=self.send.at[self.used],
            recv_sem=self.receive.at[self.used],
            device_id=partner(*to),
            device_id_type=MESH,
        )
        self.used += 1
        self.flying.append(copy)
        return copy

    def drain(self):
        for copy in self.flying:
            copy.wait_send()


SIBLING, ACROSS, SIDE, BEYOND = ("head", 1), ("head", 2), ("dp", 1), ("dp", 2)


class Share:
    def __init__(self, links, kv_ref):
        self.near = links.push(kv_ref.at[0], kv_ref.at[1], SIBLING)
        self.far = links.push(kv_ref.at[0], kv_ref.at[2], ACROSS)
        self.forth = links.push(kv_ref.at[2], kv_ref.at[3], SIBLING)

    def start(self):
        self.far.start()
        self.near.start()

    def pass_on(self):
        self.far.wait_recv()
        self.forth.start()

    def finish(self):
        self.near.wait_recv()
        self.forth.wait_recv()


class Spread:
    def __init__(self, links, own, all_ref):
        rows = own.shape[0]
        quarter = rows // 4
        cut = quarter // 32 * 16
        place = lax.axis_index("dp") % 4

        def part(ref, which, start=0, size=quarter):
            first = jnp.bitwise_xor(place, which) * quarter + start
            return ref.at[pl.ds(pl.multiple_of(first, 16), size)]

        far, diag = all_ref.at[2], all_ref.at[3]

        def move(which, to, *piece):
            return links.push(part(far, which, *piece), part(far, which, *piece), to)

        def aside(which):
            return links.push(part(far, which), part(diag, which), SIBLING)

        self.near = links.push(own, all_ref.at[1], SIBLING)
        self.cross = links.push(part(own, 0), part(far, 0), ACROSS)
        self.side, self.beyond = move(0, SIDE), move(0, BEYOND)
        self.side_half = move(2, SIDE, cut, quarter - cut)
        self.beyond_half = move(1, BEYOND, 0, cut)
        self.asides = [aside(which) for which in range(4)]

    def first(self):
        self.cross.wait_recv()
        self.side.start()
        self.beyond.start()
        self.asides[0].start()

    def second(self):
        self.side.wait_recv()
        self.beyond_half.start()
        self.asides[1].start()
        self.beyond.wait_recv()
        self.side_half.start()
        self.asides[2].start()

    def third(self):
        self.side_half.wait_recv()
        self.beyond_half.wait_recv()
        self.asides[3].start()

    def last(self):
        for copy in self.asides:
            copy.wait_recv()


COPIES_SHARE = 3
COPIES_SPREAD = 10


def forward_first_kernel(blocks, *refs):
    where_ref, h_ref, gain_one_ref, wq_ref, wk_ref, wv_ref, cos_ref, sin_ref, wo_ref, gain_two_ref = refs[:10]
    owns = refs[10:13]
    a_ref, q_ref, kv_ref, o_ref, lse_ref, m_ref, b_ref, g_ref, u_ref, out_ref = refs[13:23]
    next_a, next_q, next_kv = refs[23:26]
    kept = refs[26:29]
    bias, k_sc, vt_sc, wg, wu, wd, load, save, send, receive = refs[29:]
    rows = h_ref.shape[1]
    hidden = h_ref[...].astype(HIGH).T
    links = Links(send, receive)
    held = (wg, wu, wd)
    loads = [pltpu.make_async_copy(own, all_ref.at[0], load.at[i]) for i, (own, all_ref) in enumerate(zip(owns, held))]
    spreads = [Spread(links, own, all_ref) for own, all_ref in zip(owns, held)]
    shares = [Share(links, ref) for ref in (kv_ref, next_kv)]
    greet((SIBLING, ACROSS, SIDE, BEYOND))
    gate_way, up_way, down_way = spreads
    gate_way.cross.start()
    for spread, copy in zip(spreads, loads):
        spread.near.start()
        copy.start()
    cosine, sine = cos_ref[...], sin_ref[...]
    gain_one = gain_one_ref[...].astype(HIGH)
    project(hidden, gain_one, wq_ref, wk_ref, wv_ref, cosine, sine, a_ref, q_ref, kv_ref.at[0], shares[0].start)
    fill_bias(where_ref, bias, rows, blocks)
    gate_way.first()
    up_way.cross.start()
    shares[0].pass_on()
    shares[0].finish()
    lay_keys(kv_ref, k_sc, vt_sc, blocks, rows)

    def event(group):
        @pl.when(group == 2)
        def _():
            up_way.first()
            down_way.cross.start()

        pl.when(group == 3)(gate_way.second)

    attend(bias, k_sc, vt_sc, q_ref, o_ref, lse_ref, event)
    down_way.first()
    up_way.second()
    gate_way.third()
    middle, normed = after_attention(hidden, o_ref, wo_ref, gain_two_ref, m_ref, b_ref)
    saves = []

    def keep(step):
        for which in range(3):
            copy = pltpu.make_async_copy(held[which].at[step], kept[which].at[step - 1], save.at[which, step - 1])
            copy.start()
            saves.append(copy)

    for copy in loads:
        copy.wait()
    total = middle + hidden_part(normed, wg, wu, wd, g_ref, u_ref, 0)
    up_way.third()
    for spread in spreads:
        spread.near.wait_recv()
    keep(1)
    total = total + hidden_part(normed, wg, wu, wd, g_ref, u_ref, 1)
    down_way.second()
    down_way.third()
    keep(2)
    total = total + hidden_part(normed, wg, wu, wd, g_ref, u_ref, 2)
    for spread in spreads:
        spread.last()
    keep(3)
    total = total + hidden_part(normed, wg, wu, wd, g_ref, u_ref, 3)
    out_ref[...] = total
    project(total, gain_one, wq_ref, wk_ref, wv_ref, cosine, sine, next_a, next_q, next_kv.at[0], shares[1].start)
    shares[1].pass_on()
    shares[1].finish()
    for copy in saves:
        copy.wait()
    links.drain()


def ffn_back(grad, copies, g_ref, u_ref, m_ref, gain, wg, wu, wd, mine_ref, theirs_ref):
    low_grad = grad.astype(LOW)
    grad_normed = jnp.zeros(m_ref.shape, HIGH)
    for step in range(wg.shape[0]):
        if copies and step < 2:
            copies[step, 2].wait()
        grad_active = nn(low_grad, wd[step])
        gate = g_ref[step].astype(HIGH)
        up = u_ref[step].astype(HIGH)
        sig = sigmoid(gate)
        silu = gate * sig
        grad_gate = (grad_active * up * sig * (1.0 + gate * (1.0 - sig))).astype(LOW)
        grad_up = (grad_active * silu).astype(LOW)
        kept = mine_ref if step % 2 == 0 else theirs_ref
        kept[step // 2] = grad_gate
        kept[2 + step // 2] = grad_up
        kept[4 + step // 2] = (silu * up).astype(LOW)
        if copies and step < 2:
            copies[step, 0].wait()
            copies[step, 1].wait()
        grad_normed = grad_normed + nt(grad_gate, wg[step]) + nt(grad_up, wu[step])
    return norm_back(m_ref[...], gain, grad_normed, grad)


def lay_back(kv_ref, k_sc, v_sc, kt_sc, blocks, rows, keys_laid):
    for step in range(blocks):
        at = slice(step * rows, (step + 1) * rows)
        for group in range(KVH):
            if not keys_laid:
                k_sc[group, at] = kv_ref[step, :, group * HD : (group + 1) * HD]
            v_sc[group, at] = kv_ref[step, :, KV_WIDTH + group * HD : KV_WIDTH + (group + 1) * HD]
        kt_sc[:, at] = kv_ref[step, :, :KV_WIDTH].T


def attend_back(grad_middle, wo_ref, q_ref, o_ref, lse_ref, cosine, sine, dq_ref, dkv_ref, room, between):
    bias, k_sc, v_sc, kt_sc, do_sc, delta, dq_sc = room
    keys, rows = bias.shape
    blocks = keys // rows
    half = keys // 2
    do_sc[...] = nt(wo_ref[...], grad_middle.astype(LOW)).astype(LOW)
    for head in range(HQ):
        at = slice(head * HD, (head + 1) * HD)
        product = do_sc[at].astype(HIGH) * o_ref[at].astype(HIGH)
        delta[head : head + 1] = jnp.sum(product, axis=0, keepdims=True)

    def one_pass(start, last, event):
        cut = slice(start, start + half)

        def group_body(group, carry):
            event(group)
            group_keys = k_sc[group, cut]
            values = v_sc[group, cut]
            at = pl.ds(pl.multiple_of(group * HD, HD), HD)
            after = pl.ds(pl.multiple_of(KV_WIDTH + group * HD, HD), HD)
            keys_t = kt_sc[at, cut]
            grad_keys = jnp.zeros((HD, half), HIGH)
            grad_values = jnp.zeros((HD, half), HIGH)
            for member in range(PER_GROUP):
                head = group * PER_GROUP + member
                head_at = pl.ds(pl.multiple_of(head * HD, HD), HD)
                query = q_ref[head_at, :]
                grad_out = do_sc[head_at, :]
                scores = nn(group_keys, query) + bias[cut]
                prob = jnp.exp(scores - lse_ref[pl.ds(head, 1), :])
                grad_prob = nn(values, grad_out)
                grad_score = (prob * (grad_prob - delta[pl.ds(head, 1), :])).astype(LOW)
                grad_query = nn(keys_t, grad_score)
                if last:
                    grad_query = grad_query + dq_sc[head_at, :]
                    dq_ref[head_at, :] = turned(grad_query, cosine, sine, -1.0, SCALE).astype(LOW)
                else:
                    dq_sc[head_at, :] = grad_query
                grad_keys = grad_keys + nt(query, grad_score)
                grad_values = grad_values + nt(grad_out, prob.astype(LOW))
            for step in range(blocks // 2):
                part = slice(step * rows, (step + 1) * rows)
                dkv_ref[start // rows + step, at, :] = grad_keys[:, part].astype(LOW)
                dkv_ref[start // rows + step, after, :] = grad_values[:, part].astype(LOW)
            return carry

        lax.fori_loop(0, KVH, group_body, 0)

    one_pass(half, False, lambda group: None)
    one_pass(0, True, between)


class Settle:
    def __init__(self, links, dkv_ref, near_ref, sum_ref, far_ref):
        self.refs = dkv_ref, near_ref, sum_ref, far_ref
        self.aside = links.push(dkv_ref.at[3], near_ref.at[1], SIBLING)
        self.near = links.push(dkv_ref.at[1], near_ref.at[0], SIBLING)
        self.far = links.push(sum_ref, far_ref, ACROSS)

    def between(self, group):
        dkv_ref, near_ref, sum_ref, _ = self.refs
        pl.when(group == 0)(self.aside.start)

        @pl.when(group == 1)
        def _():
            self.aside.wait_recv()
            sum_ref[...] = (dkv_ref[2].astype(HIGH) + near_ref[1].astype(HIGH)).astype(LOW)
            self.far.start()

    def finish(self):
        dkv_ref, near_ref, _, far_ref = self.refs
        self.near.start()
        self.near.wait_recv()
        self.far.wait_recv()
        return dkv_ref[0].astype(HIGH) + near_ref[0].astype(HIGH) + far_ref[...].astype(HIGH)


def attention_room(blocks, rows, width):
    keys = blocks * rows
    return [
        pltpu.VMEM((keys, rows), HIGH),
        pltpu.VMEM((KVH, keys, HD), LOW),
        pltpu.VMEM((KVH, keys, HD), LOW),
        pltpu.VMEM((KV_WIDTH, keys), LOW),
        pltpu.VMEM((width, rows), LOW),
        pltpu.VMEM((16, rows), HIGH),
        pltpu.VMEM((width, rows), HIGH),
    ]


class Local:
    def __init__(self, sems):
        self.sems, self.used, self.flying = sems, 0, []

    def move(self, source, target, start=True):
        copy = pltpu.make_async_copy(source, target, self.sems.at[self.used])
        self.used += 1
        self.flying.append(copy)
        if start:
            copy.start()
        return copy

    def drain(self):
        for copy in self.flying:
            copy.wait()


def share_out(local, links, core, zero, one, target, own_at, got_at):
    if zero is one:
        keep = local.move(zero, target.at[own_at])
        send = links.push(zero, target.at[got_at], SIBLING)
        send.start()
        return keep, send
    keep = local.move(zero, target.at[own_at], False)
    keep_one = pltpu.make_async_copy(one, target.at[own_at], local.sems.at[local.used - 1])
    send = links.push(one, target.at[got_at], SIBLING)
    links.used -= 1
    links.flying.pop()
    send_zero = links.push(zero, target.at[got_at], SIBLING)

    @pl.when(core == 0)
    def _():
        keep.start()
        send.start()

    @pl.when(core == 1)
    def _():
        keep_one.start()
        send_zero.start()

    return keep, send


COPIES_MIDDLE = 16
LOCALS_MIDDLE = 24


def middle_kernel(blocks, *refs):
    where_ref, h_ref, q_ref, kv_ref, wo_ref, gain_one_ref, gain_two_ref, cos_ref, sin_ref = refs[:9]
    cot_any, wq_any, wk_any, wv_any, g_any, u_any, m_any, a_any, b_any = refs[9:18]
    sources = refs[18:24]
    out_ref, c_ref, dm_ref, gains_ref = refs[24:28]
    b_all, f_all, rhs_all, left_two, long_two, short_two, side_two = refs[28:35]
    room = refs[35:42]
    bias, k_sc, v_sc, kt_sc = room[:4]
    vt_sc, o_sc, lse_sc, m_sc, b_sc, f_sc, c_sc, g_sc, u_sc = refs[42:51]
    mine, theirs, dq_sc, dkv_sc, dkv_near, dkv_sum, dkv_far, dkv_low = refs[51:59]
    cot, wq, wk, wv = refs[59:63]
    wg, wu, wd, sems, load, send, receive = refs[63:]
    rows = h_ref.shape[0]
    core = lax.axis_index("head") % 2
    copies = weights_in(sources, (wg, wu, wd), sems, (0, 1, 2))
    local = Local(load)
    links = Links(send, receive)
    late = [local.move(source, target) for source, target in ((cot_any, cot), (wq_any, wq), (wk_any, wk), (wv_any, wv))]
    settle = Settle(links, dkv_sc, dkv_near, dkv_sum, dkv_far)
    spans = [pl.ds(i * rows, rows) for i in range(4)]
    everything = slice(None)

    def both(source, target, place):
        keep = local.move(source, target.at[(*place, spans[both.layer])])
        copy = links.push(source, target.at[(*place, spans[both.layer + 1])], SIBLING)
        copy.start()
        return keep, copy

    greet((SIBLING, ACROSS))
    both.layer = 2
    posted = [both(b_any, b_all, (everything,))]
    both.layer = 0
    fill_bias(where_ref, bias, rows, blocks)
    lay_keys(kv_ref, k_sc, vt_sc, blocks, rows)
    attend(bias, k_sc, vt_sc, q_ref, o_sc, lse_sc, lambda group: None)
    total, normed = after_attention(h_ref[...], o_sc, wo_ref, gain_two_ref, m_sc, b_sc)
    posted.append(both(b_sc, b_all, (everything,)))
    for step in range(blocks):
        if step < 2:
            for which in range(3):
                copies[step, which].wait()
        total = total + hidden_part(normed, wg, wu, wd, g_sc, u_sc, step)
    out_ref[...] = total.T.astype(LOW)
    lay_back(kv_ref, k_sc, v_sc, kt_sc, blocks, rows, True)

    late[0].wait()
    row = where_ref[0] * rows + lax.broadcasted_iota(jnp.int32, (rows, 1), 0)
    grad = jnp.where(row < where_ref[1], cot[...].astype(HIGH).T, 0.0)
    f_sc[...] = grad.T.astype(LOW)
    first_f = both(f_sc, f_all, (everything,))
    gain_two = gain_two_ref[...].astype(HIGH)
    gain_part, grad_middle = ffn_back(grad, None, g_sc, u_sc, m_sc, gain_two, wg, wu, wd, mine, theirs)
    first_loads = [local.move(source, target) for source, target in ((g_any, g_sc), (u_any, u_sc), (m_any, m_sc))]
    keep_mine = local.move(mine, rhs_all.at[:, spans[0]])
    send_theirs = links.push(theirs, rhs_all.at[:, spans[1]], SIBLING)
    send_theirs.start()
    gains_ref[...] = jnp.zeros(gains_ref.shape, HIGH)
    gains_ref[1:2] = gain_part
    c_sc[...] = grad_middle.T.astype(LOW)
    cosine, sine = cos_ref[...], sin_ref[...]
    attend_back(
        grad_middle, wo_ref, q_ref, o_sc, lse_sc, cosine, sine, dq_sc, dkv_sc, room, settle.between
    )
    grad_keys, grad_values = close_keys(settle.finish(), cosine, sine, dkv_low)
    low_rows, high_rows = pl.ds(0, KV_WIDTH), pl.ds(KV_WIDTH, KV_WIDTH)
    for zero, one, target in (
        (a_any, c_sc, left_two),
        (dq_sc, o_sc, long_two),
        (dkv_low.at[low_rows], dkv_low.at[high_rows], short_two),
        (a_any, a_any, side_two),
    ):
        posted.append(
            share_out(local, links, core, zero, one, target, (everything, spans[0]), (everything, spans[1]))
        )
    for copy in late[1:]:
        copy.wait()
    gain_one = gain_one_ref[...].astype(HIGH)
    gain_part, grad = close_rows(h_ref[...], gain_one, grad_middle, dq_sc, grad_keys, grad_values, wq, wk, wv)
    gains_ref[0:1] = gain_part

    first_f[0].wait()
    first_f[1].wait_send()
    keep_mine.wait()
    send_theirs.wait_send()
    for copy in first_loads:
        copy.wait()
    f_sc[...] = grad.T.astype(LOW)
    both.layer = 2
    posted.append(both(f_sc, f_all, (everything,)))
    gain_part, grad_middle = ffn_back(grad, None, g_sc, u_sc, m_sc, gain_two, wg, wu, wd, mine, theirs)
    keep_last = local.move(mine, rhs_all.at[:, spans[2]])
    send_last = links.push(theirs, rhs_all.at[:, spans[3]], SIBLING)
    send_last.start()
    gains_ref[1:2] = gains_ref[1:2] + gain_part
    dm_ref[...] = grad_middle
    c_ref[...] = grad_middle.T.astype(LOW)
    for keep, copy in posted:
        keep.wait()
        copy.wait()
    first_f[1].wait_recv()
    send_theirs.wait_recv()
    keep_last.wait()
    send_last.wait()
    settle.aside.wait_send()
    settle.near.wait_send()
    settle.far.wait_send()


def attend_back_kernel(*refs):
    where_ref, dm_ref, wo_ref, q_ref, kv_ref, o_ref, lse_ref, cos_ref, sin_ref, dq_ref, dkv_ref = refs[:11]
    room = refs[11:]
    bias, k_sc, v_sc, kt_sc = room[:4]
    blocks, rows = kv_ref.shape[:2]
    fill_bias(where_ref, bias, rows, blocks)
    lay_back(kv_ref, k_sc, v_sc, kt_sc, blocks, rows, False)
    attend_back(
        dm_ref[...], wo_ref, q_ref, o_ref, lse_ref, cos_ref[...], sin_ref[...], dq_ref, dkv_ref, room, lambda group: None
    )


def close_keys(total, cosine, sine, dkv_ref):
    turned_keys = turned(total[:KV_WIDTH], cosine, sine, -1.0, 1.0)
    dkv_ref[:KV_WIDTH] = turned_keys.astype(LOW)
    dkv_ref[KV_WIDTH:] = total[KV_WIDTH:].astype(LOW)
    return turned_keys.T.astype(LOW), total[KV_WIDTH:].T.astype(LOW)


def close_rows(hidden, gain, grad_middle, dq_ref, grad_keys, grad_values, wq_ref, wk_ref, wv_ref):
    grad_normed = nn(wq_ref[...], dq_ref[...]).T
    grad_normed = grad_normed + nn(grad_keys, wk_ref[...]) + nn(grad_values, wv_ref[...])
    return norm_back(hidden, gain, grad_normed, grad_middle)


def close_kernel(*refs):
    h_ref, gain_ref, dm_ref, dq_ref, wq_ref, wk_ref, wv_ref, cos_ref, sin_ref = refs[:9]
    own, near, far, dh_ref, dkv_ref, gain_part_ref = refs[9:]
    total = own[...].astype(HIGH) + near[...].astype(HIGH) + far[...].astype(HIGH)
    grad_keys, grad_values = close_keys(total, cos_ref[...], sin_ref[...], dkv_ref)
    hidden = h_ref[...].astype(HIGH).T
    gain = gain_ref[...].astype(HIGH)
    gain_part, grad_in = close_rows(hidden, gain, dm_ref[...], dq_ref, grad_keys, grad_values, wq_ref, wk_ref, wv_ref)
    gain_part_ref[...] = gain_part
    dh_ref[...] = grad_in.T


class Halving:
    def __init__(self, links, steps):
        self.steps = [(links.push(sent, got, to), kept, got) for sent, kept, got, to in steps]

    def start(self, which):
        self.steps[which][0].start()

    def fold(self, which):
        copy, kept, got = self.steps[which]
        copy.wait_recv()
        if which == len(self.steps) - 1:
            return kept[...].astype(HIGH) + got[...].astype(HIGH)
        total = kept[...].astype(HIGH) + got[...].astype(HIGH)
        kept[...] = total.astype(kept.dtype)
        self.steps[which + 1][0].start()
        return None


FAR_SIDE = ("dp", 4)


def halved(links, whole, rooms, order):
    where = {"X": 0, "Z1": 1, "Z0": 2, "Y": 3}
    to = {"X": ACROSS, "Z1": FAR_SIDE, "Z0": BEYOND, "Y": SIDE}
    chosen = [slice(None)] * 4
    steps = []
    for axis, room in zip(order, rooms):
        sent, kept = list(chosen), list(chosen)
        sent[where[axis]], kept[where[axis]] = 1, 0
        steps.append((whole.at[tuple(sent)], whole.at[tuple(kept)], room, to[axis]))
        chosen = kept
    return Halving(links, steps)


def halving_rooms(block, columns, order):
    left = [2, 2, 2, 2]
    where = {"X": 0, "Z1": 1, "Z0": 2, "Y": 3}
    rooms = []
    for axis in order:
        left[where[axis]] = 0
        rooms.append(pltpu.VMEM(tuple(n for n in left if n) + (block, columns), LOW))
    return rooms


ORDERS = (("X", "Y", "Z0", "Z1"), ("Y", "Z0", "X", "Z1"), ("Z0", "X", "Y", "Z1"))
ATTN_ORDERS = (("X", "Y", "Z0", "Z1"), ("Y", "X", "Z0", "Z1"))
ATTN_CUTS = (256, 384)
COPIES_FINISH = 3 * 4 + 2 * 4 + 4 + 5 + 3 + 4


def finish_kernel(*refs):
    where_ref, h_ref, gain_ref, dm_ref, wo_ref, q_ref, kv_ref, o_ref, lse_ref = refs[:9]
    wq_ref, wk_ref, wv_ref, cos_ref, sin_ref, a_ref, c_ref = refs[9:16]
    left_two, long_two, short_two, side_two = refs[16:20]
    gains_ref = refs[20]
    count = 4
    b_any, f_any, rhs_any = refs[21:24]
    dh_ref, gate_out, up_out, down_out = refs[24:28]
    query_out, key_out, value_out, output_out, gain_out = refs[28:33]
    room = refs[33:40]
    dq_ref, dkv_ref, dkv_near, dkv_sum, dkv_far, dkv_low = refs[40:46]
    b_all, f_all, rhs, left_all, long_all, short_all, side_all = refs[46:53]
    wholes, rooms = refs[53:56], (refs[56:60], refs[60:64], refs[64:68])
    attn_wholes, attn_rooms = refs[68:70], (refs[70:74], refs[74:78])
    attn_alls = refs[78:80]
    gain_whole, gain_got, gain_side = refs[80:83]
    load, send, receive = refs[83:]
    rows = h_ref.shape[1]
    block = gate_out.shape[0]
    place = lax.axis_index("dp")
    head_at = lax.axis_index("head")
    core, across = head_at % 2, head_at // 2
    links = Links(send, receive)
    reduces = [halved(links, whole, got, order) for whole, got, order in zip(wholes, rooms, ORDERS)]
    attn = [halved(links, whole, got, order) for whole, got, order in zip(attn_wholes, attn_rooms, ATTN_ORDERS)]

    local = Local(load)
    wanted = (1, 2, 3, 4, 5, 0)

    def fetch(turn):
        return local.move(rhs_any.at[wanted[turn]], rhs.at[turn % 2])

    b_load = local.move(b_any, b_all)
    coming = fetch(0)
    f_load = local.move(f_any, f_all)
    two = ((left_two, left_all), (long_two, long_all), (short_two, short_all), (side_two, side_all))
    two_loads = [local.move(source, target.at[:, pl.ds(0, 2 * rows)]) for source, target in two]
    greet((SIBLING, ACROSS, SIDE, BEYOND, FAR_SIDE))
    b_load.wait()

    def lay(product, whole, first):
        for index in range(8):
            relative = jnp.bitwise_xor(index, place)
            whole[first, relative // 4, relative // 2 % 2, relative % 2] = product[
                index * block : (index + 1) * block
            ].astype(LOW)

    for turn, which in enumerate(wanted):
        coming.wait()
        if turn < 5:
            coming = fetch(turn + 1)
        if which == 4:
            f_load.wait()
        lay(nn((b_all if which < 4 else f_all)[...], rhs[turn % 2]), wholes[which // 2], which % 2)
        if which == 1:
            reduces[0].start(0)
        if which == 3:
            reduces[1].start(0)
        if which == 5:
            reduces[2].start(0)

    cosine, sine = cos_ref[...], sin_ref[...]
    bias, k_sc, v_sc, kt_sc = room[:4]
    settle = Settle(links, dkv_ref, dkv_near, dkv_sum, dkv_far)
    fill_bias(where_ref, bias, rows, count)
    lay_back(kv_ref, k_sc, v_sc, kt_sc, count, rows, False)
    attend_back(
        dm_ref[...], wo_ref, q_ref, o_ref, lse_ref, cosine, sine, dq_ref, dkv_ref, room, settle.between
    )
    total = settle.finish()
    for reduce in reduces:
        reduce.fold(0)
    grad_keys, grad_values = close_keys(total, cosine, sine, dkv_low)

    low_rows, own_at, got_at = pl.ds(0, KV_WIDTH), pl.ds(2 * rows, rows), pl.ds(3 * rows, rows)
    high_rows, everything = pl.ds(KV_WIDTH, KV_WIDTH), slice(None)
    swaps = []
    for zero, one, target in (
        (a_ref, c_ref, left_all),
        (dq_ref, o_ref, long_all),
        (dkv_low.at[low_rows], dkv_low.at[high_rows], short_all),
        (a_ref, a_ref, side_all),
    ):
        swaps.append(share_out(local, links, core, zero, one, target, (everything, own_at), (everything, got_at)))
    hidden = h_ref[...].astype(HIGH).T
    gain = gain_ref[...].astype(HIGH)
    gain_part, grad_in = close_rows(hidden, gain, dm_ref[...], dq_ref, grad_keys, grad_values, wq_ref, wk_ref, wv_ref)
    dh_ref[...] = grad_in.T
    for copy in two_loads:
        copy.wait()
    for keep, swap_copy in swaps:
        keep.wait()
        swap_copy.wait_recv()
    long_part = nt(left_all[...], long_all[...])
    short_part = nt(side_all[...], short_all[...])
    product = jnp.concatenate([long_part, short_part], axis=1)
    start = 0
    for whole, cut in zip(attn_wholes, ATTN_CUTS):
        for half in range(2):
            lay(product[:, start : start + cut], whole, jnp.bitwise_xor(half, across))
            start += cut
    for reduce in attn:
        reduce.start(0)

    summed = gains_ref[...] + jnp.concatenate([gain_part, jnp.zeros((7, gain_part.shape[1]), HIGH)], axis=0)
    for index in range(8):
        relative = jnp.bitwise_xor(index, place)
        gain_whole[relative // 4, relative // 2 % 2, relative % 2, :, :block] = summed[
            :, index * block : (index + 1) * block
        ]
        gain_whole[relative // 4, relative // 2 % 2, relative % 2, :, block:] = jnp.zeros((8, 128 - block), HIGH)
    gain_y = links.push(gain_whole.at[:, :, 1], gain_side, SIDE)
    gain_y.start()
    for reduce in reduces:
        reduce.fold(1)
    gain_y.wait_recv()
    gain_whole[:, :, 0] = gain_whole[:, :, 0] + gain_side[...]
    gain_z = links.push(gain_whole.at[:, 1, 0], gain_got.at[pl.ds(0, 2)], BEYOND)
    gain_z.start()
    attn[0].fold(0)
    gain_z.wait_recv()
    gain_whole[:, 0, 0] = gain_whole[:, 0, 0] + gain_got[0:2]
    gain_f = links.push(gain_whole.at[1, 0, 0], gain_got.at[2], FAR_SIDE)
    gain_f.start()
    attn[1].fold(0)
    for reduce in reduces:
        reduce.fold(2)
    gain_f.wait_recv()
    gain_whole[0, 0, 0] = gain_whole[0, 0, 0] + gain_got[2]
    gain_x = links.push(gain_whole.at[0, 0, 0], gain_got.at[3], ACROSS)
    gain_x.start()
    attn[0].fold(1)
    attn[1].fold(1)
    gain_x.wait_recv()
    gain_got[4] = gain_whole[0, 0, 0] + gain_got[3]
    gain_c = links.push(gain_got.at[4], gain_got.at[5], SIBLING)
    gain_c.start()
    attn[0].fold(2)
    attn[1].fold(2)
    gain_c.wait_recv()
    gain_out[...] = gain_got[4] + gain_got[5]
    for reduce, out in zip(reduces, (gate_out, up_out, down_out)):
        out[...] = reduce.fold(3)
    shared = []
    for reduce, held in zip(attn, attn_alls):
        held[0, 0] = reduce.fold(3).astype(LOW)
        copy = links.push(held.at[0, 0], held.at[0, 1], ACROSS)
        copy.start()
        shared.append((copy, held))
    last = []
    for copy, held in shared:
        copy.wait_recv()
        copy = links.push(held.at[0], held.at[1], SIBLING)
        copy.start()
        last.append(copy)
    for copy in last:
        copy.wait_recv()
    for kind, (long_out, short_out) in enumerate(((query_out, key_out), (output_out, value_out))):
        from_core = jnp.bitwise_xor(kind, core)
        parts = [held[from_core, jnp.bitwise_xor(half, across)] for held in attn_alls for half in range(2)]
        both = jnp.concatenate([part.astype(HIGH) for part in parts], axis=1)
        long_out[...] = both[:, : long_out.shape[1]]
        short_out[...] = both[:, long_out.shape[1] :]
    links.drain()


def call(body, outs, specs, scratch, name, spots=0, collective=None):
    params = {"vmem_limit_bytes": LIMIT}
    if collective is not None:
        params.update(collective_id=collective, has_side_effects=True)
    return pl.pallas_call(
        body,
        out_shape=[jax.ShapeDtypeStruct(shape, kind) for shape, kind in outs],
        in_specs=specs,
        out_specs=[VMEM] * (len(outs) - spots) + [ANY] * spots,
        scratch_shapes=scratch,
        compiler_params=pltpu.CompilerParams(**params),
        name=name,
    )


def swap(value, distance):
    count = lax.axis_size("head")
    return lax.ppermute(value, "head", [(i, i ^ distance) for i in range(count)])


def scatter_rows(value, axis):
    count = lax.axis_size(axis)
    index = lax.axis_index(axis)
    value = value.reshape((count, value.shape[0] // count) + value.shape[1:])
    bit = 1
    while bit < count:
        mine = (index // bit) % 2
        value = value.reshape((value.shape[0] // 2, 2) + value.shape[1:])
        sent = lax.dynamic_index_in_dim(value, 1 - mine, 1, False)
        kept = lax.dynamic_index_in_dim(value, mine, 1, False)
        got = lax.ppermute(sent, axis, [(i, i ^ bit) for i in range(count)])
        value = kept.astype(HIGH) + got.astype(HIGH)
        bit *= 2
        if bit < count:
            value = value.astype(LOW)
    return value[0]


def shards(
    tokens,
    cotangent,
    lengths,
    attn_gain,
    w_query,
    w_key,
    w_value,
    w_output,
    ffn_gain,
    w_gate,
    w_up,
    w_down,
):
    blocks = lax.axis_size("head")
    me = lax.axis_index("head").astype(jnp.int32)
    low_bit = me % 2
    rows, width = tokens.shape
    hidden = w_gate.shape[1]
    keys = blocks * rows
    where = jnp.stack([me, lengths[0]])
    frequency = 10000.0 ** (-(jnp.arange(HALF, dtype=HIGH) * 2.0 / HD))
    position = (me * rows + jnp.arange(rows, dtype=jnp.int32)).astype(HIGH)
    angles = frequency[:, None] * position[None, :]
    cosine, sine = jnp.cos(angles), jnp.sin(angles)
    gain_one = attn_gain[None, :]
    gain_two = ffn_gain[None, :]

    feature_rows = (width, rows)
    project_outs = [(feature_rows, LOW), (feature_rows, LOW), ((blocks, rows, 2 * KV_WIDTH), LOW)]
    tokens, cotangent, w_key, w_value, w_down = (v.T for v in (tokens, cotangent, w_key, w_value, w_down))
    weight_room = [pltpu.VMEM((blocks, width, hidden), LOW)] * 3
    attend_room = [
        pltpu.VMEM((keys, rows), HIGH),
        pltpu.VMEM((KVH, keys, HD), LOW),
        pltpu.VMEM((KV_WIDTH, keys), LOW),
    ]
    layer_outs = [
        (feature_rows, LOW),
        ((16, rows), HIGH),
        ((rows, width), HIGH),
        (feature_rows, LOW),
        ((blocks, rows, hidden), LOW),
        ((blocks, rows, hidden), LOW),
    ]

    def forward_first():
        outs = project_outs + layer_outs + [((rows, width), HIGH)] + project_outs
        outs += [((blocks - 1, width, hidden), LOW)] * 3
        copies = 3 * COPIES_SPREAD + 2 * COPIES_SHARE
        scratch = attend_room + weight_room
        scratch += [pltpu.SemaphoreType.DMA((3,)), pltpu.SemaphoreType.DMA((3, blocks - 1))]
        scratch += [pltpu.SemaphoreType.DMA((copies,)), pltpu.SemaphoreType.DMA((copies,))]
        body = functools.partial(forward_first_kernel, blocks)
        specs = [SMEM] + [VMEM] * 9 + [ANY] * 3
        return call(body, outs, specs, scratch, "forward_first", 3, 1)(
            where, tokens, gain_one, w_query, w_key, w_value, cosine, sine, w_output, gain_two, w_gate, w_up, w_down
        )

    outs = forward_first()
    a_one, q_one, kv_one, o_one, lse_one, m_one, b_one, g_one, u_one, h_one, a_two, q_two, kv_two = outs[:13]
    weights = [w_gate, outs[13], w_up, outs[14], w_down, outs[15]]
    attend_outs = [(feature_rows, LOW), ((blocks, 2 * KV_WIDTH, rows), LOW)]
    room = attention_room(blocks, rows, width)
    key_room = [(blocks, 2 * KV_WIDTH, rows), (2, 2 * KV_WIDTH, rows)] + [(2 * KV_WIDTH, rows)] * 3

    def middle():
        outs = [(feature_rows, LOW), (feature_rows, LOW), ((rows, width), HIGH), ((8, width), HIGH)]
        outs += [((width, 4 * rows), LOW)] * 2 + [((6, 4 * rows, hidden), LOW)]
        outs += [((n, 2 * rows), LOW) for n in (width, HQ * HD, KV_WIDTH, width)]
        scratch = room + [
            pltpu.VMEM((KV_WIDTH, keys), LOW),
            pltpu.VMEM(feature_rows, LOW),
            pltpu.VMEM((16, rows), HIGH),
            pltpu.VMEM((rows, width), HIGH),
        ]
        scratch += [pltpu.VMEM(feature_rows, LOW)] * 3 + [pltpu.VMEM((blocks, rows, hidden), LOW)] * 2
        scratch += [pltpu.VMEM((6, rows, hidden), LOW)] * 2 + [pltpu.VMEM(feature_rows, LOW)]
        scratch += [pltpu.VMEM(shape, LOW) for shape in key_room]
        scratch += [pltpu.VMEM(v.shape, LOW) for v in (cotangent, w_query, w_key, w_value)]
        scratch += weight_room + [pltpu.SemaphoreType.DMA((3, 2)), pltpu.SemaphoreType.DMA((LOCALS_MIDDLE,))]
        scratch += [pltpu.SemaphoreType.DMA((COPIES_MIDDLE,)), pltpu.SemaphoreType.DMA((COPIES_MIDDLE,))]
        given = [where, h_one, q_two, kv_two, w_output, gain_one, gain_two, cosine, sine]
        given += [cotangent, w_query, w_key, w_value, g_one, u_one, m_one, a_two, b_one, *weights]
        specs = [SMEM] + [VMEM] * 8 + [ANY] * 15
        return call(functools.partial(middle_kernel, blocks), outs, specs, scratch, "middle", 7, 3)(*given)

    block_out, c_one, dm_one, gains, b_all, f_all, rhs_all, *halves_two = middle()

    def close(h, grad_middle, grad_query, partial):
        sent = swap(jnp.stack([partial[1], partial[3]]), 1)
        far = swap((partial[2].astype(HIGH) + sent[1].astype(HIGH)).astype(LOW), 2)
        outs = [(feature_rows, HIGH), ((2 * KV_WIDTH, rows), LOW), ((1, width), HIGH)]
        given = [h, gain_one, grad_middle, grad_query, w_query, w_key, w_value, cosine, sine]
        given += [partial[0], sent[0], far]
        return call(close_kernel, outs, [VMEM] * 12, [], "close")(*given)

    def beside(parts):
        return jnp.concatenate(parts, axis=-1)

    def choose(zero, one):
        return jnp.where(low_bit == 0, zero, one)

    def halves(a, c, o, dq, dkv):
        dk, dv = dkv[:KV_WIDTH], dkv[KV_WIDTH:]
        left = [choose(a, c), swap(choose(c, a), 1)]
        long = [choose(dq, o), swap(choose(o, dq), 1)]
        short = [choose(dk, dv), swap(choose(dv, dk), 1)]
        return beside(left), beside(long), beside(short), beside([a, swap(a, 1)])

    places = lax.axis_size("dp")
    block = width // places

    def finish():
        outs = [(feature_rows, HIGH)] + [((block, hidden), HIGH)] * 3
        outs += [((block, n), HIGH) for n in (HQ * HD, KV_WIDTH, KV_WIDTH, HQ * HD)] + [((8, 128), HIGH)]
        low_room = [feature_rows] + key_room
        low_room += [(width, 4 * rows), (width, 4 * rows), (2, 4 * rows, hidden)]
        low_room += [(width, 4 * rows), (width, 4 * rows), (KV_WIDTH, 4 * rows), (width, 4 * rows)]
        low_room += [(2, 2, 2, 2, block, hidden)] * 3
        scratch = room + [pltpu.VMEM(shape, LOW) for shape in low_room]
        for order in ORDERS:
            scratch += halving_rooms(block, hidden, order)
        scratch += [pltpu.VMEM((2, 2, 2, 2, block, cut), LOW) for cut in ATTN_CUTS]
        for order, cut in zip(ATTN_ORDERS, ATTN_CUTS):
            scratch += halving_rooms(block, cut, order)
        scratch += [pltpu.VMEM((2, 2, block, cut), LOW) for cut in ATTN_CUTS]
        scratch += [pltpu.VMEM(shape, HIGH) for shape in ((2, 2, 2, 8, 128), (8, 8, 128), (2, 2, 8, 128))]
        scratch += [pltpu.SemaphoreType.DMA((40,)), pltpu.SemaphoreType.DMA((COPIES_FINISH,))]
        scratch += [pltpu.SemaphoreType.DMA((COPIES_FINISH,))]
        given = [where, tokens, gain_one, dm_one, w_output, q_one, kv_one, o_one, lse_one]
        given += [w_query, w_key, w_value, cosine, sine, a_one, c_one, *halves_two, gains]
        specs = [SMEM] + [VMEM] * 15 + [ANY] * 4 + [VMEM] + [ANY] * 3
        return call(finish_kernel, outs, specs, scratch, "finish", 0, 2)(*given, b_all, f_all, rhs_all)

    if places == 8 and blocks == 4:
        outs = finish()
        input_grad, gate_grad, up_grad, down_grad, query_grad, key_grad, value_grad, output_grad, gains = outs
        gains = gains[:2, :block]
    else:
        given = [where, dm_one, w_output, q_one, kv_one, o_one, lse_one, cosine, sine]
        dq_one, part_one = call(attend_back_kernel, attend_outs, [SMEM] + [VMEM] * 8, room, "attend_back")(*given)
        input_grad, dkv_one, gain_one_a = close(tokens, dm_one, dq_one, part_one)
        kept, sent = [], []
        for which in range(6):
            product = nn(b_all if which < 4 else f_all, rhs_all[which]).astype(LOW)
            (sent if which % 2 else kept).append(product)
        got = swap(beside(sent), 2)
        ffn = scatter_rows((beside(kept).astype(HIGH) + got.astype(HIGH)).astype(LOW), "dp")
        halves_one = halves(a_one, c_one, o_one, dq_one, dkv_one)
        left, long, short, side = (beside(pair) for pair in zip(halves_two, halves_one))
        attn = scatter_rows(beside([nt(left, long), nt(side, short)]).astype(LOW), "dp").astype(LOW)
        attn = (attn.astype(HIGH) + swap(attn, 2).astype(HIGH)).astype(LOW)
        other = swap(attn, 1)
        zero, one = choose(attn, other).astype(HIGH), choose(other, attn).astype(HIGH)
        gains = jnp.concatenate([gains[:1] + gain_one_a, gains[1:2]], axis=0)
        gains = lax.psum_scatter(lax.psum(gains, "head"), "dp", scatter_dimension=1, tiled=True)
        query_grad, key_grad = zero[:, : HQ * HD], zero[:, HQ * HD :]
        output_grad, value_grad = one[:, : HQ * HD], one[:, HQ * HD :]
        gate_grad, up_grad, down_grad = (ffn[:, i * hidden : (i + 1) * hidden] for i in range(3))
    return (
        block_out.T,
        input_grad.T,
        gains[0],
        query_grad,
        key_grad,
        value_grad,
        output_grad.T,
        gains[1],
        gate_grad,
        up_grad,
        down_grad.T,
    )


def solution(mesh):
    return jax.shard_map(
        shards,
        mesh=mesh,
        in_specs=(
            P(("dp", "head"), None),
            P(("dp", "head"), None),
            P("dp"),
            P(),
            P(),
            P(),
            P(),
            P(),
            P(),
            P(None, "head"),
            P(None, "head"),
            P("head", None),
        ),
        out_specs=(
            P(("dp", "head"), None),
            P(("dp", "head"), None),
            P("dp"),
            P("dp", None),
            P("dp", None),
            P("dp", None),
            P(None, "dp"),
            P("dp"),
            P("dp", "head"),
            P("dp", "head"),
            P("head", "dp"),
        ),
        check_vma=False,
    )
```

```python
import functools

import jax
import jax.numpy as jnp
from jax import lax
from jax.experimental import pallas as pl
from jax.experimental.pallas import tpu as pltpu
from jax.sharding import PartitionSpec as P

HQ = 15
KVH = 5
HD = 64
HALF = HD // 2
PER_GROUP = HQ // KVH
KV_WIDTH = KVH * HD
EPSILON = 1e-05
SCALE = HD ** (-0.5)
BLOCKED = -1e30
LOW = jnp.bfloat16
HIGH = jnp.float32
VMEM = pl.BlockSpec(memory_space=pltpu.VMEM)
SMEM = pl.BlockSpec(memory_space=pltpu.SMEM)
ANY = pl.BlockSpec(memory_space=pl.ANY)
LIMIT = 60 * 2**20
MESH = pl.DeviceIdType.MESH


def nn(left, right):
    return lax.dot_general(left, right, (((1,), (0,)), ((), ())), preferred_element_type=HIGH)


def nt(left, right):
    return lax.dot_general(left, right, (((1,), (1,)), ((), ())), preferred_element_type=HIGH)


def sigmoid(value):
    return 0.5 * (1.0 + jnp.tanh(0.5 * value))


def inverse_rms(rows):
    return lax.rsqrt(jnp.mean(rows * rows, axis=1, keepdims=True) + EPSILON)


def norm_back(values_in, gain, grad_normed, grad_skip):
    inverse = inverse_rms(values_in)
    normal = values_in * inverse
    gain_part = jnp.sum(grad_normed * normal, axis=0, keepdims=True)
    scaled = grad_normed * gain
    back = grad_skip + inverse * (scaled - normal * jnp.mean(scaled * normal, axis=1, keepdims=True))
    return gain_part, back


def turned(columns, cosine, sine, sign, factor):
    parts = []
    for start in range(0, columns.shape[0], HD):
        first = columns[start : start + HALF] * factor
        second = columns[start + HALF : start + HD] * factor
        parts.append(first * cosine - sign * second * sine)
        parts.append(second * cosine + sign * first * sine)
    return jnp.concatenate(parts, axis=0)


def project(hidden, gain, w_query, w_key, w_value, cosine, sine, a_ref, q_ref, kv_ref, ready):
    normed = hidden * inverse_rms(hidden) * gain
    low = normed.astype(LOW)
    keys = turned(nt(w_key[...], low), cosine, sine, 1.0, 1.0)
    kv_ref[:, :KV_WIDTH] = keys.T.astype(LOW)
    kv_ref[:, KV_WIDTH:] = nt(low, w_value[...]).astype(LOW)
    ready()
    queries = nn(low, w_query[...]).T
    q_ref[...] = turned(queries, cosine, sine, 1.0, SCALE).astype(LOW)
    a_ref[...] = normed.T.astype(LOW)


def fill_bias(where_ref, bias, rows, blocks):
    me = lax.axis_index("head")
    length = where_ref[0]
    key = lax.broadcasted_iota(jnp.int32, (rows, rows), 0)
    query = lax.broadcasted_iota(jnp.int32, (rows, rows), 1)
    for step in range(blocks):
        other = jnp.bitwise_xor(me, step)
        allowed = other * rows + key < length
        if step == 0:
            allowed &= key <= query
        else:
            allowed &= other < me
        bias[step * rows : (step + 1) * rows] = jnp.where(allowed, 0.0, BLOCKED)


def weights_in(sources, holders, sems, order):
    copies = {}
    for step in range(2):
        for which in order:
            holder = holders[which]
            target = holder.at[0] if step == 0 else holder.at[pl.ds(1, holder.shape[0] - 1)]
            copies[step, which] = pltpu.make_async_copy(sources[2 * which + step], target, sems.at[which, step])
            copies[step, which].start()
    return copies


def attend(bias, k_sc, vt_sc, q_ref, o_ref, lse_ref, event):
    def group_body(group, carry):
        keys = k_sc[group]
        values = vt_sc[pl.ds(pl.multiple_of(group * HD, HD), HD), :]
        event(group)
        for member in range(PER_GROUP):
            head = group * PER_GROUP + member
            at = pl.ds(pl.multiple_of(head * HD, HD), HD)
            scores = nn(keys, q_ref[at, :]) + bias[...]
            top = jnp.max(scores, axis=0, keepdims=True)
            exponent = jnp.exp(scores - top)
            total = jnp.sum(exponent, axis=0, keepdims=True)
            attended = nn(values, exponent.astype(LOW)) * (1.0 / total)
            o_ref[at, :] = attended.astype(LOW)
            lse_ref[pl.ds(head, 1), :] = top + jnp.log(total)
        return carry

    lax.fori_loop(0, KVH, group_body, 0)


def attend_first(bias, k_sc, vt_sc, q_ref, top_ref, total_ref, part_ref, half):
    def group_body(group, carry):
        keys = k_sc[group, :half]
        values = vt_sc[pl.ds(pl.multiple_of(group * HD, HD), HD), :half]
        for member in range(PER_GROUP):
            head = group * PER_GROUP + member
            at = pl.ds(pl.multiple_of(head * HD, HD), HD)
            scores = nn(keys, q_ref[at, :]) + bias[:half]
            top = jnp.max(scores, axis=0, keepdims=True)
            exponent = jnp.exp(scores - top)
            top_ref[pl.ds(head, 1), :] = top
            total_ref[pl.ds(head, 1), :] = jnp.sum(exponent, axis=0, keepdims=True)
            part_ref[at, :] = nn(values, exponent.astype(LOW))
        return carry

    lax.fori_loop(0, KVH, group_body, 0)


def attend_rest(bias, k_sc, vt_sc, q_ref, top_ref, total_ref, part_ref, half, o_ref, lse_ref):
    def group_body(group, carry):
        keys = k_sc[group, half:]
        values = vt_sc[pl.ds(pl.multiple_of(group * HD, HD), HD), half:]
        for member in range(PER_GROUP):
            head = group * PER_GROUP + member
            at = pl.ds(pl.multiple_of(head * HD, HD), HD)
            scores = nn(keys, q_ref[at, :]) + bias[half:]
            before = top_ref[pl.ds(head, 1), :]
            top = jnp.maximum(before, jnp.max(scores, axis=0, keepdims=True))
            exponent = jnp.exp(scores - top)
            rescale = jnp.exp(before - top)
            total = total_ref[pl.ds(head, 1), :] * rescale + jnp.sum(exponent, axis=0, keepdims=True)
            attended = (part_ref[at, :] * rescale + nn(values, exponent.astype(LOW))) * (1.0 / total)
            o_ref[at, :] = attended.astype(LOW)
            lse_ref[pl.ds(head, 1), :] = top + jnp.log(total)
        return carry

    lax.fori_loop(0, KVH, group_body, 0)


def lay_keys(kv_ref, k_sc, vt_sc, steps, rows):
    for step in steps:
        at = slice(step * rows, (step + 1) * rows)
        for group in range(KVH):
            k_sc[group, at] = kv_ref[step, :, group * HD : (group + 1) * HD]
        vt_sc[:, at] = kv_ref[step, :, KV_WIDTH:].T


def after_attention(hidden, o_ref, wo_ref, gain, m_ref, b_ref):
    middle = hidden + nn(o_ref[...].T, wo_ref[...])
    m_ref[...] = middle
    normed = middle * inverse_rms(middle) * gain
    b_ref[...] = normed.T.astype(LOW)
    return middle, normed.astype(LOW)


def hidden_part(normed, wg, wu, wd, g_ref, u_ref, step):
    gate = nn(normed, wg[step])
    up = nn(normed, wu[step])
    g_ref[step] = gate.astype(LOW)
    u_ref[step] = up.astype(LOW)
    active = (gate * sigmoid(gate) * up).astype(LOW)
    return nt(active, wd[step])


def partner(axis, distance):
    return {axis: jnp.bitwise_xor(lax.axis_index(axis), distance)}


def greet(partners):
    barrier = pltpu.get_barrier_semaphore()
    for axis, distance in partners:
        pl.semaphore_signal(barrier, inc=1, device_id=partner(axis, distance), device_id_type=MESH)
    pl.semaphore_wait(barrier, len(partners))


class Links:
    def __init__(self, send, receive):
        self.send, self.receive, self.used = send, receive, 0
        self.flying = []

    def push(self, source, target, to):
        copy = pltpu.make_async_remote_copy(
            src_ref=source,
            dst_ref=target,
            send_sem=self.send.at[self.used],
            recv_sem=self.receive.at[self.used],
            device_id=partner(*to),
            device_id_type=MESH,
        )
        self.used += 1
        self.flying.append(copy)
        return copy

    def drain(self):
        for copy in self.flying:
            copy.wait_send()


class Local:
    def __init__(self, sems):
        self.sems, self.used, self.flying = sems, 0, []

    def move(self, source, target, start=True):
        copy = pltpu.make_async_copy(source, target, self.sems.at[self.used])
        self.used += 1
        self.flying.append(copy)
        if start:
            copy.start()
        return copy

    def drain(self):
        for copy in self.flying:
            copy.wait()


SIBLING, ACROSS, SIDE, BEYOND = ("head", 1), ("head", 2), ("dp", 1), ("dp", 2)


class Share:
    def __init__(self, links, kv_ref):
        self.near = links.push(kv_ref.at[0], kv_ref.at[1], SIBLING)
        self.far = links.push(kv_ref.at[0], kv_ref.at[2], ACROSS)
        self.forth = links.push(kv_ref.at[2], kv_ref.at[3], SIBLING)

    def start(self):
        self.far.start()
        self.near.start()

    def pass_on(self):
        self.far.wait_recv()
        self.forth.start()

    def finish(self):
        self.near.wait_recv()
        self.forth.wait_recv()


class Spread:
    def __init__(self, links, own, all_ref):
        rows = own.shape[0]
        quarter = rows // 4
        cut = quarter // 32 * 16
        place = lax.axis_index("dp") % 4

        def part(ref, which, start=0, size=quarter):
            first = jnp.bitwise_xor(place, which) * quarter + start
            return ref.at[pl.ds(pl.multiple_of(first, 16), size)]

        far, diag = all_ref.at[2], all_ref.at[3]

        def move(which, to, *piece):
            return links.push(part(far, which, *piece), part(far, which, *piece), to)

        def aside(which):
            return links.push(part(far, which), part(diag, which), SIBLING)

        self.near = links.push(own, all_ref.at[1], SIBLING)
        self.cross = links.push(part(own, 0), part(far, 0), ACROSS)
        self.side, self.beyond = move(0, SIDE), move(0, BEYOND)
        self.side_half = move(2, SIDE, cut, quarter - cut)
        self.beyond_half = move(1, BEYOND, 0, cut)
        self.asides = [aside(which) for which in range(4)]

    def first(self):
        self.cross.wait_recv()
        self.side.start()
        self.beyond.start()
        self.asides[0].start()

    def second(self):
        self.side.wait_recv()
        self.beyond_half.start()
        self.asides[1].start()
        self.beyond.wait_recv()
        self.side_half.start()
        self.asides[2].start()

    def third(self):
        self.side_half.wait_recv()
        self.beyond_half.wait_recv()
        self.asides[3].start()

    def last(self):
        for copy in self.asides:
            copy.wait_recv()


COPIES_SHARE = 3
COPIES_SPREAD = 10


def forward_first_kernel(blocks, *refs):
    where_ref, h_ref, gain_ref, cos_ref, sin_ref = refs[:5]
    late_refs, owns = refs[5:9], refs[9:12]
    a_ref, q_ref, kv_ref, o_ref, lse_ref, m_ref, b_ref, g_ref, u_ref, out_ref = refs[12:22]
    kept = refs[22:25]
    bias, k_sc, vt_sc, wg, wu, wd = refs[25:31]
    late, (load, send, receive) = refs[31:35], refs[35:]
    wk_ref, wv_ref, wq_ref, wo_ref = late
    rows = h_ref.shape[1]
    links, local = Links(send, receive), Local(load)
    held = (wg, wu, wd)
    lates = [local.move(source, target) for source, target in zip(late_refs, late)]
    loads = [local.move(own, all_ref.at[0], False) for own, all_ref in zip(owns, held)]
    gate_way, up_way, down_way = spreads = [Spread(links, own, all_ref) for own, all_ref in zip(owns, held)]
    share = Share(links, kv_ref)
    greet((SIBLING, ACROSS, SIDE, BEYOND))
    gate_way.cross.start()
    up_way.cross.start()
    for spread, copy in zip(spreads, loads):
        spread.near.start()
        copy.start()
    hidden = h_ref[...].astype(HIGH).T

    def queue():
        share.start()
        down_way.cross.start()
        lates[2].wait()

    lates[0].wait()
    lates[1].wait()
    gain_one = gain_ref[0:1].astype(HIGH)
    project(hidden, gain_one, wq_ref, wk_ref, wv_ref, cos_ref[...], sin_ref[...], a_ref, q_ref, kv_ref.at[0], queue)
    gate_way.first()
    fill_bias(where_ref, bias, rows, blocks)
    up_way.first()
    gate_way.second()
    share.pass_on()
    share.finish()
    lay_keys(kv_ref, k_sc, vt_sc, range(blocks), rows)

    def event(group):
        pl.when(group == 1)(up_way.second)
        pl.when(group == 2)(gate_way.third)
        pl.when(group == 3)(down_way.first)

    attend(bias, k_sc, vt_sc, q_ref, o_ref, lse_ref, event)
    lates[3].wait()
    middle, normed = after_attention(hidden, o_ref, wo_ref, gain_ref[1:2].astype(HIGH), m_ref, b_ref)
    saves = []

    def keep(step):
        for which in range(3):
            saves.append(local.move(held[which].at[step], kept[which].at[step - 1]))

    for copy in loads:
        copy.wait()
    total = middle + hidden_part(normed, wg, wu, wd, g_ref, u_ref, 0)
    up_way.third()
    down_way.second()
    for spread in spreads:
        spread.near.wait_recv()
    keep(1)
    total = total + hidden_part(normed, wg, wu, wd, g_ref, u_ref, 1)
    down_way.third()
    keep(2)
    total = total + hidden_part(normed, wg, wu, wd, g_ref, u_ref, 2)
    for spread in spreads:
        spread.last()
    keep(3)
    total = total + hidden_part(normed, wg, wu, wd, g_ref, u_ref, 3)
    out_ref[...] = total
    for copy in saves:
        copy.wait()
    links.drain()


def ffn_back(grad, copies, g_ref, u_ref, m_ref, gain, wg, wu, wd, mine_ref, theirs_ref):
    low_grad = grad.astype(LOW)
    grad_normed = jnp.zeros(m_ref.shape, HIGH)
    for step in range(wg.shape[0]):
        if copies and step < 2:
            copies[step, 2].wait()
        grad_active = nn(low_grad, wd[step])
        gate = g_ref[step].astype(HIGH)
        up = u_ref[step].astype(HIGH)
        sig = sigmoid(gate)
        silu = gate * sig
        grad_gate = (grad_active * up * sig * (1.0 + gate * (1.0 - sig))).astype(LOW)
        grad_up = (grad_active * silu).astype(LOW)
        kept = mine_ref if step % 2 == 0 else theirs_ref
        kept[step // 2] = grad_gate
        kept[2 + step // 2] = grad_up
        kept[4 + step // 2] = (silu * up).astype(LOW)
        if copies and step < 2:
            copies[step, 0].wait()
            copies[step, 1].wait()
        grad_normed = grad_normed + nt(grad_gate, wg[step]) + nt(grad_up, wu[step])
    return norm_back(m_ref[...], gain, grad_normed, grad)


def lay_back(kv_ref, k_sc, v_sc, kt_sc, blocks, rows, keys_laid):
    for step in range(blocks):
        at = slice(step * rows, (step + 1) * rows)
        for group in range(KVH):
            if not keys_laid:
                k_sc[group, at] = kv_ref[step, :, group * HD : (group + 1) * HD]
            v_sc[group, at] = kv_ref[step, :, KV_WIDTH + group * HD : KV_WIDTH + (group + 1) * HD]
        kt_sc[:, at] = kv_ref[step, :, :KV_WIDTH].T


def attend_back(grad_middle, wo_ref, q_ref, o_ref, lse_ref, cosine, sine, dq_ref, dkv_ref, room, before, between):
    bias, k_sc, v_sc, kt_sc, do_sc, delta, dq_sc = room
    keys, rows = bias.shape
    blocks = keys // rows
    half = keys // 2
    do_sc[...] = nt(wo_ref[...], grad_middle.astype(LOW)).astype(LOW)
    for head in range(HQ):
        at = slice(head * HD, (head + 1) * HD)
        product = do_sc[at].astype(HIGH) * o_ref[at].astype(HIGH)
        delta[head : head + 1] = jnp.sum(product, axis=0, keepdims=True)

    def one_pass(start, last, event):
        cut = slice(start, start + half)

        def group_body(group, carry):
            event(group)
            group_keys = k_sc[group, cut]
            values = v_sc[group, cut]
            at = pl.ds(pl.multiple_of(group * HD, HD), HD)
            after = pl.ds(pl.multiple_of(KV_WIDTH + group * HD, HD), HD)
            keys_t = kt_sc[at, cut]
            grad_keys = jnp.zeros((HD, half), HIGH)
            grad_values = jnp.zeros((HD, half), HIGH)
            for member in range(PER_GROUP):
                head = group * PER_GROUP + member
                head_at = pl.ds(pl.multiple_of(head * HD, HD), HD)
                query = q_ref[head_at, :]
                grad_out = do_sc[head_at, :]
                scores = nn(group_keys, query) + bias[cut]
                prob = jnp.exp(scores - lse_ref[pl.ds(head, 1), :])
                grad_prob = nn(values, grad_out)
                grad_score = (prob * (grad_prob - delta[pl.ds(head, 1), :])).astype(LOW)
                grad_query = nn(keys_t, grad_score)
                if last:
                    grad_query = grad_query + dq_sc[head_at, :]
                    dq_ref[head_at, :] = turned(grad_query, cosine, sine, -1.0, SCALE).astype(LOW)
                else:
                    dq_sc[head_at, :] = grad_query
                grad_keys = grad_keys + nt(query, grad_score)
                grad_values = grad_values + nt(grad_out, prob.astype(LOW))
            for step in range(blocks // 2):
                part = slice(step * rows, (step + 1) * rows)
                dkv_ref[start // rows + step, at, :] = grad_keys[:, part].astype(LOW)
                dkv_ref[start // rows + step, after, :] = grad_values[:, part].astype(LOW)
            return carry

        lax.fori_loop(0, KVH, group_body, 0)

    one_pass(half, False, before)
    one_pass(0, True, between)


class Settle:
    def __init__(self, links, dkv_ref, near_ref, sum_ref, far_ref):
        self.refs = dkv_ref, near_ref, sum_ref, far_ref
        self.aside = links.push(dkv_ref.at[3], near_ref.at[1], SIBLING)
        self.near = links.push(dkv_ref.at[1], near_ref.at[0], SIBLING)
        self.far = links.push(sum_ref, far_ref, ACROSS)

    def between(self, group):
        dkv_ref, near_ref, sum_ref, _ = self.refs
        pl.when(group == 0)(self.aside.start)

        @pl.when(group == 1)
        def _():
            self.aside.wait_recv()
            sum_ref[...] = (dkv_ref[2].astype(HIGH) + near_ref[1].astype(HIGH)).astype(LOW)
            self.far.start()

    def finish(self):
        dkv_ref, near_ref, _, far_ref = self.refs
        self.near.start()
        self.near.wait_recv()
        self.far.wait_recv()
        return dkv_ref[0].astype(HIGH) + near_ref[0].astype(HIGH) + far_ref[...].astype(HIGH)


def attention_room(blocks, rows, width):
    keys = blocks * rows
    return [
        pltpu.VMEM((keys, rows), HIGH),
        pltpu.VMEM((KVH, keys, HD), LOW),
        pltpu.VMEM((KVH, keys, HD), LOW),
        pltpu.VMEM((KV_WIDTH, keys), LOW),
        pltpu.VMEM((width, rows), LOW),
        pltpu.VMEM((16, rows), HIGH),
        pltpu.VMEM((width, rows), HIGH),
    ]


def share_out(local, links, core, zero, one, target, own_at, got_at):
    if zero is one:
        keep = local.move(zero, target.at[own_at])
        send = links.push(zero, target.at[got_at], SIBLING)
        send.start()
        return keep, send
    keep = local.move(zero, target.at[own_at], False)
    keep_one = pltpu.make_async_copy(one, target.at[own_at], local.sems.at[local.used - 1])
    send = links.push(one, target.at[got_at], SIBLING)
    links.used -= 1
    links.flying.pop()
    send_zero = links.push(zero, target.at[got_at], SIBLING)

    @pl.when(core == 0)
    def _():
        keep.start()
        send.start()

    @pl.when(core == 1)
    def _():
        keep_one.start()
        send_zero.start()

    return keep, send


COPIES_MIDDLE = 20
LOCALS_MIDDLE = 24


def middle_kernel(blocks, *refs):
    where_ref, h_ref, gain_ref, cos_ref, sin_ref = refs[:5]
    late_refs = refs[5:10]
    g_any, u_any, m_any, b_any = refs[10:14]
    sources = refs[14:20]
    out_ref, c_ref, dm_ref, gains_ref = refs[20:24]
    b_all, f_all, rhs_all, left_two, long_two, short_two, side_two = refs[24:31]
    room = refs[31:38]
    bias, k_sc, v_sc, kt_sc = room[:4]
    part_sc = room[6]
    vt_sc, o_sc, lse_sc, m_sc, b_sc, f_sc, c_sc, g_sc, u_sc = refs[38:47]
    mine, theirs, dq_sc, dkv_sc, dkv_near, dkv_sum, dkv_far, dkv_low = refs[47:55]
    late = refs[55:60]
    a_sc, q_ref, kv_ref, top_sc, total_sc = refs[60:65]
    wk, wv, wq, wo_ref, cot = late
    wg, wu, wd, sems, load, send, receive = refs[65:]
    rows = h_ref.shape[0]
    core = lax.axis_index("head") % 2
    local = Local(load)
    links = Links(send, receive)
    lates = [local.move(source, target) for source, target in zip(late_refs, late)]
    copies = weights_in(sources, (wg, wu, wd), sems, (0, 1, 2))
    share = Share(links, kv_ref)
    settle = Settle(links, dkv_sc, dkv_near, dkv_sum, dkv_far)
    spans = [pl.ds(i * rows, rows) for i in range(4)]
    everything = slice(None)

    def both(source, target, place):
        keep = local.move(source, target.at[(*place, spans[both.layer])])
        copy = links.push(source, target.at[(*place, spans[both.layer + 1])], SIBLING)
        copy.start()
        return keep, copy

    greet((SIBLING, ACROSS))
    both.layer = 2
    posted = [both(b_any, b_all, (everything,))]
    both.layer = 0
    cosine, sine = cos_ref[...], sin_ref[...]
    half = blocks * rows // 2

    def ready():
        share.start()
        lates[2].wait()

    lates[0].wait()
    lates[1].wait()
    gain_one = gain_ref[0:1].astype(HIGH)
    project(h_ref[...], gain_one, wq, wk, wv, cosine, sine, a_sc, q_ref, kv_ref.at[0], ready)
    fill_bias(where_ref, bias, rows, blocks)
    share.near.wait_recv()
    lay_keys(kv_ref, k_sc, vt_sc, range(blocks // 2), rows)
    attend_first(bias, k_sc, vt_sc, q_ref, top_sc, total_sc, part_sc, half)
    share.pass_on()
    share.forth.wait_recv()
    lay_keys(kv_ref, k_sc, vt_sc, range(blocks // 2, blocks), rows)
    attend_rest(bias, k_sc, vt_sc, q_ref, top_sc, total_sc, part_sc, half, o_sc, lse_sc)
    lates[3].wait()
    total, normed = after_attention(h_ref[...], o_sc, wo_ref, gain_ref[1:2].astype(HIGH), m_sc, b_sc)
    posted.append(both(b_sc, b_all, (everything,)))
    for step in range(blocks):
        if step < 2:
            for which in range(3):
                copies[step, which].wait()
        total = total + hidden_part(normed, wg, wu, wd, g_sc, u_sc, step)
    out_ref[...] = total.T.astype(LOW)
    lay_back(kv_ref, k_sc, v_sc, kt_sc, blocks, rows, True)

    lates[4].wait()
    row = lax.axis_index("head") * rows + lax.broadcasted_iota(jnp.int32, (rows, 1), 0)
    grad = jnp.where(row < where_ref[0], cot[...].astype(HIGH).T, 0.0)
    f_sc[...] = grad.T.astype(LOW)
    first_f = both(f_sc, f_all, (everything,))
    gain_two = gain_ref[1:2].astype(HIGH)
    gain_part, grad_middle = ffn_back(grad, None, g_sc, u_sc, m_sc, gain_two, wg, wu, wd, mine, theirs)
    first_loads = [local.move(source, target) for source, target in ((g_any, g_sc), (u_any, u_sc), (m_any, m_sc))]
    keep_mine = local.move(mine, rhs_all.at[:, spans[0]])
    send_theirs = links.push(theirs, rhs_all.at[:, spans[1]], SIBLING)
    send_theirs.start()
    gains_ref[...] = jnp.zeros(gains_ref.shape, HIGH)
    gains_ref[1:2] = gain_part
    c_sc[...] = grad_middle.T.astype(LOW)
    attend_back(
        grad_middle, wo_ref, q_ref, o_sc, lse_sc, cosine, sine, dq_sc, dkv_sc, room, lambda group: None, settle.between
    )
    grad_keys, grad_values = close_keys(settle.finish(), cosine, sine, dkv_low)
    low_rows, high_rows = pl.ds(0, KV_WIDTH), pl.ds(KV_WIDTH, KV_WIDTH)
    for zero, one, target in (
        (a_sc, c_sc, left_two),
        (dq_sc, o_sc, long_two),
        (dkv_low.at[low_rows], dkv_low.at[high_rows], short_two),
        (a_sc, a_sc, side_two),
    ):
        posted.append(
            share_out(local, links, core, zero, one, target, (everything, spans[0]), (everything, spans[1]))
        )
    gain_part, grad = close_rows(h_ref[...], gain_one, grad_middle, dq_sc, grad_keys, grad_values, wq, wk, wv)
    gains_ref[0:1] = gain_part

    first_f[0].wait()
    first_f[1].wait_send()
    keep_mine.wait()
    send_theirs.wait_send()
    for copy in first_loads:
        copy.wait()
    f_sc[...] = grad.T.astype(LOW)
    both.layer = 2
    posted.append(both(f_sc, f_all, (everything,)))
    gain_part, grad_middle = ffn_back(grad, None, g_sc, u_sc, m_sc, gain_two, wg, wu, wd, mine, theirs)
    keep_last = local.move(mine, rhs_all.at[:, spans[2]])
    send_last = links.push(theirs, rhs_all.at[:, spans[3]], SIBLING)
    send_last.start()
    gains_ref[1:2] = gains_ref[1:2] + gain_part
    dm_ref[...] = grad_middle
    c_ref[...] = grad_middle.T.astype(LOW)
    for keep, copy in posted:
        keep.wait()
        copy.wait()
    first_f[1].wait_recv()
    send_theirs.wait_recv()
    keep_last.wait()
    send_last.wait()
    for copy in (settle.aside, settle.near, settle.far, share.near, share.far, share.forth):
        copy.wait_send()


def attend_back_kernel(*refs):
    where_ref, dm_ref, wo_ref, q_ref, kv_ref, o_ref, lse_ref, cos_ref, sin_ref, dq_ref, dkv_ref = refs[:11]
    room = refs[11:]
    bias, k_sc, v_sc, kt_sc = room[:4]
    blocks, rows = kv_ref.shape[:2]
    fill_bias(where_ref, bias, rows, blocks)
    lay_back(kv_ref, k_sc, v_sc, kt_sc, blocks, rows, False)
    attend_back(
        dm_ref[...], wo_ref, q_ref, o_ref, lse_ref, cos_ref[...], sin_ref[...], dq_ref, dkv_ref, room, lambda group: None, lambda group: None
    )


def close_keys(total, cosine, sine, dkv_ref):
    turned_keys = turned(total[:KV_WIDTH], cosine, sine, -1.0, 1.0)
    dkv_ref[:KV_WIDTH] = turned_keys.astype(LOW)
    dkv_ref[KV_WIDTH:] = total[KV_WIDTH:].astype(LOW)
    return turned_keys.T.astype(LOW), total[KV_WIDTH:].T.astype(LOW)


def close_rows(hidden, gain, grad_middle, dq_ref, grad_keys, grad_values, wq_ref, wk_ref, wv_ref):
    grad_normed = nn(wq_ref[...], dq_ref[...]).T
    grad_normed = grad_normed + nn(grad_keys, wk_ref[...]) + nn(grad_values, wv_ref[...])
    return norm_back(hidden, gain, grad_normed, grad_middle)


def close_kernel(*refs):
    h_ref, gain_ref, dm_ref, dq_ref, wq_ref, wk_ref, wv_ref, cos_ref, sin_ref = refs[:9]
    own, near, far, dh_ref, dkv_ref, gain_part_ref = refs[9:]
    total = own[...].astype(HIGH) + near[...].astype(HIGH) + far[...].astype(HIGH)
    grad_keys, grad_values = close_keys(total, cos_ref[...], sin_ref[...], dkv_ref)
    hidden = h_ref[...].astype(HIGH).T
    gain = gain_ref[0:1].astype(HIGH)
    gain_part, grad_in = close_rows(hidden, gain, dm_ref[...], dq_ref, grad_keys, grad_values, wq_ref, wk_ref, wv_ref)
    gain_part_ref[...] = gain_part
    dh_ref[...] = grad_in.T


class Halving:
    def __init__(self, links, steps):
        self.steps = [(links.push(sent, got, to), kept, got) for sent, kept, got, to in steps]

    def start(self):
        self.steps[0][0].start()

    def fold(self, which):
        copy, kept, got = self.steps[which]
        copy.wait_recv()
        total = kept[...].astype(HIGH) + got[...].astype(HIGH)
        if which == len(self.steps) - 1:
            self.done(total)
        else:
            kept[...] = total.astype(kept.dtype)
            self.steps[which + 1][0].start()


class Regather(Halving):
    def share(self, links, held):
        self.held = held
        self.across = links.push(held.at[0, 0], held.at[0, 1], ACROSS)
        self.aside = links.push(held.at[0], held.at[1], SIBLING)

    def done(self, total):
        self.held[0, 0] = total.astype(LOW)
        self.across.start()

    def fold(self, which):
        if which < len(self.steps):
            Halving.fold(self, which)
        elif which == len(self.steps):
            self.across.wait_recv()
            self.aside.start()
        else:
            self.aside.wait_recv()


class Rows:
    def __init__(self, links, whole, side, got, out):
        self.steps = (
            (whole.at[:, :, 1], side, whole.at[:, :, 0], SIDE),
            (whole.at[:, 1, 0], got.at[pl.ds(0, 2)], whole.at[:, 0, 0], BEYOND),
            (whole.at[1, 0, 0], got.at[2], whole.at[0, 0, 0], FAR_SIDE),
            (whole.at[0, 0, 0], got.at[3], None, ACROSS),
            (got.at[4], got.at[5], None, SIBLING),
        )
        self.copies = [links.push(source, target, to) for source, target, _, to in self.steps]
        self.whole, self.got, self.out = whole, got, out

    def start(self):
        self.copies[0].start()

    def fold(self, which):
        self.copies[which].wait_recv()
        if which < 3:
            _, target, kept, _ = self.steps[which]
            kept[...] = kept[...] + target[...]
        elif which == 3:
            self.got[4] = self.whole[0, 0, 0] + self.got[3]
        else:
            self.out[...] = self.got[4] + self.got[5]
        if which < 4:
            self.copies[which + 1].start()


FAR_SIDE = ("dp", 4)


def halved(kind, links, whole, rooms, order):
    where = {"X": 0, "Z1": 1, "Z0": 2, "Y": 3}
    to = {"X": ACROSS, "Z1": FAR_SIDE, "Z0": BEYOND, "Y": SIDE}
    chosen = [slice(None)] * 4
    steps = []
    for axis, room in zip(order, rooms):
        sent, kept = list(chosen), list(chosen)
        sent[where[axis]], kept[where[axis]] = 1, 0
        steps.append((whole.at[tuple(sent)], whole.at[tuple(kept)], room, to[axis]))
        chosen = kept
    return kind(links, steps)


def halving_rooms(block, columns, order):
    left = [2, 2, 2, 2]
    where = {"X": 0, "Z1": 1, "Z0": 2, "Y": 3}
    rooms = []
    for axis in order:
        left[where[axis]] = 0
        rooms.append(pltpu.VMEM(tuple(n for n in left if n) + (block, columns), LOW))
    return rooms


FFN_CUTS = ((0, 256), (256, 384))
ORDERS = (
    ("Y", "X", "Z0", "Z1"),
    ("Z0", "Y", "Z1", "X"),
    ("Z0", "Z1", "X", "Y"),
    ("Y", "Z0", "X", "Z1"),
    ("X", "Y", "Z0", "Z1"),
    ("X", "Y", "Z0", "Z1"),
)
ATTN_ORDERS = (
    ("Z0", "X", "Z1", "Y"),
    ("Y", "Z0", "X", "Z1"),
    ("X", "Z0", "Y", "Z1"),
)
ATTN_CUTS = (128, 256, 256)
PLAN = (
    (("begin",), ()),
    (("w", 1, 1), ()),
    (("w", 1, 0), ()),
    (("w", 3, 1), ()),
    (("w", 3, 0), ()),
    (("w", 4, 1), ()),
    (("w", 4, 0), ()),
    (("w", 2, 1), ()),
    (("w", 2, 0), ()),
    (("prep",), ()),
    (("p", 0), ()),
    (("p", 1), ()),
    (("p", 2), ()),
    (("p", 3), ()),
    (("p", 4), ()),
    (("q", 0), ()),
    (("q", 1), ("f4",)),
    (("q", 2), ("f1",)),
    (("q", 3), ("f3",)),
    (("q", 4), ()),
    (("w", 5, 1), ()),
    (("w", 5, 0), ()),
    (("w", 0, 1), ("f4",)),
    (("w", 0, 0), ()),
    (("kf",), ("f2",)),
    (("close",), ()),
    (("attn",), ("f1",)),
    (("tail",), ("f2", "f3", "f5", "f0", "f4", "f1", "f4", "a2", "a1", "g0", "a0", "f2", "f3", "a2", "f5", "f2", "f0", "f3", "a2", "f1", "a1", "g0", "a0", "a2", "g0", "a1", "a0", "f5", "a2", "g0", "a0", "a2", "g0", "a1", "f0", "a0", "f5", "a1", "a0", "a1", "f0")),
)
PARTS = len(FFN_CUTS)
COPIES_FINISH = 4 * len(ORDERS) + 6 * len(ATTN_ORDERS) + 5 + 3 + 4


def finish_kernel(*refs):
    where_ref, gain_ref, cos_ref, sin_ref, gains_ref = refs[:5]
    late_refs, lse_any = refs[5:14], refs[14]
    a_ref, c_ref, left_two, long_two, short_two, side_two, b_any, f_any, rhs_any = refs[15:24]
    count = 4
    dh_ref, gate_out, up_out, down_out = refs[24:28]
    query_out, key_out, value_out, output_out, gain_out = refs[28:33]
    refs = refs[33:]

    def taken(count):
        nonlocal refs
        first, refs = refs[:count], refs[count:]
        return first

    room = taken(7)
    dq_ref, dkv_ref, dkv_near, dkv_sum, dkv_far, dkv_low = taken(6)
    late = taken(9)
    q_ref, kv_ref, o_ref, wo_ref, dm_ref, h_ref, wq_ref, wk_ref, wv_ref = late
    lse_ref = taken(1)[0]
    b_all, f_all, rhs, left_all, long_all, short_all, side_all = taken(7)
    wholes = taken(len(ORDERS))
    rooms = [taken(4) for _ in ORDERS]
    attn_wholes = taken(len(ATTN_ORDERS))
    attn_rooms = [taken(4) for _ in ATTN_ORDERS]
    attn_alls = taken(len(ATTN_ORDERS))
    gain_whole, gain_got, gain_side, load, send, receive = refs
    rows = h_ref.shape[1]
    block = gate_out.shape[0]
    place = lax.axis_index("dp")
    head_at = lax.axis_index("head")
    core, across = head_at % 2, head_at // 2
    links, local = Links(send, receive), Local(load)
    sums = {}
    for index, (whole, got, order) in enumerate(zip(wholes, rooms, ORDERS)):
        start, cut = FFN_CUTS[index % PARTS]
        out = (gate_out, up_out, down_out)[index // PARTS].at[:, start : start + cut]
        reduce = halved(Halving, links, whole, got, order)
        reduce.done = functools.partial(out.__setitem__, Ellipsis)
        sums["f%d" % index] = reduce
    for index, (whole, got, order) in enumerate(zip(attn_wholes, attn_rooms, ATTN_ORDERS)):
        reduce = halved(Regather, links, whole, got, order)
        reduce.share(links, attn_alls[index])
        sums["a%d" % index] = reduce
    sums["g0"] = Rows(links, gain_whole, gain_side, gain_got, gain_out)
    seen = {name: 0 for name in sums}
    plan = []
    for step, names in PLAN:
        folds = []
        for name in names:
            folds.append((name, seen[name]))
            seen[name] += 1
        plan.append((step, folds))

    def take(folds):
        for name, which in folds:
            sums[name].fold(which)

    products = [step for step, _ in plan if step[0] == "w"]

    def fetch(turn):
        _, index, half = products[turn]
        start, cut = FFN_CUTS[index % PARTS]
        source = rhs_any.at[2 * (index // PARTS) + half, :, pl.ds(start, cut)]
        return local.move(source, rhs.at[turn % 2, :, pl.ds(0, cut)])

    b_load = local.move(b_any, b_all)
    coming = {0: fetch(0)}
    f_load = local.move(f_any, f_all)
    lates = [local.move(source, target) for source, target in zip(late_refs, late)]
    lates.append(local.move(lse_any, lse_ref))
    two = ((left_two, left_all), (long_two, long_all), (short_two, short_all), (side_two, side_all))
    two_loads = [local.move(source, target.at[:, pl.ds(0, 2 * rows)]) for source, target in two]
    greet((SIBLING, ACROSS, SIDE, BEYOND, FAR_SIDE))
    b_load.wait()

    def lay(product, whole, first):
        for index in range(8):
            relative = jnp.bitwise_xor(index, place)
            whole[first, relative // 4, relative // 2 % 2, relative % 2] = product[
                index * block : (index + 1) * block
            ].astype(LOW)

    f_ready = []

    def multiply(index, half):
        turn = products.index(("w", index, half))
        coming[turn].wait()
        if turn + 1 < len(products):
            coming[turn + 1] = fetch(turn + 1)
        if index >= 2 * PARTS and not f_ready:
            f_load.wait()
            f_ready.append(True)
        cut = FFN_CUTS[index % PARTS][1]
        lay(nn((b_all if index < 2 * PARTS else f_all)[...], rhs[turn % 2, :, :cut]), wholes[index], half)
        if half == (1 if ORDERS[index][0] == "X" else 0):
            sums["f%d" % index].start()

    cosine, sine = cos_ref[...], sin_ref[...]
    settle = Settle(links, dkv_ref, dkv_near, dkv_sum, dkv_far)
    low_rows, own_at, got_at = pl.ds(0, KV_WIDTH), pl.ds(2 * rows, rows), pl.ds(3 * rows, rows)
    high_rows, everything = pl.ds(KV_WIDTH, KV_WIDTH), slice(None)
    passes = {"p": {}, "q": {}}
    for step, folds in plan:
        if step[0] in passes:
            passes[step[0]][step[1]] = folds

    def at_group(which, group):
        for when, folds in passes[which].items():
            if folds:
                pl.when(group == when)(functools.partial(take, folds))
        if which == "q":
            settle.between(group)

    for step, folds in plan:
        if step[0] in passes:
            continue
        take(folds)
        if step[0] == "w":
            multiply(step[1], step[2])
        elif step[0] == "prep":
            for copy in lates:
                copy.wait()
            bias, k_sc, v_sc, kt_sc = room[:4]
            fill_bias(where_ref, bias, rows, count)
            lay_back(kv_ref, k_sc, v_sc, kt_sc, count, rows, False)
            attend_back(
                dm_ref[...],
                wo_ref,
                q_ref,
                o_ref,
                lse_ref,
                cosine,
                sine,
                dq_ref,
                dkv_ref,
                room,
                functools.partial(at_group, "p"),
                functools.partial(at_group, "q"),
            )
        elif step[0] == "kf":
            grad_keys, grad_values = close_keys(settle.finish(), cosine, sine, dkv_low)
            swaps = []
            for zero, one, target in (
                (a_ref, c_ref, left_all),
                (dq_ref, o_ref, long_all),
                (dkv_low.at[low_rows], dkv_low.at[high_rows], short_all),
                (a_ref, a_ref, side_all),
            ):
                swaps.append(
                    share_out(local, links, core, zero, one, target, (everything, own_at), (everything, got_at))
                )
        elif step[0] == "close":
            hidden = h_ref[...].astype(HIGH).T
            gain = gain_ref[0:1].astype(HIGH)
            gain_part, grad_in = close_rows(
                hidden, gain, dm_ref[...], dq_ref, grad_keys, grad_values, wq_ref, wk_ref, wv_ref
            )
            dh_ref[...] = grad_in.T
            summed = gains_ref[...] + jnp.concatenate([gain_part, jnp.zeros((7, gain_part.shape[1]), HIGH)], axis=0)
            for index in range(8):
                relative = jnp.bitwise_xor(index, place)
                spot = relative // 4, relative // 2 % 2, relative % 2
                gain_whole[(*spot, slice(None), slice(0, block))] = summed[:, index * block : (index + 1) * block]
                gain_whole[(*spot, slice(None), slice(block, 128))] = jnp.zeros((8, 128 - block), HIGH)
            sums["g0"].start()
        elif step[0] == "attn":
            for copy in two_loads:
                copy.wait()
            for keep, swap_copy in swaps:
                keep.wait()
                swap_copy.wait_recv()
            long_part = nt(left_all[...], long_all[...])
            short_part = nt(side_all[...], short_all[...])
            product = jnp.concatenate([long_part, short_part], axis=1)
            start = 0
            for index, (whole, cut) in enumerate(zip(attn_wholes, ATTN_CUTS)):
                for half in range(2):
                    lay(product[:, start : start + cut], whole, jnp.bitwise_xor(half, across))
                    start += cut
                sums["a%d" % index].start()
    for kind, (long_out, short_out) in enumerate(((query_out, key_out), (output_out, value_out))):
        from_core = jnp.bitwise_xor(kind, core)
        parts = [held[from_core, jnp.bitwise_xor(half, across)] for held in attn_alls for half in range(2)]
        both = jnp.concatenate([part.astype(HIGH) for part in parts], axis=1)
        long_out[...] = both[:, : long_out.shape[1]]
        short_out[...] = both[:, long_out.shape[1] :]
    links.drain()


def emit_kernel(*refs):
    count = len(refs) // 2
    for source, target in zip(refs[:count], refs[count:]):
        target[...] = source[...] if source.shape == target.shape else source[...].T


def call(body, outs, specs, scratch, name, spots=0, collective=None):
    params = {"vmem_limit_bytes": LIMIT}
    if collective is not None:
        params.update(collective_id=collective, has_side_effects=True)
    return pl.pallas_call(
        body,
        out_shape=[jax.ShapeDtypeStruct(shape, kind) for shape, kind in outs],
        in_specs=specs,
        out_specs=[VMEM] * (len(outs) - spots) + [ANY] * spots,
        scratch_shapes=scratch,
        compiler_params=pltpu.CompilerParams(**params),
        name=name,
    )


def swap(value, distance):
    count = lax.axis_size("head")
    return lax.ppermute(value, "head", [(i, i ^ distance) for i in range(count)])


def scatter_rows(value, axis):
    count = lax.axis_size(axis)
    index = lax.axis_index(axis)
    value = value.reshape((count, value.shape[0] // count) + value.shape[1:])
    bit = 1
    while bit < count:
        mine = (index // bit) % 2
        value = value.reshape((value.shape[0] // 2, 2) + value.shape[1:])
        sent = lax.dynamic_index_in_dim(value, 1 - mine, 1, False)
        kept = lax.dynamic_index_in_dim(value, mine, 1, False)
        got = lax.ppermute(sent, axis, [(i, i ^ bit) for i in range(count)])
        value = kept.astype(HIGH) + got.astype(HIGH)
        bit *= 2
        if bit < count:
            value = value.astype(LOW)
    return value[0]


def shards(
    tokens,
    cotangent,
    lengths,
    attn_gain,
    w_query,
    w_key,
    w_value,
    w_output,
    ffn_gain,
    w_gate,
    w_up,
    w_down,
):
    blocks = lax.axis_size("head")
    me = lax.axis_index("head").astype(jnp.int32)
    low_bit = me % 2
    rows, width = tokens.shape
    hidden = w_gate.shape[1]
    keys = blocks * rows
    where = lengths
    frequency = 10000.0 ** (-(jnp.arange(HALF, dtype=HIGH) * 2.0 / HD))
    position = (me * rows + jnp.arange(rows, dtype=jnp.int32)).astype(HIGH)
    angles = frequency[:, None] * position[None, :]
    cosine, sine = jnp.cos(angles), jnp.sin(angles)
    gain_rows = jnp.stack([attn_gain, ffn_gain])

    feature_rows = (width, rows)
    project_outs = [(feature_rows, LOW), (feature_rows, LOW), ((blocks, rows, 2 * KV_WIDTH), LOW)]
    tokens, cotangent, w_key, w_value, w_down = (v.T for v in (tokens, cotangent, w_key, w_value, w_down))
    weight_room = [pltpu.VMEM((blocks, width, hidden), LOW)] * 3
    attend_room = [
        pltpu.VMEM((keys, rows), HIGH),
        pltpu.VMEM((KVH, keys, HD), LOW),
        pltpu.VMEM((KV_WIDTH, keys), LOW),
    ]
    layer_outs = [
        (feature_rows, LOW),
        ((16, rows), HIGH),
        ((rows, width), HIGH),
        (feature_rows, LOW),
        ((blocks, rows, hidden), LOW),
        ((blocks, rows, hidden), LOW),
    ]

    def forward_first():
        outs = project_outs + layer_outs + [((rows, width), HIGH)]
        outs += [((blocks - 1, width, hidden), LOW)] * 3
        copies = 3 * COPIES_SPREAD + COPIES_SHARE
        late = (w_key, w_value, w_query, w_output)
        scratch = attend_room + weight_room + [pltpu.VMEM(v.shape, LOW) for v in late]
        scratch += [pltpu.SemaphoreType.DMA((7 + 3 * (blocks - 1),))]
        scratch += [pltpu.SemaphoreType.DMA((copies,)), pltpu.SemaphoreType.DMA((copies,))]
        body = functools.partial(forward_first_kernel, blocks)
        specs = [SMEM] + [VMEM] * 4 + [ANY] * 7
        return call(body, outs, specs, scratch, "forward_first", 3, 1)(
            where, tokens, gain_rows, cosine, sine, *late, w_gate, w_up, w_down
        )

    outs = forward_first()
    a_one, q_one, kv_one, o_one, lse_one, m_one, b_one, g_one, u_one, h_one = outs[:10]
    weights = [w_gate, outs[10], w_up, outs[11], w_down, outs[12]]
    attend_outs = [(feature_rows, LOW), ((blocks, 2 * KV_WIDTH, rows), LOW)]
    room = attention_room(blocks, rows, width)
    key_room = [(blocks, 2 * KV_WIDTH, rows), (2, 2 * KV_WIDTH, rows)] + [(2 * KV_WIDTH, rows)] * 3

    def middle():
        outs = [(feature_rows, LOW), (feature_rows, LOW), ((rows, width), HIGH), ((8, width), HIGH)]
        outs += [((width, 4 * rows), LOW)] * 2 + [((6, 4 * rows, hidden), LOW)]
        outs += [((n, 2 * rows), LOW) for n in (width, HQ * HD, KV_WIDTH, width)]
        scratch = room + [
            pltpu.VMEM((KV_WIDTH, keys), LOW),
            pltpu.VMEM(feature_rows, LOW),
            pltpu.VMEM((16, rows), HIGH),
            pltpu.VMEM((rows, width), HIGH),
        ]
        scratch += [pltpu.VMEM(feature_rows, LOW)] * 3 + [pltpu.VMEM((blocks, rows, hidden), LOW)] * 2
        scratch += [pltpu.VMEM((6, rows, hidden), LOW)] * 2 + [pltpu.VMEM(feature_rows, LOW)]
        scratch += [pltpu.VMEM(shape, LOW) for shape in key_room]
        late = (w_key, w_value, w_query, w_output, cotangent)
        scratch += [pltpu.VMEM(v.shape, LOW) for v in late]
        scratch += [pltpu.VMEM(shape, LOW) for shape in (feature_rows, feature_rows, (blocks, rows, 2 * KV_WIDTH))]
        scratch += [pltpu.VMEM((16, rows), HIGH)] * 2
        scratch += weight_room + [pltpu.SemaphoreType.DMA((3, 2)), pltpu.SemaphoreType.DMA((LOCALS_MIDDLE,))]
        scratch += [pltpu.SemaphoreType.DMA((COPIES_MIDDLE,)), pltpu.SemaphoreType.DMA((COPIES_MIDDLE,))]
        given = [where, h_one, gain_rows, cosine, sine, *late, g_one, u_one, m_one, b_one, *weights]
        specs = [SMEM] + [VMEM] * 4 + [ANY] * 15
        return call(functools.partial(middle_kernel, blocks), outs, specs, scratch, "middle", 7, 3)(*given)

    block_out, c_one, dm_one, gains, b_all, f_all, rhs_all, *halves_two = middle()

    def close(h, grad_middle, grad_query, partial):
        sent = swap(jnp.stack([partial[1], partial[3]]), 1)
        far = swap((partial[2].astype(HIGH) + sent[1].astype(HIGH)).astype(LOW), 2)
        outs = [(feature_rows, HIGH), ((2 * KV_WIDTH, rows), LOW), ((1, width), HIGH)]
        given = [h, gain_rows, grad_middle, grad_query, w_query, w_key, w_value, cosine, sine]
        given += [partial[0], sent[0], far]
        return call(close_kernel, outs, [VMEM] * 12, [], "close")(*given)

    def beside(parts):
        return jnp.concatenate(parts, axis=-1)

    def choose(zero, one):
        return jnp.where(low_bit == 0, zero, one)

    def halves(a, c, o, dq, dkv):
        dk, dv = dkv[:KV_WIDTH], dkv[KV_WIDTH:]
        left = [choose(a, c), swap(choose(c, a), 1)]
        long = [choose(dq, o), swap(choose(o, dq), 1)]
        short = [choose(dk, dv), swap(choose(dv, dk), 1)]
        return beside(left), beside(long), beside(short), beside([a, swap(a, 1)])

    places = lax.axis_size("dp")
    block = width // places

    def finish():
        outs = [(feature_rows, HIGH)] + [((block, hidden), HIGH)] * 3
        outs += [((block, n), HIGH) for n in (HQ * HD, KV_WIDTH, KV_WIDTH, HQ * HD)] + [((8, 128), HIGH)]
        late = (q_one, kv_one, o_one, w_output, dm_one, tokens, w_query, w_key, w_value)
        scratch = room + [pltpu.VMEM(shape, LOW) for shape in [feature_rows] + key_room]
        scratch += [pltpu.VMEM(v.shape, v.dtype) for v in late] + [pltpu.VMEM(lse_one.shape, HIGH)]
        low_room = []
        low_room += [(width, 4 * rows), (width, 4 * rows), (2, 4 * rows, max(n for _, n in FFN_CUTS))]
        low_room += [(width, 4 * rows), (width, 4 * rows), (KV_WIDTH, 4 * rows), (width, 4 * rows)]
        low_room += [(2, 2, 2, 2, block, FFN_CUTS[i % PARTS][1]) for i in range(len(ORDERS))]
        scratch += [pltpu.VMEM(shape, LOW) for shape in low_room]
        for index, order in enumerate(ORDERS):
            scratch += halving_rooms(block, FFN_CUTS[index % PARTS][1], order)
        scratch += [pltpu.VMEM((2, 2, 2, 2, block, cut), LOW) for cut in ATTN_CUTS]
        for order, cut in zip(ATTN_ORDERS, ATTN_CUTS):
            scratch += halving_rooms(block, cut, order)
        scratch += [pltpu.VMEM((2, 2, block, cut), LOW) for cut in ATTN_CUTS]
        scratch += [pltpu.VMEM(shape, HIGH) for shape in ((2, 2, 2, 8, 128), (8, 8, 128), (2, 2, 8, 128))]
        scratch += [pltpu.SemaphoreType.DMA((48,)), pltpu.SemaphoreType.DMA((COPIES_FINISH,))]
        scratch += [pltpu.SemaphoreType.DMA((COPIES_FINISH,))]
        given = [where, gain_rows, cosine, sine, gains, *late, lse_one, a_one, c_one, *halves_two]
        specs = [SMEM] + [VMEM] * 4 + [ANY] * 19
        return call(finish_kernel, outs, specs, scratch, "finish", 0, 2)(*given, b_all, f_all, rhs_all)

    if places == 8 and blocks == 4:
        outs = finish()
        input_grad, gate_grad, up_grad, down_grad, query_grad, key_grad, value_grad, output_grad, gains = outs
        gains = gains[:2, :block]
        results = [block_out, input_grad, query_grad, key_grad, value_grad, output_grad, gate_grad, up_grad, down_grad]
        turned_over = (3, 4, 5)
        outs = [(v.shape[::-1] if i in turned_over else v.shape, v.dtype) for i, v in enumerate(results)]
        results = call(emit_kernel, outs, [VMEM] * len(outs), [], "emit")(*results)
        block_out, input_grad, query_grad, key_grad, value_grad, output_grad, gate_grad, up_grad, down_grad = results
        key_grad, value_grad, output_grad = key_grad.T, value_grad.T, output_grad.T
    else:
        given = [where, dm_one, w_output, q_one, kv_one, o_one, lse_one, cosine, sine]
        dq_one, part_one = call(attend_back_kernel, attend_outs, [SMEM] + [VMEM] * 8, room, "attend_back")(*given)
        input_grad, dkv_one, gain_one_a = close(tokens, dm_one, dq_one, part_one)
        kept, sent = [], []
        for which in range(6):
            product = nn(b_all if which < 4 else f_all, rhs_all[which]).astype(LOW)
            (sent if which % 2 else kept).append(product)
        got = swap(beside(sent), 2)
        ffn = scatter_rows((beside(kept).astype(HIGH) + got.astype(HIGH)).astype(LOW), "dp")
        halves_one = halves(a_one, c_one, o_one, dq_one, dkv_one)
        left, long, short, side = (beside(pair) for pair in zip(halves_two, halves_one))
        attn = scatter_rows(beside([nt(left, long), nt(side, short)]).astype(LOW), "dp").astype(LOW)
        attn = (attn.astype(HIGH) + swap(attn, 2).astype(HIGH)).astype(LOW)
        other = swap(attn, 1)
        zero, one = choose(attn, other).astype(HIGH), choose(other, attn).astype(HIGH)
        gains = jnp.concatenate([gains[:1] + gain_one_a, gains[1:2]], axis=0)
        gains = lax.psum_scatter(lax.psum(gains, "head"), "dp", scatter_dimension=1, tiled=True)
        query_grad, key_grad = zero[:, : HQ * HD], zero[:, HQ * HD :]
        output_grad, value_grad = one[:, : HQ * HD], one[:, HQ * HD :]
        gate_grad, up_grad, down_grad = (ffn[:, i * hidden : (i + 1) * hidden] for i in range(3))
    return (
        block_out.T,
        input_grad.T,
        gains[0],
        query_grad,
        key_grad,
        value_grad,
        output_grad.T,
        gains[1],
        gate_grad,
        up_grad,
        down_grad.T,
    )


def solution(mesh):
    return jax.shard_map(
        shards,
        mesh=mesh,
        in_specs=(
            P(("dp", "head"), None),
            P(("dp", "head"), None),
            P("dp"),
            P(),
            P(),
            P(),
            P(),
            P(),
            P(),
            P(None, "head"),
            P(None, "head"),
            P("head", None),
        ),
        out_specs=(
            P(("dp", "head"), None),
            P(("dp", "head"), None),
            P("dp"),
            P("dp", None),
            P("dp", None),
            P("dp", None),
            P(None, "dp"),
            P("dp"),
            P("dp", "head"),
            P("dp", "head"),
            P("head", "dp"),
        ),
        check_vma=False,
    )
```

```python
import functools

import jax
import jax.numpy as jnp
from jax import lax
from jax.experimental import pallas as pl
from jax.experimental.pallas import tpu as pltpu
from jax.sharding import PartitionSpec as P

HQ = 15
KVH = 5
HD = 64
HALF = HD // 2
PER_GROUP = HQ // KVH
KV_WIDTH = KVH * HD
EPSILON = 1e-05
SCALE = HD ** (-0.5)
BLOCKED = -1e30
LOW = jnp.bfloat16
HIGH = jnp.float32
VMEM = pl.BlockSpec(memory_space=pltpu.VMEM)
SMEM = pl.BlockSpec(memory_space=pltpu.SMEM)
ANY = pl.BlockSpec(memory_space=pl.ANY)
LIMIT = 60 * 2**20
MESH = pl.DeviceIdType.MESH


def nn(left, right):
    return lax.dot_general(left, right, (((1,), (0,)), ((), ())), preferred_element_type=HIGH)


def nt(left, right):
    return lax.dot_general(left, right, (((1,), (1,)), ((), ())), preferred_element_type=HIGH)


def sigmoid(value):
    return 0.5 * (1.0 + jnp.tanh(0.5 * value))


def inverse_rms(rows):
    return lax.rsqrt(jnp.mean(rows * rows, axis=1, keepdims=True) + EPSILON)


def norm_back(values_in, gain, grad_normed, grad_skip):
    inverse = inverse_rms(values_in)
    normal = values_in * inverse
    gain_part = jnp.sum(grad_normed * normal, axis=0, keepdims=True)
    scaled = grad_normed * gain
    back = grad_skip + inverse * (scaled - normal * jnp.mean(scaled * normal, axis=1, keepdims=True))
    return gain_part, back


def turned(columns, cosine, sine, sign, factor):
    parts = []
    for start in range(0, columns.shape[0], HD):
        first = columns[start : start + HALF] * factor
        second = columns[start + HALF : start + HD] * factor
        parts.append(first * cosine - sign * second * sine)
        parts.append(second * cosine + sign * first * sine)
    return jnp.concatenate(parts, axis=0)


def project(hidden, gain, w_query, w_key, w_value, cosine, sine, a_ref, q_ref, kv_ref, ready):
    normed = hidden * inverse_rms(hidden) * gain
    low = normed.astype(LOW)
    keys = turned(nt(w_key[...], low), cosine, sine, 1.0, 1.0)
    kv_ref[:, :KV_WIDTH] = keys.T.astype(LOW)
    kv_ref[:, KV_WIDTH:] = nt(low, w_value[...]).astype(LOW)
    ready()
    queries = nn(low, w_query[...]).T
    q_ref[...] = turned(queries, cosine, sine, 1.0, SCALE).astype(LOW)
    a_ref[...] = normed.T.astype(LOW)


def fill_bias(where_ref, bias, rows, blocks):
    me = lax.axis_index("head")
    length = where_ref[0]
    key = lax.broadcasted_iota(jnp.int32, (rows, rows), 0)
    query = lax.broadcasted_iota(jnp.int32, (rows, rows), 1)
    for step in range(blocks):
        other = jnp.bitwise_xor(me, step)
        allowed = other * rows + key < length
        if step == 0:
            allowed &= key <= query
        else:
            allowed &= other < me
        bias[step * rows : (step + 1) * rows] = jnp.where(allowed, 0.0, BLOCKED)


def side_by_side(ref, group):
    first = group * PER_GROUP
    heads = [ref[pl.ds(pl.multiple_of((first + i) * HD, HD), HD), :] for i in range(PER_GROUP)]
    return jnp.concatenate(heads, axis=1)


def one_below_other(ref, group, value):
    rows = value.shape[1] // PER_GROUP
    for member in range(PER_GROUP):
        at = pl.ds(pl.multiple_of((group * PER_GROUP + member) * HD, HD), HD)
        ref[at, :] = value[:, member * rows : (member + 1) * rows].astype(ref.dtype)


def scored(keys, queries, bias):
    return nn(keys, queries) + jnp.concatenate([bias] * PER_GROUP, axis=1)


def attend(bias, k_sc, vt_sc, q_ref, o_ref, lse_ref, event):
    def group_body(group, carry):
        keys = k_sc[group]
        values = vt_sc[pl.ds(pl.multiple_of(group * HD, HD), HD), :]
        event(group)
        scores = scored(keys, side_by_side(q_ref, group), bias[...])
        top = jnp.max(scores, axis=0, keepdims=True)
        exponent = jnp.exp(scores - top)
        total = jnp.sum(exponent, axis=0, keepdims=True)
        one_below_other(o_ref, group, nn(values, exponent.astype(LOW)) * (1.0 / total))
        lse_ref[pl.ds(group, 1), :] = top + jnp.log(total)
        return carry

    lax.fori_loop(0, KVH, group_body, 0)


def attend_first(bias, k_sc, vt_sc, q_ref, top_ref, total_ref, part_ref, half):
    def group_body(group, carry):
        keys = k_sc[group, :half]
        values = vt_sc[pl.ds(pl.multiple_of(group * HD, HD), HD), :half]
        scores = scored(keys, side_by_side(q_ref, group), bias[:half])
        top = jnp.max(scores, axis=0, keepdims=True)
        exponent = jnp.exp(scores - top)
        top_ref[pl.ds(group, 1), :] = top
        total_ref[pl.ds(group, 1), :] = jnp.sum(exponent, axis=0, keepdims=True)
        one_below_other(part_ref, group, nn(values, exponent.astype(LOW)))
        return carry

    lax.fori_loop(0, KVH, group_body, 0)


def attend_rest(bias, k_sc, vt_sc, q_ref, top_ref, total_ref, part_ref, half, o_ref, lse_ref):
    def group_body(group, carry):
        keys = k_sc[group, half:]
        values = vt_sc[pl.ds(pl.multiple_of(group * HD, HD), HD), half:]
        scores = scored(keys, side_by_side(q_ref, group), bias[half:])
        before = top_ref[pl.ds(group, 1), :]
        top = jnp.maximum(before, jnp.max(scores, axis=0, keepdims=True))
        exponent = jnp.exp(scores - top)
        rescale = jnp.exp(before - top)
        total = total_ref[pl.ds(group, 1), :] * rescale + jnp.sum(exponent, axis=0, keepdims=True)
        attended = side_by_side(part_ref, group) * rescale + nn(values, exponent.astype(LOW))
        one_below_other(o_ref, group, attended * (1.0 / total))
        lse_ref[pl.ds(group, 1), :] = top + jnp.log(total)
        return carry

    lax.fori_loop(0, KVH, group_body, 0)


def lay_keys(kv_ref, k_sc, vt_sc, steps, rows):
    for step in steps:
        at = slice(step * rows, (step + 1) * rows)
        for group in range(KVH):
            k_sc[group, at] = kv_ref[step, :, group * HD : (group + 1) * HD]
        vt_sc[:, at] = kv_ref[step, :, KV_WIDTH:].T


def after_attention(hidden, o_ref, wo_ref, gain, m_ref, b_ref):
    middle = hidden + nn(o_ref[...].T, wo_ref[...])
    m_ref[...] = middle
    normed = middle * inverse_rms(middle) * gain
    b_ref[...] = normed.T.astype(LOW)
    return middle, normed.astype(LOW)


def active_part(normed, wg, wu, g_ref, u_ref, step):
    gate = nn(normed, wg[step])
    up = nn(normed, wu[step])
    g_ref[step] = gate.astype(LOW)
    u_ref[step] = up.astype(LOW)
    return (gate * sigmoid(gate) * up).astype(LOW)


def hidden_part(normed, wg, wu, wd, g_ref, u_ref, step):
    return nt(active_part(normed, wg, wu, g_ref, u_ref, step), wd[step])


def partner(axis, distance):
    return {axis: jnp.bitwise_xor(lax.axis_index(axis), distance)}


def greet(partners):
    barrier = pltpu.get_barrier_semaphore()
    for axis, distance in partners:
        pl.semaphore_signal(barrier, inc=1, device_id=partner(axis, distance), device_id_type=MESH)
    pl.semaphore_wait(barrier, len(partners))


class Links:
    def __init__(self, send, receive):
        self.send, self.receive, self.used = send, receive, 0
        self.flying = []

    def push(self, source, target, to):
        copy = pltpu.make_async_remote_copy(
            src_ref=source,
            dst_ref=target,
            send_sem=self.send.at[self.used],
            recv_sem=self.receive.at[self.used],
            device_id=partner(*to),
            device_id_type=MESH,
        )
        self.used += 1
        self.flying.append(copy)
        return copy

    def drain(self):
        for copy in self.flying:
            copy.wait_send()


class Local:
    def __init__(self, sems):
        self.sems, self.used, self.flying = sems, 0, []

    def move(self, source, target, start=True):
        copy = pltpu.make_async_copy(source, target, self.sems.at[self.used])
        self.used += 1
        self.flying.append(copy)
        if start:
            copy.start()
        return copy

    def drain(self):
        for copy in self.flying:
            copy.wait()


SIBLING, ACROSS, SIDE, BEYOND = ("head", 1), ("head", 2), ("dp", 1), ("dp", 2)


class Share:
    def __init__(self, links, kv_ref):
        self.near = links.push(kv_ref.at[0], kv_ref.at[1], SIBLING)
        self.far = links.push(kv_ref.at[0], kv_ref.at[2], ACROSS)
        self.forth = links.push(kv_ref.at[2], kv_ref.at[3], SIBLING)

    def start(self):
        self.far.start()
        self.near.start()

    def pass_on(self):
        self.far.wait_recv()
        self.forth.start()

    def finish(self):
        self.near.wait_recv()
        self.forth.wait_recv()


class Spread:
    def __init__(self, links, own, all_ref, start, count):
        quarter = count // 4
        cut = quarter // 32 * 16
        place = lax.axis_index("dp") % 4

        def rows(which, first=0, size=quarter):
            at = start + jnp.bitwise_xor(place, which) * quarter + first
            return pl.ds(pl.multiple_of(at, 16), size)

        def move(which, to, *piece):
            ref = all_ref.at[2, rows(which, *piece)]
            return links.push(ref, ref, to)

        def aside(which):
            return links.push(all_ref.at[2, rows(which)], all_ref.at[3, rows(which)], SIBLING)

        span = pl.ds(start, count)
        self.near = links.push(own.at[span], all_ref.at[1, span], SIBLING)
        self.cross = links.push(own.at[rows(0)], all_ref.at[2, rows(0)], ACROSS)
        self.side, self.beyond = move(0, SIDE), move(0, BEYOND)
        self.side_half = move(2, SIDE, cut, quarter - cut)
        self.beyond_half = move(1, BEYOND, 0, cut)
        self.asides = [aside(which) for which in range(4)]

    def first(self):
        self.cross.wait_recv()
        self.side.start()
        self.beyond.start()
        self.asides[0].start()

    def second(self):
        self.side.wait_recv()
        self.beyond_half.start()
        self.asides[1].start()
        self.beyond.wait_recv()
        self.side_half.start()
        self.asides[2].start()

    def third(self):
        self.side_half.wait_recv()
        self.beyond_half.wait_recv()
        self.asides[3].start()

    def last(self):
        for copy in self.asides:
            copy.wait_recv()


COPIES_SHARE = 3
COPIES_SPREAD = 10


def first_forward(where_ref, h_ref, gain_ref, cos_ref, sin_ref, late, lates, owns, parts, results, attn, held, links, local):
    a_ref, q_ref, kv_ref, o_ref, lse_ref, m_ref, b_ref, g_ref, u_ref = parts
    bias, k_sc, vt_sc = attn
    wk_ref, wv_ref, wq_ref, wo_ref, _ = late
    wg, wu, wd = held
    blocks, rows = wg.shape[0], h_ref.shape[1]
    loads = [local.move(own, all_ref.at[0], False) for own, all_ref in zip(owns, held)]
    whole = owns[0].shape[0]
    middle_row = (whole // 128 + 1) * 64
    cuts = ((0, middle_row), (middle_row, whole - middle_row))
    spreads = [[Spread(links, own, all_ref, *cut) for cut in cuts] for own, all_ref in zip(owns, held)]
    (g1, g2), (u1, u2), (d1, d2) = spreads
    share = Share(links, kv_ref)
    greet((SIBLING, ACROSS, SIDE, BEYOND))
    for piece in (g1, g2):
        piece.cross.start()
    for pair, copy in zip(spreads, loads):
        for piece in pair:
            piece.near.start()
        copy.start()
    hidden = h_ref[...].astype(HIGH).T

    def queue():
        share.start()
        for piece in (u1, u2, d1, d2):
            piece.cross.start()
        lates[2].wait()

    lates[0].wait()
    lates[1].wait()
    gain_one = gain_ref[0:1].astype(HIGH)
    project(hidden, gain_one, wq_ref, wk_ref, wv_ref, cos_ref[...], sin_ref[...], a_ref, q_ref, kv_ref.at[0], queue)
    g1.first()
    g2.first()
    fill_bias(where_ref, bias, rows, blocks)
    g1.second()
    g2.second()
    share.pass_on()
    g1.third()
    share.finish()
    lay_keys(kv_ref, k_sc, vt_sc, range(blocks), rows)
    events = ((g2.third, u1.first), (), (u2.first,), (u1.second,), (d1.first, u2.second))

    def event(group):
        for when, actions in enumerate(events):

            @pl.when(group == when)
            def _():
                for action in actions:
                    action()

    attend(bias, k_sc, vt_sc, q_ref, o_ref, lse_ref, event)
    d2.first()
    u1.third()
    lates[3].wait()
    middle, normed = after_attention(hidden, o_ref, wo_ref, gain_ref[1:2].astype(HIGH), m_ref, b_ref)
    early = [local.move(source, target) for source, target in zip(parts[:7], results[:7])]
    u2.third()
    for copy in loads:
        copy.wait()
    active = [active_part(normed, wg, wu, g_ref, u_ref, 0)]
    d1.second()
    for pair in spreads:
        for piece in pair:
            piece.near.wait_recv()
    active.append(active_part(normed, wg, wu, g_ref, u_ref, 1))
    d2.second()
    d1.third()
    for step in range(2, 4):
        active.append(active_part(normed, wg, wu, g_ref, u_ref, step))
        if step == 2:
            for piece in (g1, g2, u1, u2):
                piece.last()
    early += [local.move(source, target) for source, target in zip(parts[7:], results[7:])]
    total = middle
    for step in range(blocks):
        if step == 2:
            d2.third()
        if step == 3:
            d1.last()
            d2.last()
        total = total + nt(active[step], wd[step])
    for copy in early:
        copy.wait()
    return total


def ffn_back(grad, g_ref, u_ref, m_ref, gain, wg, wu, wd, mine_ref, theirs_ref):
    low_grad = grad.astype(LOW)
    grad_normed = jnp.zeros(m_ref.shape, HIGH)
    for step in range(wg.shape[0]):
        grad_active = nn(low_grad, wd[step])
        gate = g_ref[step].astype(HIGH)
        up = u_ref[step].astype(HIGH)
        sig = sigmoid(gate)
        silu = gate * sig
        grad_gate = (grad_active * up * sig * (1.0 + gate * (1.0 - sig))).astype(LOW)
        grad_up = (grad_active * silu).astype(LOW)
        kept = mine_ref if step % 2 == 0 else theirs_ref
        kept[step // 2] = grad_gate
        kept[2 + step // 2] = grad_up
        kept[4 + step // 2] = (silu * up).astype(LOW)
        grad_normed = grad_normed + nt(grad_gate, wg[step]) + nt(grad_up, wu[step])
    return norm_back(m_ref[...], gain, grad_normed, grad)


def lay_back(kv_ref, k_sc, v_sc, kt_sc, blocks, rows, keys_laid):
    for step in range(blocks):
        at = slice(step * rows, (step + 1) * rows)
        for group in range(KVH):
            if not keys_laid:
                k_sc[group, at] = kv_ref[step, :, group * HD : (group + 1) * HD]
            v_sc[group, at] = kv_ref[step, :, KV_WIDTH + group * HD : KV_WIDTH + (group + 1) * HD]
        kt_sc[:, at] = kv_ref[step, :, :KV_WIDTH].T


def attend_back(grad_middle, wo_ref, q_ref, o_ref, lse_ref, cosine, sine, dq_ref, dkv_ref, room, before, between):
    bias, k_sc, v_sc, kt_sc, do_sc, delta, dq_sc = room
    keys, rows = bias.shape
    blocks = keys // rows
    half = keys // 2
    do_sc[...] = nt(wo_ref[...], grad_middle.astype(LOW)).astype(LOW)
    for head in range(HQ):
        at = slice(head * HD, (head + 1) * HD)
        product = do_sc[at].astype(HIGH) * o_ref[at].astype(HIGH)
        group, member = divmod(head, PER_GROUP)
        spot = slice(member * rows, (member + 1) * rows)
        delta[group : group + 1, spot] = jnp.sum(product, axis=0, keepdims=True)
    cosines, sines = (jnp.concatenate([table] * PER_GROUP, axis=1) for table in (cosine, sine))

    def one_pass(start, last, event):
        cut = slice(start, start + half)

        def group_body(group, carry):
            event(group)
            group_keys = k_sc[group, cut]
            values = v_sc[group, cut]
            at = pl.ds(pl.multiple_of(group * HD, HD), HD)
            after = pl.ds(pl.multiple_of(KV_WIDTH + group * HD, HD), HD)
            keys_t = kt_sc[at, cut]
            query, grad_out = side_by_side(q_ref, group), side_by_side(do_sc, group)
            scores = scored(group_keys, query, bias[cut])
            prob = jnp.exp(scores - lse_ref[pl.ds(group, 1), :])
            grad_prob = nn(values, grad_out)
            grad_score = (prob * (grad_prob - delta[pl.ds(group, 1), :])).astype(LOW)
            grad_query = nn(keys_t, grad_score)
            if last:
                grad_query = grad_query + side_by_side(dq_sc, group)
                one_below_other(dq_ref, group, turned(grad_query, cosines, sines, -1.0, SCALE))
            else:
                one_below_other(dq_sc, group, grad_query)
            grad_keys = nt(query, grad_score)
            grad_values = nt(grad_out, prob.astype(LOW))
            for step in range(blocks // 2):
                part = slice(step * rows, (step + 1) * rows)
                dkv_ref[start // rows + step, at, :] = grad_keys[:, part].astype(LOW)
                dkv_ref[start // rows + step, after, :] = grad_values[:, part].astype(LOW)
            return carry

        lax.fori_loop(0, KVH, group_body, 0)

    one_pass(half, False, before)
    one_pass(0, True, between)


class Settle:
    def __init__(self, links, dkv_ref, near_ref, sum_ref, far_ref):
        self.refs = dkv_ref, near_ref, sum_ref, far_ref
        self.aside = links.push(dkv_ref.at[3], near_ref.at[1], SIBLING)
        self.near = links.push(dkv_ref.at[1], near_ref.at[0], SIBLING)
        self.far = links.push(sum_ref, far_ref, ACROSS)

    def between(self, group):
        dkv_ref, near_ref, sum_ref, _ = self.refs
        pl.when(group == 0)(self.aside.start)

        @pl.when(group == 1)
        def _():
            self.aside.wait_recv()
            sum_ref[...] = (dkv_ref[2].astype(HIGH) + near_ref[1].astype(HIGH)).astype(LOW)
            self.far.start()

    def finish(self):
        dkv_ref, near_ref, _, far_ref = self.refs
        self.near.wait_recv()
        self.far.wait_recv()
        return dkv_ref[0].astype(HIGH) + near_ref[0].astype(HIGH) + far_ref[...].astype(HIGH)


def attention_room(blocks, rows, width):
    keys = blocks * rows
    return [
        pltpu.VMEM((keys, rows), HIGH),
        pltpu.VMEM((KVH, keys, HD), LOW),
        pltpu.VMEM((KVH, keys, HD), LOW),
        pltpu.VMEM((KV_WIDTH, keys), LOW),
        pltpu.VMEM((width, rows), LOW),
        pltpu.VMEM((8, PER_GROUP * rows), HIGH),
        pltpu.VMEM((width, rows), HIGH),
    ]


def share_out(local, links, core, zero, one, target, own_at, got_at):
    if zero is one:
        keep = local.move(zero, target.at[own_at])
        send = links.push(zero, target.at[got_at], SIBLING)
        send.start()
        return keep, send
    keep = local.move(zero, target.at[own_at], False)
    keep_one = pltpu.make_async_copy(one, target.at[own_at], local.sems.at[local.used - 1])
    send = links.push(one, target.at[got_at], SIBLING)
    links.used -= 1
    links.flying.pop()
    send_zero = links.push(zero, target.at[got_at], SIBLING)

    @pl.when(core == 0)
    def _():
        keep.start()
        send.start()

    @pl.when(core == 1)
    def _():
        keep_one.start()
        send_zero.start()

    return keep, send


COPIES_MIDDLE = 6 * COPIES_SPREAD + COPIES_SHARE + 20
LOCALS_MIDDLE = 40


def layers_kernel(blocks, *refs):
    where_ref, tokens_ref, gain_ref, cos_ref, sin_ref = refs[:5]
    late_refs, owns = refs[5:10], refs[10:13]
    out_ref, c_ref, dm_ref, gains_ref = refs[13:17]
    results = refs[17:26]
    m_any, b_any, g_any, u_any = results[5:]
    b_all, f_all, rhs_all, left_two, long_two, short_two, side_two = refs[26:33]
    room = refs[33:40]
    bias, k_sc, v_sc, kt_sc = room[:4]
    part_sc = room[6]
    vt_sc, o_sc, lse_sc, m_sc, b_sc, f_sc, c_sc, g_sc, u_sc = refs[40:49]
    mine, theirs, dq_sc, dkv_sc, dkv_near, dkv_sum, dkv_far, dkv_low = refs[49:57]
    late = refs[57:62]
    a_sc, q_ref, kv_first, kv_ref, top_sc, total_sc, h_ref = refs[62:69]
    wk, wv, wq, wo_ref, cot = late
    wg, wu, wd, load, send, receive = refs[69:]
    rows = h_ref.shape[0]
    core = lax.axis_index("head") % 2
    local = Local(load)
    links = Links(send, receive)
    lates = [local.move(source, target) for source, target in zip(late_refs, late)]
    parts = (a_sc, q_ref, kv_first, o_sc, lse_sc, m_sc, b_sc, g_sc, u_sc)
    h_ref[...] = first_forward(
        where_ref,
        tokens_ref,
        gain_ref,
        cos_ref,
        sin_ref,
        late,
        lates,
        owns,
        parts,
        results,
        (bias, k_sc, vt_sc),
        (wg, wu, wd),
        links,
        local,
    )
    waited = list(links.flying)
    share = Share(links, kv_ref)
    settle = Settle(links, dkv_sc, dkv_near, dkv_sum, dkv_far)
    spans = [pl.ds(i * rows, rows) for i in range(4)]
    everything = slice(None)

    def both(source, target, place):
        keep = local.move(source, target.at[(*place, spans[both.layer])])
        copy = links.push(source, target.at[(*place, spans[both.layer + 1])], SIBLING)
        copy.start()
        return keep, copy

    both.layer = 2
    posted = [both(b_any, b_all, (everything,))]
    both.layer = 0
    cosine, sine = cos_ref[...], sin_ref[...]
    half = blocks * rows // 2

    gain_one = gain_ref[0:1].astype(HIGH)
    project(h_ref[...], gain_one, wq, wk, wv, cosine, sine, a_sc, q_ref, kv_ref.at[0], share.start)
    share.near.wait_recv()
    lay_keys(kv_ref, k_sc, vt_sc, range(blocks // 2), rows)
    attend_first(bias, k_sc, vt_sc, q_ref, top_sc, total_sc, part_sc, half)
    share.pass_on()
    share.forth.wait_recv()
    lay_keys(kv_ref, k_sc, vt_sc, range(blocks // 2, blocks), rows)
    attend_rest(bias, k_sc, vt_sc, q_ref, top_sc, total_sc, part_sc, half, o_sc, lse_sc)
    total, normed = after_attention(h_ref[...], o_sc, wo_ref, gain_ref[1:2].astype(HIGH), m_sc, b_sc)
    posted.append(both(b_sc, b_all, (everything,)))
    for step in range(blocks):
        total = total + hidden_part(normed, wg, wu, wd, g_sc, u_sc, step)
    out_ref[...] = total.T.astype(LOW)
    lay_back(kv_ref, k_sc, v_sc, kt_sc, blocks, rows, True)

    lates[4].wait()
    row = lax.axis_index("head") * rows + lax.broadcasted_iota(jnp.int32, (rows, 1), 0)
    grad = jnp.where(row < where_ref[0], cot[...].astype(HIGH).T, 0.0)
    f_sc[...] = grad.T.astype(LOW)
    first_f = both(f_sc, f_all, (everything,))
    gain_two = gain_ref[1:2].astype(HIGH)
    gain_part, grad_middle = ffn_back(grad, g_sc, u_sc, m_sc, gain_two, wg, wu, wd, mine, theirs)
    first_loads = [local.move(source, target) for source, target in ((g_any, g_sc), (u_any, u_sc), (m_any, m_sc))]
    keep_mine = local.move(mine, rhs_all.at[:, spans[0]])
    send_theirs = links.push(theirs, rhs_all.at[:, spans[1]], SIBLING)
    send_theirs.start()
    gains_ref[...] = jnp.zeros(gains_ref.shape, HIGH)
    gains_ref[1:2] = gain_part
    c_sc[...] = grad_middle.T.astype(LOW)
    attend_back(
        grad_middle, wo_ref, q_ref, o_sc, lse_sc, cosine, sine, dq_sc, dkv_sc, room, lambda group: None, settle.between
    )
    settle.near.start()
    from_query = nn(wq[...], dq_sc[...]).T
    grad_keys, grad_values = close_keys(settle.finish(), cosine, sine, dkv_low)
    low_rows, high_rows = pl.ds(0, KV_WIDTH), pl.ds(KV_WIDTH, KV_WIDTH)
    for zero, one, target in (
        (a_sc, c_sc, left_two),
        (dq_sc, o_sc, long_two),
        (dkv_low.at[low_rows], dkv_low.at[high_rows], short_two),
        (a_sc, a_sc, side_two),
    ):
        posted.append(
            share_out(local, links, core, zero, one, target, (everything, spans[0]), (everything, spans[1]))
        )
    gain_part, grad = close_rows(h_ref[...], gain_one, grad_middle, from_query, grad_keys, grad_values, wk, wv)
    gains_ref[0:1] = gain_part

    first_f[0].wait()
    first_f[1].wait_send()
    keep_mine.wait()
    send_theirs.wait_send()
    for copy in first_loads:
        copy.wait()
    f_sc[...] = grad.T.astype(LOW)
    both.layer = 2
    posted.append(both(f_sc, f_all, (everything,)))
    gain_part, grad_middle = ffn_back(grad, g_sc, u_sc, m_sc, gain_two, wg, wu, wd, mine, theirs)
    keep_last = local.move(mine, rhs_all.at[:, spans[2]])
    send_last = links.push(theirs, rhs_all.at[:, spans[3]], SIBLING)
    send_last.start()
    gains_ref[1:2] = gains_ref[1:2] + gain_part
    dm_ref[...] = grad_middle
    c_ref[...] = grad_middle.T.astype(LOW)
    for keep, copy in posted:
        keep.wait()
        copy.wait()
    first_f[1].wait_recv()
    send_theirs.wait_recv()
    keep_last.wait()
    send_last.wait()
    for copy in (settle.aside, settle.near, settle.far, share.near, share.far, share.forth, *waited):
        copy.wait_send()


def attend_back_kernel(*refs):
    where_ref, dm_ref, wo_ref, q_ref, kv_ref, o_ref, lse_ref, cos_ref, sin_ref, dq_ref, dkv_ref = refs[:11]
    room = refs[11:]
    bias, k_sc, v_sc, kt_sc = room[:4]
    blocks, rows = kv_ref.shape[:2]
    fill_bias(where_ref, bias, rows, blocks)
    lay_back(kv_ref, k_sc, v_sc, kt_sc, blocks, rows, False)
    attend_back(
        dm_ref[...], wo_ref, q_ref, o_ref, lse_ref, cos_ref[...], sin_ref[...], dq_ref, dkv_ref, room, lambda group: None, lambda group: None
    )


def close_keys(total, cosine, sine, dkv_ref):
    turned_keys = turned(total[:KV_WIDTH], cosine, sine, -1.0, 1.0)
    dkv_ref[:KV_WIDTH] = turned_keys.astype(LOW)
    dkv_ref[KV_WIDTH:] = total[KV_WIDTH:].astype(LOW)
    return turned_keys.T.astype(LOW), total[KV_WIDTH:].T.astype(LOW)


def close_rows(hidden, gain, grad_middle, from_query, grad_keys, grad_values, wk_ref, wv_ref):
    grad_normed = from_query + nn(grad_keys, wk_ref[...]) + nn(grad_values, wv_ref[...])
    return norm_back(hidden, gain, grad_normed, grad_middle)


def close_kernel(*refs):
    h_ref, gain_ref, dm_ref, dq_ref, wq_ref, wk_ref, wv_ref, cos_ref, sin_ref = refs[:9]
    own, near, far, dh_ref, dkv_ref, gain_part_ref = refs[9:]
    total = own[...].astype(HIGH) + near[...].astype(HIGH) + far[...].astype(HIGH)
    grad_keys, grad_values = close_keys(total, cos_ref[...], sin_ref[...], dkv_ref)
    hidden = h_ref[...].astype(HIGH).T
    gain = gain_ref[0:1].astype(HIGH)
    from_query = nn(wq_ref[...], dq_ref[...]).T
    gain_part, grad_in = close_rows(hidden, gain, dm_ref[...], from_query, grad_keys, grad_values, wk_ref, wv_ref)
    gain_part_ref[...] = gain_part
    dh_ref[...] = grad_in.T


class Halving:
    def __init__(self, links, steps):
        self.steps = [(links.push(sent, got, to), kept, got) for sent, kept, got, to in steps]

    def start(self):
        self.steps[0][0].start()

    def fold(self, which):
        copy, kept, got = self.steps[which]
        copy.wait_recv()
        total = kept[...].astype(HIGH) + got[...].astype(HIGH)
        if which == len(self.steps) - 1:
            self.done(total)
        else:
            kept[...] = total.astype(kept.dtype)
            self.steps[which + 1][0].start()


class Regather(Halving):
    def share(self, links, held):
        self.held = held
        self.across = links.push(held.at[0, 0], held.at[0, 1], ACROSS)
        self.aside = links.push(held.at[0], held.at[1], SIBLING)

    def done(self, total):
        self.held[0, 0] = total.astype(LOW)
        self.across.start()

    def fold(self, which):
        if which < len(self.steps):
            Halving.fold(self, which)
        elif which == len(self.steps):
            self.across.wait_recv()
            self.aside.start()
        else:
            self.aside.wait_recv()


class Rows:
    def __init__(self, links, whole, side, got, out):
        self.steps = (
            (whole.at[:, :, 1], side, whole.at[:, :, 0], SIDE),
            (whole.at[:, 1, 0], got.at[pl.ds(0, 2)], whole.at[:, 0, 0], BEYOND),
            (whole.at[1, 0, 0], got.at[2], whole.at[0, 0, 0], FAR_SIDE),
            (whole.at[0, 0, 0], got.at[3], None, ACROSS),
            (got.at[4], got.at[5], None, SIBLING),
        )
        self.copies = [links.push(source, target, to) for source, target, _, to in self.steps]
        self.whole, self.got, self.out = whole, got, out

    def start(self):
        self.copies[0].start()

    def fold(self, which):
        self.copies[which].wait_recv()
        if which < 3:
            _, target, kept, _ = self.steps[which]
            kept[...] = kept[...] + target[...]
        elif which == 3:
            self.got[4] = self.whole[0, 0, 0] + self.got[3]
        else:
            self.out[...] = self.got[4] + self.got[5]
        if which < 4:
            self.copies[which + 1].start()


FAR_SIDE = ("dp", 4)


def halved(kind, links, whole, rooms, order):
    where = {"X": 0, "Z1": 1, "Z0": 2, "Y": 3}
    to = {"X": ACROSS, "Z1": FAR_SIDE, "Z0": BEYOND, "Y": SIDE}
    chosen = [slice(None)] * 4
    steps = []
    for axis, room in zip(order, rooms):
        sent, kept = list(chosen), list(chosen)
        sent[where[axis]], kept[where[axis]] = 1, 0
        steps.append((whole.at[tuple(sent)], whole.at[tuple(kept)], room, to[axis]))
        chosen = kept
    return kind(links, steps)


def halving_rooms(block, columns, order):
    left = [2, 2, 2, 2]
    where = {"X": 0, "Z1": 1, "Z0": 2, "Y": 3}
    rooms = []
    for axis in order:
        left[where[axis]] = 0
        rooms.append(pltpu.VMEM(tuple(n for n in left if n) + (block, columns), LOW))
    return rooms


FFN_CUTS = ((0, 256), (256, 384))
ORDERS = (
    ("Y", "X", "Z0", "Z1"),
    ("Z0", "Y", "Z1", "X"),
    ("Z0", "Z1", "X", "Y"),
    ("Y", "Z0", "X", "Z1"),
    ("X", "Y", "Z0", "Z1"),
    ("X", "Y", "Z0", "Z1"),
)
ATTN_ORDERS = (
    ("Z0", "X", "Z1", "Y"),
    ("Y", "Z0", "X", "Z1"),
    ("X", "Z0", "Y", "Z1"),
)
ATTN_CUTS = (128, 256, 256)
PLAN = (
    (("begin",), ()),
    (("w", 1, 1), ()),
    (("w", 1, 0), ()),
    (("w", 3, 1), ()),
    (("w", 3, 0), ()),
    (("w", 4, 1), ()),
    (("w", 4, 0), ()),
    (("w", 2, 1), ()),
    (("w", 2, 0), ()),
    (("prep",), ()),
    (("p", 0), ()),
    (("p", 1), ()),
    (("p", 2), ()),
    (("p", 3), ()),
    (("p", 4), ()),
    (("q", 0), ()),
    (("q", 1), ("f4",)),
    (("q", 2), ("f1",)),
    (("q", 3), ("f3",)),
    (("q", 4), ()),
    (("w", 5, 1), ()),
    (("w", 5, 0), ()),
    (("w", 0, 1), ("f4",)),
    (("w", 0, 0), ()),
    (("kf",), ("f2",)),
    (("close",), ()),
    (("attn",), ("f1",)),
    (("tail",), ("f2", "f3", "f5", "f0", "f4", "f1", "f4", "a2", "a1", "g0", "a0", "f2", "f3", "a2", "f5", "f2", "f0", "f3", "a2", "f1", "a1", "g0", "a0", "a2", "g0", "a1", "a0", "f5", "a2", "g0", "a0", "a2", "g0", "a1", "f0", "a0", "f5", "a1", "a0", "a1", "f0")),
)
PARTS = len(FFN_CUTS)
COPIES_FINISH = 4 * len(ORDERS) + 6 * len(ATTN_ORDERS) + 5 + 3 + 4


def finish_kernel(*refs):
    where_ref, gain_ref, cos_ref, sin_ref, gains_ref = refs[:5]
    late_refs, lse_any = refs[5:14], refs[14]
    a_ref, c_ref, left_two, long_two, short_two, side_two, b_any, f_any, rhs_any = refs[15:24]
    count = 4
    dh_ref, gate_out, up_out, down_out = refs[24:28]
    query_out, key_out, value_out, output_out, gain_out = refs[28:33]
    refs = refs[33:]

    def taken(count):
        nonlocal refs
        first, refs = refs[:count], refs[count:]
        return first

    room = taken(7)
    dq_ref, dkv_ref, dkv_near, dkv_sum, dkv_far, dkv_low = taken(6)
    late = taken(9)
    q_ref, kv_ref, o_ref, wo_ref, dm_ref, h_ref, wq_ref, wk_ref, wv_ref = late
    lse_ref = taken(1)[0]
    b_all, f_all, rhs, left_all, long_all, short_all, side_all = taken(7)
    wholes = taken(len(ORDERS))
    rooms = [taken(4) for _ in ORDERS]
    attn_wholes = taken(len(ATTN_ORDERS))
    attn_rooms = [taken(4) for _ in ATTN_ORDERS]
    attn_alls = taken(len(ATTN_ORDERS))
    gain_whole, gain_got, gain_side, load, send, receive = refs
    rows = h_ref.shape[1]
    block = gate_out.shape[0]
    place = lax.axis_index("dp")
    head_at = lax.axis_index("head")
    core, across = head_at % 2, head_at // 2
    links, local = Links(send, receive), Local(load)
    sums = {}
    for index, (whole, got, order) in enumerate(zip(wholes, rooms, ORDERS)):
        start, cut = FFN_CUTS[index % PARTS]
        out = (gate_out, up_out, down_out)[index // PARTS].at[:, start : start + cut]
        reduce = halved(Halving, links, whole, got, order)
        reduce.done = functools.partial(out.__setitem__, Ellipsis)
        sums["f%d" % index] = reduce
    for index, (whole, got, order) in enumerate(zip(attn_wholes, attn_rooms, ATTN_ORDERS)):
        reduce = halved(Regather, links, whole, got, order)
        reduce.share(links, attn_alls[index])
        sums["a%d" % index] = reduce
    sums["g0"] = Rows(links, gain_whole, gain_side, gain_got, gain_out)
    seen = {name: 0 for name in sums}
    plan = []
    for step, names in PLAN:
        folds = []
        for name in names:
            folds.append((name, seen[name]))
            seen[name] += 1
        plan.append((step, folds))

    def take(folds):
        for name, which in folds:
            sums[name].fold(which)

    products = [step for step, _ in plan if step[0] == "w"]

    def fetch(turn):
        _, index, half = products[turn]
        start, cut = FFN_CUTS[index % PARTS]
        source = rhs_any.at[2 * (index // PARTS) + half, :, pl.ds(start, cut)]
        return local.move(source, rhs.at[turn % 2, :, pl.ds(0, cut)])

    b_load = local.move(b_any, b_all)
    coming = {0: fetch(0)}
    f_load = local.move(f_any, f_all)
    lates = [local.move(source, target) for source, target in zip(late_refs, late)]
    lates.append(local.move(lse_any, lse_ref))
    two = ((left_two, left_all), (long_two, long_all), (short_two, short_all), (side_two, side_all))
    two_loads = [local.move(source, target.at[:, pl.ds(0, 2 * rows)]) for source, target in two]
    greet((SIBLING, ACROSS, SIDE, BEYOND, FAR_SIDE))
    b_load.wait()

    def lay(product, whole, first):
        for index in range(8):
            relative = jnp.bitwise_xor(index, place)
            whole[first, relative // 4, relative // 2 % 2, relative % 2] = product[
                index * block : (index + 1) * block
            ].astype(LOW)

    f_ready = []

    def multiply(index, half):
        turn = products.index(("w", index, half))
        coming[turn].wait()
        if turn + 1 < len(products):
            coming[turn + 1] = fetch(turn + 1)
        if index >= 2 * PARTS and not f_ready:
            f_load.wait()
            f_ready.append(True)
        cut = FFN_CUTS[index % PARTS][1]
        lay(nn((b_all if index < 2 * PARTS else f_all)[...], rhs[turn % 2, :, :cut]), wholes[index], half)
        if half == (1 if ORDERS[index][0] == "X" else 0):
            sums["f%d" % index].start()

    cosine, sine = cos_ref[...], sin_ref[...]
    settle = Settle(links, dkv_ref, dkv_near, dkv_sum, dkv_far)
    low_rows, own_at, got_at = pl.ds(0, KV_WIDTH), pl.ds(2 * rows, rows), pl.ds(3 * rows, rows)
    high_rows, everything = pl.ds(KV_WIDTH, KV_WIDTH), slice(None)
    passes = {"p": {}, "q": {}}
    for step, folds in plan:
        if step[0] in passes:
            passes[step[0]][step[1]] = folds

    def at_group(which, group):
        for when, folds in passes[which].items():
            if folds:
                pl.when(group == when)(functools.partial(take, folds))
        if which == "q":
            settle.between(group)

    for step, folds in plan:
        if step[0] in passes:
            continue
        take(folds)
        if step[0] == "w":
            multiply(step[1], step[2])
        elif step[0] == "prep":
            for copy in lates:
                copy.wait()
            bias, k_sc, v_sc, kt_sc = room[:4]
            fill_bias(where_ref, bias, rows, count)
            lay_back(kv_ref, k_sc, v_sc, kt_sc, count, rows, False)
            attend_back(
                dm_ref[...],
                wo_ref,
                q_ref,
                o_ref,
                lse_ref,
                cosine,
                sine,
                dq_ref,
                dkv_ref,
                room,
                functools.partial(at_group, "p"),
                functools.partial(at_group, "q"),
            )
        elif step[0] == "kf":
            settle.near.start()
            from_query = nn(wq_ref[...], dq_ref[...]).T
            grad_keys, grad_values = close_keys(settle.finish(), cosine, sine, dkv_low)
            swaps = []
            for zero, one, target in (
                (a_ref, c_ref, left_all),
                (dq_ref, o_ref, long_all),
                (dkv_low.at[low_rows], dkv_low.at[high_rows], short_all),
                (a_ref, a_ref, side_all),
            ):
                swaps.append(
                    share_out(local, links, core, zero, one, target, (everything, own_at), (everything, got_at))
                )
        elif step[0] == "close":
            hidden = h_ref[...].astype(HIGH).T
            gain = gain_ref[0:1].astype(HIGH)
            gain_part, grad_in = close_rows(
                hidden, gain, dm_ref[...], from_query, grad_keys, grad_values, wk_ref, wv_ref
            )
            dh_ref[...] = grad_in.T
            summed = gains_ref[...] + jnp.concatenate([gain_part, jnp.zeros((7, gain_part.shape[1]), HIGH)], axis=0)
            for index in range(8):
                relative = jnp.bitwise_xor(index, place)
                spot = relative // 4, relative // 2 % 2, relative % 2
                gain_whole[(*spot, slice(None), slice(0, block))] = summed[:, index * block : (index + 1) * block]
                gain_whole[(*spot, slice(None), slice(block, 128))] = jnp.zeros((8, 128 - block), HIGH)
            sums["g0"].start()
        elif step[0] == "attn":
            for copy in two_loads:
                copy.wait()
            for keep, swap_copy in swaps:
                keep.wait()
                swap_copy.wait_recv()
            long_part = nt(left_all[...], long_all[...])
            short_part = nt(side_all[...], short_all[...])
            product = jnp.concatenate([long_part, short_part], axis=1)
            start = 0
            for index, (whole, cut) in enumerate(zip(attn_wholes, ATTN_CUTS)):
                for half in range(2):
                    lay(product[:, start : start + cut], whole, jnp.bitwise_xor(half, across))
                    start += cut
                sums["a%d" % index].start()
    for kind, (long_out, short_out) in enumerate(((query_out, key_out), (output_out, value_out))):
        from_core = jnp.bitwise_xor(kind, core)
        parts = [held[from_core, jnp.bitwise_xor(half, across)] for held in attn_alls for half in range(2)]
        both = jnp.concatenate([part.astype(HIGH) for part in parts], axis=1)
        long_out[...] = both[:, : long_out.shape[1]]
        short_out[...] = both[:, long_out.shape[1] :]
    links.drain()


def emit_kernel(gains, *refs):
    refs, rows = refs[:-2], refs[-2:]
    for index, row in enumerate(rows):
        row[...] = gains[index : index + 1, : row.shape[1]]
    count = len(refs) // 2
    for source, target in zip(refs[:count], refs[count:]):
        target[...] = source[...] if source.shape == target.shape else source[...].T


def call(body, outs, specs, scratch, name, spots=0, collective=None):
    params = {"vmem_limit_bytes": LIMIT}
    if collective is not None:
        params.update(collective_id=collective, has_side_effects=True)
    return pl.pallas_call(
        body,
        out_shape=[jax.ShapeDtypeStruct(shape, kind) for shape, kind in outs],
        in_specs=specs,
        out_specs=[VMEM] * (len(outs) - spots) + [ANY] * spots,
        scratch_shapes=scratch,
        compiler_params=pltpu.CompilerParams(**params),
        name=name,
    )


def swap(value, distance):
    count = lax.axis_size("head")
    return lax.ppermute(value, "head", [(i, i ^ distance) for i in range(count)])


def scatter_rows(value, axis):
    count = lax.axis_size(axis)
    index = lax.axis_index(axis)
    value = value.reshape((count, value.shape[0] // count) + value.shape[1:])
    bit = 1
    while bit < count:
        mine = (index // bit) % 2
        value = value.reshape((value.shape[0] // 2, 2) + value.shape[1:])
        sent = lax.dynamic_index_in_dim(value, 1 - mine, 1, False)
        kept = lax.dynamic_index_in_dim(value, mine, 1, False)
        got = lax.ppermute(sent, axis, [(i, i ^ bit) for i in range(count)])
        value = kept.astype(HIGH) + got.astype(HIGH)
        bit *= 2
        if bit < count:
            value = value.astype(LOW)
    return value[0]


def shards(
    tokens,
    cotangent,
    lengths,
    attn_gain,
    w_query,
    w_key,
    w_value,
    w_output,
    ffn_gain,
    w_gate,
    w_up,
    w_down,
):
    blocks = lax.axis_size("head")
    me = lax.axis_index("head").astype(jnp.int32)
    low_bit = me % 2
    rows, width = tokens.shape
    hidden = w_gate.shape[1]
    keys = blocks * rows
    where = lengths
    frequency = 10000.0 ** (-(jnp.arange(HALF, dtype=HIGH) * 2.0 / HD))
    position = (me * rows + jnp.arange(rows, dtype=jnp.int32)).astype(HIGH)
    angles = frequency[:, None] * position[None, :]
    cosine, sine = jnp.cos(angles), jnp.sin(angles)
    gain_rows = jnp.stack([attn_gain, ffn_gain])

    feature_rows = (width, rows)
    project_outs = [(feature_rows, LOW), (feature_rows, LOW), ((blocks, rows, 2 * KV_WIDTH), LOW)]
    tokens, cotangent, w_key, w_value, w_down = (v.T for v in (tokens, cotangent, w_key, w_value, w_down))
    weight_room = [pltpu.VMEM((blocks, width, hidden), LOW)] * 3
    layer_outs = [
        (feature_rows, LOW),
        ((8, PER_GROUP * rows), HIGH),
        ((rows, width), HIGH),
        (feature_rows, LOW),
        ((blocks, rows, hidden), LOW),
        ((blocks, rows, hidden), LOW),
    ]

    attend_outs = [(feature_rows, LOW), ((blocks, 2 * KV_WIDTH, rows), LOW)]
    room = attention_room(blocks, rows, width)
    key_room = [(blocks, 2 * KV_WIDTH, rows), (2, 2 * KV_WIDTH, rows)] + [(2 * KV_WIDTH, rows)] * 3

    def layers():
        outs = [(feature_rows, LOW), (feature_rows, LOW), ((rows, width), HIGH), ((8, width), HIGH)]
        outs += project_outs + layer_outs
        outs += [((width, 4 * rows), LOW)] * 2 + [((6, 4 * rows, hidden), LOW)]
        outs += [((n, 2 * rows), LOW) for n in (width, HQ * HD, KV_WIDTH, width)]
        statistics = pltpu.VMEM((8, PER_GROUP * rows), HIGH)
        scratch = room + [pltpu.VMEM((KV_WIDTH, keys), LOW), pltpu.VMEM(feature_rows, LOW)]
        scratch += [statistics, pltpu.VMEM((rows, width), HIGH)]
        scratch += [pltpu.VMEM(feature_rows, LOW)] * 3 + [pltpu.VMEM((blocks, rows, hidden), LOW)] * 2
        scratch += [pltpu.VMEM((6, rows, hidden), LOW)] * 2 + [pltpu.VMEM(feature_rows, LOW)]
        scratch += [pltpu.VMEM(shape, LOW) for shape in key_room]
        late = (w_key, w_value, w_query, w_output, cotangent)
        scratch += [pltpu.VMEM(v.shape, LOW) for v in late]
        kv_shape = (blocks, rows, 2 * KV_WIDTH)
        scratch += [pltpu.VMEM(shape, LOW) for shape in (feature_rows, feature_rows, kv_shape, kv_shape)]
        scratch += [statistics, statistics, pltpu.VMEM((rows, width), HIGH)]
        scratch += weight_room + [pltpu.SemaphoreType.DMA((LOCALS_MIDDLE,))]
        scratch += [pltpu.SemaphoreType.DMA((COPIES_MIDDLE,)), pltpu.SemaphoreType.DMA((COPIES_MIDDLE,))]
        given = [where, tokens, gain_rows, cosine, sine, *late, w_gate, w_up, w_down]
        specs = [SMEM] + [VMEM] * 4 + [ANY] * 8
        return call(functools.partial(layers_kernel, blocks), outs, specs, scratch, "layers", 16, 3)(*given)

    outs = layers()
    block_out, c_one, dm_one, gains, a_one, q_one, kv_one, o_one, lse_one = outs[:9]
    b_all, f_all, rhs_all, *halves_two = outs[13:]

    def close(h, grad_middle, grad_query, partial):
        sent = swap(jnp.stack([partial[1], partial[3]]), 1)
        far = swap((partial[2].astype(HIGH) + sent[1].astype(HIGH)).astype(LOW), 2)
        outs = [(feature_rows, HIGH), ((2 * KV_WIDTH, rows), LOW), ((1, width), HIGH)]
        given = [h, gain_rows, grad_middle, grad_query, w_query, w_key, w_value, cosine, sine]
        given += [partial[0], sent[0], far]
        return call(close_kernel, outs, [VMEM] * 12, [], "close")(*given)

    def beside(parts):
        return jnp.concatenate(parts, axis=-1)

    def choose(zero, one):
        return jnp.where(low_bit == 0, zero, one)

    def halves(a, c, o, dq, dkv):
        dk, dv = dkv[:KV_WIDTH], dkv[KV_WIDTH:]
        left = [choose(a, c), swap(choose(c, a), 1)]
        long = [choose(dq, o), swap(choose(o, dq), 1)]
        short = [choose(dk, dv), swap(choose(dv, dk), 1)]
        return beside(left), beside(long), beside(short), beside([a, swap(a, 1)])

    places = lax.axis_size("dp")
    block = width // places

    def finish():
        outs = [(feature_rows, HIGH)] + [((block, hidden), HIGH)] * 3
        outs += [((block, n), HIGH) for n in (HQ * HD, KV_WIDTH, KV_WIDTH, HQ * HD)] + [((8, 128), HIGH)]
        late = (q_one, kv_one, o_one, w_output, dm_one, tokens, w_query, w_key, w_value)
        scratch = room + [pltpu.VMEM(shape, LOW) for shape in [feature_rows] + key_room]
        scratch += [pltpu.VMEM(v.shape, v.dtype) for v in late] + [pltpu.VMEM(lse_one.shape, HIGH)]
        low_room = []
        low_room += [(width, 4 * rows), (width, 4 * rows), (2, 4 * rows, max(n for _, n in FFN_CUTS))]
        low_room += [(width, 4 * rows), (width, 4 * rows), (KV_WIDTH, 4 * rows), (width, 4 * rows)]
        low_room += [(2, 2, 2, 2, block, FFN_CUTS[i % PARTS][1]) for i in range(len(ORDERS))]
        scratch += [pltpu.VMEM(shape, LOW) for shape in low_room]
        for index, order in enumerate(ORDERS):
            scratch += halving_rooms(block, FFN_CUTS[index % PARTS][1], order)
        scratch += [pltpu.VMEM((2, 2, 2, 2, block, cut), LOW) for cut in ATTN_CUTS]
        for order, cut in zip(ATTN_ORDERS, ATTN_CUTS):
            scratch += halving_rooms(block, cut, order)
        scratch += [pltpu.VMEM((2, 2, block, cut), LOW) for cut in ATTN_CUTS]
        scratch += [pltpu.VMEM(shape, HIGH) for shape in ((2, 2, 2, 8, 128), (8, 8, 128), (2, 2, 8, 128))]
        scratch += [pltpu.SemaphoreType.DMA((48,)), pltpu.SemaphoreType.DMA((COPIES_FINISH,))]
        scratch += [pltpu.SemaphoreType.DMA((COPIES_FINISH,))]
        given = [where, gain_rows, cosine, sine, gains, *late, lse_one, a_one, c_one, *halves_two]
        specs = [SMEM] + [VMEM] * 4 + [ANY] * 19
        return call(finish_kernel, outs, specs, scratch, "finish", 0, 2)(*given, b_all, f_all, rhs_all)

    if places == 8 and blocks == 4:
        outs = finish()
        input_grad, gate_grad, up_grad, down_grad, query_grad, key_grad, value_grad, output_grad, gains = outs
        results = [block_out, input_grad, query_grad, key_grad, value_grad, output_grad, gate_grad, up_grad, down_grad]
        turned_over = (3, 4, 5)
        outs = [(v.shape[::-1] if i in turned_over else v.shape, v.dtype) for i, v in enumerate(results)]
        outs += [((1, block), HIGH)] * 2
        *results, one, two = call(emit_kernel, outs, [VMEM] * (len(results) + 1), [], "emit")(gains, *results)
        gains = one[0], two[0]
        block_out, input_grad, query_grad, key_grad, value_grad, output_grad, gate_grad, up_grad, down_grad = results
        key_grad, value_grad, output_grad = key_grad.T, value_grad.T, output_grad.T
    else:
        given = [where, dm_one, w_output, q_one, kv_one, o_one, lse_one, cosine, sine]
        dq_one, part_one = call(attend_back_kernel, attend_outs, [SMEM] + [VMEM] * 8, room, "attend_back")(*given)
        input_grad, dkv_one, gain_one_a = close(tokens, dm_one, dq_one, part_one)
        kept, sent = [], []
        for which in range(6):
            product = nn(b_all if which < 4 else f_all, rhs_all[which]).astype(LOW)
            (sent if which % 2 else kept).append(product)
        got = swap(beside(sent), 2)
        ffn = scatter_rows((beside(kept).astype(HIGH) + got.astype(HIGH)).astype(LOW), "dp")
        halves_one = halves(a_one, c_one, o_one, dq_one, dkv_one)
        left, long, short, side = (beside(pair) for pair in zip(halves_two, halves_one))
        attn = scatter_rows(beside([nt(left, long), nt(side, short)]).astype(LOW), "dp").astype(LOW)
        attn = (attn.astype(HIGH) + swap(attn, 2).astype(HIGH)).astype(LOW)
        other = swap(attn, 1)
        zero, one = choose(attn, other).astype(HIGH), choose(other, attn).astype(HIGH)
        gains = jnp.concatenate([gains[:1] + gain_one_a, gains[1:2]], axis=0)
        gains = lax.psum_scatter(lax.psum(gains, "head"), "dp", scatter_dimension=1, tiled=True)
        query_grad, key_grad = zero[:, : HQ * HD], zero[:, HQ * HD :]
        output_grad, value_grad = one[:, : HQ * HD], one[:, HQ * HD :]
        gate_grad, up_grad, down_grad = (ffn[:, i * hidden : (i + 1) * hidden] for i in range(3))
    return (
        block_out.T,
        input_grad.T,
        gains[0],
        query_grad,
        key_grad,
        value_grad,
        output_grad.T,
        gains[1],
        gate_grad,
        up_grad,
        down_grad.T,
    )


def solution(mesh):
    return jax.shard_map(
        shards,
        mesh=mesh,
        in_specs=(
            P(("dp", "head"), None),
            P(("dp", "head"), None),
            P("dp"),
            P(),
            P(),
            P(),
            P(),
            P(),
            P(),
            P(None, "head"),
            P(None, "head"),
            P("head", None),
        ),
        out_specs=(
            P(("dp", "head"), None),
            P(("dp", "head"), None),
            P("dp"),
            P("dp", None),
            P("dp", None),
            P("dp", None),
            P(None, "dp"),
            P("dp"),
            P("dp", "head"),
            P("dp", "head"),
            P("head", "dp"),
        ),
        check_vma=False,
    )
```

```python
import functools

import jax
import jax.numpy as jnp
from jax import lax
from jax.experimental import pallas as pl
from jax.experimental.pallas import tpu as pltpu
from jax.sharding import PartitionSpec as P

HQ = 15
KVH = 5
HD = 64
HALF = HD // 2
PER_GROUP = HQ // KVH
KV_WIDTH = KVH * HD
EPSILON = 1e-05
SCALE = HD ** (-0.5)
BLOCKED = -1e30
LOW = jnp.bfloat16
HIGH = jnp.float32
VMEM = pl.BlockSpec(memory_space=pltpu.VMEM)
SMEM = pl.BlockSpec(memory_space=pltpu.SMEM)
ANY = pl.BlockSpec(memory_space=pl.ANY)
LIMIT = 60 * 2**20
MESH = pl.DeviceIdType.MESH


def nn(left, right):
    return lax.dot_general(left, right, (((1,), (0,)), ((), ())), preferred_element_type=HIGH)


def nt(left, right):
    return lax.dot_general(left, right, (((1,), (1,)), ((), ())), preferred_element_type=HIGH)


def sigmoid(value):
    return 0.5 * (1.0 + jnp.tanh(0.5 * value))


def wide(gain_ref):
    return gain_ref[...].astype(HIGH).reshape(1, gain_ref.shape[0])


def inverse_rms(rows):
    return lax.rsqrt(jnp.mean(rows * rows, axis=1, keepdims=True) + EPSILON)


def norm_back(values_in, gain, grad_normed, grad_skip):
    inverse = inverse_rms(values_in)
    normal = values_in * inverse
    gain_part = jnp.sum(grad_normed * normal, axis=0, keepdims=True)
    scaled = grad_normed * gain
    back = grad_skip + inverse * (scaled - normal * jnp.mean(scaled * normal, axis=1, keepdims=True))
    return gain_part, back


def turned(columns, cosine, sine, sign, factor):
    parts = []
    for start in range(0, columns.shape[0], HD):
        first = columns[start : start + HALF] * factor
        second = columns[start + HALF : start + HD] * factor
        parts.append(first * cosine - sign * second * sine)
        parts.append(second * cosine + sign * first * sine)
    return jnp.concatenate(parts, axis=0)


def project(hidden, gain, w_query, w_key, w_value, cosine, sine, a_ref, q_ref, kv_ref, ready):
    normed = hidden * inverse_rms(hidden) * gain
    low = normed.astype(LOW)
    keys = turned(nt(w_key[...], low), cosine, sine, 1.0, 1.0)
    kv_ref[:, :KV_WIDTH] = keys.T.astype(LOW)
    kv_ref[:, KV_WIDTH:] = nt(low, w_value[...]).astype(LOW)
    ready()
    queries = nn(low, w_query[...]).T
    q_ref[...] = turned(queries, cosine, sine, 1.0, SCALE).astype(LOW)
    a_ref[...] = normed.T.astype(LOW)


def fill_bias(where_ref, bias, rows, blocks):
    me = lax.axis_index("head")
    length = where_ref[0]
    key = lax.broadcasted_iota(jnp.int32, (rows, rows), 0)
    query = lax.broadcasted_iota(jnp.int32, (rows, rows), 1)
    for step in range(blocks):
        other = jnp.bitwise_xor(me, step)
        allowed = other * rows + key < length
        if step == 0:
            allowed &= key <= query
        else:
            allowed &= other < me
        bias[step * rows : (step + 1) * rows] = jnp.where(allowed, 0.0, BLOCKED)


def side_by_side(ref, group):
    first = group * PER_GROUP
    heads = [ref[pl.ds(pl.multiple_of((first + i) * HD, HD), HD), :] for i in range(PER_GROUP)]
    return jnp.concatenate(heads, axis=1)


def one_below_other(ref, group, value):
    rows = value.shape[1] // PER_GROUP
    for member in range(PER_GROUP):
        at = pl.ds(pl.multiple_of((group * PER_GROUP + member) * HD, HD), HD)
        ref[at, :] = value[:, member * rows : (member + 1) * rows].astype(ref.dtype)


def scored(keys, queries, bias):
    return nn(keys, queries) + jnp.concatenate([bias] * PER_GROUP, axis=1)


def attend(bias, k_sc, vt_sc, q_ref, o_ref, lse_ref, event):
    def group_body(group, carry):
        keys = k_sc[group]
        values = vt_sc[pl.ds(pl.multiple_of(group * HD, HD), HD), :]
        event(group)
        scores = scored(keys, side_by_side(q_ref, group), bias[...])
        top = jnp.max(scores, axis=0, keepdims=True)
        exponent = jnp.exp(scores - top)
        total = jnp.sum(exponent, axis=0, keepdims=True)
        one_below_other(o_ref, group, nn(values, exponent.astype(LOW)) * (1.0 / total))
        lse_ref[pl.ds(group, 1), :] = top + jnp.log(total)
        return carry

    lax.fori_loop(0, KVH, group_body, 0)


def attend_first(bias, k_sc, vt_sc, q_ref, top_ref, total_ref, part_ref, half):
    def group_body(group, carry):
        keys = k_sc[group, :half]
        values = vt_sc[pl.ds(pl.multiple_of(group * HD, HD), HD), :half]
        scores = scored(keys, side_by_side(q_ref, group), bias[:half])
        top = jnp.max(scores, axis=0, keepdims=True)
        exponent = jnp.exp(scores - top)
        top_ref[pl.ds(group, 1), :] = top
        total_ref[pl.ds(group, 1), :] = jnp.sum(exponent, axis=0, keepdims=True)
        one_below_other(part_ref, group, nn(values, exponent.astype(LOW)))
        return carry

    lax.fori_loop(0, KVH, group_body, 0)


def attend_rest(bias, k_sc, vt_sc, q_ref, top_ref, total_ref, part_ref, half, o_ref, lse_ref):
    def group_body(group, carry):
        keys = k_sc[group, half:]
        values = vt_sc[pl.ds(pl.multiple_of(group * HD, HD), HD), half:]
        scores = scored(keys, side_by_side(q_ref, group), bias[half:])
        before = top_ref[pl.ds(group, 1), :]
        top = jnp.maximum(before, jnp.max(scores, axis=0, keepdims=True))
        exponent = jnp.exp(scores - top)
        rescale = jnp.exp(before - top)
        total = total_ref[pl.ds(group, 1), :] * rescale + jnp.sum(exponent, axis=0, keepdims=True)
        attended = side_by_side(part_ref, group) * rescale + nn(values, exponent.astype(LOW))
        one_below_other(o_ref, group, attended * (1.0 / total))
        lse_ref[pl.ds(group, 1), :] = top + jnp.log(total)
        return carry

    lax.fori_loop(0, KVH, group_body, 0)


def lay_keys(kv_ref, k_sc, vt_sc, steps, rows):
    for step in steps:
        at = slice(step * rows, (step + 1) * rows)
        for group in range(KVH):
            k_sc[group, at] = kv_ref[step, :, group * HD : (group + 1) * HD]
        vt_sc[:, at] = kv_ref[step, :, KV_WIDTH:].T


def after_attention(hidden, o_ref, wo_ref, gain, m_ref, b_ref):
    middle = hidden + nn(o_ref[...].T, wo_ref[...])
    m_ref[...] = middle
    normed = middle * inverse_rms(middle) * gain
    b_ref[...] = normed.T.astype(LOW)
    return middle, normed.astype(LOW)


def active_part(normed, wg, wu, g_ref, u_ref, step):
    gate = nn(normed, wg[step])
    up = nn(normed, wu[step])
    g_ref[step] = gate.astype(LOW)
    u_ref[step] = up.astype(LOW)
    return (gate * sigmoid(gate) * up).astype(LOW)


def hidden_part(normed, wg, wu, wd, g_ref, u_ref, step):
    return nt(active_part(normed, wg, wu, g_ref, u_ref, step), wd[step])


def partner(axis, distance):
    return {axis: jnp.bitwise_xor(lax.axis_index(axis), distance)}


def greet(partners):
    barrier = pltpu.get_barrier_semaphore()
    for axis, distance in partners:
        pl.semaphore_signal(barrier, inc=1, device_id=partner(axis, distance), device_id_type=MESH)
    pl.semaphore_wait(barrier, len(partners))


class Links:
    def __init__(self, send, receive):
        self.send, self.receive, self.used = send, receive, 0
        self.flying = []

    def push(self, source, target, to):
        copy = pltpu.make_async_remote_copy(
            src_ref=source,
            dst_ref=target,
            send_sem=self.send.at[self.used],
            recv_sem=self.receive.at[self.used],
            device_id=partner(*to),
            device_id_type=MESH,
        )
        self.used += 1
        self.flying.append(copy)
        return copy

    def drain(self):
        for copy in self.flying:
            copy.wait_send()


class Local:
    def __init__(self, sems):
        self.sems, self.used, self.flying = sems, 0, []

    def move(self, source, target, start=True):
        copy = pltpu.make_async_copy(source, target, self.sems.at[self.used])
        self.used += 1
        self.flying.append(copy)
        if start:
            copy.start()
        return copy

    def drain(self):
        for copy in self.flying:
            copy.wait()


SIBLING, ACROSS, SIDE, BEYOND = ("head", 1), ("head", 2), ("dp", 1), ("dp", 2)


class Share:
    def __init__(self, links, kv_ref):
        self.near = links.push(kv_ref.at[0], kv_ref.at[1], SIBLING)
        self.far = links.push(kv_ref.at[0], kv_ref.at[2], ACROSS)
        self.forth = links.push(kv_ref.at[2], kv_ref.at[3], SIBLING)

    def start(self):
        self.far.start()
        self.near.start()

    def pass_on(self):
        self.far.wait_recv()
        self.forth.start()

    def finish(self):
        self.near.wait_recv()
        self.forth.wait_recv()


class Spread:
    def __init__(self, links, own, all_ref, start, count):
        quarter = count // 4
        cut = quarter // 32 * 16
        place = lax.axis_index("dp") % 4

        def rows(which, first=0, size=quarter):
            at = start + jnp.bitwise_xor(place, which) * quarter + first
            return pl.ds(pl.multiple_of(at, 16), size)

        def move(which, to, *piece):
            ref = all_ref.at[2, rows(which, *piece)]
            return links.push(ref, ref, to)

        def aside(which):
            return links.push(all_ref.at[2, rows(which)], all_ref.at[3, rows(which)], SIBLING)

        span = pl.ds(start, count)
        self.near = links.push(own.at[span], all_ref.at[1, span], SIBLING)
        self.cross = links.push(own.at[rows(0)], all_ref.at[2, rows(0)], ACROSS)
        self.side, self.beyond = move(0, SIDE), move(0, BEYOND)
        self.side_half = move(2, SIDE, cut, quarter - cut)
        self.beyond_half = move(1, BEYOND, 0, cut)
        self.asides = [aside(which) for which in range(4)]

    def first(self):
        self.cross.wait_recv()
        self.side.start()
        self.beyond.start()
        self.asides[0].start()

    def second(self):
        self.side.wait_recv()
        self.beyond_half.start()
        self.asides[1].start()
        self.beyond.wait_recv()
        self.side_half.start()
        self.asides[2].start()

    def third(self):
        self.side_half.wait_recv()
        self.beyond_half.wait_recv()
        self.asides[3].start()

    def last(self):
        for copy in self.asides:
            copy.wait_recv()


COPIES_SHARE = 3
COPIES_SPREAD = 10


def first_forward(where_ref, h_ref, gain_one_ref, gain_two_ref, cos_ref, sin_ref, late, lates, owns, parts, results, attn, held, links, local):
    a_ref, q_ref, kv_ref, o_ref, lse_ref, m_ref, b_ref, g_ref, u_ref = parts
    bias, k_sc, vt_sc = attn
    wk_ref, wv_ref, wq_ref, wo_ref, _ = late
    wg, wu, wd = held
    blocks, rows = wg.shape[0], h_ref.shape[1]
    loads = [local.move(own, all_ref.at[0], False) for own, all_ref in zip(owns, held)]
    whole = owns[0].shape[0]
    middle_row = (whole // 128 + 1) * 64
    cuts = ((0, middle_row), (middle_row, whole - middle_row))
    spreads = [[Spread(links, own, all_ref, *cut) for cut in cuts] for own, all_ref in zip(owns, held)]
    (g1, g2), (u1, u2), (d1, d2) = spreads
    share = Share(links, kv_ref)
    greet((SIBLING, ACROSS, SIDE, BEYOND))
    for piece in (g1, g2):
        piece.cross.start()
    for pair, copy in zip(spreads, loads):
        for piece in pair:
            piece.near.start()
        copy.start()
    hidden = h_ref[...].astype(HIGH).T

    def queue():
        share.start()
        for piece in (u1, u2, d1, d2):
            piece.cross.start()
        lates[2].wait()

    lates[0].wait()
    lates[1].wait()
    gain_one = wide(gain_one_ref)
    project(hidden, gain_one, wq_ref, wk_ref, wv_ref, cos_ref[...], sin_ref[...], a_ref, q_ref, kv_ref.at[0], queue)
    g1.first()
    g2.first()
    fill_bias(where_ref, bias, rows, blocks)
    g1.second()
    g2.second()
    share.pass_on()
    g1.third()
    share.finish()
    lay_keys(kv_ref, k_sc, vt_sc, range(blocks), rows)
    events = ((g2.third, u1.first), (), (u2.first,), (u1.second,), (d1.first, u2.second))

    def event(group):
        for when, actions in enumerate(events):

            @pl.when(group == when)
            def _():
                for action in actions:
                    action()

    attend(bias, k_sc, vt_sc, q_ref, o_ref, lse_ref, event)
    d2.first()
    u1.third()
    lates[3].wait()
    middle, normed = after_attention(hidden, o_ref, wo_ref, wide(gain_two_ref), m_ref, b_ref)
    early = [local.move(source, target) for source, target in zip(parts[:7], results[:7])]
    u2.third()
    for copy in loads:
        copy.wait()
    active = [active_part(normed, wg, wu, g_ref, u_ref, 0)]
    d1.second()
    for pair in spreads:
        for piece in pair:
            piece.near.wait_recv()
    active.append(active_part(normed, wg, wu, g_ref, u_ref, 1))
    d2.second()
    d1.third()
    for step in range(2, 4):
        active.append(active_part(normed, wg, wu, g_ref, u_ref, step))
        if step == 2:
            for piece in (g1, g2, u1, u2):
                piece.last()
    early += [local.move(source, target) for source, target in zip(parts[7:], results[7:])]
    total = middle
    for step in range(blocks):
        if step == 2:
            d2.third()
        if step == 3:
            d1.last()
            d2.last()
        total = total + nt(active[step], wd[step])
    for copy in early:
        copy.wait()
    return total


def ffn_back(grad, g_ref, u_ref, m_ref, gain, wg, wu, wd, mine_ref, theirs_ref, ready):
    low_grad = grad.astype(LOW)
    grad_normed = jnp.zeros(m_ref.shape, HIGH)
    for step in (1, 3, 0, 2):
        grad_active = nn(low_grad, wd[step])
        gate = g_ref[step].astype(HIGH)
        up = u_ref[step].astype(HIGH)
        sig = sigmoid(gate)
        silu = gate * sig
        grad_gate = (grad_active * up * sig * (1.0 + gate * (1.0 - sig))).astype(LOW)
        grad_up = (grad_active * silu).astype(LOW)
        kept = mine_ref if step % 2 == 0 else theirs_ref
        kept[step // 2] = grad_gate
        kept[2 + step // 2] = grad_up
        kept[4 + step // 2] = (silu * up).astype(LOW)
        if step == 3:
            ready()
        grad_normed = grad_normed + nt(grad_gate, wg[step]) + nt(grad_up, wu[step])
    return norm_back(m_ref[...], gain, grad_normed, grad)


def lay_back(kv_ref, k_sc, v_sc, kt_sc, blocks, rows, keys_laid):
    for step in range(blocks):
        at = slice(step * rows, (step + 1) * rows)
        for group in range(KVH):
            if not keys_laid:
                k_sc[group, at] = kv_ref[step, :, group * HD : (group + 1) * HD]
            v_sc[group, at] = kv_ref[step, :, KV_WIDTH + group * HD : KV_WIDTH + (group + 1) * HD]
        kt_sc[:, at] = kv_ref[step, :, :KV_WIDTH].T


def attend_back(grad_middle, wo_ref, q_ref, o_ref, lse_ref, cosine, sine, dq_ref, dkv_ref, room, before, between):
    bias, k_sc, v_sc, kt_sc, do_sc, delta, dq_sc = room
    keys, rows = bias.shape
    blocks = keys // rows
    half = keys // 2
    do_sc[...] = nt(wo_ref[...], grad_middle.astype(LOW)).astype(LOW)
    for head in range(HQ):
        at = slice(head * HD, (head + 1) * HD)
        product = do_sc[at].astype(HIGH) * o_ref[at].astype(HIGH)
        group, member = divmod(head, PER_GROUP)
        spot = slice(member * rows, (member + 1) * rows)
        delta[group : group + 1, spot] = jnp.sum(product, axis=0, keepdims=True)
    cosines, sines = (jnp.concatenate([table] * PER_GROUP, axis=1) for table in (cosine, sine))

    def one_pass(start, last, event):
        cut = slice(start, start + half)

        def group_body(group, carry):
            event(group)
            group_keys = k_sc[group, cut]
            values = v_sc[group, cut]
            at = pl.ds(pl.multiple_of(group * HD, HD), HD)
            key_rows = pl.ds(pl.multiple_of(group * 2 * HD, HD), HD)
            value_rows = pl.ds(pl.multiple_of(group * 2 * HD + HD, HD), HD)
            keys_t = kt_sc[at, cut]
            query, grad_out = side_by_side(q_ref, group), side_by_side(do_sc, group)
            scores = scored(group_keys, query, bias[cut])
            prob = jnp.exp(scores - lse_ref[pl.ds(group, 1), :])
            grad_prob = nn(values, grad_out)
            grad_score = (prob * (grad_prob - delta[pl.ds(group, 1), :])).astype(LOW)
            grad_query = nn(keys_t, grad_score)
            if last:
                grad_query = grad_query + side_by_side(dq_sc, group)
                one_below_other(dq_ref, group, turned(grad_query, cosines, sines, -1.0, SCALE))
            else:
                one_below_other(dq_sc, group, grad_query)
            grad_keys = nt(query, grad_score)
            grad_values = nt(grad_out, prob.astype(LOW))
            for step in range(blocks // 2):
                part = slice(step * rows, (step + 1) * rows)
                dkv_ref[start // rows + step, key_rows, :] = grad_keys[:, part].astype(LOW)
                dkv_ref[start // rows + step, value_rows, :] = grad_values[:, part].astype(LOW)
            return carry

        lax.fori_loop(0, KVH, group_body, 0)

    one_pass(half, False, before)
    one_pass(0, True, between)


class Settle:
    def __init__(self, links, dkv_ref, near_ref, sum_ref, far_ref):
        self.refs = dkv_ref, near_ref, sum_ref, far_ref
        cut = 3 * 2 * HD
        self.spans = [pl.ds(0, cut), pl.ds(cut, dkv_ref.shape[1] - cut)]
        self.asides = [links.push(dkv_ref.at[3, span], near_ref.at[1, span], SIBLING) for span in self.spans]
        self.near = links.push(dkv_ref.at[1], near_ref.at[0], SIBLING)
        self.fars = [links.push(sum_ref.at[span], far_ref.at[span], ACROSS) for span in self.spans]
        self.copies = [*self.asides, self.near, *self.fars]

    def across(self, which):
        dkv_ref, near_ref, sum_ref, _ = self.refs
        span = self.spans[which]
        self.asides[which].wait_recv()
        sum_ref[span] = (dkv_ref[2, span].astype(HIGH) + near_ref[1, span].astype(HIGH)).astype(LOW)
        self.fars[which].start()

    def before(self, group):
        pl.when(group == 3)(self.asides[0].start)
        pl.when(group == 4)(functools.partial(self.across, 0))

    def between(self, group):
        pl.when(group == 0)(self.asides[1].start)
        pl.when(group == 1)(functools.partial(self.across, 1))

    def finish(self):
        dkv_ref, near_ref, _, far_ref = self.refs
        self.near.wait_recv()
        for copy in self.fars:
            copy.wait_recv()
        return dkv_ref[0].astype(HIGH) + near_ref[0].astype(HIGH) + far_ref[...].astype(HIGH)


def attention_room(blocks, rows, width):
    keys = blocks * rows
    return [
        pltpu.VMEM((keys, rows), HIGH),
        pltpu.VMEM((KVH, keys, HD), LOW),
        pltpu.VMEM((KVH, keys, HD), LOW),
        pltpu.VMEM((KV_WIDTH, keys), LOW),
        pltpu.VMEM((width, rows), LOW),
        pltpu.VMEM((8, PER_GROUP * rows), HIGH),
        pltpu.VMEM((width, rows), HIGH),
    ]


def share_out(local, links, core, zero, one, target, own_at, got_at):
    if zero is one:
        keep = local.move(zero, target.at[own_at])
        send = links.push(zero, target.at[got_at], SIBLING)
        send.start()
        return keep, send
    keep = local.move(zero, target.at[own_at], False)
    keep_one = pltpu.make_async_copy(one, target.at[own_at], local.sems.at[local.used - 1])
    send = links.push(one, target.at[got_at], SIBLING)
    links.used -= 1
    links.flying.pop()
    send_zero = links.push(zero, target.at[got_at], SIBLING)

    @pl.when(core == 0)
    def _():
        keep.start()
        send.start()

    @pl.when(core == 1)
    def _():
        keep_one.start()
        send_zero.start()

    return keep, send


COPIES_MIDDLE = 6 * COPIES_SPREAD + COPIES_SHARE + 22
LOCALS_MIDDLE = 40


def layers_kernel(blocks, *refs):
    where_ref, tokens_ref, gain_one_ref, gain_two_ref, cos_ref, sin_ref = refs[:6]
    refs = refs[1:]
    late_refs, owns = refs[5:10], refs[10:13]
    out_ref, c_ref, dm_ref, gains_ref = refs[13:17]
    results = refs[17:26]
    m_any, b_any, g_any, u_any = results[5:]
    b_all, f_all, rhs_all, left_two, long_two, short_two, side_two = refs[26:33]
    room = refs[33:40]
    bias, k_sc, v_sc, kt_sc = room[:4]
    part_sc = room[6]
    vt_sc, o_sc, lse_sc, m_sc, b_sc, f_sc, c_sc, g_sc, u_sc = refs[40:49]
    mine, theirs, dq_sc, dkv_sc, dkv_near, dkv_sum, dkv_far, dkv_low = refs[49:57]
    late = refs[57:62]
    a_sc, q_ref, kv_first, kv_ref, top_sc, total_sc, h_ref = refs[62:69]
    wk, wv, wq, wo_ref, cot = late
    wg, wu, wd, load, send, receive = refs[69:]
    rows = h_ref.shape[0]
    core = lax.axis_index("head") % 2
    local = Local(load)
    links = Links(send, receive)
    lates = [local.move(source, target) for source, target in zip(late_refs, late)]
    parts = (a_sc, q_ref, kv_first, o_sc, lse_sc, m_sc, b_sc, g_sc, u_sc)
    h_ref[...] = first_forward(
        where_ref,
        tokens_ref,
        gain_one_ref,
        gain_two_ref,
        cos_ref,
        sin_ref,
        late,
        lates,
        owns,
        parts,
        results,
        (bias, k_sc, vt_sc),
        (wg, wu, wd),
        links,
        local,
    )
    waited = list(links.flying)
    share = Share(links, kv_ref)
    settle = Settle(links, dkv_sc, dkv_near, dkv_sum, dkv_far)
    spans = [pl.ds(i * rows, rows) for i in range(4)]
    everything = slice(None)

    def both(source, target, place):
        keep = local.move(source, target.at[(*place, spans[both.layer])])
        copy = links.push(source, target.at[(*place, spans[both.layer + 1])], SIBLING)
        copy.start()
        return keep, copy

    both.layer = 2
    posted = [both(b_any, b_all, (everything,))]
    both.layer = 0
    cosine, sine = cos_ref[...], sin_ref[...]
    half = blocks * rows // 2

    gain_one = wide(gain_one_ref)
    project(h_ref[...], gain_one, wq, wk, wv, cosine, sine, a_sc, q_ref, kv_ref.at[0], share.start)
    share.near.wait_recv()
    lay_keys(kv_ref, k_sc, vt_sc, range(blocks // 2), rows)
    attend_first(bias, k_sc, vt_sc, q_ref, top_sc, total_sc, part_sc, half)
    share.pass_on()
    share.forth.wait_recv()
    lay_keys(kv_ref, k_sc, vt_sc, range(blocks // 2, blocks), rows)
    attend_rest(bias, k_sc, vt_sc, q_ref, top_sc, total_sc, part_sc, half, o_sc, lse_sc)
    total, normed = after_attention(h_ref[...], o_sc, wo_ref, wide(gain_two_ref), m_sc, b_sc)
    posted.append(both(b_sc, b_all, (everything,)))
    for step in range(blocks):
        total = total + hidden_part(normed, wg, wu, wd, g_sc, u_sc, step)
    out_ref[...] = total.T.astype(LOW)
    lay_back(kv_ref, k_sc, v_sc, kt_sc, blocks, rows, True)

    lates[4].wait()
    row = lax.axis_index("head") * rows + lax.broadcasted_iota(jnp.int32, (rows, 1), 0)
    grad = jnp.where(row < where_ref[0], cot[...].astype(HIGH).T, 0.0)
    f_sc[...] = grad.T.astype(LOW)
    first_f = both(f_sc, f_all, (everything,))
    gain_two = wide(gain_two_ref)
    send_theirs = links.push(theirs, rhs_all.at[:, spans[1]], SIBLING)
    gain_part, grad_middle = ffn_back(
        grad, g_sc, u_sc, m_sc, gain_two, wg, wu, wd, mine, theirs, send_theirs.start
    )
    first_loads = [local.move(source, target) for source, target in ((g_any, g_sc), (u_any, u_sc), (m_any, m_sc))]
    keep_mine = local.move(mine, rhs_all.at[:, spans[0]])
    gains_ref[...] = jnp.zeros(gains_ref.shape, HIGH)
    gains_ref[1:2] = gain_part
    c_sc[...] = grad_middle.T.astype(LOW)
    attend_back(
        grad_middle, wo_ref, q_ref, o_sc, lse_sc, cosine, sine, dq_sc, dkv_sc, room, settle.before, settle.between
    )
    settle.near.start()
    from_query = nn(wq[...], dq_sc[...]).T
    grad_keys, grad_values = close_keys(settle.finish(), cosine, sine, dkv_low)
    low_rows, high_rows = pl.ds(0, KV_WIDTH), pl.ds(KV_WIDTH, KV_WIDTH)
    for zero, one, target in (
        (a_sc, c_sc, left_two),
        (dq_sc, o_sc, long_two),
        (dkv_low.at[low_rows], dkv_low.at[high_rows], short_two),
        (a_sc, a_sc, side_two),
    ):
        posted.append(
            share_out(local, links, core, zero, one, target, (everything, spans[0]), (everything, spans[1]))
        )
    gain_part, grad = close_rows(h_ref[...], gain_one, grad_middle, from_query, grad_keys, grad_values, wk, wv)
    gains_ref[0:1] = gain_part

    first_f[0].wait()
    first_f[1].wait_send()
    keep_mine.wait()
    send_theirs.wait_send()
    for copy in first_loads:
        copy.wait()
    f_sc[...] = grad.T.astype(LOW)
    both.layer = 2
    posted.append(both(f_sc, f_all, (everything,)))
    send_last = links.push(theirs, rhs_all.at[:, spans[3]], SIBLING)
    gain_part, grad_middle = ffn_back(
        grad, g_sc, u_sc, m_sc, gain_two, wg, wu, wd, mine, theirs, send_last.start
    )
    keep_last = local.move(mine, rhs_all.at[:, spans[2]])
    gains_ref[1:2] = gains_ref[1:2] + gain_part
    dm_ref[...] = grad_middle
    c_ref[...] = grad_middle.T.astype(LOW)
    for keep, copy in posted:
        keep.wait()
        copy.wait()
    first_f[1].wait_recv()
    send_theirs.wait_recv()
    keep_last.wait()
    send_last.wait()
    for copy in (*settle.copies, share.near, share.far, share.forth, *waited):
        copy.wait_send()


def attend_back_kernel(*refs):
    where_ref, dm_ref, wo_ref, q_ref, kv_ref, o_ref, lse_ref, cos_ref, sin_ref, dq_ref, dkv_ref = refs[:11]
    room = refs[11:]
    bias, k_sc, v_sc, kt_sc = room[:4]
    blocks, rows = kv_ref.shape[:2]
    fill_bias(where_ref, bias, rows, blocks)
    lay_back(kv_ref, k_sc, v_sc, kt_sc, blocks, rows, False)
    attend_back(
        dm_ref[...], wo_ref, q_ref, o_ref, lse_ref, cos_ref[...], sin_ref[...], dq_ref, dkv_ref, room, lambda group: None, lambda group: None
    )


def close_keys(total, cosine, sine, dkv_ref):
    starts = range(0, total.shape[0], 2 * HD)
    parts = [total[start : start + HD] for start in starts] + [total[start + HD : start + 2 * HD] for start in starts]
    total = jnp.concatenate(parts, axis=0)
    turned_keys = turned(total[:KV_WIDTH], cosine, sine, -1.0, 1.0)
    dkv_ref[:KV_WIDTH] = turned_keys.astype(LOW)
    dkv_ref[KV_WIDTH:] = total[KV_WIDTH:].astype(LOW)
    return turned_keys.T.astype(LOW), total[KV_WIDTH:].T.astype(LOW)


def close_rows(hidden, gain, grad_middle, from_query, grad_keys, grad_values, wk_ref, wv_ref):
    grad_normed = from_query + nn(grad_keys, wk_ref[...]) + nn(grad_values, wv_ref[...])
    return norm_back(hidden, gain, grad_normed, grad_middle)


def close_kernel(*refs):
    h_ref, gain_one_ref, dm_ref, dq_ref, wq_ref, wk_ref, wv_ref, cos_ref, sin_ref = refs[:9]
    own, near, far, dh_ref, dkv_ref, gain_part_ref = refs[9:]
    total = own[...].astype(HIGH) + near[...].astype(HIGH) + far[...].astype(HIGH)
    grad_keys, grad_values = close_keys(total, cos_ref[...], sin_ref[...], dkv_ref)
    hidden = h_ref[...].astype(HIGH).T
    gain = wide(gain_one_ref)
    from_query = nn(wq_ref[...], dq_ref[...]).T
    gain_part, grad_in = close_rows(hidden, gain, dm_ref[...], from_query, grad_keys, grad_values, wk_ref, wv_ref)
    gain_part_ref[...] = gain_part
    dh_ref[...] = grad_in.T


class Halving:
    def __init__(self, links, steps):
        self.steps = [(links.push(sent, got, to), kept, got) for sent, kept, got, to in steps]

    def start(self):
        self.steps[0][0].start()

    def fold(self, which):
        copy, kept, got = self.steps[which]
        copy.wait_recv()
        total = kept[...].astype(HIGH) + got[...].astype(HIGH)
        if which == len(self.steps) - 1:
            self.done(total)
        else:
            kept[...] = total.astype(kept.dtype)
            self.steps[which + 1][0].start()


class Regather(Halving):
    def share(self, links, held):
        self.held = held
        self.across = links.push(held.at[0, 0], held.at[0, 1], ACROSS)
        self.aside = links.push(held.at[0], held.at[1], SIBLING)

    def done(self, total):
        self.held[0, 0] = total.astype(LOW)
        self.across.start()

    def fold(self, which):
        if which < len(self.steps):
            Halving.fold(self, which)
        elif which == len(self.steps):
            self.across.wait_recv()
            self.aside.start()
        else:
            self.aside.wait_recv()


class Rows:
    def __init__(self, links, whole, side, got, out):
        self.steps = (
            (whole.at[:, :, 1], side, whole.at[:, :, 0], SIDE),
            (whole.at[:, 1, 0], got.at[pl.ds(0, 2)], whole.at[:, 0, 0], BEYOND),
            (whole.at[1, 0, 0], got.at[2], whole.at[0, 0, 0], FAR_SIDE),
            (whole.at[0, 0, 0], got.at[3], None, ACROSS),
            (got.at[4], got.at[5], None, SIBLING),
        )
        self.copies = [links.push(source, target, to) for source, target, _, to in self.steps]
        self.whole, self.got, self.out = whole, got, out

    def start(self):
        self.copies[0].start()

    def fold(self, which):
        self.copies[which].wait_recv()
        if which < 3:
            _, target, kept, _ = self.steps[which]
            kept[...] = kept[...] + target[...]
        elif which == 3:
            self.got[4] = self.whole[0, 0, 0] + self.got[3]
        else:
            self.out[...] = self.got[4] + self.got[5]
        if which < 4:
            self.copies[which + 1].start()


FAR_SIDE = ("dp", 4)


def halved(kind, links, whole, rooms, order):
    where = {"X": 0, "Z1": 1, "Z0": 2, "Y": 3}
    to = {"X": ACROSS, "Z1": FAR_SIDE, "Z0": BEYOND, "Y": SIDE}
    chosen = [slice(None)] * 4
    steps = []
    for axis, room in zip(order, rooms):
        sent, kept = list(chosen), list(chosen)
        sent[where[axis]], kept[where[axis]] = 1, 0
        steps.append((whole.at[tuple(sent)], whole.at[tuple(kept)], room, to[axis]))
        chosen = kept
    return kind(links, steps)


def halving_rooms(block, columns, order):
    left = [2, 2, 2, 2]
    where = {"X": 0, "Z1": 1, "Z0": 2, "Y": 3}
    rooms = []
    for axis in order:
        left[where[axis]] = 0
        rooms.append(pltpu.VMEM(tuple(n for n in left if n) + (block, columns), LOW))
    return rooms


FFN_CUTS = ((0, 256), (256, 384))
ORDERS = (
    ("Y", "X", "Z0", "Z1"),
    ("Z0", "Y", "Z1", "X"),
    ("Z0", "Z1", "X", "Y"),
    ("Y", "Z0", "X", "Z1"),
    ("X", "Y", "Z0", "Z1"),
    ("X", "Y", "Z0", "Z1"),
)
ATTN_ORDERS = (
    ("Z0", "X", "Z1", "Y"),
    ("Y", "Z0", "X", "Z1"),
    ("X", "Z0", "Y", "Z1"),
)
ATTN_CUTS = (128, 256, 256)
PLAN = (
    (("begin",), ()),
    (("w", 1, 1), ()),
    (("w", 1, 0), ()),
    (("w", 3, 1), ()),
    (("w", 3, 0), ()),
    (("w", 4, 1), ()),
    (("w", 4, 0), ()),
    (("w", 2, 1), ()),
    (("w", 2, 0), ()),
    (("prep",), ()),
    (("p", 0), ()),
    (("p", 1), ()),
    (("p", 2), ()),
    (("p", 3), ()),
    (("p", 4), ()),
    (("q", 0), ()),
    (("q", 1), ("f4",)),
    (("q", 2), ("f1",)),
    (("q", 3), ("f3",)),
    (("q", 4), ()),
    (("w", 5, 1), ()),
    (("w", 5, 0), ()),
    (("w", 0, 1), ("f4",)),
    (("w", 0, 0), ()),
    (("kf",), ("f2",)),
    (("close",), ()),
    (("attn",), ("f1",)),
    (("tail",), ("f2", "f3", "f5", "f0", "f4", "f1", "f4", "a2", "a1", "g0", "a0", "f2", "f3", "a2", "f5", "f2", "f0", "f3", "a2", "f1", "a1", "g0", "a0", "a2", "g0", "a1", "a0", "f5", "a2", "g0", "a0", "a2", "g0", "a1", "f0", "a0", "f5", "a1", "a0", "a1", "f0")),
)
PARTS = len(FFN_CUTS)
COPIES_FINISH = 4 * len(ORDERS) + 6 * len(ATTN_ORDERS) + 5 + 5 + 4


def finish_kernel(*refs):
    where_ref, gain_one_ref, cos_ref, sin_ref, gains_ref = refs[:5]
    late_refs, lse_any = refs[5:14], refs[14]
    a_ref, c_ref, left_two, long_two, short_two, side_two, b_any, f_any, rhs_any = refs[15:24]
    count = 4
    dh_ref, gate_out, up_out, down_out = refs[24:28]
    query_out, key_out, value_out, output_out, gain_out = refs[28:33]
    refs = refs[33:]

    def taken(count):
        nonlocal refs
        first, refs = refs[:count], refs[count:]
        return first

    room = taken(7)
    dq_ref, dkv_ref, dkv_near, dkv_sum, dkv_far, dkv_low = taken(6)
    late = taken(9)
    q_ref, kv_ref, o_ref, wo_ref, dm_ref, h_ref, wq_ref, wk_ref, wv_ref = late
    lse_ref = taken(1)[0]
    b_all, f_all, rhs, left_all, long_all, short_all, side_all = taken(7)
    wholes = taken(len(ORDERS))
    rooms = [taken(4) for _ in ORDERS]
    attn_wholes = taken(len(ATTN_ORDERS))
    attn_rooms = [taken(4) for _ in ATTN_ORDERS]
    attn_alls = taken(len(ATTN_ORDERS))
    gain_whole, gain_got, gain_side, load, send, receive = refs
    rows = h_ref.shape[1]
    block = gate_out.shape[0]
    place = lax.axis_index("dp")
    head_at = lax.axis_index("head")
    core, across = head_at % 2, head_at // 2
    links, local = Links(send, receive), Local(load)
    sums = {}
    for index, (whole, got, order) in enumerate(zip(wholes, rooms, ORDERS)):
        start, cut = FFN_CUTS[index % PARTS]
        out = (gate_out, up_out, down_out)[index // PARTS].at[:, start : start + cut]
        reduce = halved(Halving, links, whole, got, order)
        reduce.done = functools.partial(out.__setitem__, Ellipsis)
        sums["f%d" % index] = reduce
    for index, (whole, got, order) in enumerate(zip(attn_wholes, attn_rooms, ATTN_ORDERS)):
        reduce = halved(Regather, links, whole, got, order)
        reduce.share(links, attn_alls[index])
        sums["a%d" % index] = reduce
    sums["g0"] = Rows(links, gain_whole, gain_side, gain_got, gain_out)
    seen = {name: 0 for name in sums}
    plan = []
    for step, names in PLAN:
        folds = []
        for name in names:
            folds.append((name, seen[name]))
            seen[name] += 1
        plan.append((step, folds))

    def take(folds):
        for name, which in folds:
            sums[name].fold(which)

    products = [step for step, _ in plan if step[0] == "w"]

    def fetch(turn):
        _, index, half = products[turn]
        start, cut = FFN_CUTS[index % PARTS]
        source = rhs_any.at[2 * (index // PARTS) + half, :, pl.ds(start, cut)]
        return local.move(source, rhs.at[turn % 2, :, pl.ds(0, cut)])

    b_load = local.move(b_any, b_all)
    coming = {0: fetch(0)}
    f_load = local.move(f_any, f_all)
    lates = [local.move(source, target) for source, target in zip(late_refs, late)]
    lates.append(local.move(lse_any, lse_ref))
    two = ((left_two, left_all), (long_two, long_all), (short_two, short_all), (side_two, side_all))
    two_loads = [local.move(source, target.at[:, pl.ds(0, 2 * rows)]) for source, target in two]
    greet((SIBLING, ACROSS, SIDE, BEYOND, FAR_SIDE))
    b_load.wait()

    def lay(product, whole, first):
        for index in range(8):
            relative = jnp.bitwise_xor(index, place)
            whole[first, relative // 4, relative // 2 % 2, relative % 2] = product[
                index * block : (index + 1) * block
            ].astype(LOW)

    f_ready = []

    def multiply(index, half):
        turn = products.index(("w", index, half))
        coming[turn].wait()
        if turn + 1 < len(products):
            coming[turn + 1] = fetch(turn + 1)
        if index >= 2 * PARTS and not f_ready:
            f_load.wait()
            f_ready.append(True)
        cut = FFN_CUTS[index % PARTS][1]
        lay(nn((b_all if index < 2 * PARTS else f_all)[...], rhs[turn % 2, :, :cut]), wholes[index], half)
        if half == (1 if ORDERS[index][0] == "X" else 0):
            sums["f%d" % index].start()

    cosine, sine = cos_ref[...], sin_ref[...]
    settle = Settle(links, dkv_ref, dkv_near, dkv_sum, dkv_far)
    low_rows, own_at, got_at = pl.ds(0, KV_WIDTH), pl.ds(2 * rows, rows), pl.ds(3 * rows, rows)
    high_rows, everything = pl.ds(KV_WIDTH, KV_WIDTH), slice(None)
    passes = {"p": {}, "q": {}}
    for step, folds in plan:
        if step[0] in passes:
            passes[step[0]][step[1]] = folds

    def at_group(which, group):
        for when, folds in passes[which].items():
            if folds:
                pl.when(group == when)(functools.partial(take, folds))
        (settle.between if which == "q" else settle.before)(group)

    for step, folds in plan:
        if step[0] in passes:
            continue
        take(folds)
        if step[0] == "w":
            multiply(step[1], step[2])
        elif step[0] == "prep":
            for copy in lates:
                copy.wait()
            bias, k_sc, v_sc, kt_sc = room[:4]
            fill_bias(where_ref, bias, rows, count)
            lay_back(kv_ref, k_sc, v_sc, kt_sc, count, rows, False)
            attend_back(
                dm_ref[...],
                wo_ref,
                q_ref,
                o_ref,
                lse_ref,
                cosine,
                sine,
                dq_ref,
                dkv_ref,
                room,
                functools.partial(at_group, "p"),
                functools.partial(at_group, "q"),
            )
        elif step[0] == "kf":
            settle.near.start()
            from_query = nn(wq_ref[...], dq_ref[...]).T
            grad_keys, grad_values = close_keys(settle.finish(), cosine, sine, dkv_low)
            swaps = []
            for zero, one, target in (
                (a_ref, c_ref, left_all),
                (dq_ref, o_ref, long_all),
                (dkv_low.at[low_rows], dkv_low.at[high_rows], short_all),
                (a_ref, a_ref, side_all),
            ):
                swaps.append(
                    share_out(local, links, core, zero, one, target, (everything, own_at), (everything, got_at))
                )
        elif step[0] == "close":
            hidden = h_ref[...].astype(HIGH).T
            gain = wide(gain_one_ref)
            gain_part, grad_in = close_rows(
                hidden, gain, dm_ref[...], from_query, grad_keys, grad_values, wk_ref, wv_ref
            )
            dh_ref[...] = grad_in.T
            summed = gains_ref[...] + jnp.concatenate([gain_part, jnp.zeros((7, gain_part.shape[1]), HIGH)], axis=0)
            for index in range(8):
                relative = jnp.bitwise_xor(index, place)
                spot = relative // 4, relative // 2 % 2, relative % 2
                gain_whole[(*spot, slice(None), slice(0, block))] = summed[:, index * block : (index + 1) * block]
                gain_whole[(*spot, slice(None), slice(block, 128))] = jnp.zeros((8, 128 - block), HIGH)
            sums["g0"].start()
        elif step[0] == "attn":
            for copy in two_loads:
                copy.wait()
            for keep, swap_copy in swaps:
                keep.wait()
                swap_copy.wait_recv()
            long_part = nt(left_all[...], long_all[...])
            short_part = nt(side_all[...], short_all[...])
            product = jnp.concatenate([long_part, short_part], axis=1)
            start = 0
            for index, (whole, cut) in enumerate(zip(attn_wholes, ATTN_CUTS)):
                for half in range(2):
                    lay(product[:, start : start + cut], whole, jnp.bitwise_xor(half, across))
                    start += cut
                sums["a%d" % index].start()
    for kind, (long_out, short_out) in enumerate(((query_out, key_out), (output_out, value_out))):
        from_core = jnp.bitwise_xor(kind, core)
        parts = [held[from_core, jnp.bitwise_xor(half, across)] for held in attn_alls for half in range(2)]
        both = jnp.concatenate([part.astype(HIGH) for part in parts], axis=1)
        long_out[...] = both[:, : long_out.shape[1]]
        short_out[...] = both[:, long_out.shape[1] :]
    links.drain()


def emit_kernel(gains, *refs):
    refs, rows = refs[:-2], refs[-2:]
    for index, row in enumerate(rows):
        row[...] = gains[index : index + 1, : row.shape[1]]
    count = len(refs) // 2
    for source, target in zip(refs[:count], refs[count:]):
        target[...] = source[...] if source.shape == target.shape else source[...].T


def call(body, outs, specs, scratch, name, spots=0, collective=None):
    params = {"vmem_limit_bytes": LIMIT}
    if collective is not None:
        params.update(collective_id=collective, has_side_effects=True)
    return pl.pallas_call(
        body,
        out_shape=[jax.ShapeDtypeStruct(shape, kind) for shape, kind in outs],
        in_specs=specs,
        out_specs=[VMEM] * (len(outs) - spots) + [ANY] * spots,
        scratch_shapes=scratch,
        compiler_params=pltpu.CompilerParams(**params),
        name=name,
    )


def swap(value, distance):
    count = lax.axis_size("head")
    return lax.ppermute(value, "head", [(i, i ^ distance) for i in range(count)])


def scatter_rows(value, axis):
    count = lax.axis_size(axis)
    index = lax.axis_index(axis)
    value = value.reshape((count, value.shape[0] // count) + value.shape[1:])
    bit = 1
    while bit < count:
        mine = (index // bit) % 2
        value = value.reshape((value.shape[0] // 2, 2) + value.shape[1:])
        sent = lax.dynamic_index_in_dim(value, 1 - mine, 1, False)
        kept = lax.dynamic_index_in_dim(value, mine, 1, False)
        got = lax.ppermute(sent, axis, [(i, i ^ bit) for i in range(count)])
        value = kept.astype(HIGH) + got.astype(HIGH)
        bit *= 2
        if bit < count:
            value = value.astype(LOW)
    return value[0]


def shards(
    tokens,
    cotangent,
    lengths,
    attn_gain,
    w_query,
    w_key,
    w_value,
    w_output,
    ffn_gain,
    w_gate,
    w_up,
    w_down,
):
    blocks = lax.axis_size("head")
    me = lax.axis_index("head").astype(jnp.int32)
    low_bit = me % 2
    rows, width = tokens.shape
    hidden = w_gate.shape[1]
    keys = blocks * rows
    where = lengths
    frequency = 10000.0 ** (-(jnp.arange(HALF, dtype=HIGH) * 2.0 / HD))
    position = (me * rows + jnp.arange(rows, dtype=jnp.int32)).astype(HIGH)
    angles = frequency[:, None] * position[None, :]
    cosine, sine = jnp.cos(angles), jnp.sin(angles)

    feature_rows = (width, rows)
    project_outs = [(feature_rows, LOW), (feature_rows, LOW), ((blocks, rows, 2 * KV_WIDTH), LOW)]
    tokens, cotangent, w_key, w_value, w_down = (v.T for v in (tokens, cotangent, w_key, w_value, w_down))
    weight_room = [pltpu.VMEM((blocks, width, hidden), LOW)] * 3
    layer_outs = [
        (feature_rows, LOW),
        ((8, PER_GROUP * rows), HIGH),
        ((rows, width), HIGH),
        (feature_rows, LOW),
        ((blocks, rows, hidden), LOW),
        ((blocks, rows, hidden), LOW),
    ]

    attend_outs = [(feature_rows, LOW), ((blocks, 2 * KV_WIDTH, rows), LOW)]
    room = attention_room(blocks, rows, width)
    key_room = [(blocks, 2 * KV_WIDTH, rows), (2, 2 * KV_WIDTH, rows)] + [(2 * KV_WIDTH, rows)] * 3

    def layers():
        outs = [(feature_rows, LOW), (feature_rows, LOW), ((rows, width), HIGH), ((8, width), HIGH)]
        outs += project_outs + layer_outs
        outs += [((width, 4 * rows), LOW)] * 2 + [((6, 4 * rows, hidden), LOW)]
        outs += [((n, 2 * rows), LOW) for n in (width, HQ * HD, KV_WIDTH, width)]
        statistics = pltpu.VMEM((8, PER_GROUP * rows), HIGH)
        scratch = room + [pltpu.VMEM((KV_WIDTH, keys), LOW), pltpu.VMEM(feature_rows, LOW)]
        scratch += [statistics, pltpu.VMEM((rows, width), HIGH)]
        scratch += [pltpu.VMEM(feature_rows, LOW)] * 3 + [pltpu.VMEM((blocks, rows, hidden), LOW)] * 2
        scratch += [pltpu.VMEM((6, rows, hidden), LOW)] * 2 + [pltpu.VMEM(feature_rows, LOW)]
        scratch += [pltpu.VMEM(shape, LOW) for shape in key_room]
        late = (w_key, w_value, w_query, w_output, cotangent)
        scratch += [pltpu.VMEM(v.shape, LOW) for v in late]
        kv_shape = (blocks, rows, 2 * KV_WIDTH)
        scratch += [pltpu.VMEM(shape, LOW) for shape in (feature_rows, feature_rows, kv_shape, kv_shape)]
        scratch += [statistics, statistics, pltpu.VMEM((rows, width), HIGH)]
        scratch += weight_room + [pltpu.SemaphoreType.DMA((LOCALS_MIDDLE,))]
        scratch += [pltpu.SemaphoreType.DMA((COPIES_MIDDLE,)), pltpu.SemaphoreType.DMA((COPIES_MIDDLE,))]
        given = [where, tokens, attn_gain, ffn_gain, cosine, sine, *late, w_gate, w_up, w_down]
        specs = [SMEM] + [VMEM] * 5 + [ANY] * 8
        return call(functools.partial(layers_kernel, blocks), outs, specs, scratch, "layers", 16, 3)(*given)

    outs = layers()
    block_out, c_one, dm_one, gains, a_one, q_one, kv_one, o_one, lse_one = outs[:9]
    b_all, f_all, rhs_all, *halves_two = outs[13:]

    def close(h, grad_middle, grad_query, partial):
        sent = swap(jnp.stack([partial[1], partial[3]]), 1)
        far = swap((partial[2].astype(HIGH) + sent[1].astype(HIGH)).astype(LOW), 2)
        outs = [(feature_rows, HIGH), ((2 * KV_WIDTH, rows), LOW), ((1, width), HIGH)]
        given = [h, attn_gain, grad_middle, grad_query, w_query, w_key, w_value, cosine, sine]
        given += [partial[0], sent[0], far]
        return call(close_kernel, outs, [VMEM] * 12, [], "close")(*given)

    def beside(parts):
        return jnp.concatenate(parts, axis=-1)

    def choose(zero, one):
        return jnp.where(low_bit == 0, zero, one)

    def halves(a, c, o, dq, dkv):
        dk, dv = dkv[:KV_WIDTH], dkv[KV_WIDTH:]
        left = [choose(a, c), swap(choose(c, a), 1)]
        long = [choose(dq, o), swap(choose(o, dq), 1)]
        short = [choose(dk, dv), swap(choose(dv, dk), 1)]
        return beside(left), beside(long), beside(short), beside([a, swap(a, 1)])

    places = lax.axis_size("dp")
    block = width // places

    def finish():
        outs = [(feature_rows, HIGH)] + [((block, hidden), HIGH)] * 3
        outs += [((block, n), HIGH) for n in (HQ * HD, KV_WIDTH, KV_WIDTH, HQ * HD)] + [((8, 128), HIGH)]
        late = (q_one, kv_one, o_one, w_output, dm_one, tokens, w_query, w_key, w_value)
        scratch = room + [pltpu.VMEM(shape, LOW) for shape in [feature_rows] + key_room]
        scratch += [pltpu.VMEM(v.shape, v.dtype) for v in late] + [pltpu.VMEM(lse_one.shape, HIGH)]
        low_room = []
        low_room += [(width, 4 * rows), (width, 4 * rows), (2, 4 * rows, max(n for _, n in FFN_CUTS))]
        low_room += [(width, 4 * rows), (width, 4 * rows), (KV_WIDTH, 4 * rows), (width, 4 * rows)]
        low_room += [(2, 2, 2, 2, block, FFN_CUTS[i % PARTS][1]) for i in range(len(ORDERS))]
        scratch += [pltpu.VMEM(shape, LOW) for shape in low_room]
        for index, order in enumerate(ORDERS):
            scratch += halving_rooms(block, FFN_CUTS[index % PARTS][1], order)
        scratch += [pltpu.VMEM((2, 2, 2, 2, block, cut), LOW) for cut in ATTN_CUTS]
        for order, cut in zip(ATTN_ORDERS, ATTN_CUTS):
            scratch += halving_rooms(block, cut, order)
        scratch += [pltpu.VMEM((2, 2, block, cut), LOW) for cut in ATTN_CUTS]
        scratch += [pltpu.VMEM(shape, HIGH) for shape in ((2, 2, 2, 8, 128), (8, 8, 128), (2, 2, 8, 128))]
        scratch += [pltpu.SemaphoreType.DMA((48,)), pltpu.SemaphoreType.DMA((COPIES_FINISH,))]
        scratch += [pltpu.SemaphoreType.DMA((COPIES_FINISH,))]
        given = [where, attn_gain, cosine, sine, gains, *late, lse_one, a_one, c_one, *halves_two]
        specs = [SMEM] + [VMEM] * 4 + [ANY] * 19
        return call(finish_kernel, outs, specs, scratch, "finish", 0, 2)(*given, b_all, f_all, rhs_all)

    if places == 8 and blocks == 4:
        outs = finish()
        input_grad, gate_grad, up_grad, down_grad, query_grad, key_grad, value_grad, output_grad, gains = outs
        results = [block_out, input_grad, query_grad, key_grad, value_grad, output_grad, gate_grad, up_grad, down_grad]
        turned_over = (3, 4, 5)
        outs = [(v.shape[::-1] if i in turned_over else v.shape, v.dtype) for i, v in enumerate(results)]
        outs += [((1, block), HIGH)] * 2
        *results, one, two = call(emit_kernel, outs, [VMEM] * (len(results) + 1), [], "emit")(gains, *results)
        gains = one[0], two[0]
        block_out, input_grad, query_grad, key_grad, value_grad, output_grad, gate_grad, up_grad, down_grad = results
        key_grad, value_grad, output_grad = key_grad.T, value_grad.T, output_grad.T
    else:
        given = [where, dm_one, w_output, q_one, kv_one, o_one, lse_one, cosine, sine]
        dq_one, part_one = call(attend_back_kernel, attend_outs, [SMEM] + [VMEM] * 8, room, "attend_back")(*given)
        input_grad, dkv_one, gain_one_a = close(tokens, dm_one, dq_one, part_one)
        kept, sent = [], []
        for which in range(6):
            product = nn(b_all if which < 4 else f_all, rhs_all[which]).astype(LOW)
            (sent if which % 2 else kept).append(product)
        got = swap(beside(sent), 2)
        ffn = scatter_rows((beside(kept).astype(HIGH) + got.astype(HIGH)).astype(LOW), "dp")
        halves_one = halves(a_one, c_one, o_one, dq_one, dkv_one)
        left, long, short, side = (beside(pair) for pair in zip(halves_two, halves_one))
        attn = scatter_rows(beside([nt(left, long), nt(side, short)]).astype(LOW), "dp").astype(LOW)
        attn = (attn.astype(HIGH) + swap(attn, 2).astype(HIGH)).astype(LOW)
        other = swap(attn, 1)
        zero, one = choose(attn, other).astype(HIGH), choose(other, attn).astype(HIGH)
        gains = jnp.concatenate([gains[:1] + gain_one_a, gains[1:2]], axis=0)
        gains = lax.psum_scatter(lax.psum(gains, "head"), "dp", scatter_dimension=1, tiled=True)
        query_grad, key_grad = zero[:, : HQ * HD], zero[:, HQ * HD :]
        output_grad, value_grad = one[:, : HQ * HD], one[:, HQ * HD :]
        gate_grad, up_grad, down_grad = (ffn[:, i * hidden : (i + 1) * hidden] for i in range(3))
    return (
        block_out.T,
        input_grad.T,
        gains[0],
        query_grad,
        key_grad,
        value_grad,
        output_grad.T,
        gains[1],
        gate_grad,
        up_grad,
        down_grad.T,
    )


def solution(mesh):
    return jax.shard_map(
        shards,
        mesh=mesh,
        in_specs=(
            P(("dp", "head"), None),
            P(("dp", "head"), None),
            P("dp"),
            P(),
            P(),
            P(),
            P(),
            P(),
            P(),
            P(None, "head"),
            P(None, "head"),
            P("head", None),
        ),
        out_specs=(
            P(("dp", "head"), None),
            P(("dp", "head"), None),
            P("dp"),
            P("dp", None),
            P("dp", None),
            P("dp", None),
            P(None, "dp"),
            P("dp"),
            P("dp", "head"),
            P("dp", "head"),
            P("head", "dp"),
        ),
        check_vma=False,
    )
```

```python
import functools

import jax
import jax.numpy as jnp
from jax import lax
from jax.experimental import pallas as pl
from jax.experimental.pallas import tpu as pltpu
from jax.sharding import PartitionSpec as P

HQ = 15
KVH = 5
HD = 64
HALF = HD // 2
PER_GROUP = HQ // KVH
KV_WIDTH = KVH * HD
EPSILON = 1e-05
SCALE = HD ** (-0.5)
BLOCKED = -1e30
LOW = jnp.bfloat16
HIGH = jnp.float32
VMEM = pl.BlockSpec(memory_space=pltpu.VMEM)
SMEM = pl.BlockSpec(memory_space=pltpu.SMEM)
ANY = pl.BlockSpec(memory_space=pl.ANY)
LIMIT = 60 * 2**20
MESH = pl.DeviceIdType.MESH


def nn(left, right):
    return lax.dot_general(left, right, (((1,), (0,)), ((), ())), preferred_element_type=HIGH)


def nt(left, right):
    return lax.dot_general(left, right, (((1,), (1,)), ((), ())), preferred_element_type=HIGH)


def sigmoid(value):
    return 0.5 * (1.0 + jnp.tanh(0.5 * value))


def wide(gain_ref):
    return gain_ref[...].astype(HIGH).reshape(1, gain_ref.shape[0])


def inverse_rms(rows):
    return lax.rsqrt(jnp.mean(rows * rows, axis=1, keepdims=True) + EPSILON)


def norm_back(values_in, gain, grad_normed, grad_skip):
    inverse = inverse_rms(values_in)
    normal = values_in * inverse
    gain_part = jnp.sum(grad_normed * normal, axis=0, keepdims=True)
    scaled = grad_normed * gain
    back = grad_skip + inverse * (scaled - normal * jnp.mean(scaled * normal, axis=1, keepdims=True))
    return gain_part, back


def turned(columns, cosine, sine, sign, factor):
    parts = []
    for start in range(0, columns.shape[0], HD):
        first = columns[start : start + HALF] * factor
        second = columns[start + HALF : start + HD] * factor
        parts.append(first * cosine - sign * second * sine)
        parts.append(second * cosine + sign * first * sine)
    return jnp.concatenate(parts, axis=0)


def project(hidden, gain, w_query, w_key, w_value, cosine, sine, a_ref, q_ref, kv_ref, ready):
    normed = hidden * inverse_rms(hidden) * gain
    low = normed.astype(LOW)
    keys = turned(nt(w_key[...], low), cosine, sine, 1.0, 1.0)
    kv_ref[:, :KV_WIDTH] = keys.T.astype(LOW)
    kv_ref[:, KV_WIDTH:] = nt(low, w_value[...]).astype(LOW)
    ready()
    queries = nn(low, w_query[...]).T
    q_ref[...] = turned(queries, cosine, sine, 1.0, SCALE).astype(LOW)
    a_ref[...] = normed.T.astype(LOW)


def fill_bias(where_ref, bias, rows, blocks):
    me = lax.axis_index("head")
    length = where_ref[0]
    key = lax.broadcasted_iota(jnp.int32, (rows, rows), 0)
    query = lax.broadcasted_iota(jnp.int32, (rows, rows), 1)
    for step in range(blocks):
        other = jnp.bitwise_xor(me, step)
        allowed = other * rows + key < length
        if step == 0:
            allowed &= key <= query
        else:
            allowed &= other < me
        bias[step * rows : (step + 1) * rows] = jnp.where(allowed, 0.0, BLOCKED)


def side_by_side(ref, group):
    first = group * PER_GROUP
    heads = [ref[pl.ds(pl.multiple_of((first + i) * HD, HD), HD), :] for i in range(PER_GROUP)]
    return jnp.concatenate(heads, axis=1)


def one_below_other(ref, group, value):
    rows = value.shape[1] // PER_GROUP
    for member in range(PER_GROUP):
        at = pl.ds(pl.multiple_of((group * PER_GROUP + member) * HD, HD), HD)
        ref[at, :] = value[:, member * rows : (member + 1) * rows].astype(ref.dtype)


def scored(keys, queries, bias):
    return nn(keys, queries) + jnp.concatenate([bias] * PER_GROUP, axis=1)


def attend(bias, k_sc, vt_sc, q_ref, o_ref, lse_ref, event):
    def group_body(group, carry):
        keys = k_sc[group]
        values = vt_sc[pl.ds(pl.multiple_of(group * HD, HD), HD), :]
        event(group)
        scores = scored(keys, side_by_side(q_ref, group), bias[...])
        top = jnp.max(scores, axis=0, keepdims=True)
        exponent = jnp.exp(scores - top)
        total = jnp.sum(exponent, axis=0, keepdims=True)
        one_below_other(o_ref, group, nn(values, exponent.astype(LOW)) * (1.0 / total))
        lse_ref[pl.ds(group, 1), :] = top + jnp.log(total)
        return carry

    lax.fori_loop(0, KVH, group_body, 0)


def attend_first(bias, k_sc, vt_sc, q_ref, top_ref, total_ref, part_ref, half):
    def group_body(group, carry):
        keys = k_sc[group, :half]
        values = vt_sc[pl.ds(pl.multiple_of(group * HD, HD), HD), :half]
        scores = scored(keys, side_by_side(q_ref, group), bias[:half])
        top = jnp.max(scores, axis=0, keepdims=True)
        exponent = jnp.exp(scores - top)
        top_ref[pl.ds(group, 1), :] = top
        total_ref[pl.ds(group, 1), :] = jnp.sum(exponent, axis=0, keepdims=True)
        one_below_other(part_ref, group, nn(values, exponent.astype(LOW)))
        return carry

    lax.fori_loop(0, KVH, group_body, 0)


def attend_rest(bias, k_sc, vt_sc, q_ref, top_ref, total_ref, part_ref, half, o_ref, lse_ref):
    def group_body(group, carry):
        keys = k_sc[group, half:]
        values = vt_sc[pl.ds(pl.multiple_of(group * HD, HD), HD), half:]
        scores = scored(keys, side_by_side(q_ref, group), bias[half:])
        before = top_ref[pl.ds(group, 1), :]
        top = jnp.maximum(before, jnp.max(scores, axis=0, keepdims=True))
        exponent = jnp.exp(scores - top)
        rescale = jnp.exp(before - top)
        total = total_ref[pl.ds(group, 1), :] * rescale + jnp.sum(exponent, axis=0, keepdims=True)
        attended = side_by_side(part_ref, group) * rescale + nn(values, exponent.astype(LOW))
        one_below_other(o_ref, group, attended * (1.0 / total))
        lse_ref[pl.ds(group, 1), :] = top + jnp.log(total)
        return carry

    lax.fori_loop(0, KVH, group_body, 0)


def lay_keys(kv_ref, k_sc, vt_sc, steps, rows):
    for step in steps:
        at = slice(step * rows, (step + 1) * rows)
        for group in range(KVH):
            k_sc[group, at] = kv_ref[step, :, group * HD : (group + 1) * HD]
        vt_sc[:, at] = kv_ref[step, :, KV_WIDTH:].T


def after_attention(hidden, o_ref, wo_ref, gain, m_ref, b_ref):
    middle = hidden + nn(o_ref[...].T, wo_ref[...])
    m_ref[...] = middle
    normed = middle * inverse_rms(middle) * gain
    b_ref[...] = normed.T.astype(LOW)
    return middle, normed.astype(LOW)


def active_part(normed, wg, wu, g_ref, u_ref, step):
    gate = nn(normed, wg[step])
    up = nn(normed, wu[step])
    g_ref[step] = gate.astype(LOW)
    u_ref[step] = up.astype(LOW)
    return (gate * sigmoid(gate) * up).astype(LOW)


def hidden_part(normed, wg, wu, wd, g_ref, u_ref, step):
    return nt(active_part(normed, wg, wu, g_ref, u_ref, step), wd[step])


def partner(axis, distance):
    return {axis: jnp.bitwise_xor(lax.axis_index(axis), distance)}


def greet(partners):
    barrier = pltpu.get_barrier_semaphore()
    for axis, distance in partners:
        pl.semaphore_signal(barrier, inc=1, device_id=partner(axis, distance), device_id_type=MESH)
    pl.semaphore_wait(barrier, len(partners))


class Links:
    def __init__(self, send, receive):
        self.send, self.receive, self.used = send, receive, 0
        self.flying = []

    def push(self, source, target, to):
        copy = pltpu.make_async_remote_copy(
            src_ref=source,
            dst_ref=target,
            send_sem=self.send.at[self.used],
            recv_sem=self.receive.at[self.used],
            device_id=partner(*to),
            device_id_type=MESH,
        )
        self.used += 1
        self.flying.append(copy)
        return copy

    def drain(self):
        for copy in self.flying:
            copy.wait_send()


class Local:
    def __init__(self, sems):
        self.sems, self.used, self.flying = sems, 0, []

    def move(self, source, target, start=True):
        copy = pltpu.make_async_copy(source, target, self.sems.at[self.used])
        self.used += 1
        self.flying.append(copy)
        if start:
            copy.start()
        return copy

    def drain(self):
        for copy in self.flying:
            copy.wait()


SIBLING, ACROSS, SIDE, BEYOND = ("head", 1), ("head", 2), ("dp", 1), ("dp", 2)


class Share:
    def __init__(self, links, kv_ref):
        self.near = links.push(kv_ref.at[0], kv_ref.at[1], SIBLING)
        self.far = links.push(kv_ref.at[0], kv_ref.at[2], ACROSS)
        self.forth = links.push(kv_ref.at[2], kv_ref.at[3], SIBLING)

    def start(self):
        self.far.start()
        self.near.start()

    def pass_on(self):
        self.far.wait_recv()
        self.forth.start()

    def finish(self):
        self.near.wait_recv()
        self.forth.wait_recv()


class Spread:
    def __init__(self, links, own, all_ref, start, count):
        quarter = count // 4
        cut = quarter // 32 * 16
        place = lax.axis_index("dp") % 4

        def rows(which, first=0, size=quarter):
            at = start + jnp.bitwise_xor(place, which) * quarter + first
            return pl.ds(pl.multiple_of(at, 16), size)

        def move(which, to, *piece):
            ref = all_ref.at[2, rows(which, *piece)]
            return links.push(ref, ref, to)

        def aside(which):
            return links.push(all_ref.at[2, rows(which)], all_ref.at[3, rows(which)], SIBLING)

        span = pl.ds(start, count)
        self.near = links.push(own.at[span], all_ref.at[1, span], SIBLING)
        self.cross = links.push(own.at[rows(0)], all_ref.at[2, rows(0)], ACROSS)
        self.side, self.beyond = move(0, SIDE), move(0, BEYOND)
        self.side_half = move(2, SIDE, cut, quarter - cut)
        self.beyond_half = move(1, BEYOND, 0, cut)
        self.asides = [aside(which) for which in range(4)]

    def first(self):
        self.cross.wait_recv()
        self.side.start()
        self.beyond.start()
        self.asides[0].start()

    def second(self):
        self.side.wait_recv()
        self.beyond_half.start()
        self.asides[1].start()
        self.beyond.wait_recv()
        self.side_half.start()
        self.asides[2].start()

    def third(self):
        self.side_half.wait_recv()
        self.beyond_half.wait_recv()
        self.asides[3].start()

    def last(self):
        for copy in self.asides:
            copy.wait_recv()


COPIES_SHARE = 3
COPIES_SPREAD = 10


def first_forward(where_ref, h_ref, gain_one_ref, gain_two_ref, cos_ref, sin_ref, late, lates, owns, parts, results, attn, held, links, local):
    a_ref, q_ref, kv_ref, o_ref, lse_ref, m_ref, b_ref, g_ref, u_ref = parts
    bias, k_sc, vt_sc = attn
    wk_ref, wv_ref, wq_ref, wo_ref, _ = late
    wg, wu, wd = held
    blocks, rows = wg.shape[0], h_ref.shape[1]
    loads = [local.move(own, all_ref.at[0], False) for own, all_ref in zip(owns, held)]
    whole = owns[0].shape[0]
    middle_row = (whole // 128 + 1) * 64
    cuts = ((0, middle_row), (middle_row, whole - middle_row))
    spreads = [[Spread(links, own, all_ref, *cut) for cut in cuts] for own, all_ref in zip(owns, held)]
    (g1, g2), (u1, u2), (d1, d2) = spreads
    share = Share(links, kv_ref)
    greet((SIBLING, ACROSS, SIDE, BEYOND))
    for piece in (g1, g2):
        piece.cross.start()
    for pair, copy in zip(spreads, loads):
        for piece in pair:
            piece.near.start()
        copy.start()
    hidden = h_ref[...].astype(HIGH).T

    def queue():
        share.start()
        for piece in (u1, u2, d1, d2):
            piece.cross.start()
        lates[2].wait()

    lates[0].wait()
    lates[1].wait()
    gain_one = wide(gain_one_ref)
    project(hidden, gain_one, wq_ref, wk_ref, wv_ref, cos_ref[...], sin_ref[...], a_ref, q_ref, kv_ref.at[0], queue)
    g1.first()
    g2.first()
    fill_bias(where_ref, bias, rows, blocks)
    g1.second()
    g2.second()
    share.pass_on()
    g1.third()
    share.finish()
    lay_keys(kv_ref, k_sc, vt_sc, range(blocks), rows)
    events = ((g2.third, u1.first), (), (u2.first,), (u1.second,), (d1.first, u2.second))

    def event(group):
        for when, actions in enumerate(events):

            @pl.when(group == when)
            def _():
                for action in actions:
                    action()

    attend(bias, k_sc, vt_sc, q_ref, o_ref, lse_ref, event)
    d2.first()
    u1.third()
    lates[3].wait()
    middle, normed = after_attention(hidden, o_ref, wo_ref, wide(gain_two_ref), m_ref, b_ref)
    early = [local.move(source, target) for source, target in zip(parts[:7], results[:7])]
    u2.third()
    for copy in loads:
        copy.wait()
    active = [active_part(normed, wg, wu, g_ref, u_ref, 0)]
    d1.second()
    for pair in spreads:
        for piece in pair:
            piece.near.wait_recv()
    active.append(active_part(normed, wg, wu, g_ref, u_ref, 1))
    d2.second()
    d1.third()
    for step in range(2, 4):
        active.append(active_part(normed, wg, wu, g_ref, u_ref, step))
        if step == 2:
            for piece in (g1, g2, u1, u2):
                piece.last()
    early += [local.move(source, target) for source, target in zip(parts[7:], results[7:])]
    total = middle
    for step in range(blocks):
        if step == 2:
            d2.third()
        if step == 3:
            d1.last()
            d2.last()
        total = total + nt(active[step], wd[step])
    for copy in early:
        copy.wait()
    return total


def ffn_back(grad, g_ref, u_ref, m_ref, gain, wg, wu, wd, mine_ref, theirs_ref, ready):
    low_grad = grad.astype(LOW)
    grad_normed = jnp.zeros(m_ref.shape, HIGH)
    order, products = (1, 3, 0, 2), []
    coming = nn(low_grad, wd[order[0]])
    for turn, step in enumerate(order):
        grad_active = coming
        if turn < 3:
            coming = nn(low_grad, wd[order[turn + 1]])
        gate = g_ref[step].astype(HIGH)
        up = u_ref[step].astype(HIGH)
        sig = sigmoid(gate)
        silu = gate * sig
        grad_gate = (grad_active * up * sig * (1.0 + gate * (1.0 - sig))).astype(LOW)
        grad_up = (grad_active * silu).astype(LOW)
        kept = mine_ref if step % 2 == 0 else theirs_ref
        kept[step // 2] = grad_gate
        kept[2 + step // 2] = grad_up
        kept[4 + step // 2] = (silu * up).astype(LOW)
        if step == 3:
            ready()
        products.append((step, grad_gate, grad_up))
        if turn:
            before, one, two = products[turn - 1]
            grad_normed = grad_normed + nt(one, wg[before]) + nt(two, wu[before])
    before, one, two = products[-1]
    grad_normed = grad_normed + nt(one, wg[before]) + nt(two, wu[before])
    return norm_back(m_ref[...], gain, grad_normed, grad)


def lay_back(kv_ref, k_sc, v_sc, kt_sc, blocks, rows, keys_laid):
    for step in range(blocks):
        at = slice(step * rows, (step + 1) * rows)
        for group in range(KVH):
            if not keys_laid:
                k_sc[group, at] = kv_ref[step, :, group * HD : (group + 1) * HD]
            v_sc[group, at] = kv_ref[step, :, KV_WIDTH + group * HD : KV_WIDTH + (group + 1) * HD]
        kt_sc[:, at] = kv_ref[step, :, :KV_WIDTH].T


def attend_back(grad_middle, wo_ref, q_ref, o_ref, lse_ref, cosine, sine, dq_ref, dkv_ref, room, before, between):
    bias, k_sc, v_sc, kt_sc, do_sc, delta, dq_sc = room
    keys, rows = bias.shape
    blocks = keys // rows
    half = keys // 2
    do_sc[...] = nt(wo_ref[...], grad_middle.astype(LOW)).astype(LOW)
    for head in range(HQ):
        at = slice(head * HD, (head + 1) * HD)
        product = do_sc[at].astype(HIGH) * o_ref[at].astype(HIGH)
        group, member = divmod(head, PER_GROUP)
        spot = slice(member * rows, (member + 1) * rows)
        delta[group : group + 1, spot] = jnp.sum(product, axis=0, keepdims=True)
    cosines, sines = (jnp.concatenate([table] * PER_GROUP, axis=1) for table in (cosine, sine))

    def one_pass(start, last, event):
        cut = slice(start, start + half)

        def group_body(group, carry):
            event(group)
            group_keys = k_sc[group, cut]
            values = v_sc[group, cut]
            at = pl.ds(pl.multiple_of(group * HD, HD), HD)
            key_rows = pl.ds(pl.multiple_of(group * 2 * HD, HD), HD)
            value_rows = pl.ds(pl.multiple_of(group * 2 * HD + HD, HD), HD)
            keys_t = kt_sc[at, cut]
            query, grad_out = side_by_side(q_ref, group), side_by_side(do_sc, group)
            scores = scored(group_keys, query, bias[cut])
            prob = jnp.exp(scores - lse_ref[pl.ds(group, 1), :])
            grad_prob = nn(values, grad_out)
            grad_score = (prob * (grad_prob - delta[pl.ds(group, 1), :])).astype(LOW)
            grad_query = nn(keys_t, grad_score)
            if last:
                grad_query = grad_query + side_by_side(dq_sc, group)
                one_below_other(dq_ref, group, turned(grad_query, cosines, sines, -1.0, SCALE))
            else:
                one_below_other(dq_sc, group, grad_query)
            grad_keys = nt(query, grad_score)
            grad_values = nt(grad_out, prob.astype(LOW))
            for step in range(blocks // 2):
                part = slice(step * rows, (step + 1) * rows)
                dkv_ref[start // rows + step, key_rows, :] = grad_keys[:, part].astype(LOW)
                dkv_ref[start // rows + step, value_rows, :] = grad_values[:, part].astype(LOW)
            return carry

        lax.fori_loop(0, KVH, group_body, 0)

    one_pass(half, False, before)
    one_pass(0, True, between)


class Settle:
    def __init__(self, links, dkv_ref, near_ref, sum_ref, far_ref):
        self.refs = dkv_ref, near_ref, sum_ref, far_ref
        cut = 3 * 2 * HD
        self.spans = [pl.ds(0, cut), pl.ds(cut, dkv_ref.shape[1] - cut)]
        self.asides = [links.push(dkv_ref.at[3, span], near_ref.at[1, span], SIBLING) for span in self.spans]
        self.near = links.push(dkv_ref.at[1], near_ref.at[0], SIBLING)
        self.fars = [links.push(sum_ref.at[span], far_ref.at[span], ACROSS) for span in self.spans]
        self.copies = [*self.asides, self.near, *self.fars]

    def across(self, which):
        dkv_ref, near_ref, sum_ref, _ = self.refs
        span = self.spans[which]
        self.asides[which].wait_recv()
        sum_ref[span] = (dkv_ref[2, span].astype(HIGH) + near_ref[1, span].astype(HIGH)).astype(LOW)
        self.fars[which].start()

    def before(self, group):
        pl.when(group == 3)(self.asides[0].start)
        pl.when(group == 4)(functools.partial(self.across, 0))

    def between(self, group):
        pl.when(group == 0)(self.asides[1].start)
        pl.when(group == 1)(functools.partial(self.across, 1))

    def finish(self):
        dkv_ref, near_ref, _, far_ref = self.refs
        self.near.wait_recv()
        for copy in self.fars:
            copy.wait_recv()
        return dkv_ref[0].astype(HIGH) + near_ref[0].astype(HIGH) + far_ref[...].astype(HIGH)


def attention_room(blocks, rows, width):
    keys = blocks * rows
    return [
        pltpu.VMEM((keys, rows), HIGH),
        pltpu.VMEM((KVH, keys, HD), LOW),
        pltpu.VMEM((KVH, keys, HD), LOW),
        pltpu.VMEM((KV_WIDTH, keys), LOW),
        pltpu.VMEM((width, rows), LOW),
        pltpu.VMEM((8, PER_GROUP * rows), HIGH),
        pltpu.VMEM((width, rows), HIGH),
    ]


def share_out(local, links, core, zero, one, target, own_at, got_at):
    if zero is one:
        keep = local.move(zero, target.at[own_at])
        send = links.push(zero, target.at[got_at], SIBLING)
        send.start()
        return keep, send
    keep = local.move(zero, target.at[own_at], False)
    keep_one = pltpu.make_async_copy(one, target.at[own_at], local.sems.at[local.used - 1])
    send = links.push(one, target.at[got_at], SIBLING)
    links.used -= 1
    links.flying.pop()
    send_zero = links.push(zero, target.at[got_at], SIBLING)

    @pl.when(core == 0)
    def _():
        keep.start()
        send.start()

    @pl.when(core == 1)
    def _():
        keep_one.start()
        send_zero.start()

    return keep, send


COPIES_MIDDLE = 6 * COPIES_SPREAD + COPIES_SHARE + 22
LOCALS_MIDDLE = 40


def layers_kernel(blocks, *refs):
    where_ref, tokens_ref, gain_one_ref, gain_two_ref, cos_ref, sin_ref = refs[:6]
    refs = refs[1:]
    late_refs, owns = refs[5:10], refs[10:13]
    out_ref, c_ref, dm_ref, gains_ref = refs[13:17]
    results = refs[17:26]
    m_any, b_any, g_any, u_any = results[5:]
    b_all, f_all, rhs_all, left_two, long_two, short_two, side_two = refs[26:33]
    room = refs[33:40]
    bias, k_sc, v_sc, kt_sc = room[:4]
    part_sc = room[6]
    vt_sc, o_sc, lse_sc, m_sc, b_sc, f_sc, c_sc, g_sc, u_sc = refs[40:49]
    mine, theirs, dq_sc, dkv_sc, dkv_near, dkv_sum, dkv_far, dkv_low = refs[49:57]
    late = refs[57:62]
    a_sc, q_ref, kv_first, kv_ref, top_sc, total_sc, h_ref = refs[62:69]
    wk, wv, wq, wo_ref, cot = late
    wg, wu, wd, load, send, receive = refs[69:]
    rows = h_ref.shape[0]
    core = lax.axis_index("head") % 2
    local = Local(load)
    links = Links(send, receive)
    lates = [local.move(source, target) for source, target in zip(late_refs, late)]
    parts = (a_sc, q_ref, kv_first, o_sc, lse_sc, m_sc, b_sc, g_sc, u_sc)
    h_ref[...] = first_forward(
        where_ref,
        tokens_ref,
        gain_one_ref,
        gain_two_ref,
        cos_ref,
        sin_ref,
        late,
        lates,
        owns,
        parts,
        results,
        (bias, k_sc, vt_sc),
        (wg, wu, wd),
        links,
        local,
    )
    waited = list(links.flying)
    share = Share(links, kv_ref)
    settle = Settle(links, dkv_sc, dkv_near, dkv_sum, dkv_far)
    spans = [pl.ds(i * rows, rows) for i in range(4)]
    everything = slice(None)

    def both(source, target, place):
        keep = local.move(source, target.at[(*place, spans[both.layer])])
        copy = links.push(source, target.at[(*place, spans[both.layer + 1])], SIBLING)
        copy.start()
        return keep, copy

    both.layer = 2
    posted = [both(b_any, b_all, (everything,))]
    both.layer = 0
    cosine, sine = cos_ref[...], sin_ref[...]
    half = blocks * rows // 2

    gain_one = wide(gain_one_ref)
    project(h_ref[...], gain_one, wq, wk, wv, cosine, sine, a_sc, q_ref, kv_ref.at[0], share.start)
    share.near.wait_recv()
    lay_keys(kv_ref, k_sc, vt_sc, range(blocks // 2), rows)
    attend_first(bias, k_sc, vt_sc, q_ref, top_sc, total_sc, part_sc, half)
    share.pass_on()
    share.forth.wait_recv()
    lay_keys(kv_ref, k_sc, vt_sc, range(blocks // 2, blocks), rows)
    attend_rest(bias, k_sc, vt_sc, q_ref, top_sc, total_sc, part_sc, half, o_sc, lse_sc)
    total, normed = after_attention(h_ref[...], o_sc, wo_ref, wide(gain_two_ref), m_sc, b_sc)
    posted.append(both(b_sc, b_all, (everything,)))
    for step in range(blocks):
        total = total + hidden_part(normed, wg, wu, wd, g_sc, u_sc, step)
    out_ref[...] = total.T.astype(LOW)
    lay_back(kv_ref, k_sc, v_sc, kt_sc, blocks, rows, True)

    lates[4].wait()
    row = lax.axis_index("head") * rows + lax.broadcasted_iota(jnp.int32, (rows, 1), 0)
    grad = jnp.where(row < where_ref[0], cot[...].astype(HIGH).T, 0.0)
    f_sc[...] = grad.T.astype(LOW)
    first_f = both(f_sc, f_all, (everything,))
    gain_two = wide(gain_two_ref)
    send_theirs = links.push(theirs, rhs_all.at[:, spans[1]], SIBLING)
    gain_part, grad_middle = ffn_back(
        grad, g_sc, u_sc, m_sc, gain_two, wg, wu, wd, mine, theirs, send_theirs.start
    )
    first_loads = [local.move(source, target) for source, target in ((g_any, g_sc), (u_any, u_sc), (m_any, m_sc))]
    keep_mine = local.move(mine, rhs_all.at[:, spans[0]])
    gains_ref[...] = jnp.zeros(gains_ref.shape, HIGH)
    gains_ref[1:2] = gain_part
    c_sc[...] = grad_middle.T.astype(LOW)
    attend_back(
        grad_middle, wo_ref, q_ref, o_sc, lse_sc, cosine, sine, dq_sc, dkv_sc, room, settle.before, settle.between
    )
    settle.near.start()
    from_query = nn(wq[...], dq_sc[...]).T
    grad_keys, grad_values = close_keys(settle.finish(), cosine, sine, dkv_low)
    low_rows, high_rows = pl.ds(0, KV_WIDTH), pl.ds(KV_WIDTH, KV_WIDTH)
    for zero, one, target in (
        (a_sc, c_sc, left_two),
        (dq_sc, o_sc, long_two),
        (dkv_low.at[low_rows], dkv_low.at[high_rows], short_two),
        (a_sc, a_sc, side_two),
    ):
        posted.append(
            share_out(local, links, core, zero, one, target, (everything, spans[0]), (everything, spans[1]))
        )
    gain_part, grad = close_rows(h_ref[...], gain_one, grad_middle, from_query, grad_keys, grad_values, wk, wv)
    gains_ref[0:1] = gain_part

    first_f[0].wait()
    first_f[1].wait_send()
    keep_mine.wait()
    send_theirs.wait_send()
    for copy in first_loads:
        copy.wait()
    f_sc[...] = grad.T.astype(LOW)
    both.layer = 2
    posted.append(both(f_sc, f_all, (everything,)))
    send_last = links.push(theirs, rhs_all.at[:, spans[3]], SIBLING)
    gain_part, grad_middle = ffn_back(
        grad, g_sc, u_sc, m_sc, gain_two, wg, wu, wd, mine, theirs, send_last.start
    )
    keep_last = local.move(mine, rhs_all.at[:, spans[2]])
    gains_ref[1:2] = gains_ref[1:2] + gain_part
    dm_ref[...] = grad_middle
    c_ref[...] = grad_middle.T.astype(LOW)
    for keep, copy in posted:
        keep.wait()
        copy.wait()
    first_f[1].wait_recv()
    send_theirs.wait_recv()
    keep_last.wait()
    send_last.wait()
    for copy in (*settle.copies, share.near, share.far, share.forth, *waited):
        copy.wait_send()


def attend_back_kernel(*refs):
    where_ref, dm_ref, wo_ref, q_ref, kv_ref, o_ref, lse_ref, cos_ref, sin_ref, dq_ref, dkv_ref = refs[:11]
    room = refs[11:]
    bias, k_sc, v_sc, kt_sc = room[:4]
    blocks, rows = kv_ref.shape[:2]
    fill_bias(where_ref, bias, rows, blocks)
    lay_back(kv_ref, k_sc, v_sc, kt_sc, blocks, rows, False)
    attend_back(
        dm_ref[...], wo_ref, q_ref, o_ref, lse_ref, cos_ref[...], sin_ref[...], dq_ref, dkv_ref, room, lambda group: None, lambda group: None
    )


def close_keys(total, cosine, sine, dkv_ref):
    starts = range(0, total.shape[0], 2 * HD)
    parts = [total[start : start + HD] for start in starts] + [total[start + HD : start + 2 * HD] for start in starts]
    total = jnp.concatenate(parts, axis=0)
    turned_keys = turned(total[:KV_WIDTH], cosine, sine, -1.0, 1.0)
    dkv_ref[:KV_WIDTH] = turned_keys.astype(LOW)
    dkv_ref[KV_WIDTH:] = total[KV_WIDTH:].astype(LOW)
    return turned_keys.T.astype(LOW), total[KV_WIDTH:].T.astype(LOW)


def close_rows(hidden, gain, grad_middle, from_query, grad_keys, grad_values, wk_ref, wv_ref):
    grad_normed = from_query + nn(grad_keys, wk_ref[...]) + nn(grad_values, wv_ref[...])
    return norm_back(hidden, gain, grad_normed, grad_middle)


def close_kernel(*refs):
    h_ref, gain_one_ref, dm_ref, dq_ref, wq_ref, wk_ref, wv_ref, cos_ref, sin_ref = refs[:9]
    own, near, far, dh_ref, dkv_ref, gain_part_ref = refs[9:]
    total = own[...].astype(HIGH) + near[...].astype(HIGH) + far[...].astype(HIGH)
    grad_keys, grad_values = close_keys(total, cos_ref[...], sin_ref[...], dkv_ref)
    hidden = h_ref[...].astype(HIGH).T
    gain = wide(gain_one_ref)
    from_query = nn(wq_ref[...], dq_ref[...]).T
    gain_part, grad_in = close_rows(hidden, gain, dm_ref[...], from_query, grad_keys, grad_values, wk_ref, wv_ref)
    gain_part_ref[...] = gain_part
    dh_ref[...] = grad_in.T


class Halving:
    def __init__(self, links, steps):
        self.steps = [(links.push(sent, got, to), kept, got) for sent, kept, got, to in steps]

    def start(self):
        self.steps[0][0].start()

    def fold(self, which):
        copy, kept, got = self.steps[which]
        copy.wait_recv()
        total = kept[...].astype(HIGH) + got[...].astype(HIGH)
        if which == len(self.steps) - 1:
            self.done(total)
        else:
            kept[...] = total.astype(kept.dtype)
            self.steps[which + 1][0].start()


class Regather(Halving):
    def share(self, links, held):
        self.held = held
        self.across = links.push(held.at[0, 0], held.at[0, 1], ACROSS)
        self.aside = links.push(held.at[0], held.at[1], SIBLING)

    def done(self, total):
        self.held[0, 0] = total.astype(LOW)
        self.across.start()

    def fold(self, which):
        if which < len(self.steps):
            Halving.fold(self, which)
        elif which == len(self.steps):
            self.across.wait_recv()
            self.aside.start()
        else:
            self.aside.wait_recv()


class Rows:
    def __init__(self, links, whole, side, got, out):
        self.steps = (
            (whole.at[:, :, 1], side, whole.at[:, :, 0], SIDE),
            (whole.at[:, 1, 0], got.at[pl.ds(0, 2)], whole.at[:, 0, 0], BEYOND),
            (whole.at[1, 0, 0], got.at[2], whole.at[0, 0, 0], FAR_SIDE),
            (whole.at[0, 0, 0], got.at[3], None, ACROSS),
            (got.at[4], got.at[5], None, SIBLING),
        )
        self.copies = [links.push(source, target, to) for source, target, _, to in self.steps]
        self.whole, self.got, self.out = whole, got, out

    def start(self):
        self.copies[0].start()

    def fold(self, which):
        self.copies[which].wait_recv()
        if which < 3:
            _, target, kept, _ = self.steps[which]
            kept[...] = kept[...] + target[...]
        elif which == 3:
            self.got[4] = self.whole[0, 0, 0] + self.got[3]
        else:
            self.out[...] = self.got[4] + self.got[5]
        if which < 4:
            self.copies[which + 1].start()


FAR_SIDE = ("dp", 4)


def halved(kind, links, whole, rooms, order):
    where = {"X": 0, "Z1": 1, "Z0": 2, "Y": 3}
    to = {"X": ACROSS, "Z1": FAR_SIDE, "Z0": BEYOND, "Y": SIDE}
    chosen = [slice(None)] * 4
    steps = []
    for axis, room in zip(order, rooms):
        sent, kept = list(chosen), list(chosen)
        sent[where[axis]], kept[where[axis]] = 1, 0
        steps.append((whole.at[tuple(sent)], whole.at[tuple(kept)], room, to[axis]))
        chosen = kept
    return kind(links, steps)


def halving_rooms(block, columns, order):
    left = [2, 2, 2, 2]
    where = {"X": 0, "Z1": 1, "Z0": 2, "Y": 3}
    rooms = []
    for axis in order:
        left[where[axis]] = 0
        rooms.append(pltpu.VMEM(tuple(n for n in left if n) + (block, columns), LOW))
    return rooms


FFN_CUTS = ((0, 256), (256, 384))
ORDERS = (
    ("Z0", "Z1", "Y", "X"),
    ("Y", "X", "Z0", "Z1"),
    ("Y", "Z0", "X", "Z1"),
    ("Y", "X", "Z0", "Z1"),
    ("Z0", "Y", "X", "Z1"),
    ("X", "Z0", "Y", "Z1"),
)
ATTN_ORDERS = (
    ("Y", "Z0", "X", "Z1"),
    ("X", "Z0", "Y", "Z1"),
    ("Z0", "X", "Y", "Z1"),
)
ATTN_CUTS = (128, 256, 256)
PLAN = (
    (("begin",), ()),
    (("w", 0, 1), ()),
    (("w", 0, 0), ()),
    (("w", 1, 1), ()),
    (("w", 1, 0), ()),
    (("w", 5, 1), ()),
    (("w", 5, 0), ()),
    (("w", 2, 1), ()),
    (("w", 2, 0), ()),
    (("w", 4, 1), ()),
    (("w", 4, 0), ()),
    (("prep",), ()),
    (("p", 0), ()),
    (("p", 1), ()),
    (("p", 2), ("f0",)),
    (("p", 3), ()),
    (("p", 4), ()),
    (("q", 0), ()),
    (("q", 1), ()),
    (("q", 2), ("f1", "f5")),
    (("q", 3), ()),
    (("q", 4), ()),
    (("kf",), ("f0", "f4")),
    (("close",), ()),
    (("w", 3, 1), ("f2",)),
    (("w", 3, 0), ()),
    (("attn",), ("f0",)),
    (("tail",), ("f1", "f5", "f0", "f4", "f2", "a1", "a2", "f4", "f3", "f2", "f1", "f4", "a0", "g0", "f2", "a2", "f5", "f1", "a1", "a2", "f3", "f5", "a1", "a0", "g0", "a2", "a0", "a1", "g0", "a2", "f3", "a0", "a2", "a1", "g0", "a0", "a1", "g0", "f3", "a0")),
)
PARTS = len(FFN_CUTS)
COPIES_FINISH = 4 * len(ORDERS) + 6 * len(ATTN_ORDERS) + 5 + 5 + 4


def finish_kernel(*refs):
    where_ref, gain_one_ref, cos_ref, sin_ref, gains_ref = refs[:5]
    late_refs, lse_any = refs[5:14], refs[14]
    a_ref, c_ref, left_two, long_two, short_two, side_two, b_any, f_any, rhs_any = refs[15:24]
    count = 4
    dh_ref, gate_out, up_out, down_out = refs[24:28]
    query_out, key_out, value_out, output_out, gain_out = refs[28:33]
    refs = refs[33:]

    def taken(count):
        nonlocal refs
        first, refs = refs[:count], refs[count:]
        return first

    room = taken(7)
    dq_ref, dkv_ref, dkv_near, dkv_sum, dkv_far, dkv_low = taken(6)
    late = taken(9)
    q_ref, kv_ref, o_ref, wo_ref, dm_ref, h_ref, wq_ref, wk_ref, wv_ref = late
    lse_ref = taken(1)[0]
    b_all, f_all, rhs, left_all, long_all, short_all, side_all = taken(7)
    wholes = taken(len(ORDERS))
    rooms = [taken(4) for _ in ORDERS]
    attn_wholes = taken(len(ATTN_ORDERS))
    attn_rooms = [taken(4) for _ in ATTN_ORDERS]
    attn_alls = taken(len(ATTN_ORDERS))
    gain_whole, gain_got, gain_side, load, send, receive = refs
    rows = h_ref.shape[1]
    block = gate_out.shape[0]
    place = lax.axis_index("dp")
    head_at = lax.axis_index("head")
    core, across = head_at % 2, head_at // 2
    links, local = Links(send, receive), Local(load)
    sums = {}
    for index, (whole, got, order) in enumerate(zip(wholes, rooms, ORDERS)):
        start, cut = FFN_CUTS[index % PARTS]
        out = (gate_out, up_out, down_out)[index // PARTS].at[:, start : start + cut]
        reduce = halved(Halving, links, whole, got, order)
        reduce.done = functools.partial(out.__setitem__, Ellipsis)
        sums["f%d" % index] = reduce
    for index, (whole, got, order) in enumerate(zip(attn_wholes, attn_rooms, ATTN_ORDERS)):
        reduce = halved(Regather, links, whole, got, order)
        reduce.share(links, attn_alls[index])
        sums["a%d" % index] = reduce
    sums["g0"] = Rows(links, gain_whole, gain_side, gain_got, gain_out)
    seen = {name: 0 for name in sums}
    plan = []
    for step, names in PLAN:
        folds = []
        for name in names:
            folds.append((name, seen[name]))
            seen[name] += 1
        plan.append((step, folds))

    def take(folds):
        for name, which in folds:
            sums[name].fold(which)

    products = [step for step, _ in plan if step[0] == "w"]

    def fetch(turn):
        _, index, half = products[turn]
        start, cut = FFN_CUTS[index % PARTS]
        source = rhs_any.at[2 * (index // PARTS) + half, :, pl.ds(start, cut)]
        return local.move(source, rhs.at[turn % 2, :, pl.ds(0, cut)])

    b_load = local.move(b_any, b_all)
    coming = {0: fetch(0)}
    f_load = local.move(f_any, f_all)
    lates = [local.move(source, target) for source, target in zip(late_refs, late)]
    lates.append(local.move(lse_any, lse_ref))
    two = ((left_two, left_all), (long_two, long_all), (short_two, short_all), (side_two, side_all))
    two_loads = [local.move(source, target.at[:, pl.ds(0, 2 * rows)]) for source, target in two]
    greet((SIBLING, ACROSS, SIDE, BEYOND, FAR_SIDE))
    b_load.wait()

    def lay(product, whole, first):
        for index in range(8):
            relative = jnp.bitwise_xor(index, place)
            whole[first, relative // 4, relative // 2 % 2, relative % 2] = product[
                index * block : (index + 1) * block
            ].astype(LOW)

    f_ready = []

    def multiply(index, half):
        turn = products.index(("w", index, half))
        coming[turn].wait()
        if turn + 1 < len(products):
            coming[turn + 1] = fetch(turn + 1)
        if index >= 2 * PARTS and not f_ready:
            f_load.wait()
            f_ready.append(True)
        cut = FFN_CUTS[index % PARTS][1]
        lay(nn((b_all if index < 2 * PARTS else f_all)[...], rhs[turn % 2, :, :cut]), wholes[index], half)
        if half == (1 if ORDERS[index][0] == "X" else 0):
            sums["f%d" % index].start()

    cosine, sine = cos_ref[...], sin_ref[...]
    settle = Settle(links, dkv_ref, dkv_near, dkv_sum, dkv_far)
    low_rows, own_at, got_at = pl.ds(0, KV_WIDTH), pl.ds(2 * rows, rows), pl.ds(3 * rows, rows)
    high_rows, everything = pl.ds(KV_WIDTH, KV_WIDTH), slice(None)
    passes = {"p": {}, "q": {}}
    for step, folds in plan:
        if step[0] in passes:
            passes[step[0]][step[1]] = folds

    def at_group(which, group):
        for when, folds in passes[which].items():
            if folds:
                pl.when(group == when)(functools.partial(take, folds))
        (settle.between if which == "q" else settle.before)(group)

    for step, folds in plan:
        if step[0] in passes:
            continue
        take(folds)
        if step[0] == "w":
            multiply(step[1], step[2])
        elif step[0] == "prep":
            for copy in lates:
                copy.wait()
            bias, k_sc, v_sc, kt_sc = room[:4]
            fill_bias(where_ref, bias, rows, count)
            lay_back(kv_ref, k_sc, v_sc, kt_sc, count, rows, False)
            attend_back(
                dm_ref[...],
                wo_ref,
                q_ref,
                o_ref,
                lse_ref,
                cosine,
                sine,
                dq_ref,
                dkv_ref,
                room,
                functools.partial(at_group, "p"),
                functools.partial(at_group, "q"),
            )
        elif step[0] == "kf":
            settle.near.start()
            from_query = nn(wq_ref[...], dq_ref[...]).T
            grad_keys, grad_values = close_keys(settle.finish(), cosine, sine, dkv_low)
            swaps = []
            for zero, one, target in (
                (a_ref, c_ref, left_all),
                (dq_ref, o_ref, long_all),
                (dkv_low.at[low_rows], dkv_low.at[high_rows], short_all),
                (a_ref, a_ref, side_all),
            ):
                swaps.append(
                    share_out(local, links, core, zero, one, target, (everything, own_at), (everything, got_at))
                )
        elif step[0] == "close":
            hidden = h_ref[...].astype(HIGH).T
            gain = wide(gain_one_ref)
            gain_part, grad_in = close_rows(
                hidden, gain, dm_ref[...], from_query, grad_keys, grad_values, wk_ref, wv_ref
            )
            dh_ref[...] = grad_in.T
            summed = gains_ref[...] + jnp.concatenate([gain_part, jnp.zeros((7, gain_part.shape[1]), HIGH)], axis=0)
            for index in range(8):
                relative = jnp.bitwise_xor(index, place)
                spot = relative // 4, relative // 2 % 2, relative % 2
                gain_whole[(*spot, slice(None), slice(0, block))] = summed[:, index * block : (index + 1) * block]
                gain_whole[(*spot, slice(None), slice(block, 128))] = jnp.zeros((8, 128 - block), HIGH)
            sums["g0"].start()
        elif step[0] == "attn":
            for copy in two_loads:
                copy.wait()
            for keep, swap_copy in swaps:
                keep.wait()
                swap_copy.wait_recv()
            long_part = nt(left_all[...], long_all[...])
            short_part = nt(side_all[...], short_all[...])
            product = jnp.concatenate([long_part, short_part], axis=1)
            start = 0
            for index, (whole, cut) in enumerate(zip(attn_wholes, ATTN_CUTS)):
                for half in range(2):
                    lay(product[:, start : start + cut], whole, jnp.bitwise_xor(half, across))
                    start += cut
                sums["a%d" % index].start()
    for kind, (long_out, short_out) in enumerate(((query_out, key_out), (output_out, value_out))):
        from_core = jnp.bitwise_xor(kind, core)
        parts = [held[from_core, jnp.bitwise_xor(half, across)] for held in attn_alls for half in range(2)]
        both = jnp.concatenate([part.astype(HIGH) for part in parts], axis=1)
        long_out[...] = both[:, : long_out.shape[1]]
        short_out[...] = both[:, long_out.shape[1] :]
    links.drain()


def emit_kernel(gains, *refs):
    refs, rows = refs[:-2], refs[-2:]
    for index, row in enumerate(rows):
        row[...] = gains[index : index + 1, : row.shape[1]]
    count = len(refs) // 2
    for source, target in zip(refs[:count], refs[count:]):
        target[...] = source[...] if source.shape == target.shape else source[...].T


def call(body, outs, specs, scratch, name, spots=0, collective=None):
    params = {"vmem_limit_bytes": LIMIT}
    if collective is not None:
        params.update(collective_id=collective, has_side_effects=True)
    return pl.pallas_call(
        body,
        out_shape=[jax.ShapeDtypeStruct(shape, kind) for shape, kind in outs],
        in_specs=specs,
        out_specs=[VMEM] * (len(outs) - spots) + [ANY] * spots,
        scratch_shapes=scratch,
        compiler_params=pltpu.CompilerParams(**params),
        name=name,
    )


def swap(value, distance):
    count = lax.axis_size("head")
    return lax.ppermute(value, "head", [(i, i ^ distance) for i in range(count)])


def scatter_rows(value, axis):
    count = lax.axis_size(axis)
    index = lax.axis_index(axis)
    value = value.reshape((count, value.shape[0] // count) + value.shape[1:])
    bit = 1
    while bit < count:
        mine = (index // bit) % 2
        value = value.reshape((value.shape[0] // 2, 2) + value.shape[1:])
        sent = lax.dynamic_index_in_dim(value, 1 - mine, 1, False)
        kept = lax.dynamic_index_in_dim(value, mine, 1, False)
        got = lax.ppermute(sent, axis, [(i, i ^ bit) for i in range(count)])
        value = kept.astype(HIGH) + got.astype(HIGH)
        bit *= 2
        if bit < count:
            value = value.astype(LOW)
    return value[0]


def shards(
    tokens,
    cotangent,
    lengths,
    attn_gain,
    w_query,
    w_key,
    w_value,
    w_output,
    ffn_gain,
    w_gate,
    w_up,
    w_down,
):
    blocks = lax.axis_size("head")
    me = lax.axis_index("head").astype(jnp.int32)
    low_bit = me % 2
    rows, width = tokens.shape
    hidden = w_gate.shape[1]
    keys = blocks * rows
    where = lengths
    frequency = 10000.0 ** (-(jnp.arange(HALF, dtype=HIGH) * 2.0 / HD))
    position = (me * rows + jnp.arange(rows, dtype=jnp.int32)).astype(HIGH)
    angles = frequency[:, None] * position[None, :]
    cosine, sine = jnp.cos(angles), jnp.sin(angles)

    feature_rows = (width, rows)
    project_outs = [(feature_rows, LOW), (feature_rows, LOW), ((blocks, rows, 2 * KV_WIDTH), LOW)]
    tokens, cotangent, w_key, w_value, w_down = (v.T for v in (tokens, cotangent, w_key, w_value, w_down))
    weight_room = [pltpu.VMEM((blocks, width, hidden), LOW)] * 3
    layer_outs = [
        (feature_rows, LOW),
        ((8, PER_GROUP * rows), HIGH),
        ((rows, width), HIGH),
        (feature_rows, LOW),
        ((blocks, rows, hidden), LOW),
        ((blocks, rows, hidden), LOW),
    ]

    attend_outs = [(feature_rows, LOW), ((blocks, 2 * KV_WIDTH, rows), LOW)]
    room = attention_room(blocks, rows, width)
    key_room = [(blocks, 2 * KV_WIDTH, rows), (2, 2 * KV_WIDTH, rows)] + [(2 * KV_WIDTH, rows)] * 3

    def layers():
        outs = [(feature_rows, LOW), (feature_rows, LOW), ((rows, width), HIGH), ((8, width), HIGH)]
        outs += project_outs + layer_outs
        outs += [((width, 4 * rows), LOW)] * 2 + [((6, 4 * rows, hidden), LOW)]
        outs += [((n, 2 * rows), LOW) for n in (width, HQ * HD, KV_WIDTH, width)]
        statistics = pltpu.VMEM((8, PER_GROUP * rows), HIGH)
        scratch = room + [pltpu.VMEM((KV_WIDTH, keys), LOW), pltpu.VMEM(feature_rows, LOW)]
        scratch += [statistics, pltpu.VMEM((rows, width), HIGH)]
        scratch += [pltpu.VMEM(feature_rows, LOW)] * 3 + [pltpu.VMEM((blocks, rows, hidden), LOW)] * 2
        scratch += [pltpu.VMEM((6, rows, hidden), LOW)] * 2 + [pltpu.VMEM(feature_rows, LOW)]
        scratch += [pltpu.VMEM(shape, LOW) for shape in key_room]
        late = (w_key, w_value, w_query, w_output, cotangent)
        scratch += [pltpu.VMEM(v.shape, LOW) for v in late]
        kv_shape = (blocks, rows, 2 * KV_WIDTH)
        scratch += [pltpu.VMEM(shape, LOW) for shape in (feature_rows, feature_rows, kv_shape, kv_shape)]
        scratch += [statistics, statistics, pltpu.VMEM((rows, width), HIGH)]
        scratch += weight_room + [pltpu.SemaphoreType.DMA((LOCALS_MIDDLE,))]
        scratch += [pltpu.SemaphoreType.DMA((COPIES_MIDDLE,)), pltpu.SemaphoreType.DMA((COPIES_MIDDLE,))]
        given = [where, tokens, attn_gain, ffn_gain, cosine, sine, *late, w_gate, w_up, w_down]
        specs = [SMEM] + [VMEM] * 5 + [ANY] * 8
        return call(functools.partial(layers_kernel, blocks), outs, specs, scratch, "layers", 16, 3)(*given)

    outs = layers()
    block_out, c_one, dm_one, gains, a_one, q_one, kv_one, o_one, lse_one = outs[:9]
    b_all, f_all, rhs_all, *halves_two = outs[13:]

    def close(h, grad_middle, grad_query, partial):
        sent = swap(jnp.stack([partial[1], partial[3]]), 1)
        far = swap((partial[2].astype(HIGH) + sent[1].astype(HIGH)).astype(LOW), 2)
        outs = [(feature_rows, HIGH), ((2 * KV_WIDTH, rows), LOW), ((1, width), HIGH)]
        given = [h, attn_gain, grad_middle, grad_query, w_query, w_key, w_value, cosine, sine]
        given += [partial[0], sent[0], far]
        return call(close_kernel, outs, [VMEM] * 12, [], "close")(*given)

    def beside(parts):
        return jnp.concatenate(parts, axis=-1)

    def choose(zero, one):
        return jnp.where(low_bit == 0, zero, one)

    def halves(a, c, o, dq, dkv):
        dk, dv = dkv[:KV_WIDTH], dkv[KV_WIDTH:]
        left = [choose(a, c), swap(choose(c, a), 1)]
        long = [choose(dq, o), swap(choose(o, dq), 1)]
        short = [choose(dk, dv), swap(choose(dv, dk), 1)]
        return beside(left), beside(long), beside(short), beside([a, swap(a, 1)])

    places = lax.axis_size("dp")
    block = width // places

    def finish():
        outs = [(feature_rows, HIGH)] + [((block, hidden), HIGH)] * 3
        outs += [((block, n), HIGH) for n in (HQ * HD, KV_WIDTH, KV_WIDTH, HQ * HD)] + [((8, 128), HIGH)]
        late = (q_one, kv_one, o_one, w_output, dm_one, tokens, w_query, w_key, w_value)
        scratch = room + [pltpu.VMEM(shape, LOW) for shape in [feature_rows] + key_room]
        scratch += [pltpu.VMEM(v.shape, v.dtype) for v in late] + [pltpu.VMEM(lse_one.shape, HIGH)]
        low_room = []
        low_room += [(width, 4 * rows), (width, 4 * rows), (2, 4 * rows, max(n for _, n in FFN_CUTS))]
        low_room += [(width, 4 * rows), (width, 4 * rows), (KV_WIDTH, 4 * rows), (width, 4 * rows)]
        low_room += [(2, 2, 2, 2, block, FFN_CUTS[i % PARTS][1]) for i in range(len(ORDERS))]
        scratch += [pltpu.VMEM(shape, LOW) for shape in low_room]
        for index, order in enumerate(ORDERS):
            scratch += halving_rooms(block, FFN_CUTS[index % PARTS][1], order)
        scratch += [pltpu.VMEM((2, 2, 2, 2, block, cut), LOW) for cut in ATTN_CUTS]
        for order, cut in zip(ATTN_ORDERS, ATTN_CUTS):
            scratch += halving_rooms(block, cut, order)
        scratch += [pltpu.VMEM((2, 2, block, cut), LOW) for cut in ATTN_CUTS]
        scratch += [pltpu.VMEM(shape, HIGH) for shape in ((2, 2, 2, 8, 128), (8, 8, 128), (2, 2, 8, 128))]
        scratch += [pltpu.SemaphoreType.DMA((48,)), pltpu.SemaphoreType.DMA((COPIES_FINISH,))]
        scratch += [pltpu.SemaphoreType.DMA((COPIES_FINISH,))]
        given = [where, attn_gain, cosine, sine, gains, *late, lse_one, a_one, c_one, *halves_two]
        specs = [SMEM] + [VMEM] * 4 + [ANY] * 19
        return call(finish_kernel, outs, specs, scratch, "finish", 0, 2)(*given, b_all, f_all, rhs_all)

    if places == 8 and blocks == 4:
        outs = finish()
        input_grad, gate_grad, up_grad, down_grad, query_grad, key_grad, value_grad, output_grad, gains = outs
        results = [block_out, input_grad, query_grad, key_grad, value_grad, output_grad, gate_grad, up_grad, down_grad]
        turned_over = (3, 4, 5)
        outs = [(v.shape[::-1] if i in turned_over else v.shape, v.dtype) for i, v in enumerate(results)]
        outs += [((1, block), HIGH)] * 2
        *results, one, two = call(emit_kernel, outs, [VMEM] * (len(results) + 1), [], "emit")(gains, *results)
        gains = one[0], two[0]
        block_out, input_grad, query_grad, key_grad, value_grad, output_grad, gate_grad, up_grad, down_grad = results
        key_grad, value_grad, output_grad = key_grad.T, value_grad.T, output_grad.T
    else:
        given = [where, dm_one, w_output, q_one, kv_one, o_one, lse_one, cosine, sine]
        dq_one, part_one = call(attend_back_kernel, attend_outs, [SMEM] + [VMEM] * 8, room, "attend_back")(*given)
        input_grad, dkv_one, gain_one_a = close(tokens, dm_one, dq_one, part_one)
        kept, sent = [], []
        for which in range(6):
            product = nn(b_all if which < 4 else f_all, rhs_all[which]).astype(LOW)
            (sent if which % 2 else kept).append(product)
        got = swap(beside(sent), 2)
        ffn = scatter_rows((beside(kept).astype(HIGH) + got.astype(HIGH)).astype(LOW), "dp")
        halves_one = halves(a_one, c_one, o_one, dq_one, dkv_one)
        left, long, short, side = (beside(pair) for pair in zip(halves_two, halves_one))
        attn = scatter_rows(beside([nt(left, long), nt(side, short)]).astype(LOW), "dp").astype(LOW)
        attn = (attn.astype(HIGH) + swap(attn, 2).astype(HIGH)).astype(LOW)
        other = swap(attn, 1)
        zero, one = choose(attn, other).astype(HIGH), choose(other, attn).astype(HIGH)
        gains = jnp.concatenate([gains[:1] + gain_one_a, gains[1:2]], axis=0)
        gains = lax.psum_scatter(lax.psum(gains, "head"), "dp", scatter_dimension=1, tiled=True)
        query_grad, key_grad = zero[:, : HQ * HD], zero[:, HQ * HD :]
        output_grad, value_grad = one[:, : HQ * HD], one[:, HQ * HD :]
        gate_grad, up_grad, down_grad = (ffn[:, i * hidden : (i + 1) * hidden] for i in range(3))
    return (
        block_out.T,
        input_grad.T,
        gains[0],
        query_grad,
        key_grad,
        value_grad,
        output_grad.T,
        gains[1],
        gate_grad,
        up_grad,
        down_grad.T,
    )


def solution(mesh):
    return jax.shard_map(
        shards,
        mesh=mesh,
        in_specs=(
            P(("dp", "head"), None),
            P(("dp", "head"), None),
            P("dp"),
            P(),
            P(),
            P(),
            P(),
            P(),
            P(),
            P(None, "head"),
            P(None, "head"),
            P("head", None),
        ),
        out_specs=(
            P(("dp", "head"), None),
            P(("dp", "head"), None),
            P("dp"),
            P("dp", None),
            P("dp", None),
            P("dp", None),
            P(None, "dp"),
            P("dp"),
            P("dp", "head"),
            P("dp", "head"),
            P("head", "dp"),
        ),
        check_vma=False,
    )
```

```python
import functools

import jax
import jax.numpy as jnp
from jax import lax
from jax.experimental import pallas as pl
from jax.experimental.pallas import tpu as pltpu
from jax.sharding import PartitionSpec as P

HQ = 15
KVH = 5
HD = 64
HALF = HD // 2
PER_GROUP = HQ // KVH
KV_WIDTH = KVH * HD
EPSILON = 1e-05
SCALE = HD ** (-0.5)
BLOCKED = -1e30
LOW = jnp.bfloat16
HIGH = jnp.float32
VMEM = pl.BlockSpec(memory_space=pltpu.VMEM)
SMEM = pl.BlockSpec(memory_space=pltpu.SMEM)
ANY = pl.BlockSpec(memory_space=pl.ANY)
LIMIT = 60 * 2**20
MESH = pl.DeviceIdType.MESH


def nn(left, right):
    return lax.dot_general(left, right, (((1,), (0,)), ((), ())), preferred_element_type=HIGH)


def nt(left, right):
    return lax.dot_general(left, right, (((1,), (1,)), ((), ())), preferred_element_type=HIGH)


def sigmoid(value):
    return 0.5 * (1.0 + jnp.tanh(0.5 * value))


def wide(gain_ref):
    return gain_ref[...].astype(HIGH).reshape(1, gain_ref.shape[0])


def inverse_rms(rows):
    return lax.rsqrt(jnp.mean(rows * rows, axis=1, keepdims=True) + EPSILON)


def norm_back(values_in, gain, grad_normed, grad_skip):
    inverse = inverse_rms(values_in)
    normal = values_in * inverse
    gain_part = jnp.sum(grad_normed * normal, axis=0, keepdims=True)
    scaled = grad_normed * gain
    back = grad_skip + inverse * (scaled - normal * jnp.mean(scaled * normal, axis=1, keepdims=True))
    return gain_part, back


def turned(columns, cosine, sine, sign, factor):
    parts = []
    for start in range(0, columns.shape[0], HD):
        first = columns[start : start + HALF] * factor
        second = columns[start + HALF : start + HD] * factor
        parts.append(first * cosine - sign * second * sine)
        parts.append(second * cosine + sign * first * sine)
    return jnp.concatenate(parts, axis=0)


def project(hidden, gain, w_query, w_key, w_value, cosine, sine, a_ref, q_ref, kv_ref, ready):
    normed = hidden * inverse_rms(hidden) * gain
    low = normed.astype(LOW)
    keys = turned(nt(w_key[...], low), cosine, sine, 1.0, 1.0)
    kv_ref[:, :KV_WIDTH] = keys.T.astype(LOW)
    kv_ref[:, KV_WIDTH:] = nt(low, w_value[...]).astype(LOW)
    ready()
    queries = nn(low, w_query[...]).T
    q_ref[...] = turned(queries, cosine, sine, 1.0, SCALE).astype(LOW)
    a_ref[...] = normed.T.astype(LOW)


def fill_bias(where_ref, bias, rows, blocks):
    me = lax.axis_index("head")
    length = where_ref[0]
    key = lax.broadcasted_iota(jnp.int32, (rows, rows), 0)
    query = lax.broadcasted_iota(jnp.int32, (rows, rows), 1)
    for step in range(blocks):
        other = jnp.bitwise_xor(me, step)
        allowed = other * rows + key < length
        if step == 0:
            allowed &= key <= query
        else:
            allowed &= other < me
        bias[step * rows : (step + 1) * rows] = jnp.where(allowed, 0.0, BLOCKED)


def side_by_side(ref, group):
    first = group * PER_GROUP
    heads = [ref[pl.ds(pl.multiple_of((first + i) * HD, HD), HD), :] for i in range(PER_GROUP)]
    return jnp.concatenate(heads, axis=1)


def one_below_other(ref, group, value):
    rows = value.shape[1] // PER_GROUP
    for member in range(PER_GROUP):
        at = pl.ds(pl.multiple_of((group * PER_GROUP + member) * HD, HD), HD)
        ref[at, :] = value[:, member * rows : (member + 1) * rows].astype(ref.dtype)


def scored(keys, queries, bias):
    return nn(keys, queries) + jnp.concatenate([bias] * PER_GROUP, axis=1)


def attend(bias, k_sc, vt_sc, q_ref, o_ref, lse_ref, event):
    def group_body(group, carry):
        keys = k_sc[group]
        values = vt_sc[pl.ds(pl.multiple_of(group * HD, HD), HD), :]
        event(group)
        scores = scored(keys, side_by_side(q_ref, group), bias[...])
        top = jnp.max(scores, axis=0, keepdims=True)
        exponent = jnp.exp(scores - top)
        total = jnp.sum(exponent, axis=0, keepdims=True)
        one_below_other(o_ref, group, nn(values, exponent.astype(LOW)) * (1.0 / total))
        lse_ref[pl.ds(group, 1), :] = top + jnp.log(total)
        return carry

    lax.fori_loop(0, KVH, group_body, 0)


def attend_first(bias, k_sc, vt_sc, q_ref, top_ref, total_ref, part_ref, half):
    def group_body(group, carry):
        keys = k_sc[group, :half]
        values = vt_sc[pl.ds(pl.multiple_of(group * HD, HD), HD), :half]
        scores = scored(keys, side_by_side(q_ref, group), bias[:half])
        top = jnp.max(scores, axis=0, keepdims=True)
        exponent = jnp.exp(scores - top)
        top_ref[pl.ds(group, 1), :] = top
        total_ref[pl.ds(group, 1), :] = jnp.sum(exponent, axis=0, keepdims=True)
        one_below_other(part_ref, group, nn(values, exponent.astype(LOW)))
        return carry

    lax.fori_loop(0, KVH, group_body, 0)


def attend_rest(bias, k_sc, vt_sc, q_ref, top_ref, total_ref, part_ref, half, o_ref, lse_ref):
    def group_body(group, carry):
        keys = k_sc[group, half:]
        values = vt_sc[pl.ds(pl.multiple_of(group * HD, HD), HD), half:]
        scores = scored(keys, side_by_side(q_ref, group), bias[half:])
        before = top_ref[pl.ds(group, 1), :]
        top = jnp.maximum(before, jnp.max(scores, axis=0, keepdims=True))
        exponent = jnp.exp(scores - top)
        rescale = jnp.exp(before - top)
        total = total_ref[pl.ds(group, 1), :] * rescale + jnp.sum(exponent, axis=0, keepdims=True)
        attended = side_by_side(part_ref, group) * rescale + nn(values, exponent.astype(LOW))
        one_below_other(o_ref, group, attended * (1.0 / total))
        lse_ref[pl.ds(group, 1), :] = top + jnp.log(total)
        return carry

    lax.fori_loop(0, KVH, group_body, 0)


def lay_keys(kv_ref, k_sc, vt_sc, steps, rows):
    for step in steps:
        at = slice(step * rows, (step + 1) * rows)
        for group in range(KVH):
            k_sc[group, at] = kv_ref[step, :, group * HD : (group + 1) * HD]
        vt_sc[:, at] = kv_ref[step, :, KV_WIDTH:].T


def after_attention(hidden, o_ref, wo_ref, gain, m_ref, b_ref):
    middle = hidden + nn(o_ref[...].T, wo_ref[...])
    m_ref[...] = middle
    normed = middle * inverse_rms(middle) * gain
    b_ref[...] = normed.T.astype(LOW)
    return middle, normed.astype(LOW)


def active_part(normed, wg, wu, g_ref, u_ref, step):
    gate = nn(normed, wg[step])
    up = nn(normed, wu[step])
    g_ref[step] = gate.astype(LOW)
    u_ref[step] = up.astype(LOW)
    return (gate * sigmoid(gate) * up).astype(LOW)


def hidden_part(normed, wg, wu, wd, g_ref, u_ref, step):
    return nt(active_part(normed, wg, wu, g_ref, u_ref, step), wd[step])


def partner(axis, distance):
    return {axis: jnp.bitwise_xor(lax.axis_index(axis), distance)}


def hail(partners):
    for axis, distance in partners:
        pl.semaphore_signal(
            pltpu.get_barrier_semaphore(), inc=1, device_id=partner(axis, distance), device_id_type=MESH
        )


def greet(partners):
    pl.semaphore_wait(pltpu.get_barrier_semaphore(), len(partners))


class Links:
    def __init__(self, send, receive):
        self.send, self.receive, self.used = send, receive, 0
        self.flying = []

    def push(self, source, target, to):
        copy = pltpu.make_async_remote_copy(
            src_ref=source,
            dst_ref=target,
            send_sem=self.send.at[self.used],
            recv_sem=self.receive.at[self.used],
            device_id=partner(*to),
            device_id_type=MESH,
        )
        self.used += 1
        self.flying.append(copy)
        return copy

    def drain(self):
        for copy in self.flying:
            copy.wait_send()


class Local:
    def __init__(self, sems):
        self.sems, self.used, self.flying = sems, 0, []

    def move(self, source, target, start=True):
        copy = pltpu.make_async_copy(source, target, self.sems.at[self.used])
        self.used += 1
        self.flying.append(copy)
        if start:
            copy.start()
        return copy

    def drain(self):
        for copy in self.flying:
            copy.wait()


SIBLING, ACROSS, SIDE, BEYOND = ("head", 1), ("head", 2), ("dp", 1), ("dp", 2)


class Share:
    def __init__(self, links, kv_ref):
        self.near = links.push(kv_ref.at[0], kv_ref.at[1], SIBLING)
        self.far = links.push(kv_ref.at[0], kv_ref.at[2], ACROSS)
        self.forth = links.push(kv_ref.at[2], kv_ref.at[3], SIBLING)

    def start(self):
        self.far.start()
        self.near.start()

    def pass_on(self):
        self.far.wait_recv()
        self.forth.start()

    def finish(self):
        self.near.wait_recv()
        self.forth.wait_recv()


class Spread:
    def __init__(self, links, own, all_ref, start, count):
        quarter = count // 4
        cut = quarter // 32 * 16
        place = lax.axis_index("dp") % 4

        def rows(which, first=0, size=quarter):
            at = start + jnp.bitwise_xor(place, which) * quarter + first
            return pl.ds(pl.multiple_of(at, 16), size)

        def move(which, to, *piece):
            ref = all_ref.at[2, rows(which, *piece)]
            return links.push(ref, ref, to)

        def aside(which):
            return links.push(all_ref.at[2, rows(which)], all_ref.at[3, rows(which)], SIBLING)

        span = pl.ds(start, count)
        self.near = links.push(own.at[span], all_ref.at[1, span], SIBLING)
        self.cross = links.push(own.at[rows(0)], all_ref.at[2, rows(0)], ACROSS)
        self.side, self.beyond = move(0, SIDE), move(0, BEYOND)
        self.side_half = move(2, SIDE, cut, quarter - cut)
        self.beyond_half = move(1, BEYOND, 0, cut)
        self.asides = [aside(which) for which in range(4)]

    def first(self):
        self.cross.wait_recv()
        self.side.start()
        self.beyond.start()
        self.asides[0].start()

    def second(self):
        self.side.wait_recv()
        self.beyond_half.start()
        self.asides[1].start()
        self.beyond.wait_recv()
        self.side_half.start()
        self.asides[2].start()

    def third(self):
        self.side_half.wait_recv()
        self.beyond_half.wait_recv()
        self.asides[3].start()

    def last(self):
        for copy in self.asides:
            copy.wait_recv()


COPIES_SHARE = 3
COPIES_SPREAD = 10


def first_forward(where_ref, h_ref, gain_one_ref, gain_two_ref, cos_ref, sin_ref, late, lates, owns, parts, results, attn, held, links, local):
    a_ref, q_ref, kv_ref, o_ref, lse_ref, m_ref, b_ref, g_ref, u_ref = parts
    bias, k_sc, vt_sc = attn
    wk_ref, wv_ref, wq_ref, wo_ref, _ = late
    wg, wu, wd = held
    blocks, rows = wg.shape[0], h_ref.shape[1]
    loads = [local.move(own, all_ref.at[0], False) for own, all_ref in zip(owns, held)]
    whole = owns[0].shape[0]
    middle_row = (whole // 128 + 1) * 64
    cuts = ((0, middle_row), (middle_row, whole - middle_row))
    spreads = [[Spread(links, own, all_ref, *cut) for cut in cuts] for own, all_ref in zip(owns, held)]
    (g1, g2), (u1, u2), (d1, d2) = spreads
    share = Share(links, kv_ref)
    greet((SIBLING, ACROSS, SIDE, BEYOND))
    for piece in (g1, g2):
        piece.cross.start()
    for pair, copy in zip(spreads, loads):
        for piece in pair:
            piece.near.start()
        copy.start()
    hidden = h_ref[...].astype(HIGH).T

    def queue():
        share.start()
        for piece in (u1, u2, d1, d2):
            piece.cross.start()
        lates[2].wait()

    lates[0].wait()
    lates[1].wait()
    gain_one = wide(gain_one_ref)
    project(hidden, gain_one, wq_ref, wk_ref, wv_ref, cos_ref[...], sin_ref[...], a_ref, q_ref, kv_ref.at[0], queue)
    g1.first()
    g2.first()
    fill_bias(where_ref, bias, rows, blocks)
    g1.second()
    g2.second()
    share.pass_on()
    g1.third()
    share.finish()
    lay_keys(kv_ref, k_sc, vt_sc, range(blocks), rows)
    events = ((g2.third, u1.first), (), (u2.first,), (u1.second,), (d1.first, u2.second))

    def event(group):
        for when, actions in enumerate(events):

            @pl.when(group == when)
            def _():
                for action in actions:
                    action()

    attend(bias, k_sc, vt_sc, q_ref, o_ref, lse_ref, event)
    d2.first()
    u1.third()
    lates[3].wait()
    middle, normed = after_attention(hidden, o_ref, wo_ref, wide(gain_two_ref), m_ref, b_ref)
    early = [local.move(source, target) for source, target in zip(parts[:7], results[:7])]
    u2.third()
    for copy in loads:
        copy.wait()
    active = [active_part(normed, wg, wu, g_ref, u_ref, 0)]
    d1.second()
    for pair in spreads:
        for piece in pair:
            piece.near.wait_recv()
    active.append(active_part(normed, wg, wu, g_ref, u_ref, 1))
    d2.second()
    d1.third()
    for step in range(2, 4):
        active.append(active_part(normed, wg, wu, g_ref, u_ref, step))
        if step == 2:
            for piece in (g1, g2, u1, u2):
                piece.last()
    early += [local.move(source, target) for source, target in zip(parts[7:], results[7:])]
    total = middle
    for step in range(blocks):
        if step == 2:
            d2.third()
        if step == 3:
            d1.last()
            d2.last()
        total = total + nt(active[step], wd[step])
    for copy in early:
        copy.wait()
    return total


def ffn_back(grad, g_ref, u_ref, m_ref, gain, wg, wu, wd, mine_ref, theirs_ref, ready):
    low_grad = grad.astype(LOW)
    grad_normed = jnp.zeros(m_ref.shape, HIGH)
    order, products = (1, 3, 0, 2), []
    coming = nn(low_grad, wd[order[0]])
    for turn, step in enumerate(order):
        grad_active = coming
        if turn < 3:
            coming = nn(low_grad, wd[order[turn + 1]])
        gate = g_ref[step].astype(HIGH)
        up = u_ref[step].astype(HIGH)
        sig = sigmoid(gate)
        silu = gate * sig
        grad_gate = (grad_active * up * sig * (1.0 + gate * (1.0 - sig))).astype(LOW)
        grad_up = (grad_active * silu).astype(LOW)
        kept = mine_ref if step % 2 == 0 else theirs_ref
        kept[step // 2] = grad_gate
        kept[2 + step // 2] = grad_up
        kept[4 + step // 2] = (silu * up).astype(LOW)
        if step == 3:
            ready()
        products.append((step, grad_gate, grad_up))
        if turn:
            before, one, two = products[turn - 1]
            grad_normed = grad_normed + nt(one, wg[before]) + nt(two, wu[before])
    before, one, two = products[-1]
    grad_normed = grad_normed + nt(one, wg[before]) + nt(two, wu[before])
    return norm_back(m_ref[...], gain, grad_normed, grad)


def lay_back(kv_ref, k_sc, v_sc, kt_sc, blocks, rows, keys_laid):
    for step in range(blocks):
        at = slice(step * rows, (step + 1) * rows)
        for group in range(KVH):
            if not keys_laid:
                k_sc[group, at] = kv_ref[step, :, group * HD : (group + 1) * HD]
            v_sc[group, at] = kv_ref[step, :, KV_WIDTH + group * HD : KV_WIDTH + (group + 1) * HD]
        kt_sc[:, at] = kv_ref[step, :, :KV_WIDTH].T


def attend_back(grad_middle, wo_ref, q_ref, o_ref, lse_ref, cosine, sine, dq_ref, dkv_ref, room, before, between):
    bias, k_sc, v_sc, kt_sc, do_sc, delta, dq_sc = room
    keys, rows = bias.shape
    blocks = keys // rows
    half = keys // 2
    do_sc[...] = nt(wo_ref[...], grad_middle.astype(LOW)).astype(LOW)
    for head in range(HQ):
        at = slice(head * HD, (head + 1) * HD)
        product = do_sc[at].astype(HIGH) * o_ref[at].astype(HIGH)
        group, member = divmod(head, PER_GROUP)
        spot = slice(member * rows, (member + 1) * rows)
        delta[group : group + 1, spot] = jnp.sum(product, axis=0, keepdims=True)
    cosines, sines = (jnp.concatenate([table] * PER_GROUP, axis=1) for table in (cosine, sine))

    def one_pass(start, last, event):
        cut = slice(start, start + half)

        def group_body(group, carry):
            event(group)
            group_keys = k_sc[group, cut]
            values = v_sc[group, cut]
            at = pl.ds(pl.multiple_of(group * HD, HD), HD)
            key_rows = pl.ds(pl.multiple_of(group * 2 * HD, HD), HD)
            value_rows = pl.ds(pl.multiple_of(group * 2 * HD + HD, HD), HD)
            keys_t = kt_sc[at, cut]
            query, grad_out = side_by_side(q_ref, group), side_by_side(do_sc, group)
            scores = scored(group_keys, query, bias[cut])
            prob = jnp.exp(scores - lse_ref[pl.ds(group, 1), :])
            grad_prob = nn(values, grad_out)
            grad_score = (prob * (grad_prob - delta[pl.ds(group, 1), :])).astype(LOW)
            grad_query = nn(keys_t, grad_score)
            if last:
                grad_query = grad_query + side_by_side(dq_sc, group)
                one_below_other(dq_ref, group, turned(grad_query, cosines, sines, -1.0, SCALE))
            else:
                one_below_other(dq_sc, group, grad_query)
            grad_keys = nt(query, grad_score)
            grad_values = nt(grad_out, prob.astype(LOW))
            for step in range(blocks // 2):
                part = slice(step * rows, (step + 1) * rows)
                dkv_ref[start // rows + step, key_rows, :] = grad_keys[:, part].astype(LOW)
                dkv_ref[start // rows + step, value_rows, :] = grad_values[:, part].astype(LOW)
            return carry

        lax.fori_loop(0, KVH, group_body, 0)

    one_pass(half, False, before)
    one_pass(0, True, between)


class Settle:
    def __init__(self, links, dkv_ref, near_ref, sum_ref, far_ref):
        self.refs = dkv_ref, near_ref, sum_ref, far_ref
        cut = 3 * 2 * HD
        self.spans = [pl.ds(0, cut), pl.ds(cut, dkv_ref.shape[1] - cut)]
        self.asides = [links.push(dkv_ref.at[3, span], near_ref.at[1, span], SIBLING) for span in self.spans]
        self.near = links.push(dkv_ref.at[1], near_ref.at[0], SIBLING)
        self.fars = [links.push(sum_ref.at[span], far_ref.at[span], ACROSS) for span in self.spans]
        self.copies = [*self.asides, self.near, *self.fars]

    def across(self, which):
        dkv_ref, near_ref, sum_ref, _ = self.refs
        span = self.spans[which]
        self.asides[which].wait_recv()
        sum_ref[span] = (dkv_ref[2, span].astype(HIGH) + near_ref[1, span].astype(HIGH)).astype(LOW)
        self.fars[which].start()

    def before(self, group):
        pl.when(group == 3)(self.asides[0].start)
        pl.when(group == 4)(functools.partial(self.across, 0))

    def between(self, group):
        pl.when(group == 0)(self.asides[1].start)
        pl.when(group == 1)(functools.partial(self.across, 1))

    def finish(self):
        dkv_ref, near_ref, _, far_ref = self.refs
        self.near.wait_recv()
        for copy in self.fars:
            copy.wait_recv()
        return dkv_ref[0].astype(HIGH) + near_ref[0].astype(HIGH) + far_ref[...].astype(HIGH)


def attention_room(blocks, rows, width):
    keys = blocks * rows
    return [
        pltpu.VMEM((keys, rows), HIGH),
        pltpu.VMEM((KVH, keys, HD), LOW),
        pltpu.VMEM((KVH, keys, HD), LOW),
        pltpu.VMEM((KV_WIDTH, keys), LOW),
        pltpu.VMEM((width, rows), LOW),
        pltpu.VMEM((8, PER_GROUP * rows), HIGH),
        pltpu.VMEM((width, rows), HIGH),
    ]


def share_out(local, links, core, zero, one, target, own_at, got_at):
    if zero is one:
        keep = local.move(zero, target.at[own_at])
        send = links.push(zero, target.at[got_at], SIBLING)
        send.start()
        return keep, send
    keep = local.move(zero, target.at[own_at], False)
    keep_one = pltpu.make_async_copy(one, target.at[own_at], local.sems.at[local.used - 1])
    send = links.push(one, target.at[got_at], SIBLING)
    links.used -= 1
    links.flying.pop()
    send_zero = links.push(zero, target.at[got_at], SIBLING)

    @pl.when(core == 0)
    def _():
        keep.start()
        send.start()

    @pl.when(core == 1)
    def _():
        keep_one.start()
        send_zero.start()

    return keep, send


COPIES_MIDDLE = 6 * COPIES_SPREAD + COPIES_SHARE + 22
LOCALS_MIDDLE = 40


def layers_kernel(blocks, *refs):
    where_ref, tokens_ref, gain_one_ref, gain_two_ref, cos_ref, sin_ref = refs[:6]
    refs = refs[1:]
    late_refs, owns = refs[5:10], refs[10:13]
    out_ref, c_ref, dm_ref, gains_ref = refs[13:17]
    results = refs[17:26]
    m_any, b_any, g_any, u_any = results[5:]
    b_all, f_all, rhs_all, left_two, long_two, short_two, side_two = refs[26:33]
    room = refs[33:40]
    bias, k_sc, v_sc, kt_sc = room[:4]
    part_sc = room[6]
    vt_sc, o_sc, lse_sc, m_sc, b_sc, f_sc, c_sc, g_sc, u_sc = refs[40:49]
    mine, theirs, dq_sc, dkv_sc, dkv_near, dkv_sum, dkv_far, dkv_low = refs[49:57]
    late = refs[57:62]
    a_sc, q_ref, kv_first, kv_ref, top_sc, total_sc, h_ref = refs[62:69]
    wk, wv, wq, wo_ref, cot = late
    wg, wu, wd, load, send, receive = refs[69:]
    rows = h_ref.shape[0]
    core = lax.axis_index("head") % 2
    hail((SIBLING, ACROSS, SIDE, BEYOND))
    local = Local(load)
    links = Links(send, receive)
    lates = [local.move(source, target) for source, target in zip(late_refs, late)]
    parts = (a_sc, q_ref, kv_first, o_sc, lse_sc, m_sc, b_sc, g_sc, u_sc)
    h_ref[...] = first_forward(
        where_ref,
        tokens_ref,
        gain_one_ref,
        gain_two_ref,
        cos_ref,
        sin_ref,
        late,
        lates,
        owns,
        parts,
        results,
        (bias, k_sc, vt_sc),
        (wg, wu, wd),
        links,
        local,
    )
    waited = list(links.flying)
    share = Share(links, kv_ref)
    settle = Settle(links, dkv_sc, dkv_near, dkv_sum, dkv_far)
    spans = [pl.ds(i * rows, rows) for i in range(4)]
    everything = slice(None)

    def both(source, target, place):
        keep = local.move(source, target.at[(*place, spans[both.layer])])
        copy = links.push(source, target.at[(*place, spans[both.layer + 1])], SIBLING)
        copy.start()
        return keep, copy

    both.layer = 2
    posted = [both(b_any, b_all, (everything,))]
    both.layer = 0
    cosine, sine = cos_ref[...], sin_ref[...]
    half = blocks * rows // 2

    gain_one = wide(gain_one_ref)
    project(h_ref[...], gain_one, wq, wk, wv, cosine, sine, a_sc, q_ref, kv_ref.at[0], share.start)
    share.near.wait_recv()
    lay_keys(kv_ref, k_sc, vt_sc, range(blocks // 2), rows)
    attend_first(bias, k_sc, vt_sc, q_ref, top_sc, total_sc, part_sc, half)
    share.pass_on()
    share.forth.wait_recv()
    lay_keys(kv_ref, k_sc, vt_sc, range(blocks // 2, blocks), rows)
    attend_rest(bias, k_sc, vt_sc, q_ref, top_sc, total_sc, part_sc, half, o_sc, lse_sc)
    total, normed = after_attention(h_ref[...], o_sc, wo_ref, wide(gain_two_ref), m_sc, b_sc)
    posted.append(both(b_sc, b_all, (everything,)))
    for step in range(blocks):
        total = total + hidden_part(normed, wg, wu, wd, g_sc, u_sc, step)
    out_ref[...] = total.T.astype(LOW)
    lay_back(kv_ref, k_sc, v_sc, kt_sc, blocks, rows, True)

    lates[4].wait()
    row = lax.axis_index("head") * rows + lax.broadcasted_iota(jnp.int32, (rows, 1), 0)
    grad = jnp.where(row < where_ref[0], cot[...].astype(HIGH).T, 0.0)
    f_sc[...] = grad.T.astype(LOW)
    first_f = both(f_sc, f_all, (everything,))
    gain_two = wide(gain_two_ref)
    send_theirs = links.push(theirs, rhs_all.at[:, spans[1]], SIBLING)
    gain_part, grad_middle = ffn_back(
        grad, g_sc, u_sc, m_sc, gain_two, wg, wu, wd, mine, theirs, send_theirs.start
    )
    first_loads = [local.move(source, target) for source, target in ((g_any, g_sc), (u_any, u_sc), (m_any, m_sc))]
    keep_mine = local.move(mine, rhs_all.at[:, spans[0]])
    gains_ref[...] = jnp.zeros(gains_ref.shape, HIGH)
    gains_ref[1:2] = gain_part
    c_sc[...] = grad_middle.T.astype(LOW)
    attend_back(
        grad_middle, wo_ref, q_ref, o_sc, lse_sc, cosine, sine, dq_sc, dkv_sc, room, settle.before, settle.between
    )
    settle.near.start()
    from_query = nn(wq[...], dq_sc[...]).T
    grad_keys, grad_values = close_keys(settle.finish(), cosine, sine, dkv_low)
    low_rows, high_rows = pl.ds(0, KV_WIDTH), pl.ds(KV_WIDTH, KV_WIDTH)
    for zero, one, target in (
        (a_sc, c_sc, left_two),
        (dq_sc, o_sc, long_two),
        (dkv_low.at[low_rows], dkv_low.at[high_rows], short_two),
        (a_sc, a_sc, side_two),
    ):
        posted.append(
            share_out(local, links, core, zero, one, target, (everything, spans[0]), (everything, spans[1]))
        )
    gain_part, grad = close_rows(h_ref[...], gain_one, grad_middle, from_query, grad_keys, grad_values, wk, wv)
    gains_ref[0:1] = gain_part

    first_f[0].wait()
    first_f[1].wait_send()
    keep_mine.wait()
    send_theirs.wait_send()
    for copy in first_loads:
        copy.wait()
    f_sc[...] = grad.T.astype(LOW)
    both.layer = 2
    posted.append(both(f_sc, f_all, (everything,)))
    send_last = links.push(theirs, rhs_all.at[:, spans[3]], SIBLING)
    gain_part, grad_middle = ffn_back(
        grad, g_sc, u_sc, m_sc, gain_two, wg, wu, wd, mine, theirs, send_last.start
    )
    keep_last = local.move(mine, rhs_all.at[:, spans[2]])
    gains_ref[1:2] = gains_ref[1:2] + gain_part
    dm_ref[...] = grad_middle
    c_ref[...] = grad_middle.T.astype(LOW)
    for keep, copy in posted:
        keep.wait()
        copy.wait()
    first_f[1].wait_recv()
    send_theirs.wait_recv()
    keep_last.wait()
    send_last.wait()
    for copy in (*settle.copies, share.near, share.far, share.forth, *waited):
        copy.wait_send()


def attend_back_kernel(*refs):
    where_ref, dm_ref, wo_ref, q_ref, kv_ref, o_ref, lse_ref, cos_ref, sin_ref, dq_ref, dkv_ref = refs[:11]
    room = refs[11:]
    bias, k_sc, v_sc, kt_sc = room[:4]
    blocks, rows = kv_ref.shape[:2]
    fill_bias(where_ref, bias, rows, blocks)
    lay_back(kv_ref, k_sc, v_sc, kt_sc, blocks, rows, False)
    attend_back(
        dm_ref[...], wo_ref, q_ref, o_ref, lse_ref, cos_ref[...], sin_ref[...], dq_ref, dkv_ref, room, lambda group: None, lambda group: None
    )


def close_keys(total, cosine, sine, dkv_ref):
    starts = range(0, total.shape[0], 2 * HD)
    parts = [total[start : start + HD] for start in starts] + [total[start + HD : start + 2 * HD] for start in starts]
    total = jnp.concatenate(parts, axis=0)
    turned_keys = turned(total[:KV_WIDTH], cosine, sine, -1.0, 1.0)
    dkv_ref[:KV_WIDTH] = turned_keys.astype(LOW)
    dkv_ref[KV_WIDTH:] = total[KV_WIDTH:].astype(LOW)
    return turned_keys.T.astype(LOW), total[KV_WIDTH:].T.astype(LOW)


def close_rows(hidden, gain, grad_middle, from_query, grad_keys, grad_values, wk_ref, wv_ref):
    grad_normed = from_query + nn(grad_keys, wk_ref[...]) + nn(grad_values, wv_ref[...])
    return norm_back(hidden, gain, grad_normed, grad_middle)


def close_kernel(*refs):
    h_ref, gain_one_ref, dm_ref, dq_ref, wq_ref, wk_ref, wv_ref, cos_ref, sin_ref = refs[:9]
    own, near, far, dh_ref, dkv_ref, gain_part_ref = refs[9:]
    total = own[...].astype(HIGH) + near[...].astype(HIGH) + far[...].astype(HIGH)
    grad_keys, grad_values = close_keys(total, cos_ref[...], sin_ref[...], dkv_ref)
    hidden = h_ref[...].astype(HIGH).T
    gain = wide(gain_one_ref)
    from_query = nn(wq_ref[...], dq_ref[...]).T
    gain_part, grad_in = close_rows(hidden, gain, dm_ref[...], from_query, grad_keys, grad_values, wk_ref, wv_ref)
    gain_part_ref[...] = gain_part
    dh_ref[...] = grad_in.T


class Halving:
    def __init__(self, links, steps):
        self.steps = [(links.push(sent, got, to), kept, got) for sent, kept, got, to in steps]

    def start(self):
        self.steps[0][0].start()

    def fold(self, which):
        copy, kept, got = self.steps[which]
        copy.wait_recv()
        total = kept[...].astype(HIGH) + got[...].astype(HIGH)
        if which == len(self.steps) - 1:
            self.done(total)
        else:
            kept[...] = total.astype(kept.dtype)
            self.steps[which + 1][0].start()


class Regather(Halving):
    def share(self, links, held):
        self.held = held
        self.across = links.push(held.at[0, 0], held.at[0, 1], ACROSS)
        self.aside = links.push(held.at[0], held.at[1], SIBLING)

    def done(self, total):
        self.held[0, 0] = total.astype(LOW)
        self.across.start()

    def fold(self, which):
        if which < len(self.steps):
            Halving.fold(self, which)
        elif which == len(self.steps):
            self.across.wait_recv()
            self.aside.start()
        else:
            self.aside.wait_recv()


class Rows:
    def __init__(self, links, whole, side, got, out):
        self.steps = (
            (whole.at[:, :, 1], side, whole.at[:, :, 0], SIDE),
            (whole.at[:, 1, 0], got.at[pl.ds(0, 2)], whole.at[:, 0, 0], BEYOND),
            (whole.at[1, 0, 0], got.at[2], whole.at[0, 0, 0], FAR_SIDE),
            (whole.at[0, 0, 0], got.at[3], None, ACROSS),
            (got.at[4], got.at[5], None, SIBLING),
        )
        self.copies = [links.push(source, target, to) for source, target, _, to in self.steps]
        self.whole, self.got, self.out = whole, got, out

    def start(self):
        self.copies[0].start()

    def fold(self, which):
        self.copies[which].wait_recv()
        if which < 3:
            _, target, kept, _ = self.steps[which]
            kept[...] = kept[...] + target[...]
        elif which == 3:
            self.got[4] = self.whole[0, 0, 0] + self.got[3]
        else:
            self.out[...] = self.got[4] + self.got[5]
        if which < 4:
            self.copies[which + 1].start()


FAR_SIDE = ("dp", 4)


def halved(kind, links, whole, rooms, order):
    where = {"X": 0, "Z1": 1, "Z0": 2, "Y": 3}
    to = {"X": ACROSS, "Z1": FAR_SIDE, "Z0": BEYOND, "Y": SIDE}
    chosen = [slice(None)] * 4
    steps = []
    for axis, room in zip(order, rooms):
        sent, kept = list(chosen), list(chosen)
        sent[where[axis]], kept[where[axis]] = 1, 0
        steps.append((whole.at[tuple(sent)], whole.at[tuple(kept)], room, to[axis]))
        chosen = kept
    return kind(links, steps)


def halving_rooms(block, columns, order):
    left = [2, 2, 2, 2]
    where = {"X": 0, "Z1": 1, "Z0": 2, "Y": 3}
    rooms = []
    for axis in order:
        left[where[axis]] = 0
        rooms.append(pltpu.VMEM(tuple(n for n in left if n) + (block, columns), LOW))
    return rooms


FFN_CUTS = ((0, 256), (256, 384))
ORDERS = (
    ("Z0", "Z1", "Y", "X"),
    ("Y", "X", "Z0", "Z1"),
    ("Y", "Z0", "X", "Z1"),
    ("Y", "X", "Z0", "Z1"),
    ("Z0", "Y", "X", "Z1"),
    ("X", "Z0", "Y", "Z1"),
)
ATTN_ORDERS = (
    ("Y", "Z0", "X", "Z1"),
    ("X", "Z0", "Y", "Z1"),
    ("Z0", "X", "Y", "Z1"),
)
ATTN_CUTS = (128, 256, 256)
PLAN = (
    (("begin",), ()),
    (("w", 0, 1), ()),
    (("w", 0, 0), ()),
    (("w", 1, 1), ()),
    (("w", 1, 0), ()),
    (("w", 5, 1), ()),
    (("w", 5, 0), ()),
    (("w", 2, 1), ()),
    (("w", 2, 0), ()),
    (("w", 4, 1), ()),
    (("w", 4, 0), ()),
    (("prep",), ()),
    (("p", 0), ()),
    (("p", 1), ()),
    (("p", 2), ("f0",)),
    (("p", 3), ()),
    (("p", 4), ()),
    (("q", 0), ()),
    (("q", 1), ()),
    (("q", 2), ("f1", "f5")),
    (("q", 3), ()),
    (("q", 4), ()),
    (("kf",), ("f0", "f4")),
    (("close",), ()),
    (("w", 3, 1), ("f2",)),
    (("w", 3, 0), ()),
    (("attn",), ("f0",)),
    (("tail",), ("f1", "f5", "f0", "f4", "f2", "a1", "a2", "f4", "f3", "f2", "f1", "f4", "a0", "g0", "f2", "a2", "f5", "f1", "a1", "a2", "f3", "f5", "a1", "a0", "g0", "a2", "a0", "a1", "g0", "a2", "f3", "a0", "a2", "a1", "g0", "a0", "a1", "g0", "f3", "a0")),
)
PARTS = len(FFN_CUTS)
COPIES_FINISH = 4 * len(ORDERS) + 6 * len(ATTN_ORDERS) + 5 + 5 + 4


def finish_kernel(*refs):
    where_ref, gain_one_ref, cos_ref, sin_ref, gains_ref = refs[:5]
    late_refs, lse_any = refs[5:14], refs[14]
    a_ref, c_ref, left_two, long_two, short_two, side_two, b_any, f_any, rhs_any = refs[15:24]
    count = 4
    dh_ref, gate_out, up_out, down_out = refs[24:28]
    query_out, key_out, value_out, output_out, gain_out = refs[28:33]
    refs = refs[33:]

    def taken(count):
        nonlocal refs
        first, refs = refs[:count], refs[count:]
        return first

    room = taken(7)
    dq_ref, dkv_ref, dkv_near, dkv_sum, dkv_far, dkv_low = taken(6)
    late = taken(9)
    q_ref, kv_ref, o_ref, wo_ref, dm_ref, h_ref, wq_ref, wk_ref, wv_ref = late
    lse_ref = taken(1)[0]
    b_all, f_all, rhs, left_all, long_all, short_all, side_all = taken(7)
    wholes = taken(len(ORDERS))
    rooms = [taken(4) for _ in ORDERS]
    attn_wholes = taken(len(ATTN_ORDERS))
    attn_rooms = [taken(4) for _ in ATTN_ORDERS]
    attn_alls = taken(len(ATTN_ORDERS))
    gain_whole, gain_got, gain_side, load, send, receive = refs
    rows = h_ref.shape[1]
    block = gate_out.shape[0]
    place = lax.axis_index("dp")
    head_at = lax.axis_index("head")
    core, across = head_at % 2, head_at // 2
    hail((SIBLING, ACROSS, SIDE, BEYOND, FAR_SIDE))
    links, local = Links(send, receive), Local(load)
    sums = {}
    for index, (whole, got, order) in enumerate(zip(wholes, rooms, ORDERS)):
        start, cut = FFN_CUTS[index % PARTS]
        out = (gate_out, up_out, down_out)[index // PARTS].at[:, start : start + cut]
        reduce = halved(Halving, links, whole, got, order)
        reduce.done = functools.partial(out.__setitem__, Ellipsis)
        sums["f%d" % index] = reduce
    for index, (whole, got, order) in enumerate(zip(attn_wholes, attn_rooms, ATTN_ORDERS)):
        reduce = halved(Regather, links, whole, got, order)
        reduce.share(links, attn_alls[index])
        sums["a%d" % index] = reduce
    sums["g0"] = Rows(links, gain_whole, gain_side, gain_got, gain_out)
    seen = {name: 0 for name in sums}
    plan = []
    for step, names in PLAN:
        folds = []
        for name in names:
            folds.append((name, seen[name]))
            seen[name] += 1
        plan.append((step, folds))

    def take(folds):
        for name, which in folds:
            sums[name].fold(which)

    products = [step for step, _ in plan if step[0] == "w"]

    def fetch(turn):
        _, index, half = products[turn]
        start, cut = FFN_CUTS[index % PARTS]
        source = rhs_any.at[2 * (index // PARTS) + half, :, pl.ds(start, cut)]
        return local.move(source, rhs.at[turn % 2, :, pl.ds(0, cut)])

    b_load = local.move(b_any, b_all)
    coming = {0: fetch(0)}
    f_load = local.move(f_any, f_all)
    lates = [local.move(source, target) for source, target in zip(late_refs, late)]
    lates.append(local.move(lse_any, lse_ref))
    two = ((left_two, left_all), (long_two, long_all), (short_two, short_all), (side_two, side_all))
    two_loads = [local.move(source, target.at[:, pl.ds(0, 2 * rows)]) for source, target in two]
    greet((SIBLING, ACROSS, SIDE, BEYOND, FAR_SIDE))
    b_load.wait()

    def lay(product, whole, first):
        for index in range(8):
            relative = jnp.bitwise_xor(index, place)
            whole[first, relative // 4, relative // 2 % 2, relative % 2] = product[
                index * block : (index + 1) * block
            ].astype(LOW)

    f_ready = []

    def multiply(index, half):
        turn = products.index(("w", index, half))
        coming[turn].wait()
        if turn + 1 < len(products):
            coming[turn + 1] = fetch(turn + 1)
        if index >= 2 * PARTS and not f_ready:
            f_load.wait()
            f_ready.append(True)
        cut = FFN_CUTS[index % PARTS][1]
        lay(nn((b_all if index < 2 * PARTS else f_all)[...], rhs[turn % 2, :, :cut]), wholes[index], half)
        if half == (1 if ORDERS[index][0] == "X" else 0):
            sums["f%d" % index].start()

    cosine, sine = cos_ref[...], sin_ref[...]
    settle = Settle(links, dkv_ref, dkv_near, dkv_sum, dkv_far)
    low_rows, own_at, got_at = pl.ds(0, KV_WIDTH), pl.ds(2 * rows, rows), pl.ds(3 * rows, rows)
    high_rows, everything = pl.ds(KV_WIDTH, KV_WIDTH), slice(None)
    passes = {"p": {}, "q": {}}
    for step, folds in plan:
        if step[0] in passes:
            passes[step[0]][step[1]] = folds

    def at_group(which, group):
        for when, folds in passes[which].items():
            if folds:
                pl.when(group == when)(functools.partial(take, folds))
        (settle.between if which == "q" else settle.before)(group)

    for step, folds in plan:
        if step[0] in passes:
            continue
        take(folds)
        if step[0] == "w":
            multiply(step[1], step[2])
        elif step[0] == "prep":
            for copy in lates:
                copy.wait()
            bias, k_sc, v_sc, kt_sc = room[:4]
            fill_bias(where_ref, bias, rows, count)
            lay_back(kv_ref, k_sc, v_sc, kt_sc, count, rows, False)
            attend_back(
                dm_ref[...],
                wo_ref,
                q_ref,
                o_ref,
                lse_ref,
                cosine,
                sine,
                dq_ref,
                dkv_ref,
                room,
                functools.partial(at_group, "p"),
                functools.partial(at_group, "q"),
            )
        elif step[0] == "kf":
            settle.near.start()
            from_query = nn(wq_ref[...], dq_ref[...]).T
            grad_keys, grad_values = close_keys(settle.finish(), cosine, sine, dkv_low)
            swaps = []
            for zero, one, target in (
                (a_ref, c_ref, left_all),
                (dq_ref, o_ref, long_all),
                (dkv_low.at[low_rows], dkv_low.at[high_rows], short_all),
                (a_ref, a_ref, side_all),
            ):
                swaps.append(
                    share_out(local, links, core, zero, one, target, (everything, own_at), (everything, got_at))
                )
        elif step[0] == "close":
            hidden = h_ref[...].astype(HIGH).T
            gain = wide(gain_one_ref)
            gain_part, grad_in = close_rows(
                hidden, gain, dm_ref[...], from_query, grad_keys, grad_values, wk_ref, wv_ref
            )
            dh_ref[...] = grad_in.T
            summed = gains_ref[...] + jnp.concatenate([gain_part, jnp.zeros((7, gain_part.shape[1]), HIGH)], axis=0)
            for index in range(8):
                relative = jnp.bitwise_xor(index, place)
                spot = relative // 4, relative // 2 % 2, relative % 2
                gain_whole[(*spot, slice(None), slice(0, block))] = summed[:, index * block : (index + 1) * block]
                gain_whole[(*spot, slice(None), slice(block, 128))] = jnp.zeros((8, 128 - block), HIGH)
            sums["g0"].start()
        elif step[0] == "attn":
            for copy in two_loads:
                copy.wait()
            for keep, swap_copy in swaps:
                keep.wait()
                swap_copy.wait_recv()
            long_part = nt(left_all[...], long_all[...])
            short_part = nt(side_all[...], short_all[...])
            product = jnp.concatenate([long_part, short_part], axis=1)
            start = 0
            for index, (whole, cut) in enumerate(zip(attn_wholes, ATTN_CUTS)):
                for half in range(2):
                    lay(product[:, start : start + cut], whole, jnp.bitwise_xor(half, across))
                    start += cut
                sums["a%d" % index].start()
    for kind, (long_out, short_out) in enumerate(((query_out, key_out), (output_out, value_out))):
        from_core = jnp.bitwise_xor(kind, core)
        parts = [held[from_core, jnp.bitwise_xor(half, across)] for held in attn_alls for half in range(2)]
        both = jnp.concatenate([part.astype(HIGH) for part in parts], axis=1)
        long_out[...] = both[:, : long_out.shape[1]]
        short_out[...] = both[:, long_out.shape[1] :]
    links.drain()


def emit_kernel(gains, *refs):
    refs, rows = refs[:-2], refs[-2:]
    for index, row in enumerate(rows):
        row[...] = gains[index : index + 1, : row.shape[1]]
    count = len(refs) // 2
    for source, target in zip(refs[:count], refs[count:]):
        target[...] = source[...] if source.shape == target.shape else source[...].T


def call(body, outs, specs, scratch, name, spots=0, collective=None):
    params = {"vmem_limit_bytes": LIMIT}
    if collective is not None:
        params.update(collective_id=collective, has_side_effects=True)
    return pl.pallas_call(
        body,
        out_shape=[jax.ShapeDtypeStruct(shape, kind) for shape, kind in outs],
        in_specs=specs,
        out_specs=[VMEM] * (len(outs) - spots) + [ANY] * spots,
        scratch_shapes=scratch,
        compiler_params=pltpu.CompilerParams(**params),
        name=name,
    )


def swap(value, distance):
    count = lax.axis_size("head")
    return lax.ppermute(value, "head", [(i, i ^ distance) for i in range(count)])


def scatter_rows(value, axis):
    count = lax.axis_size(axis)
    index = lax.axis_index(axis)
    value = value.reshape((count, value.shape[0] // count) + value.shape[1:])
    bit = 1
    while bit < count:
        mine = (index // bit) % 2
        value = value.reshape((value.shape[0] // 2, 2) + value.shape[1:])
        sent = lax.dynamic_index_in_dim(value, 1 - mine, 1, False)
        kept = lax.dynamic_index_in_dim(value, mine, 1, False)
        got = lax.ppermute(sent, axis, [(i, i ^ bit) for i in range(count)])
        value = kept.astype(HIGH) + got.astype(HIGH)
        bit *= 2
        if bit < count:
            value = value.astype(LOW)
    return value[0]


def shards(
    tokens,
    cotangent,
    lengths,
    attn_gain,
    w_query,
    w_key,
    w_value,
    w_output,
    ffn_gain,
    w_gate,
    w_up,
    w_down,
):
    blocks = lax.axis_size("head")
    me = lax.axis_index("head").astype(jnp.int32)
    low_bit = me % 2
    rows, width = tokens.shape
    hidden = w_gate.shape[1]
    keys = blocks * rows
    where = lengths
    frequency = 10000.0 ** (-(jnp.arange(HALF, dtype=HIGH) * 2.0 / HD))
    position = (me * rows + jnp.arange(rows, dtype=jnp.int32)).astype(HIGH)
    angles = frequency[:, None] * position[None, :]
    cosine, sine = jnp.cos(angles), jnp.sin(angles)

    feature_rows = (width, rows)
    project_outs = [(feature_rows, LOW), (feature_rows, LOW), ((blocks, rows, 2 * KV_WIDTH), LOW)]
    tokens, cotangent, w_key, w_value, w_down = (v.T for v in (tokens, cotangent, w_key, w_value, w_down))
    weight_room = [pltpu.VMEM((blocks, width, hidden), LOW)] * 3
    layer_outs = [
        (feature_rows, LOW),
        ((8, PER_GROUP * rows), HIGH),
        ((rows, width), HIGH),
        (feature_rows, LOW),
        ((blocks, rows, hidden), LOW),
        ((blocks, rows, hidden), LOW),
    ]

    attend_outs = [(feature_rows, LOW), ((blocks, 2 * KV_WIDTH, rows), LOW)]
    room = attention_room(blocks, rows, width)
    key_room = [(blocks, 2 * KV_WIDTH, rows), (2, 2 * KV_WIDTH, rows)] + [(2 * KV_WIDTH, rows)] * 3

    def layers():
        outs = [(feature_rows, LOW), (feature_rows, LOW), ((rows, width), HIGH), ((8, width), HIGH)]
        outs += project_outs + layer_outs
        outs += [((width, 4 * rows), LOW)] * 2 + [((6, 4 * rows, hidden), LOW)]
        outs += [((n, 2 * rows), LOW) for n in (width, HQ * HD, KV_WIDTH, width)]
        statistics = pltpu.VMEM((8, PER_GROUP * rows), HIGH)
        scratch = room + [pltpu.VMEM((KV_WIDTH, keys), LOW), pltpu.VMEM(feature_rows, LOW)]
        scratch += [statistics, pltpu.VMEM((rows, width), HIGH)]
        scratch += [pltpu.VMEM(feature_rows, LOW)] * 3 + [pltpu.VMEM((blocks, rows, hidden), LOW)] * 2
        scratch += [pltpu.VMEM((6, rows, hidden), LOW)] * 2 + [pltpu.VMEM(feature_rows, LOW)]
        scratch += [pltpu.VMEM(shape, LOW) for shape in key_room]
        late = (w_key, w_value, w_query, w_output, cotangent)
        scratch += [pltpu.VMEM(v.shape, LOW) for v in late]
        kv_shape = (blocks, rows, 2 * KV_WIDTH)
        scratch += [pltpu.VMEM(shape, LOW) for shape in (feature_rows, feature_rows, kv_shape, kv_shape)]
        scratch += [statistics, statistics, pltpu.VMEM((rows, width), HIGH)]
        scratch += weight_room + [pltpu.SemaphoreType.DMA((LOCALS_MIDDLE,))]
        scratch += [pltpu.SemaphoreType.DMA((COPIES_MIDDLE,)), pltpu.SemaphoreType.DMA((COPIES_MIDDLE,))]
        given = [where, tokens, attn_gain, ffn_gain, cosine, sine, *late, w_gate, w_up, w_down]
        specs = [SMEM] + [VMEM] * 5 + [ANY] * 8
        return call(functools.partial(layers_kernel, blocks), outs, specs, scratch, "layers", 16, 3)(*given)

    outs = layers()
    block_out, c_one, dm_one, gains, a_one, q_one, kv_one, o_one, lse_one = outs[:9]
    b_all, f_all, rhs_all, *halves_two = outs[13:]

    def close(h, grad_middle, grad_query, partial):
        sent = swap(jnp.stack([partial[1], partial[3]]), 1)
        far = swap((partial[2].astype(HIGH) + sent[1].astype(HIGH)).astype(LOW), 2)
        outs = [(feature_rows, HIGH), ((2 * KV_WIDTH, rows), LOW), ((1, width), HIGH)]
        given = [h, attn_gain, grad_middle, grad_query, w_query, w_key, w_value, cosine, sine]
        given += [partial[0], sent[0], far]
        return call(close_kernel, outs, [VMEM] * 12, [], "close")(*given)

    def beside(parts):
        return jnp.concatenate(parts, axis=-1)

    def choose(zero, one):
        return jnp.where(low_bit == 0, zero, one)

    def halves(a, c, o, dq, dkv):
        dk, dv = dkv[:KV_WIDTH], dkv[KV_WIDTH:]
        left = [choose(a, c), swap(choose(c, a), 1)]
        long = [choose(dq, o), swap(choose(o, dq), 1)]
        short = [choose(dk, dv), swap(choose(dv, dk), 1)]
        return beside(left), beside(long), beside(short), beside([a, swap(a, 1)])

    places = lax.axis_size("dp")
    block = width // places

    def finish():
        outs = [(feature_rows, HIGH)] + [((block, hidden), HIGH)] * 3
        outs += [((block, n), HIGH) for n in (HQ * HD, KV_WIDTH, KV_WIDTH, HQ * HD)] + [((8, 128), HIGH)]
        late = (q_one, kv_one, o_one, w_output, dm_one, tokens, w_query, w_key, w_value)
        scratch = room + [pltpu.VMEM(shape, LOW) for shape in [feature_rows] + key_room]
        scratch += [pltpu.VMEM(v.shape, v.dtype) for v in late] + [pltpu.VMEM(lse_one.shape, HIGH)]
        low_room = []
        low_room += [(width, 4 * rows), (width, 4 * rows), (2, 4 * rows, max(n for _, n in FFN_CUTS))]
        low_room += [(width, 4 * rows), (width, 4 * rows), (KV_WIDTH, 4 * rows), (width, 4 * rows)]
        low_room += [(2, 2, 2, 2, block, FFN_CUTS[i % PARTS][1]) for i in range(len(ORDERS))]
        scratch += [pltpu.VMEM(shape, LOW) for shape in low_room]
        for index, order in enumerate(ORDERS):
            scratch += halving_rooms(block, FFN_CUTS[index % PARTS][1], order)
        scratch += [pltpu.VMEM((2, 2, 2, 2, block, cut), LOW) for cut in ATTN_CUTS]
        for order, cut in zip(ATTN_ORDERS, ATTN_CUTS):
            scratch += halving_rooms(block, cut, order)
        scratch += [pltpu.VMEM((2, 2, block, cut), LOW) for cut in ATTN_CUTS]
        scratch += [pltpu.VMEM(shape, HIGH) for shape in ((2, 2, 2, 8, 128), (8, 8, 128), (2, 2, 8, 128))]
        scratch += [pltpu.SemaphoreType.DMA((48,)), pltpu.SemaphoreType.DMA((COPIES_FINISH,))]
        scratch += [pltpu.SemaphoreType.DMA((COPIES_FINISH,))]
        given = [where, attn_gain, cosine, sine, gains, *late, lse_one, a_one, c_one, *halves_two]
        specs = [SMEM] + [VMEM] * 4 + [ANY] * 19
        return call(finish_kernel, outs, specs, scratch, "finish", 0, 2)(*given, b_all, f_all, rhs_all)

    if places == 8 and blocks == 4:
        outs = finish()
        input_grad, gate_grad, up_grad, down_grad, query_grad, key_grad, value_grad, output_grad, gains = outs
        results = [block_out, input_grad, query_grad, key_grad, value_grad, output_grad, gate_grad, up_grad, down_grad]
        turned_over = (3, 4, 5)
        outs = [(v.shape[::-1] if i in turned_over else v.shape, v.dtype) for i, v in enumerate(results)]
        outs += [((1, block), HIGH)] * 2
        *results, one, two = call(emit_kernel, outs, [VMEM] * (len(results) + 1), [], "emit")(gains, *results)
        gains = one[0], two[0]
        block_out, input_grad, query_grad, key_grad, value_grad, output_grad, gate_grad, up_grad, down_grad = results
        key_grad, value_grad, output_grad = key_grad.T, value_grad.T, output_grad.T
    else:
        given = [where, dm_one, w_output, q_one, kv_one, o_one, lse_one, cosine, sine]
        dq_one, part_one = call(attend_back_kernel, attend_outs, [SMEM] + [VMEM] * 8, room, "attend_back")(*given)
        input_grad, dkv_one, gain_one_a = close(tokens, dm_one, dq_one, part_one)
        kept, sent = [], []
        for which in range(6):
            product = nn(b_all if which < 4 else f_all, rhs_all[which]).astype(LOW)
            (sent if which % 2 else kept).append(product)
        got = swap(beside(sent), 2)
        ffn = scatter_rows((beside(kept).astype(HIGH) + got.astype(HIGH)).astype(LOW), "dp")
        halves_one = halves(a_one, c_one, o_one, dq_one, dkv_one)
        left, long, short, side = (beside(pair) for pair in zip(halves_two, halves_one))
        attn = scatter_rows(beside([nt(left, long), nt(side, short)]).astype(LOW), "dp").astype(LOW)
        attn = (attn.astype(HIGH) + swap(attn, 2).astype(HIGH)).astype(LOW)
        other = swap(attn, 1)
        zero, one = choose(attn, other).astype(HIGH), choose(other, attn).astype(HIGH)
        gains = jnp.concatenate([gains[:1] + gain_one_a, gains[1:2]], axis=0)
        gains = lax.psum_scatter(lax.psum(gains, "head"), "dp", scatter_dimension=1, tiled=True)
        query_grad, key_grad = zero[:, : HQ * HD], zero[:, HQ * HD :]
        output_grad, value_grad = one[:, : HQ * HD], one[:, HQ * HD :]
        gate_grad, up_grad, down_grad = (ffn[:, i * hidden : (i + 1) * hidden] for i in range(3))
    return (
        block_out.T,
        input_grad.T,
        gains[0],
        query_grad,
        key_grad,
        value_grad,
        output_grad.T,
        gains[1],
        gate_grad,
        up_grad,
        down_grad.T,
    )


def solution(mesh):
    return jax.shard_map(
        shards,
        mesh=mesh,
        in_specs=(
            P(("dp", "head"), None),
            P(("dp", "head"), None),
            P("dp"),
            P(),
            P(),
            P(),
            P(),
            P(),
            P(),
            P(None, "head"),
            P(None, "head"),
            P("head", None),
        ),
        out_specs=(
            P(("dp", "head"), None),
            P(("dp", "head"), None),
            P("dp"),
            P("dp", None),
            P("dp", None),
            P("dp", None),
            P(None, "dp"),
            P("dp"),
            P("dp", "head"),
            P("dp", "head"),
            P("head", "dp"),
        ),
        check_vma=False,
    )
```
